32 devices in a mesh: dp: 8 (over z, x), tensor: 4 (over y, core).
Axes of the slice: x: 2, y: 2, z: 4, core: 2. Of those that a mesh axis runs over, the one named last changes fastest.
Arguments:
- inputs: bfloat16 [12288, 1280], P(('dp', 'tensor')), may hold values from -6 to 6
- lengths: int32 [8], P('dp'), may hold values from 1153 to 1536, as said below
- cotangent: bfloat16 [12288, 1280], P(('dp', 'tensor')), may hold values from -6 to 6
- w_qkv: float32 [1280, 3, 1280], P('dp', None, 'tensor')
- w_out: float32 [1280, 1280], P('dp', 'tensor')
- w_up: float32 [1280, 5120], P('dp', 'tensor')
- w_down: float32 [1280, 5120], P('dp', 'tensor')
- vectors: float32 [1280, 6], P('dp')
- bias_qkv: float32 [1280, 2], P(('tensor', 'dp')), may hold values from -1.8 to 1.8
- bias_up: float32 [5120], P(('tensor', 'dp')), may hold values from -1.8 to 1.8
- mom_qkv: float32 [1280, 3, 1280], P('dp', None, 'tensor'), may hold values from -665.1075 to 665.1075
- mom_out: float32 [1280, 1280], P('dp', 'tensor'), may hold values from -133.0215 to 133.0215
- mom_up: float32 [1280, 5120], P('dp', 'tensor'), may hold values from -199.53226 to 199.53226
- mom_down: float32 [1280, 5120], P('dp', 'tensor'), may hold values from -399.0645 to 399.0645
- mom_vectors: float32 [1280, 6], P('dp'), may hold values from -665.1075 to 665.1075
- mom_bias_qkv: float32 [1280, 2], P(('tensor', 'dp')), may hold values from -665.1075 to 665.1075
- mom_bias_up: float32 [5120], P(('tensor', 'dp')), may hold values from -199.53226 to 199.53226
Outputs:
- output: float32 [12288, 1280], P(('dp', 'tensor'))
- input_grad: float32 [12288, 1280], P(('dp', 'tensor'))
- new_w_qkv: float32 [1280, 3, 1280], P('dp', None, 'tensor')
- new_w_out: float32 [1280, 1280], P('dp', 'tensor')
- new_w_up: float32 [1280, 5120], P('dp', 'tensor')
- new_w_down: float32 [1280, 5120], P('dp', 'tensor')
- new_vectors: float32 [1280, 6], P('dp')
- new_bias_qkv: float32 [1280, 2], P(('tensor', 'dp'))
- new_bias_up: float32 [5120], P(('tensor', 'dp'))
- new_mom_qkv: float32 [1280, 3, 1280], P('dp', None, 'tensor')
- new_mom_out: float32 [1280, 1280], P('dp', 'tensor')
- new_mom_up: float32 [1280, 5120], P('dp', 'tensor')
- new_mom_down: float32 [1280, 5120], P('dp', 'tensor')
- new_mom_vectors: float32 [1280, 6], P('dp')
- new_mom_bias_qkv: float32 [1280, 2], P(('tensor', 'dp'))
- new_mom_bias_up: float32 [5120], P(('tensor', 'dp'))
The draws below stay inside these ranges and needn't reach their ends.
Inputs may be any that keep to these rules, and one draw needn't show every extreme that they name: `lengths`: frames of a clip at positions below its length are keys; every clip is longer than three quarters of 1536, and one clip has exactly 1536.
All inputs are finite; a program needn't handle non-finite values.
Results may differ from the reference program's by a relative error of at most 0.018.
The reference program's roundings to bfloat16 on the way count: a program that leaves them out, or rounds other values in their place, can miss the bound.
Values may be sent and summed in bfloat16 or wider, within the bound.
No kernel may reach another device: no remote copies, remote signals or barrier semaphores. Data moves between devices by JAX's collectives and lax.ppermute only.
A program may use at most 256 MiB of HBM per device.

```python
import math
import jax
import jax.numpy as jnp
from jax import lax

D = 1280
HEADS = 16
HD = 80
FF = 5120
SWEEPS = 5
FRAMES = 1536
CLIPS = 8
TOKENS = 12288
ROW_BLOCK = 160
Q_BLOCK = 512


def rising(count, start_val, end_val):
    steps_along = jnp.arange(count, dtype=jnp.float32) / max(count - 1, 1)
    return start_val + (end_val - start_val) * steps_along


def draw_lengths(key, part):
    key = jax.random.fold_in(key, 5)
    first_key, second_key = jax.random.split(key)
    drawn = jax.random.randint(first_key, (CLIPS,), 3 * FRAMES // 4 + 1, FRAMES + 1)
    chosen = jax.random.randint(second_key, (), 0, CLIPS)
    return jnp.where(jnp.arange(CLIPS) == chosen, FRAMES, drawn).astype(jnp.int32)


def draw_w_qkv(key, part):
    key = jax.random.fold_in(key, 11)
    noise_vals = jax.random.normal(key, (D, 3, D), jnp.float32)
    ramp_lo, ramp_hi = (0.6, 1.8)
    sharp = jnp.full((D,), 1.4142135, jnp.float32)
    column_scale = jnp.stack([sharp, sharp, rising(D, ramp_lo, ramp_hi)])
    return noise_vals * column_scale[None, :, :] / jnp.sqrt(jnp.float32(D))


def draw_w_out(key, part):
    key = jax.random.fold_in(key, 13)
    noise_vals = jax.random.normal(key, (D, D), jnp.float32)
    ramp_lo, ramp_hi = (0.6, 1.8)
    return noise_vals * rising(D, ramp_lo, ramp_hi)[None, :] * 4.0 / jnp.sqrt(jnp.float32(D))


def draw_w_up(key, part):
    key = jax.random.fold_in(key, 17)
    noise_vals = jax.random.normal(key, (D, FF), jnp.float32)
    ramp_lo, ramp_hi = (0.6, 1.8)
    return noise_vals * rising(FF, ramp_lo, ramp_hi)[None, :] / jnp.sqrt(jnp.float32(D))


def draw_w_down(key, part):
    key = jax.random.fold_in(key, 19)
    noise_vals = jax.random.normal(key, (D, FF), jnp.float32)
    ramp_lo, ramp_hi = (0.6, 1.8)
    return noise_vals * rising(FF, ramp_lo, ramp_hi)[None, :] / jnp.sqrt(jnp.float32(FF))


def draw_vectors(key, part):
    key = jax.random.fold_in(key, 23)
    noise_vals = jax.random.normal(key, (D, 6), jnp.float32)
    spreads = jnp.array([0.25, 0.3, 0.3, 0.25, 0.3, 0.3], jnp.float32)
    centers = jnp.array([1.0, 0.0, 0.0, 1.0, 0.0, 0.0], jnp.float32)
    return centers[None, :] + spreads[None, :] * noise_vals


def level_of(key, shape, shards, smallest, top_value):
    level, own = 1.0, jax.random.fold_in(key, 6)
    for position, shards_of in shards:
        steps = jnp.exp(jax.random.uniform(jax.random.fold_in(own, position), (shards_of,), jnp.float32, smallest / len(shards), top_value / len(shards)))
        level = level * jnp.repeat(steps, shape[position] // shards_of).reshape([-1 if axis == position else 1 for axis in range(len(shape))])
    return level


def scatter_about(rng, extent, width, bound, cuts=(), kind=jnp.bfloat16):
    level = level_of(rng, extent, cuts, -0.22, 0.18) if cuts else 1.0
    entries = jax.random.normal(rng, extent, jnp.float32) * width * level
    return jnp.minimum(jnp.maximum(entries, -bound), bound).astype(kind)


def setup_inputs(seed: int = 0) -> dict:
    arg_keys = jax.random.split(jax.random.key(seed), 18)
    return {
        "inputs": scatter_about(arg_keys[0], (TOKENS, D), 1.0, 6.0, ((0, 32),)),
        "lengths": draw_lengths(jax.random.fold_in(arg_keys[17], 71), 0),
        "cotangent": scatter_about(arg_keys[2], (TOKENS, D), 1.0, 6.0, ((0, 32),)),
        "w_qkv": draw_w_qkv(jax.random.fold_in(arg_keys[17], 71), 0),
        "w_out": draw_w_out(jax.random.fold_in(arg_keys[17], 71), 0),
        "w_up": draw_w_up(jax.random.fold_in(arg_keys[17], 71), 0),
        "w_down": draw_w_down(jax.random.fold_in(arg_keys[17], 71), 0),
        "vectors": draw_vectors(jax.random.fold_in(arg_keys[17], 71), 0),
        "bias_qkv": scatter_about(arg_keys[8], (D, 2), 0.3, 1.8, ((0, 32),), jnp.float32),
        "bias_up": scatter_about(arg_keys[9], (FF,), 0.3, 1.8, ((0, 32),), jnp.float32),
        "mom_qkv": scatter_about(arg_keys[10], (D, 3, D), (TOKENS ** 0.5), 665.1075, ((0, 8), (2, 4)), jnp.float32),
        "mom_out": scatter_about(arg_keys[11], (D, D), (0.2 * TOKENS ** 0.5), 133.0215, ((0, 8), (1, 4)), jnp.float32),
        "mom_up": scatter_about(arg_keys[12], (D, FF), (0.3 * TOKENS ** 0.5), 199.53226, ((0, 8), (1, 4)), jnp.float32),
        "mom_down": scatter_about(arg_keys[13], (D, FF), (0.6 * TOKENS ** 0.5), 399.0645, ((0, 8), (1, 4)), jnp.float32),
        "mom_vectors": scatter_about(arg_keys[14], (D, 6), (TOKENS ** 0.5), 665.1075, ((0, 8),), jnp.float32),
        "mom_bias_qkv": scatter_about(arg_keys[15], (D, 2), (TOKENS ** 0.5), 665.1075, ((0, 32),), jnp.float32),
        "mom_bias_up": scatter_about(arg_keys[16], (FF,), (0.3 * TOKENS ** 0.5), 199.53226, ((0, 32),), jnp.float32),
    }


HIGHEST = lax.Precision.HIGHEST
NORM_EPS = 1e-05
POLAR_EPS = 1e-07
MASKED = -1e+30
QUINTIC_A = 3.4445
QUINTIC_B = -4.775
QUINTIC_C = 2.0315
MUON_DECAY = 0.95
VEC_DECAY = 0.9
VEC_RATE = 0.1
STEP_QKV = 0.5 * math.sqrt(3.0)
STEP_OUT = 2.0
STEP_UP = 1.0
STEP_DOWN = 0.5

@jax.custom_vjp
def low(v):
    return lax.optimization_barrier(v.astype(jnp.bfloat16)).astype(jnp.float32)

@jax.custom_vjp
def low_back(v):
    return v

def low_keep(v):
    return (low(v), None)

def low_pass(kept, grad):
    return (grad,)

def back_keep(v):
    return (v, None)

def back_low(kept, grad):
    return (low(grad),)
low.defvjp(low_keep, low_pass)
low_back.defvjp(back_keep, back_low)

def layer_norm(values, gain, shift):
    center = values - lax.optimization_barrier(jnp.mean(values, axis=-1, keepdims=True))
    spread = lax.optimization_barrier(jnp.mean(center * center, axis=-1, keepdims=True))
    return center * lax.rsqrt(spread + NORM_EPS) * gain + shift

def matmul_high(left, right):
    return jnp.dot(left, right, precision=HIGHEST)

def clip_layer(params, clip_rows, clip_length):
    w_qkv, w_out, w_up, w_down, vectors, bias_qkv, bias_up = params
    frames = clip_rows.shape[0]
    score_scale = 1.0 / math.sqrt(HD)
    attn_in = low(layer_norm(clip_rows, vectors[:, 0], vectors[:, 1]))
    projected = matmul_high(attn_in, w_qkv.reshape(D, 3 * D)).reshape(frames, 3, D)
    bias_rows = jnp.stack([bias_qkv[:, 0], jnp.zeros((D,), jnp.float32), bias_qkv[:, 1]])
    qkv_rows = low_back(low(projected + bias_rows))
    queries = qkv_rows[:, 0].reshape(frames, HEADS, HD)
    key_side = qkv_rows[:, 1].reshape(frames, HEADS, HD)
    value_side = qkv_rows[:, 2].reshape(frames, HEADS, HD)
    key_valid = (jnp.arange(frames) < clip_length)[None, None, :]

    def attend(q_part):
        scores = low_back(jnp.einsum('qhd,khd->hqk', q_part, key_side, precision=HIGHEST))
        logits = jnp.where(key_valid, scores * score_scale, MASKED)
        prob_low = low(jax.nn.softmax(logits, axis=-1))
        return jnp.einsum('hqk,khd->qhd', prob_low, value_side, precision=HIGHEST)
    blocks = queries.reshape(frames // Q_BLOCK, Q_BLOCK, HEADS, HD)
    attended = lax.map(jax.checkpoint(attend), blocks).reshape(frames, D)
    attended = low_back(low(attended))
    residual = clip_rows + low_back(matmul_high(attended, w_out.T)) + vectors[:, 2]
    mlp_in = low(layer_norm(residual, vectors[:, 3], vectors[:, 4]))
    pre_act = low_back(matmul_high(mlp_in, w_up) + bias_up)
    hidden = low(jax.nn.gelu(pre_act, approximate=False))
    return residual + low_back(matmul_high(hidden, w_down.T)) + vectors[:, 5]

def polar_block(block):
    iterate = block / (jnp.sqrt(jnp.sum(block * block)) + POLAR_EPS)
    for sweep_index in range(SWEEPS):
        gram = jnp.dot(iterate, iterate.T, precision=HIGHEST)
        polynomial = QUINTIC_B * gram + QUINTIC_C * jnp.dot(gram, gram, precision=HIGHEST)
        iterate = QUINTIC_A * iterate + jnp.dot(polynomial, iterate, precision=HIGHEST)
    return iterate

def muon_step(weight, moment, gradient, factor):
    row_count = weight.shape[0]
    flat_grad = gradient.reshape(row_count, -1)
    moment_new = MUON_DECAY * moment.reshape(row_count, -1) + flat_grad
    update = flat_grad + MUON_DECAY * moment_new
    blocks = update.reshape(row_count // ROW_BLOCK, ROW_BLOCK, -1)
    polar = lax.map(polar_block, blocks).reshape(row_count, -1)
    new_weight = weight.reshape(row_count, -1) - factor * polar
    return (new_weight.reshape(weight.shape), moment_new.reshape(weight.shape))

def reference(inputs, lengths, cotangent, w_qkv, w_out, w_up, w_down, vectors, bias_qkv, bias_up, mom_qkv, mom_out, mom_up, mom_down, mom_vectors, mom_bias_qkv, mom_bias_up):
    weights = (w_qkv, w_out, w_up, w_down, vectors, bias_qkv, bias_up)

    def forward(params, values):
        rounded = tuple((low(param) for param in params))
        clips = values.reshape(CLIPS, FRAMES, D)

        def one_clip(item):
            return clip_layer(rounded, item[0], item[1])
        outs = lax.map(jax.checkpoint(one_clip), (clips, lengths))
        return outs.reshape(TOKENS, D)
    output, backward = jax.vjp(forward, weights, inputs.astype(jnp.float32))
    grads, input_grad = backward(cotangent.astype(jnp.float32))
    g_qkv, g_out, g_up, g_down, g_vectors, g_bias_qkv, g_bias_up = grads
    new_w_qkv, new_mom_qkv = muon_step(w_qkv, mom_qkv, g_qkv, STEP_QKV)
    new_w_out, new_mom_out = muon_step(w_out, mom_out, g_out, STEP_OUT)
    new_w_up, new_mom_up = muon_step(w_up, mom_up, g_up, STEP_UP)
    new_w_down, new_mom_down = muon_step(w_down, mom_down, g_down, STEP_DOWN)
    vec_rate = VEC_RATE / math.sqrt(TOKENS)
    new_mom_vectors = VEC_DECAY * mom_vectors + g_vectors
    new_mom_bias_qkv = VEC_DECAY * mom_bias_qkv + g_bias_qkv
    new_mom_bias_up = VEC_DECAY * mom_bias_up + g_bias_up
    new_vectors = vectors - vec_rate * new_mom_vectors
    new_bias_qkv = bias_qkv - vec_rate * new_mom_bias_qkv
    new_bias_up = bias_up - vec_rate * new_mom_bias_up
    return (output, input_grad, new_w_qkv, new_w_out, new_w_up, new_w_down, new_vectors, new_bias_qkv, new_bias_up, new_mom_qkv, new_mom_out, new_mom_up, new_mom_down, new_mom_vectors, new_mom_bias_qkv, new_mom_bias_up)
```

```python
from functools import partial
import math

import jax
import jax.numpy as jnp
from jax import lax
from jax.experimental import pallas as pl
from jax.experimental.pallas import tpu as pltpu
from jax.sharding import PartitionSpec as P

HD = 80
SWEEPS = 5
LANES = 128
WINDOW = 256
BIAS_LANE = WINDOW - 1
VMEM_LIMIT = 58 * 1024 * 1024

HIGHEST = lax.Precision.HIGHEST
NORM_EPS = 1e-05
POLAR_EPS = 1e-07
MASKED = -1e30
QUINTIC_A = 3.4445
QUINTIC_B = -4.775
QUINTIC_C = 2.0315
MUON_DECAY = 0.95
VEC_DECAY = 0.9
VEC_RATE = 0.1
STEP_QKV = 0.5 * math.sqrt(3.0)
STEP_OUT = 2.0
STEP_UP = 1.0
STEP_DOWN = 0.5
LOG2E = math.log2(math.e)
SCORE_SCALE = 1.0 / math.sqrt(HD)
F32 = jnp.float32
BF16 = jnp.bfloat16
LITTLE = pl.CostEstimate(flops=1_000_000, bytes_accessed=100_000, transcendentals=0)
NN = (((1,), (0,)), ((), ()))
NT = (((1,), (1,)), ((), ()))
TN = (((0,), (0,)), ((), ()))


def mm(left, right, dims=NN):
    return lax.dot_general(left, right, dims, preferred_element_type=F32)


def norm_parts(values):
    center = values - jnp.mean(values, axis=-1, keepdims=True)
    spread = jnp.mean(center * center, axis=-1, keepdims=True)
    scale = lax.rsqrt(spread + NORM_EPS)
    return center * scale, scale


def norm_back(grad, gain, unit, scale):
    inner = grad * gain
    mean_grad = jnp.mean(inner, axis=-1, keepdims=True)
    mean_unit = jnp.mean(inner * unit, axis=-1, keepdims=True)
    return scale * (inner - mean_grad - unit * mean_unit)


def params(*semantics):
    return pltpu.CompilerParams(
        dimension_semantics=semantics or None, vmem_limit_bytes=VMEM_LIMIT
    )


def swap(value, axis, mask):
    size = lax.axis_size(axis)
    return lax.ppermute(value, axis, [(i, i ^ mask) for i in range(size)])


def tensor_slots(own):
    near = swap(own, "tensor", 1)
    far = swap(own, "tensor", 2)
    return [own, near, far, swap(far, "tensor", 1)]


def tensor_gather(own):
    return jnp.concatenate(tensor_slots(own), axis=0)


def tensor_sum(value):
    value = value + swap(value, "tensor", 1)
    return value + swap(value, "tensor", 2)


def pair_sum(own, sent):
    arrived = swap(sent, "tensor", 1)
    return (own.astype(F32) + arrived.astype(F32)).astype(BF16)


def near_swap(sent):
    rows = sent.shape[0] // 2
    return jnp.concatenate(
        [swap(sent[:rows], "tensor", 1), swap(sent[rows:], "tensor", 1)], axis=0
    )


def after(value, *others):
    return lax.optimization_barrier((value, *others))[0]


def qkv_body(x_ref, vec_ref, w_ref, bias_ref, attn_ref, qkv_ref):
    unit, _ = norm_parts(x_ref[...].astype(F32))
    attn_in = (unit * vec_ref[0:1, :] + vec_ref[1:2, :]).astype(BF16)
    attn_ref[...] = attn_in
    qkv_ref[...] = (mm(attn_in, w_ref[...]) + bias_ref[0:1, :]).astype(BF16)


def qkv_call(x_rows, vec_rows, weight, bias, block):
    rows, width = x_rows.shape
    columns = weight.shape[1]
    return pl.pallas_call(
        qkv_body,
        grid=(rows // block,),
        in_specs=[
            pl.BlockSpec((block, width), lambda i: (i, 0)),
            pl.BlockSpec(vec_rows.shape, lambda i: (0, 0)),
            pl.BlockSpec(weight.shape, lambda i: (0, 0)),
            pl.BlockSpec(bias.shape, lambda i: (0, 0)),
        ],
        out_specs=[
            pl.BlockSpec((block, width), lambda i: (i, 0)),
            pl.BlockSpec((block, columns), lambda i: (i, 0)),
        ],
        out_shape=[
            jax.ShapeDtypeStruct((rows, width), BF16),
            jax.ShapeDtypeStruct((rows, columns), BF16),
        ],
        compiler_params=params("arbitrary"),
        cost_estimate=LITTLE,
        name="norm_qkv",
    )(x_rows, vec_rows, weight, bias)


def rows_body(dims, x_ref, w_ref, out_ref):
    out_ref[...] = mm(x_ref[...], w_ref[...], dims).astype(out_ref.dtype)


def rows_mm(x_rows, weight, dims, kind, block, first=0, count=None):
    rows, depth = x_rows.shape
    count = rows if count is None else count
    columns = weight.shape[1 - dims[0][1][0]]
    base = first // block
    return pl.pallas_call(
        partial(rows_body, dims),
        grid=(count // block,),
        in_specs=[
            pl.BlockSpec((block, depth), lambda i: (i + base, 0)),
            pl.BlockSpec(weight.shape, lambda i: (0, 0)),
        ],
        out_specs=pl.BlockSpec((block, columns), lambda i: (i, 0)),
        out_shape=jax.ShapeDtypeStruct((count, columns), kind),
        compiler_params=params("arbitrary"),
        cost_estimate=LITTLE,
        name="rows_product",
    )(x_rows, weight)


def sum_body(steps, *refs):
    lefts, (right_ref, out_ref, total) = refs[:-3], refs[-3:]
    step = pl.program_id(0)
    for index, left_ref in enumerate(lefts):

        @pl.when(step // steps == index)
        def _():
            term = mm(left_ref[...], right_ref[...], TN)
            if index:
                total[...] += term
            else:

                @pl.when(step == 0)
                def _():
                    total[...] = term

                @pl.when(step > 0)
                def _():
                    total[...] += term

    @pl.when(step == pl.num_programs(0) - 1)
    def _():
        out_ref[...] = total[...].astype(BF16)


def sum_mm(lefts, right, block):
    rows, width = lefts[0].shape
    columns = right.shape[1]
    steps = rows // block

    def spot(index):
        return lambda i: (jnp.clip(i - index * steps, 0, steps - 1), 0)

    return pl.pallas_call(
        partial(sum_body, steps),
        grid=(steps * len(lefts),),
        in_specs=[pl.BlockSpec((block, width), spot(index)) for index in range(len(lefts))]
        + [pl.BlockSpec((block, columns), lambda i: (i, 0))],
        out_specs=pl.BlockSpec((width, columns), lambda i: (0, 0)),
        out_shape=jax.ShapeDtypeStruct((width, columns), BF16),
        scratch_shapes=[pltpu.VMEM((width, columns), F32)],
        compiler_params=params("arbitrary"),
        cost_estimate=LITTLE,
        name="sum_product",
    )(*lefts, right)


def head_place(head):
    start = 0 if head * HD + HD <= BIAS_LANE else LANES
    return start, head * HD - start


def lane_mask(rows, head):
    _, offset = head_place(head)
    lane = lax.broadcasted_iota(jnp.int32, (rows, WINDOW), 1)
    return (lane >= offset) & (lane < offset + HD), lane == BIAS_LANE


def window(value, head):
    start, _ = head_place(head)
    return value[:, start : start + WINDOW].astype(F32)


def key_columns(qkv_ref):
    third = (qkv_ref.shape[1] + LANES) // 3
    return qkv_ref[:, third : 2 * third]


def value_columns(qkv_ref):
    third = (qkv_ref.shape[1] + LANES) // 3
    tail = qkv_ref[:, qkv_ref.shape[1] - third :].astype(F32)
    return pltpu.roll(tail, third - LANES // 2, 1)


def fill_keys(qkv_ref, bias_ref, keys_out, heads):
    columns = key_columns(qkv_ref)
    for head in range(heads):
        inside, last = lane_mask(columns.shape[0], head)
        picked = jnp.where(inside, window(columns, head), 0.0)
        keys_out[head] = jnp.where(last, bias_ref[...], picked).astype(BF16)


def join_windows(parts):
    low, high = None, None
    for head, part in enumerate(parts):
        if head_place(head)[0] == 0:
            low = part if low is None else low + part
        else:
            high = part if high is None else high + part
    return jnp.concatenate(
        [low[:, :LANES], low[:, LANES:] + high[:, :LANES], high[:, LANES:]], axis=1
    )


def attn_body(heads, q_ref, qkv_ref, bias_ref, wo_ref, *rest):
    att_ref, part_ref, lse_ref, keys, vals = rest[-5:]
    block = q_ref.shape[0]
    frames = qkv_ref.shape[0]

    @pl.when(pl.program_id(0) == 0)
    def _():
        fill_keys(qkv_ref, bias_ref, keys, heads)
        columns = value_columns(qkv_ref)
        for head in range(heads):
            inside, _ = lane_mask(frames, head)
            vals[head] = jnp.where(inside, window(columns, head), 0.0).astype(BF16)

    log_scale = SCORE_SCALE * LOG2E
    outs = []
    lane = lax.broadcasted_iota(jnp.int32, (block, LANES), 1)
    lse_cols = jnp.zeros((block, LANES), F32)
    for head in range(heads):
        _, last = lane_mask(block, head)
        query = jnp.where(last, 1.0, window(q_ref, head)).astype(BF16)
        scores = mm(query, keys[head], NT)
        row_max = jnp.max(scores, axis=1, keepdims=True)
        powers = jnp.exp2((scores - row_max) * log_scale)
        totals = jnp.sum(powers, axis=1, keepdims=True)
        outs.append(mm(powers.astype(BF16), vals[head]) * (1.0 / totals))
        lse_cols = jnp.where(lane == head, row_max * log_scale + jnp.log2(totals), lse_cols)
    attended = join_windows(outs).astype(BF16)
    att_ref[...] = attended
    lse_ref[...] = jnp.transpose(lse_cols)[:8]
    part_ref[...] = mm(attended, wo_ref[...], NT).astype(BF16)


def attn_call(heads, qkv, key_bias, wo, block, first, count, earlier=None):
    frames = qkv.shape[0]
    part_width = wo.shape[1]
    width = wo.shape[0]
    held = [] if earlier is None else list(earlier)
    base = first // block
    return pl.pallas_call(
        partial(attn_body, heads),
        grid=(count // block,),
        in_specs=[
            pl.BlockSpec((block, part_width), lambda i: (i + base, 0)),
            pl.BlockSpec(qkv.shape, lambda i: (0, 0)),
            pl.BlockSpec(key_bias.shape, lambda i: (0, 0)),
            pl.BlockSpec(wo.shape, lambda i: (0, 0)),
        ]
        + [pl.BlockSpec(memory_space=pl.ANY)] * len(held),
        out_specs=[
            pl.BlockSpec((block, part_width), lambda i: (i + base, 0)),
            pl.BlockSpec((block, width), lambda i: (i, 0)),
            pl.BlockSpec((8, block), lambda i: (0, i + base)),
        ],
        out_shape=[
            jax.ShapeDtypeStruct((frames, part_width), BF16),
            jax.ShapeDtypeStruct((count, width), BF16),
            jax.ShapeDtypeStruct((8, frames), F32),
        ],
        scratch_shapes=[
            pltpu.VMEM((heads, frames, WINDOW), BF16),
            pltpu.VMEM((heads, frames, WINDOW), BF16),
        ],
        input_output_aliases={} if earlier is None else {4: 0, 5: 2},
        compiler_params=params("arbitrary"),
        cost_estimate=LITTLE,
        name="attn_fwd",
    )(qkv, qkv, key_bias, wo, *held)


def attn_back_body(heads, last_part, first, dout_ref, wo_ref, att_ref, q_ref, qkv_ref, bias_ref, lse_ref, *rest):
    if last_part:
        dkey_in, dval_in, sums_in, _, dqkv_ref, sums_ref, keys, vals, d_query, d_key, d_val, packed, sems = rest
    else:
        dqkv_ref, sums_ref, d_key, d_val, keys, vals, d_query, sems = rest
    step = pl.program_id(0)
    block, part_width = q_ref.shape
    count = d_query.shape[0]

    @pl.when(step == 0)
    def _():
        fill_keys(qkv_ref, bias_ref, keys, heads)
        vals[...] = value_columns(qkv_ref).astype(BF16)
        if last_part:
            d_key[...] = dkey_in[...]
            d_val[...] = dval_in[...]
            sums_ref[...] = sums_in[...]
        else:
            d_key[...] = jnp.zeros_like(d_key)
            d_val[...] = jnp.zeros_like(d_val)
            sums_ref[...] = jnp.zeros_like(sums_ref)

    log_scale = SCORE_SCALE * LOG2E
    d_att = mm(dout_ref[...], wo_ref[...]).astype(BF16)
    inner_cols = jnp.transpose(d_att.astype(F32) * att_ref[...].astype(F32))
    outs = []
    for head in range(heads):
        start, _ = head_place(head)
        inside, last = lane_mask(block, head)
        q_window = window(q_ref, head)
        query = jnp.where(last, 1.0, q_window).astype(BF16)
        q_only = jnp.where(inside, q_window, 0.0).astype(BF16)
        d_only = jnp.where(inside, window(d_att, head), 0.0).astype(BF16)
        inner = jnp.sum(inner_cols[head * HD : head * HD + HD], axis=0, keepdims=True)
        scores = mm(keys[head], query, NT)
        probs = jnp.exp2(scores * log_scale - lse_ref[head : head + 1, :])
        d_probs = mm(vals[:, start : start + WINDOW], d_only, NT)
        d_scores = (probs * (d_probs - inner)).astype(BF16)
        d_val[:, start : start + WINDOW] += mm(probs.astype(BF16), d_only)
        d_key[:, start : start + WINDOW] += mm(d_scores, q_only)
        outs.append(mm(d_scores, keys[head], TN))
    low = (join_windows(outs) * SCORE_SCALE).astype(BF16)
    d_query[pl.ds(pl.multiple_of(step * block, block), block), :] = low
    sums_ref[0:1, :] += jnp.sum(low.astype(F32), axis=0, keepdims=True)

    @pl.when(step == pl.num_programs(0) - 1)
    def _():
        copies = [
            pltpu.make_async_copy(
                d_query, dqkv_ref.at[pl.ds(first, count), pl.ds(0, part_width)], sems.at[0]
            )
        ]
        copies[0].start()
        if last_part:
            key_low = d_key[...] * SCORE_SCALE
            value_low = d_val[...]
            sums_ref[1:2, :] = jnp.sum(value_low.astype(BF16).astype(F32), axis=0, keepdims=True)
            value_low = pltpu.roll(value_low, LANES // 2, 1)
            whole = part_width - LANES
            packed[:, :whole] = key_low[:, :whole].astype(BF16)
            packed[:, whole:part_width] = (key_low[:, whole:] + value_low[:, :LANES]).astype(BF16)
            packed[:, part_width:] = value_low[:, LANES:].astype(BF16)
            copies.append(
                pltpu.make_async_copy(
                    packed,
                    dqkv_ref.at[pl.ds(0, packed.shape[0]), pl.ds(part_width, packed.shape[1])],
                    sems.at[1],
                )
            )
            copies[1].start()
        for copy in copies:
            copy.wait()


def attn_back_call(heads, d_out, wo, attended, qkv, key_bias, lse, block, first, earlier=None):
    count, width = d_out.shape
    frames = qkv.shape[0]
    part_width = wo.shape[1]
    base = first // block
    last_part = earlier is not None
    whole = pl.BlockSpec((frames, part_width), lambda i: (0, 0))
    sums_spec = pl.BlockSpec((8, part_width), lambda i: (0, 0))
    anywhere = pl.BlockSpec(memory_space=pl.ANY)
    out_shape = [
        jax.ShapeDtypeStruct(qkv.shape, BF16),
        jax.ShapeDtypeStruct((8, part_width), F32),
    ]
    out_specs = [anywhere, sums_spec]
    scratch = [
        pltpu.VMEM((heads, frames, WINDOW), BF16),
        pltpu.VMEM((frames, part_width), BF16),
        pltpu.VMEM((count, part_width), BF16),
    ]
    held = []
    if last_part:
        d_qkv, sums, d_key, d_val = earlier
        held = [d_key, d_val, sums, d_qkv]
        scratch += [pltpu.VMEM((frames, part_width), F32)] * 2
        scratch += [pltpu.VMEM((frames, qkv.shape[1] - part_width), BF16)]
    else:
        out_shape += [jax.ShapeDtypeStruct((frames, part_width), F32)] * 2
        out_specs += [whole, whole]
    return pl.pallas_call(
        partial(attn_back_body, heads, last_part, first),
        grid=(count // block,),
        in_specs=[
            pl.BlockSpec((block, width), lambda i: (i, 0)),
            pl.BlockSpec(wo.shape, lambda i: (0, 0)),
            pl.BlockSpec((block, part_width), lambda i: (i + base, 0)),
            pl.BlockSpec((block, part_width), lambda i: (i + base, 0)),
            pl.BlockSpec(qkv.shape, lambda i: (0, 0)),
            pl.BlockSpec(key_bias.shape, lambda i: (0, 0)),
            pl.BlockSpec((8, block), lambda i: (0, i + base)),
        ]
        + [whole, whole, sums_spec, anywhere][: len(held)],
        out_specs=out_specs,
        out_shape=out_shape,
        scratch_shapes=scratch + [pltpu.SemaphoreType.DMA((2,))],
        input_output_aliases={10: 0} if last_part else {},
        compiler_params=params("arbitrary"),
        cost_estimate=LITTLE,
        name="attn_bwd",
    )(d_out, wo, attended, qkv, qkv, key_bias, lse, *held)


def gelu_parts(values):
    size = jnp.abs(values)
    bell = jnp.exp2(values * values * (-0.5 * LOG2E))
    inv = 1.0 / (1.0 + (0.3275911 * math.sqrt(0.5)) * size)
    tail = inv * (
        0.5 * 0.254829592
        + inv
        * (
            0.5 * -0.284496736
            + inv * (0.5 * 1.421413741 + inv * (0.5 * -1.453152027 + inv * (0.5 * 1.061405429)))
        )
    )
    tail = tail * bell
    share = jnp.where(values < 0.0, tail, 1.0 - tail)
    return share, share + values * bell * (1.0 / math.sqrt(2.0 * math.pi))


def mlp_body(chunk, in_ref, w_ref, bias_ref, dhid_ref, *rest):
    hid_ref, dpre_ref, part_ref, sums_ref = rest[-4:]

    @pl.when(pl.program_id(0) == 0)
    def _():
        sums_ref[...] = jnp.zeros_like(sums_ref)

    for start in range(0, w_ref.shape[1], chunk):
        cols = slice(start, start + chunk)
        pre = mm(in_ref[...], w_ref[:, cols]) + bias_ref[0:1, cols]
        share, slope = gelu_parts(pre)
        hid_ref[:, cols] = (pre * share).astype(BF16)
        d_pre = (dhid_ref[:, cols] * slope).astype(BF16)
        dpre_ref[:, cols] = d_pre
        sums_ref[0:1, cols] += jnp.sum(d_pre.astype(F32), axis=0, keepdims=True)
    part_ref[...] = mm(dpre_ref[...], w_ref[...], NT).astype(BF16)


def mlp_call(mlp_in, weight, bias, d_hidden, block, first, frames, earlier=None):
    count, width = mlp_in.shape
    hidden_width = weight.shape[1]
    held = [] if earlier is None else list(earlier)
    base = first // block
    return pl.pallas_call(
        partial(mlp_body, min(256, hidden_width)),
        grid=(count // block,),
        in_specs=[
            pl.BlockSpec((block, width), lambda i: (i, 0)),
            pl.BlockSpec(weight.shape, lambda i: (0, 0)),
            pl.BlockSpec(bias.shape, lambda i: (0, 0)),
            pl.BlockSpec((block, hidden_width), lambda i: (i + base, 0)),
        ]
        + [pl.BlockSpec(memory_space=pl.ANY)] * len(held),
        out_specs=[
            pl.BlockSpec((block, hidden_width), lambda i: (i + base, 0)),
            pl.BlockSpec((block, hidden_width), lambda i: (i + base, 0)),
            pl.BlockSpec((block, width), lambda i: (i, 0)),
            pl.BlockSpec((8, hidden_width), lambda i: (0, 0)),
        ],
        out_shape=[
            jax.ShapeDtypeStruct((frames, hidden_width), BF16),
            jax.ShapeDtypeStruct((frames, hidden_width), BF16),
            jax.ShapeDtypeStruct((count, width), BF16),
            jax.ShapeDtypeStruct((8, hidden_width), F32),
        ],
        input_output_aliases={} if earlier is None else {4: 0, 5: 1},
        compiler_params=params("arbitrary"),
        cost_estimate=LITTLE,
        name="mlp_up",
    )(mlp_in, weight, bias, d_hidden, *held)


def residual_body(x_ref, mine_ref, near_ref, far_ref, vec_ref, res_ref, in_ref):
    total = mine_ref[...].astype(F32) + near_ref[...].astype(F32) + far_ref[...].astype(F32)
    residual = x_ref[...].astype(F32) + total + vec_ref[2:3, :]
    res_ref[...] = residual
    unit, _ = norm_parts(residual)
    in_ref[...] = (unit * vec_ref[3:4, :] + vec_ref[4:5, :]).astype(BF16)


def second_back_body(
    res_ref, mine_ref, near_ref, far_ref, cot_ref, vec_ref, dres_ref, low_ref, sums_ref
):
    @pl.when(pl.program_id(0) == 0)
    def _():
        sums_ref[...] = jnp.zeros_like(sums_ref)

    grad = mine_ref[...].astype(F32) + near_ref[...].astype(F32) + far_ref[...].astype(F32)
    unit, scale = norm_parts(res_ref[...])
    cot = cot_ref[...].astype(F32)
    d_res = norm_back(grad, vec_ref[3:4, :], unit, scale) + cot
    dres_ref[...] = d_res
    low_ref[...] = d_res.astype(BF16)
    sums_ref[2:3, :] += jnp.sum(d_res, axis=0, keepdims=True)
    sums_ref[3:4, :] += jnp.sum(grad * unit, axis=0, keepdims=True)
    sums_ref[4:5, :] += jnp.sum(grad, axis=0, keepdims=True)
    sums_ref[5:6, :] += jnp.sum(cot, axis=0, keepdims=True)


def first_back_body(x_ref, mine_ref, near_ref, far_ref, dres_ref, vec_ref, out_ref, sums_ref):
    @pl.when(pl.program_id(0) == 0)
    def _():
        sums_ref[...] = jnp.zeros_like(sums_ref)

    grad = mine_ref[...].astype(F32) + near_ref[...].astype(F32) + far_ref[...].astype(F32)
    unit, scale = norm_parts(x_ref[...].astype(F32))
    out_ref[...] = norm_back(grad, vec_ref[0:1, :], unit, scale) + dres_ref[...]
    sums_ref[0:1, :] += jnp.sum(grad * unit, axis=0, keepdims=True)
    sums_ref[1:2, :] += jnp.sum(grad, axis=0, keepdims=True)


def row_call(body, rows_in, vec_rows, out_types, with_sums, block, name):
    rows, width = rows_in[0].shape
    row_spec = pl.BlockSpec((block, width), lambda i: (i, 0))
    whole = pl.BlockSpec((8, width), lambda i: (0, 0))
    return pl.pallas_call(
        body,
        grid=(rows // block,),
        in_specs=[row_spec] * len(rows_in) + [whole],
        out_specs=[row_spec] * len(out_types) + [whole] * with_sums,
        out_shape=[jax.ShapeDtypeStruct((rows, width), kind) for kind in out_types]
        + [jax.ShapeDtypeStruct((8, width), F32)] * with_sums,
        compiler_params=params("arbitrary"),
        name=name,
    )(*rows_in, vec_rows)


def polar_factors(grams, eye):
    def high(left, right):
        return jnp.dot(left, right, precision=HIGHEST, preferred_element_type=F32)

    scales = [1.0 / (jnp.sqrt(jnp.sum(gram * eye, keepdims=True)) + POLAR_EPS) for gram in grams]
    grams = [gram * scale * scale for gram, scale in zip(grams, scales)]
    factors = None
    for sweep in range(SWEEPS):
        squares = [high(gram, gram) for gram in grams]
        steps = [
            QUINTIC_A * eye + QUINTIC_B * gram + QUINTIC_C * square
            for gram, square in zip(grams, squares)
        ]
        if sweep < SWEEPS - 1:
            halves = [high(step, gram) for step, gram in zip(steps, grams)]
        if factors is None:
            factors = steps
        else:
            factors = [high(step, factor) for step, factor in zip(steps, factors)]
        if sweep < SWEEPS - 1:
            grams = [high(step, part) for step, part in zip(steps, halves)]
    return [factor * scale for factor, scale in zip(factors, scales)]


def polar_body(gram_ref, out_ref):
    count, rows, _ = gram_ref.shape
    row = lax.broadcasted_iota(jnp.int32, (rows, rows), 0)
    col = lax.broadcasted_iota(jnp.int32, (rows, rows), 1)
    eye = jnp.where(row == col, 1.0, 0.0)
    for index, factor in enumerate(polar_factors([gram_ref[i] for i in range(count)], eye)):
        out_ref[index] = factor


def polar_call(grams):
    count, rows, _ = grams.shape
    if rows % 32:
        return jnp.stack(polar_factors([grams[i] for i in range(count)], jnp.eye(rows, dtype=F32)))
    return pl.pallas_call(
        polar_body,
        out_shape=jax.ShapeDtypeStruct(grams.shape, F32),
        compiler_params=params(),
        name="polar",
    )(grams)


def gram_of(update):
    return lax.dot_general(update, update, NT, precision=HIGHEST, preferred_element_type=F32)


def momentum(moment, gradient):
    moved = MUON_DECAY * moment + gradient
    return moved, gradient + MUON_DECAY * moved


def applied(weight, factor, update, rate):
    return weight - rate * jnp.dot(factor, update, precision=HIGHEST)


def place_body(splits, me_ref, *refs):
    slots, outs = refs[:8], refs[8:]
    rows = slots[0].shape[0]
    for mask, slot in enumerate(slots):
        start = pl.multiple_of((me_ref[0] ^ mask) * rows, rows)
        for (low, high), out in zip(splits, outs):
            out[pl.ds(start, rows), :] = slot[:, low:high]


def place_rows(slots, splits):
    rows = slots[0].shape[0]
    return pl.pallas_call(
        partial(place_body, splits),
        in_specs=[pl.BlockSpec(memory_space=pltpu.SMEM)]
        + [pl.BlockSpec(memory_space=pltpu.VMEM)] * 8,
        out_specs=[pl.BlockSpec(memory_space=pltpu.VMEM)] * len(splits),
        out_shape=[
            jax.ShapeDtypeStruct((8 * rows, high - low), slots[0].dtype) for low, high in splits
        ],
        compiler_params=params(),
        cost_estimate=LITTLE,
        name="place_rows",
    )(lax.axis_index("dp").astype(jnp.int32)[None], *slots)


def dp_slots(own):
    slots = {0: own}
    for mask in (4, 6, 2):
        slots[mask] = swap(own, "dp", mask)
    for mask in (0, 2, 4, 6):
        slots[mask + 1] = swap(slots[mask], "dp", 1)
    return [slots[mask] for mask in range(8)]


def dp_send(own):
    if lax.axis_size("dp") != 8:
        return [lax.all_gather(own, "dp", axis=0, tiled=True)]
    return dp_slots(own)


def dp_place(slots, splits):
    if len(slots) == 1:
        return [slots[0][:, low:high] for low, high in splits]
    return place_rows(slots, splits)


def dp_scatter(part):
    size = lax.axis_size("dp")
    if size != 8:
        return dp_scatter_plain(part), []
    rows = part.shape[0] // size
    me = lax.axis_index("dp")

    def block(mask):
        return lax.dynamic_slice(part, ((me ^ mask) * rows, 0), (rows, part.shape[1]))

    total, arrivals = None, []
    for mask in (4, 6, 2, 0):
        arrived = swap(block(mask + 1), "dp", 1)
        arrivals.append(arrived)
        pair = block(mask).astype(F32) + arrived.astype(F32)
        if mask:
            pair = swap(pair.astype(BF16), "dp", mask).astype(F32)
        total = pair if total is None else total + pair
    return total, arrivals


def dp_scatter_plain(part):
    return lax.psum_scatter(part, "dp", scatter_dimension=0, tiled=True).astype(F32)


def dp_sum(value):
    if lax.axis_size("dp") != 8:
        return lax.psum(value, "dp")
    for mask in (1, 2, 4):
        value = value + swap(value, "dp", mask)
    return value


def local(
    inputs,
    lengths,
    cotangent,
    w_qkv,
    w_out,
    w_up,
    w_down,
    vectors,
    bias_qkv,
    bias_up,
    mom_qkv,
    mom_out,
    mom_up,
    mom_down,
    mom_vectors,
    mom_bias_qkv,
    mom_bias_up,
):
    dp_size = lax.axis_size("dp")
    tensor_size = lax.axis_size("tensor")
    dp_index = lax.axis_index("dp")
    tok = inputs.shape[0]
    frames = tok * tensor_size
    tokens = frames * dp_size
    half = 2 * tok
    width = inputs.shape[1]
    own_rows = w_qkv.shape[0]
    head_width = w_qkv.shape[2]
    heads = head_width // HD
    padded = -(-head_width // LANES) * LANES
    extra = padded - head_width
    own_bias = bias_qkv.shape[0]

    w_parts = w_qkv.astype(BF16)
    small = jnp.concatenate(
        [
            vectors.astype(BF16),
            bias_up.astype(BF16)[:, None],
            jnp.pad(bias_qkv.astype(BF16), ((0, own_rows - own_bias), (0, 0))),
        ],
        axis=1,
    )
    small = jnp.pad(small, ((0, 0), (0, extra - small.shape[1])))
    packed = 3 * head_width + extra
    w_cols = jnp.concatenate(
        [
            w_parts[:, 0],
            small,
            w_parts[:, 1],
            w_parts[:, 2],
            jnp.pad(w_out.astype(BF16), ((0, 0), (0, extra))),
        ],
        axis=1,
    )
    wd = lax.all_gather(w_down.astype(BF16), "dp", axis=0, tiled=True)
    x_rows = tensor_gather(inputs)
    cot_rows = tensor_gather(cotangent)
    first_slots = dp_send(w_cols)
    wq, wo = dp_place(first_slots, ((0, packed), (packed, packed + padded)))
    x_rows, cot_rows, wq, wo = lax.optimization_barrier((x_rows, cot_rows, wq, wo))
    w_up_low = after(w_up.astype(BF16), *first_slots)
    up_slots = dp_send(w_up_low)
    smalls = jnp.transpose(wq[:, head_width : head_width + 16].astype(F32))
    vec_rows = smalls[:8]
    bu = smalls[6:7]
    bq = smalls[7:9].reshape(2, dp_size, own_rows)[:, :, :own_bias].reshape(2, head_width)
    qkv_bias = jnp.concatenate(
        [bq[0:1], jnp.zeros((1, padded), F32), bq[1:2]], axis=1
    )

    me = lax.axis_index("tensor")
    place = jnp.concatenate([(me ^ s) * tok + jnp.arange(tok, dtype=jnp.int32) for s in range(4)])
    key_bias = jnp.where(place < lengths[0], 0.0, MASKED).astype(F32)[:, None]

    attn_in, qkv = qkv_call(x_rows, vec_rows, wq, qkv_bias, tok)
    att, part_three, lse = attn_call(heads, qkv, key_bias, wo, tok, 3 * tok, tok)
    att, part_two, lse = attn_call(heads, qkv, key_bias, wo, tok, 2 * tok, tok, (att, lse))
    total = pair_sum(part_two, part_three)
    far = swap(total, "tensor", 2)
    att, part_mine, lse = attn_call(
        heads, after(qkv, total, *up_slots[0:8:2]), key_bias, wo, tok, 0, half, (att, lse)
    )
    near = near_swap(part_mine[tok:])
    row_block = tok // 3
    residual, mlp_in = row_call(
        residual_body, (inputs, part_mine[:tok], near, after(far, wd)), vec_rows, (F32, BF16), 0, row_block, "residual"
    )

    near = swap(mlp_in, "tensor", 1)
    far = swap(mlp_in, "tensor", 2)
    block = tok * 2 // 3
    d_hidden = rows_mm(after(cot_rows, mlp_in), wd, NN, F32, block)
    parts = {}
    (wu,) = dp_place([*up_slots[:-1], after(up_slots[-1], d_hidden)], ((0, w_up.shape[1]),))
    in_mine = jnp.concatenate([mlp_in, near], axis=0)
    hidden, d_pre, part_mine, bu_sums = mlp_call(in_mine, wu, bu, d_hidden, block, 0, frames)
    parts[0], parts[1] = part_mine[:tok], part_mine[tok:]
    far = after(far, part_mine)
    slots = [mlp_in, near, far, swap(far, "tensor", 1)]
    for index in (3, 2):
        hidden, d_pre, parts[index], sums = mlp_call(
            slots[index], wu, bu, d_hidden, tok // 2, index * tok, frames, (hidden, d_pre)
        )
        bu_sums = bu_sums + sums
    total = pair_sum(parts[2], parts[3])
    far = swap(total, "tensor", 2)
    near = near_swap(parts[1])
    hidden_later, d_pre_later = lax.optimization_barrier((hidden, d_pre, total))[:2]
    raw_wd = sum_mm([cot_rows], hidden_later, half)
    in_rows = jnp.concatenate([in_mine, *slots[2:]], axis=0)
    raw_wu = sum_mm([in_rows], d_pre_later, half)
    near = after(near, raw_wd, raw_wu)
    grad_wd = dp_scatter_plain(raw_wd)
    grad_wu = dp_scatter_plain(raw_wu)
    d_residual, d_out, sums_two = row_call(
        second_back_body,
        (residual, parts[0], near, far, cotangent),
        vec_rows,
        (F32, BF16),
        1,
        row_block,
        "second_back",
    )
    near = swap(d_out, "tensor", 1)
    far = swap(d_out, "tensor", 2)
    out_mine = jnp.concatenate([d_out, near], axis=0)
    carried = attn_back_call(heads, out_mine, wo, att, qkv, key_bias, lse, block, 0)
    far = after(far, carried[1])
    out_far = jnp.concatenate([far, swap(far, "tensor", 1)], axis=0)
    d_qkv, bias_sums = attn_back_call(
        heads, out_far, wo, att, qkv, key_bias, lse, block, half, carried
    )
    raw_wo = sum_mm([out_mine, out_far], att, half)
    raw_wq = sum_mm([attn_in], d_qkv, half)
    grad_first, arrivals = dp_scatter(jnp.concatenate([raw_wq, raw_wo], axis=1))
    grad_wq, grad_wo = grad_first[:, :packed], grad_first[:, packed : packed + head_width]
    d_qkv, hidden = lax.optimization_barrier((d_qkv, hidden, raw_wq, raw_wo))[:2]
    first_far = rows_mm(d_qkv, wq, NT, BF16, tok, half, half)
    far = swap(pair_sum(first_far[:tok], first_far[tok:]), "tensor", 2)
    first_mine = rows_mm(d_qkv, wq, NT, BF16, tok, 0, half)
    near = swap(first_mine[tok:], "tensor", 1)
    hidden = after(hidden, *arrivals[:3])
    down_far = rows_mm(hidden, wd, NT, BF16, tok, half, half)
    output_far = swap(pair_sum(down_far[:tok], down_far[tok:]), "tensor", 2)
    down_mine = rows_mm(hidden, wd, NT, BF16, tok, 0, half)
    output_near = swap(down_mine[tok:], "tensor", 1)
    output = (
        residual
        + (down_mine[:tok].astype(F32) + output_near.astype(F32) + output_far.astype(F32))
        + vec_rows[5]
    )
    input_grad, sums_one = row_call(
        first_back_body,
        (inputs, first_mine[:tok], near, far, d_residual),
        vec_rows,
        (F32,),
        1,
        row_block,
        "first_back",
    )

    vec_sums = tensor_sum(sums_one + sums_two)
    rows_of = jnp.concatenate(
        [
            vec_sums[:6],
            bu_sums[0:1],
            jnp.pad(bias_sums[:2], ((0, 0), (0, width - padded))),
        ],
        axis=0,
    )
    rows_of = dp_sum(rows_of)
    own_cols = lax.dynamic_slice(rows_of, (0, dp_index * own_rows), (7, own_rows))
    vec_grad = jnp.transpose(own_cols[:6])
    bu_grad = own_cols[6]
    bq_grad = jnp.transpose(
        lax.dynamic_slice(rows_of, (7, dp_index * own_bias), (2, own_bias))
    )

    mom_down_new, update_down = momentum(mom_down, grad_wd)
    mom_up_new, update_up = momentum(mom_up, grad_wu)
    mom_out_new, update_out = momentum(mom_out, grad_wo)
    spots = (0, padded, padded + head_width)
    grad_parts = jnp.stack([grad_wq[:, spot : spot + head_width] for spot in spots], axis=1)
    mom_qkv_new, update_qkv = momentum(mom_qkv, grad_parts)
    flat = jnp.concatenate(
        [update_qkv[:, 0], jnp.zeros((own_rows, extra), F32), update_qkv[:, 1], update_qkv[:, 2]], axis=1
    )
    updates = (update_down, update_up, update_out, flat)
    factors = polar_call(tensor_sum(jnp.stack([gram_of(update) for update in updates])))
    new_w_down = applied(w_down, factors[0], update_down, STEP_DOWN)
    new_w_up = applied(w_up, factors[1], update_up, STEP_UP)
    new_w_out = applied(w_out, factors[2], update_out, STEP_OUT)
    polar_qkv = jnp.dot(factors[3], flat, precision=HIGHEST)
    new_w_qkv = w_qkv - STEP_QKV * jnp.stack(
        [polar_qkv[:, spot : spot + head_width] for spot in spots], axis=1
    )

    vec_rate = VEC_RATE / math.sqrt(tokens)
    new_mom_vectors = VEC_DECAY * mom_vectors + vec_grad
    new_mom_bias_qkv = VEC_DECAY * mom_bias_qkv + bq_grad
    new_mom_bias_up = VEC_DECAY * mom_bias_up + bu_grad
    new_vectors = vectors - vec_rate * new_mom_vectors
    new_bias_qkv = bias_qkv - vec_rate * new_mom_bias_qkv
    new_bias_up = bias_up - vec_rate * new_mom_bias_up
    return (
        output,
        input_grad,
        new_w_qkv,
        new_w_out,
        new_w_up,
        new_w_down,
        new_vectors,
        new_bias_qkv,
        new_bias_up,
        mom_qkv_new,
        mom_out_new,
        mom_up_new,
        mom_down_new,
        new_mom_vectors,
        new_mom_bias_qkv,
        new_mom_bias_up,
    )


def solution(mesh):
    in_specs = (
        P(("dp", "tensor"), None),
        P("dp"),
        P(("dp", "tensor"), None),
        P("dp", None, "tensor"),
        P("dp", "tensor"),
        P("dp", "tensor"),
        P("dp", "tensor"),
        P("dp", None),
        P(("tensor", "dp"), None),
        P(("tensor", "dp")),
        P("dp", None, "tensor"),
        P("dp", "tensor"),
        P("dp", "tensor"),
        P("dp", "tensor"),
        P("dp", None),
        P(("tensor", "dp"), None),
        P(("tensor", "dp")),
    )
    out_specs = (
        P(("dp", "tensor"), None),
        P(("dp", "tensor"), None),
        P("dp", None, "tensor"),
        P("dp", "tensor"),
        P("dp", "tensor"),
        P("dp", "tensor"),
        P("dp", None),
        P(("tensor", "dp"), None),
        P(("tensor", "dp")),
        P("dp", None, "tensor"),
        P("dp", "tensor"),
        P("dp", "tensor"),
        P("dp", "tensor"),
        P("dp", None),
        P(("tensor", "dp"), None),
        P(("tensor", "dp")),
    )
    return jax.shard_map(local, mesh=mesh, in_specs=in_specs, out_specs=out_specs, check_vma=False)
```

```python
from functools import partial
import math

import jax
import jax.numpy as jnp
from jax import lax
from jax.experimental import pallas as pl
from jax.experimental.pallas import tpu as pltpu
from jax.sharding import PartitionSpec as P

HD = 80
SWEEPS = 5
LANES = 128
WINDOW = 256
BIAS_LANE = WINDOW - 1
VMEM_LIMIT = 58 * 1024 * 1024

HIGHEST = lax.Precision.HIGHEST
NORM_EPS = 1e-05
POLAR_EPS = 1e-07
MASKED = -1e30
QUINTIC_A = 3.4445
QUINTIC_B = -4.775
QUINTIC_C = 2.0315
MUON_DECAY = 0.95
VEC_DECAY = 0.9
VEC_RATE = 0.1
STEP_QKV = 0.5 * math.sqrt(3.0)
STEP_OUT = 2.0
STEP_UP = 1.0
STEP_DOWN = 0.5
LOG2E = math.log2(math.e)
SCORE_SCALE = 1.0 / math.sqrt(HD)
F32 = jnp.float32
BF16 = jnp.bfloat16
LITTLE = pl.CostEstimate(flops=1_000_000, bytes_accessed=100_000, transcendentals=0)
NN = (((1,), (0,)), ((), ()))
NT = (((1,), (1,)), ((), ()))
TN = (((0,), (0,)), ((), ()))


def mm(left, right, dims=NN):
    return lax.dot_general(left, right, dims, preferred_element_type=F32)


def norm_parts(values):
    center = values - jnp.mean(values, axis=-1, keepdims=True)
    spread = jnp.mean(center * center, axis=-1, keepdims=True)
    scale = lax.rsqrt(spread + NORM_EPS)
    return center * scale, scale


def norm_back(grad, gain, unit, scale):
    inner = grad * gain
    mean_grad = jnp.mean(inner, axis=-1, keepdims=True)
    mean_unit = jnp.mean(inner * unit, axis=-1, keepdims=True)
    return scale * (inner - mean_grad - unit * mean_unit)


def params(*semantics):
    return pltpu.CompilerParams(
        dimension_semantics=semantics or None, vmem_limit_bytes=VMEM_LIMIT
    )


def swap(value, axis, mask):
    size = lax.axis_size(axis)
    return lax.ppermute(value, axis, [(i, i ^ mask) for i in range(size)])


def tensor_slots(own):
    near = swap(own, "tensor", 1)
    far = swap(own, "tensor", 2)
    return [own, near, far, swap(far, "tensor", 1)]


def tensor_gather(own):
    return jnp.concatenate(tensor_slots(own), axis=0)


def tensor_sum(value):
    value = value + swap(value, "tensor", 1)
    return value + swap(value, "tensor", 2)


def pair_sum(own, sent):
    arrived = swap(sent, "tensor", 1)
    return (own.astype(F32) + arrived.astype(F32)).astype(BF16)


def after(value, *others):
    return lax.optimization_barrier((value, *others))[0]


def tie(values, *others):
    return list(lax.optimization_barrier((*values, *others))[: len(values)])


def qkv_body(x_ref, vec_ref, w_ref, bias_ref, attn_ref, qkv_ref):
    unit, _ = norm_parts(x_ref[...].astype(F32))
    attn_in = (unit * vec_ref[0:1, :] + vec_ref[1:2, :]).astype(BF16)
    attn_ref[...] = attn_in
    qkv_ref[...] = (mm(attn_in, w_ref[...]) + bias_ref[0:1, :]).astype(BF16)


def qkv_call(x_rows, vec_rows, weight, bias, block):
    rows, width = x_rows.shape
    columns = weight.shape[1]
    return pl.pallas_call(
        qkv_body,
        grid=(rows // block,),
        in_specs=[
            pl.BlockSpec((block, width), lambda i: (i, 0)),
            pl.BlockSpec(vec_rows.shape, lambda i: (0, 0)),
            pl.BlockSpec(weight.shape, lambda i: (0, 0)),
            pl.BlockSpec(bias.shape, lambda i: (0, 0)),
        ],
        out_specs=[
            pl.BlockSpec((block, width), lambda i: (i, 0)),
            pl.BlockSpec((block, columns), lambda i: (i, 0)),
        ],
        out_shape=[
            jax.ShapeDtypeStruct((rows, width), BF16),
            jax.ShapeDtypeStruct((rows, columns), BF16),
        ],
        compiler_params=params("arbitrary"),
        cost_estimate=LITTLE,
        name="norm_qkv",
    )(x_rows, vec_rows, weight, bias)


PIECES = 4


def part_shapes(emits, rows, width):
    shapes = []
    for kind in emits:
        count = PIECES if kind == "pieces" else 1
        shapes += [jax.ShapeDtypeStruct((rows // count, width), BF16)] * count
    return shapes, [pl.BlockSpec(shape.shape, lambda i: (0, 0)) for shape in shapes]


def part_store(emits, refs, value):
    spot = 0
    for index, kind in enumerate(emits):
        count = PIECES if kind == "pieces" else 1
        group = refs[spot : spot + count]
        spot += count

        @pl.when(pl.program_id(0) == index)
        def _():
            rows = value.shape[0] // count
            for piece, ref in enumerate(group):
                ref[...] = value[piece * rows : piece * rows + rows].astype(BF16)


def swap_all(values, axis, mask):
    return [swap(value, axis, mask) for value in values]


def pair_body(own_ref, *rest):
    pieces, out_ref = rest[:-1], rest[-1]
    for index, piece in enumerate(pieces):

        @pl.when(pl.program_id(0) == index)
        def _():
            out_ref[...] = (own_ref[...].astype(F32) + piece[...].astype(F32)).astype(BF16)


def pair_pieces(own, pieces):
    rows, width = own.shape
    spec = pl.BlockSpec((rows // PIECES, width), lambda i: (i, 0))
    return pl.pallas_call(
        pair_body,
        grid=(PIECES,),
        in_specs=[spec] + [pl.BlockSpec(pieces[0].shape, lambda i: (0, 0))] * PIECES,
        out_specs=spec,
        out_shape=jax.ShapeDtypeStruct(own.shape, BF16),
        compiler_params=params("arbitrary"),
        cost_estimate=LITTLE,
        name="pair_sum",
    )(own, *pieces)


def head_place(head):
    start = 0 if head * HD + HD <= BIAS_LANE else LANES
    return start, head * HD - start


def lane_mask(rows, head):
    _, offset = head_place(head)
    lane = lax.broadcasted_iota(jnp.int32, (rows, WINDOW), 1)
    return (lane >= offset) & (lane < offset + HD), lane == BIAS_LANE


def window(value, head):
    start, _ = head_place(head)
    return value[:, start : start + WINDOW].astype(F32)


def key_columns(qkv_ref):
    third = (qkv_ref.shape[1] + LANES) // 3
    return qkv_ref[:, third : 2 * third]


def value_columns(qkv_ref):
    third = (qkv_ref.shape[1] + LANES) // 3
    tail = qkv_ref[:, qkv_ref.shape[1] - third :].astype(F32)
    return pltpu.roll(tail, third - LANES // 2, 1)


def fill_keys(qkv_ref, bias_ref, keys_out, heads):
    columns = key_columns(qkv_ref)
    for head in range(heads):
        inside, last = lane_mask(columns.shape[0], head)
        picked = jnp.where(inside, window(columns, head), 0.0)
        keys_out[head] = jnp.where(last, bias_ref[...], picked).astype(BF16)


def join_windows(parts):
    low, high = None, None
    for head, part in enumerate(parts):
        if head_place(head)[0] == 0:
            low = part if low is None else low + part
        else:
            high = part if high is None else high + part
    return jnp.concatenate(
        [low[:, :LANES], low[:, LANES:] + high[:, :LANES], high[:, LANES:]], axis=1
    )


def attn_body(heads, emits, skip, q_ref, qkv_ref, bias_ref, wo_ref, *rest):
    (att_ref, lse_ref), parts, (keys, vals) = rest[skip : skip + 2], rest[skip + 2 : -2], rest[-2:]
    block = q_ref.shape[0]
    frames = qkv_ref.shape[0]

    @pl.when(pl.program_id(0) == 0)
    def _():
        fill_keys(qkv_ref, bias_ref, keys, heads)
        columns = value_columns(qkv_ref)
        for head in range(heads):
            inside, _ = lane_mask(frames, head)
            vals[head] = jnp.where(inside, window(columns, head), 0.0).astype(BF16)

    log_scale = SCORE_SCALE * LOG2E
    outs = []
    lane = lax.broadcasted_iota(jnp.int32, (block, LANES), 1)
    lse_cols = jnp.zeros((block, LANES), F32)
    for head in range(heads):
        _, last = lane_mask(block, head)
        query = jnp.where(last, 1.0, window(q_ref, head)).astype(BF16)
        scores = mm(query, keys[head], NT)
        row_max = jnp.max(scores, axis=1, keepdims=True)
        powers = jnp.exp2((scores - row_max) * log_scale)
        totals = jnp.sum(powers, axis=1, keepdims=True)
        outs.append(mm(powers.astype(BF16), vals[head]) * (1.0 / totals))
        lse_cols = jnp.where(lane == head, row_max * log_scale + jnp.log2(totals), lse_cols)
    attended = join_windows(outs).astype(BF16)
    att_ref[...] = attended
    lse_ref[...] = jnp.transpose(lse_cols)[:8]
    part_store(emits, parts, mm(attended, wo_ref[...], NT))


def attn_call(heads, emits, qkv, key_bias, wo, block, first, earlier=None):
    count = block * len(emits)
    frames = qkv.shape[0]
    part_width = wo.shape[1]
    width = wo.shape[0]
    held = [] if earlier is None else list(earlier)
    base = first // block
    shapes, specs = part_shapes(emits, block, width)
    return pl.pallas_call(
        partial(attn_body, heads, emits, len(held)),
        grid=(count // block,),
        in_specs=[
            pl.BlockSpec((block, part_width), lambda i: (i + base, 0)),
            pl.BlockSpec(qkv.shape, lambda i: (0, 0)),
            pl.BlockSpec(key_bias.shape, lambda i: (0, 0)),
            pl.BlockSpec(wo.shape, lambda i: (0, 0)),
        ]
        + [pl.BlockSpec(memory_space=pl.ANY)] * len(held),
        out_specs=[
            pl.BlockSpec((block, part_width), lambda i: (i + base, 0)),
            pl.BlockSpec((8, block), lambda i: (0, i + base)),
        ]
        + specs,
        out_shape=[
            jax.ShapeDtypeStruct((frames, part_width), BF16),
            jax.ShapeDtypeStruct((8, frames), F32),
        ]
        + shapes,
        scratch_shapes=[
            pltpu.VMEM((heads, frames, WINDOW), BF16),
            pltpu.VMEM((heads, frames, WINDOW), BF16),
        ],
        input_output_aliases={} if earlier is None else {4: 0, 5: 1},
        compiler_params=params("arbitrary"),
        cost_estimate=LITTLE,
        name="attn_fwd",
    )(qkv, qkv, key_bias, wo, *held)


def attn_back_body(heads, last_part, first, dout_ref, wo_ref, att_ref, q_ref, qkv_ref, bias_ref, lse_ref, *rest):
    if last_part:
        dkey_in, dval_in, sums_in, _, dqkv_ref, sums_ref, keys, vals, d_query, d_key, d_val, packed, sems = rest
    else:
        dqkv_ref, sums_ref, d_key, d_val, keys, vals, d_query, sems = rest
    step = pl.program_id(0)
    block, part_width = q_ref.shape
    count = d_query.shape[0]

    @pl.when(step == 0)
    def _():
        fill_keys(qkv_ref, bias_ref, keys, heads)
        vals[...] = value_columns(qkv_ref).astype(BF16)
        if last_part:
            d_key[...] = dkey_in[...]
            d_val[...] = dval_in[...]
            sums_ref[...] = sums_in[...]
        else:
            d_key[...] = jnp.zeros_like(d_key)
            d_val[...] = jnp.zeros_like(d_val)
            sums_ref[...] = jnp.zeros_like(sums_ref)

    log_scale = SCORE_SCALE * LOG2E
    d_att = mm(dout_ref[...], wo_ref[...]).astype(BF16)
    inner_cols = jnp.transpose(d_att.astype(F32) * att_ref[...].astype(F32))
    outs = []
    for head in range(heads):
        start, _ = head_place(head)
        inside, last = lane_mask(block, head)
        q_window = window(q_ref, head)
        query = jnp.where(last, 1.0, q_window).astype(BF16)
        q_only = jnp.where(inside, q_window, 0.0).astype(BF16)
        d_only = jnp.where(inside, window(d_att, head), 0.0).astype(BF16)
        inner = jnp.sum(inner_cols[head * HD : head * HD + HD], axis=0, keepdims=True)
        scores = mm(keys[head], query, NT)
        probs = jnp.exp2(scores * log_scale - lse_ref[head : head + 1, :])
        d_probs = mm(vals[:, start : start + WINDOW], d_only, NT)
        d_scores = (probs * (d_probs - inner)).astype(BF16)
        d_val[:, start : start + WINDOW] += mm(probs.astype(BF16), d_only)
        d_key[:, start : start + WINDOW] += mm(d_scores, q_only)
        outs.append(mm(d_scores, keys[head], TN))
    low = (join_windows(outs) * SCORE_SCALE).astype(BF16)
    d_query[pl.ds(pl.multiple_of(step * block, block), block), :] = low
    sums_ref[0:1, :] += jnp.sum(low.astype(F32), axis=0, keepdims=True)

    @pl.when(step == pl.num_programs(0) - 1)
    def _():
        copies = [
            pltpu.make_async_copy(
                d_query, dqkv_ref.at[pl.ds(first, count), pl.ds(0, part_width)], sems.at[0]
            )
        ]
        copies[0].start()
        if last_part:
            key_low = d_key[...] * SCORE_SCALE
            value_low = d_val[...]
            sums_ref[1:2, :] = jnp.sum(value_low.astype(BF16).astype(F32), axis=0, keepdims=True)
            value_low = pltpu.roll(value_low, LANES // 2, 1)
            whole = part_width - LANES
            packed[:, :whole] = key_low[:, :whole].astype(BF16)
            packed[:, whole:part_width] = (key_low[:, whole:] + value_low[:, :LANES]).astype(BF16)
            packed[:, part_width:] = value_low[:, LANES:].astype(BF16)
            copies.append(
                pltpu.make_async_copy(
                    packed,
                    dqkv_ref.at[pl.ds(0, packed.shape[0]), pl.ds(part_width, packed.shape[1])],
                    sems.at[1],
                )
            )
            copies[1].start()
        for copy in copies:
            copy.wait()


def attn_back_call(heads, d_out, wo, attended, qkv, key_bias, lse, block, first, earlier=None):
    count, width = d_out.shape
    frames = qkv.shape[0]
    part_width = wo.shape[1]
    base = first // block
    last_part = earlier is not None
    whole = pl.BlockSpec((frames, part_width), lambda i: (0, 0))
    sums_spec = pl.BlockSpec((8, part_width), lambda i: (0, 0))
    anywhere = pl.BlockSpec(memory_space=pl.ANY)
    out_shape = [
        jax.ShapeDtypeStruct(qkv.shape, BF16),
        jax.ShapeDtypeStruct((8, part_width), F32),
    ]
    out_specs = [anywhere, sums_spec]
    scratch = [
        pltpu.VMEM((heads, frames, WINDOW), BF16),
        pltpu.VMEM((frames, part_width), BF16),
        pltpu.VMEM((count, part_width), BF16),
    ]
    held = []
    if last_part:
        d_qkv, sums, d_key, d_val = earlier
        held = [d_key, d_val, sums, d_qkv]
        scratch += [pltpu.VMEM((frames, part_width), F32)] * 2
        scratch += [pltpu.VMEM((frames, qkv.shape[1] - part_width), BF16)]
    else:
        out_shape += [jax.ShapeDtypeStruct((frames, part_width), F32)] * 2
        out_specs += [whole, whole]
    return pl.pallas_call(
        partial(attn_back_body, heads, last_part, first),
        grid=(count // block,),
        in_specs=[
            pl.BlockSpec((block, width), lambda i: (i, 0)),
            pl.BlockSpec(wo.shape, lambda i: (0, 0)),
            pl.BlockSpec((block, part_width), lambda i: (i + base, 0)),
            pl.BlockSpec((block, part_width), lambda i: (i + base, 0)),
            pl.BlockSpec(qkv.shape, lambda i: (0, 0)),
            pl.BlockSpec(key_bias.shape, lambda i: (0, 0)),
            pl.BlockSpec((8, block), lambda i: (0, i + base)),
        ]
        + [whole, whole, sums_spec, anywhere][: len(held)],
        out_specs=out_specs,
        out_shape=out_shape,
        scratch_shapes=scratch + [pltpu.SemaphoreType.DMA((2,))],
        input_output_aliases={10: 0} if last_part else {},
        compiler_params=params("arbitrary"),
        cost_estimate=LITTLE,
        name="attn_bwd",
    )(d_out, wo, attended, qkv, qkv, key_bias, lse, *held)


def gelu_parts(values):
    size = jnp.abs(values)
    bell = jnp.exp2(values * values * (-0.5 * LOG2E))
    inv = 1.0 / (1.0 + (0.3275911 * math.sqrt(0.5)) * size)
    tail = inv * (
        0.5 * 0.254829592
        + inv
        * (
            0.5 * -0.284496736
            + inv * (0.5 * 1.421413741 + inv * (0.5 * -1.453152027 + inv * (0.5 * 1.061405429)))
        )
    )
    tail = tail * bell
    share = jnp.where(values < 0.0, tail, 1.0 - tail)
    return share, share + values * bell * (1.0 / math.sqrt(2.0 * math.pi))


def mlp_body(chunk, emits, skip, *refs):
    slot_refs, (w_ref, bias_ref, dhid_ref) = refs[: len(emits)], refs[len(emits) : len(emits) + 3]
    outs = refs[len(emits) + 3 + skip :]
    hid_ref, dpre_ref, sums_ref, parts, in_ref = *outs[:3], outs[3:-1], outs[-1]
    for index, slot_ref in enumerate(slot_refs):

        @pl.when(pl.program_id(0) == index)
        def _():
            in_ref[...] = slot_ref[...]

    @pl.when(pl.program_id(0) == 0)
    def _():
        sums_ref[...] = jnp.zeros_like(sums_ref)

    for start in range(0, w_ref.shape[1], chunk):
        cols = slice(start, start + chunk)
        pre = mm(in_ref[...], w_ref[:, cols]) + bias_ref[0:1, cols]
        share, slope = gelu_parts(pre)
        hid_ref[:, cols] = (pre * share).astype(BF16)
        d_pre = (dhid_ref[:, cols] * slope).astype(BF16)
        dpre_ref[:, cols] = d_pre
        sums_ref[0:1, cols] += jnp.sum(d_pre.astype(F32), axis=0, keepdims=True)
    part_store(emits, parts, mm(dpre_ref[...], w_ref[...], NT))


def mlp_call(emits, slots, weight, bias, d_hidden, first, frames, earlier=None):
    block, width = slots[0].shape
    count = block * len(slots)
    hidden_width = weight.shape[1]
    held = [] if earlier is None else list(earlier)
    base = first // block
    shapes, specs = part_shapes(emits, block, width)
    return pl.pallas_call(
        partial(mlp_body, min(256, hidden_width), emits, len(held)),
        grid=(count // block,),
        in_specs=[pl.BlockSpec((block, width), lambda i: (0, 0))] * len(slots)
        + [
            pl.BlockSpec(weight.shape, lambda i: (0, 0)),
            pl.BlockSpec(bias.shape, lambda i: (0, 0)),
            pl.BlockSpec((block, hidden_width), lambda i: (i + base, 0)),
        ]
        + [pl.BlockSpec(memory_space=pl.ANY)] * len(held),
        out_specs=[
            pl.BlockSpec((block, hidden_width), lambda i: (i + base, 0)),
            pl.BlockSpec((block, hidden_width), lambda i: (i + base, 0)),
            pl.BlockSpec((8, hidden_width), lambda i: (0, 0)),
        ]
        + specs,
        out_shape=[
            jax.ShapeDtypeStruct((frames, hidden_width), BF16),
            jax.ShapeDtypeStruct((frames, hidden_width), BF16),
            jax.ShapeDtypeStruct((8, hidden_width), F32),
        ]
        + shapes,
        scratch_shapes=[pltpu.VMEM((block, width), BF16)],
        input_output_aliases=(
            {} if earlier is None else {len(slots) + 3: 0, len(slots) + 4: 1}
        ),
        compiler_params=params("arbitrary"),
        cost_estimate=LITTLE,
        name="mlp_up",
    )(*slots, weight, bias, d_hidden, *held)


def residual_body(x_ref, mine_ref, far_ref, near_ref, vec_ref, res_ref, in_ref):
    total = mine_ref[...].astype(F32) + near_ref[...].astype(F32) + far_ref[...].astype(F32)
    residual = x_ref[...].astype(F32) + total + vec_ref[2:3, :]
    res_ref[...] = residual
    unit, _ = norm_parts(residual)
    in_ref[...] = (unit * vec_ref[3:4, :] + vec_ref[4:5, :]).astype(BF16)


def second_back_body(
    res_ref, mine_ref, far_ref, cot_ref, near_ref, vec_ref, dres_ref, low_ref, sums_ref
):
    @pl.when(pl.program_id(0) == 0)
    def _():
        sums_ref[...] = jnp.zeros_like(sums_ref)

    grad = mine_ref[...].astype(F32) + near_ref[...].astype(F32) + far_ref[...].astype(F32)
    unit, scale = norm_parts(res_ref[...])
    cot = cot_ref[...].astype(F32)
    d_res = norm_back(grad, vec_ref[3:4, :], unit, scale) + cot
    dres_ref[...] = d_res
    low_ref[...] = d_res.astype(BF16)
    sums_ref[2:3, :] += jnp.sum(d_res, axis=0, keepdims=True)
    sums_ref[3:4, :] += jnp.sum(grad * unit, axis=0, keepdims=True)
    sums_ref[4:5, :] += jnp.sum(grad, axis=0, keepdims=True)
    sums_ref[5:6, :] += jnp.sum(cot, axis=0, keepdims=True)


def first_back_body(x_ref, mine_ref, far_ref, dres_ref, near_ref, vec_ref, out_ref, sums_ref):
    @pl.when(pl.program_id(0) == 0)
    def _():
        sums_ref[...] = jnp.zeros_like(sums_ref)

    grad = mine_ref[...].astype(F32) + near_ref[...].astype(F32) + far_ref[...].astype(F32)
    unit, scale = norm_parts(x_ref[...].astype(F32))
    out_ref[...] = norm_back(grad, vec_ref[0:1, :], unit, scale) + dres_ref[...]
    sums_ref[0:1, :] += jnp.sum(grad * unit, axis=0, keepdims=True)
    sums_ref[1:2, :] += jnp.sum(grad, axis=0, keepdims=True)


def row_body(body, count, *refs):
    row_refs, pieces, vec_ref = refs[:count], refs[count : count + PIECES], refs[count + PIECES]
    near_ref = refs[-1]
    for index, piece in enumerate(pieces):

        @pl.when(pl.program_id(0) == index)
        def _():
            near_ref[...] = piece[...]

    body(*row_refs, near_ref, vec_ref, *refs[count + PIECES + 1 : -1])


def row_call(body, rows_in, near, vec_rows, out_types, with_sums, name):
    rows, width = rows_in[0].shape
    block = rows // PIECES
    row_spec = pl.BlockSpec((block, width), lambda i: (i, 0))
    whole = pl.BlockSpec((8, width), lambda i: (0, 0))
    return pl.pallas_call(
        partial(row_body, body, len(rows_in)),
        grid=(PIECES,),
        in_specs=[row_spec] * len(rows_in)
        + [pl.BlockSpec((block, width), lambda i: (0, 0))] * PIECES
        + [whole],
        out_specs=[row_spec] * len(out_types) + [whole] * with_sums,
        out_shape=[jax.ShapeDtypeStruct((rows, width), kind) for kind in out_types]
        + [jax.ShapeDtypeStruct((8, width), F32)] * with_sums,
        scratch_shapes=[pltpu.VMEM((block, width), BF16)],
        compiler_params=params("arbitrary"),
        cost_estimate=LITTLE,
        name=name,
    )(*rows_in, *near, vec_rows)


def polar_factors(grams, eye):
    def high(left, right):
        return jnp.dot(left, right, precision=HIGHEST, preferred_element_type=F32)

    scales = [1.0 / (jnp.sqrt(jnp.sum(gram * eye, keepdims=True)) + POLAR_EPS) for gram in grams]
    grams = [gram * scale * scale for gram, scale in zip(grams, scales)]
    factors = None
    for sweep in range(SWEEPS):
        squares = [high(gram, gram) for gram in grams]
        steps = [
            QUINTIC_A * eye + QUINTIC_B * gram + QUINTIC_C * square
            for gram, square in zip(grams, squares)
        ]
        if sweep < SWEEPS - 1:
            halves = [high(step, gram) for step, gram in zip(steps, grams)]
        if factors is None:
            factors = steps
        else:
            factors = [high(step, factor) for step, factor in zip(steps, factors)]
        if sweep < SWEEPS - 1:
            grams = [high(step, part) for step, part in zip(steps, halves)]
    return [factor * scale for factor, scale in zip(factors, scales)]


def polar_body(gram_ref, out_ref):
    count, rows, _ = gram_ref.shape
    row = lax.broadcasted_iota(jnp.int32, (rows, rows), 0)
    col = lax.broadcasted_iota(jnp.int32, (rows, rows), 1)
    eye = jnp.where(row == col, 1.0, 0.0)
    for index, factor in enumerate(polar_factors([gram_ref[i] for i in range(count)], eye)):
        out_ref[index] = factor


def polar_call(grams):
    count, rows, _ = grams.shape
    if rows % 32:
        return jnp.stack(polar_factors([grams[i] for i in range(count)], jnp.eye(rows, dtype=F32)))
    return pl.pallas_call(
        polar_body,
        out_shape=jax.ShapeDtypeStruct(grams.shape, F32),
        compiler_params=params(),
        name="polar",
    )(grams)


def gram_of(update):
    return lax.dot_general(update, update, NT, precision=HIGHEST, preferred_element_type=F32)


def momentum(moment, gradient):
    moved = MUON_DECAY * moment + gradient
    return moved, gradient + MUON_DECAY * moved


def applied(weight, factor, update, rate):
    return weight - rate * jnp.dot(factor, update, precision=HIGHEST)


def place_body(splits, me_ref, *refs):
    slots, outs = refs[:8], refs[8:]
    rows = slots[0].shape[0]
    for mask, slot in enumerate(slots):
        start = pl.multiple_of((me_ref[0] ^ mask) * rows, rows)
        for (low, high), out in zip(splits, outs):
            out[pl.ds(start, rows), :] = slot[:, low:high]


def place_rows(slots, splits):
    rows = slots[0].shape[0]
    return pl.pallas_call(
        partial(place_body, splits),
        in_specs=[pl.BlockSpec(memory_space=pltpu.SMEM)]
        + [pl.BlockSpec(memory_space=pltpu.VMEM)] * 8,
        out_specs=[pl.BlockSpec(memory_space=pltpu.VMEM)] * len(splits),
        out_shape=[
            jax.ShapeDtypeStruct((8 * rows, high - low), slots[0].dtype) for low, high in splits
        ],
        compiler_params=params(),
        cost_estimate=LITTLE,
        name="place_rows",
    )(lax.axis_index("dp").astype(jnp.int32)[None], *slots)


def dp_slots(own, ordered=False):
    line = {mask: swap(own, "dp", mask) for mask in (6, 2, 4)}
    slots = [own, swap(own, "dp", 1)] + [None] * 6
    for mask in (6, 2, 4):
        arrived = line[mask]
        if ordered:
            held = [slots[1]] if mask == 2 else [slots[3], slots[7]] if mask == 4 else []
            arrived = after(arrived, *held)
        slots[mask] = arrived
        slots[mask + 1] = swap(arrived, "dp", 1)
    return slots


def dp_send(own, ordered=False):
    if lax.axis_size("dp") != 8:
        return [lax.all_gather(own, "dp", axis=0, tiled=True)]
    return dp_slots(own, ordered)


def dp_place(slots, splits):
    if len(slots) == 1:
        return [slots[0][:, low:high] for low, high in splits]
    return place_rows(slots, splits)


LINE = (4, 6, 2, 0)


def dp_cross(part):
    size = lax.axis_size("dp")
    if size != 8:
        return [], [dp_scatter_plain(part)]
    rows = part.shape[0] // size
    me = lax.axis_index("dp")

    def block(mask):
        return lax.dynamic_slice(part, ((me ^ mask) * rows, 0), (rows, part.shape[1]))

    return [block(mask) for mask in LINE], [swap(block(mask + 1), "dp", 1) for mask in LINE]


def dp_line(owns, arrivals):
    if not owns:
        return arrivals
    sums, pair = [], None
    for mask, own, arrived in zip(LINE, owns, arrivals):
        arrived = arrived if pair is None else after(arrived, pair)
        pair = own.astype(F32) + arrived.astype(F32)
        sums.append(swap(pair.astype(BF16), "dp", mask) if mask else pair)
    return sums


def dp_total(sums):
    total = sums[-1].astype(F32)
    for value in sums[:-1]:
        total = total + value.astype(F32)
    return total


def dp_scatter_plain(part):
    return lax.psum_scatter(part, "dp", scatter_dimension=0, tiled=True)


def dp_sum(value):
    if lax.axis_size("dp") != 8:
        return lax.psum(value, "dp")
    for mask in (1, 2, 4):
        value = value + swap(value, "dp", mask)
    return value


def local(
    inputs,
    lengths,
    cotangent,
    w_qkv,
    w_out,
    w_up,
    w_down,
    vectors,
    bias_qkv,
    bias_up,
    mom_qkv,
    mom_out,
    mom_up,
    mom_down,
    mom_vectors,
    mom_bias_qkv,
    mom_bias_up,
):
    dp_size = lax.axis_size("dp")
    tensor_size = lax.axis_size("tensor")
    dp_index = lax.axis_index("dp")
    tok = inputs.shape[0]
    frames = tok * tensor_size
    tokens = frames * dp_size
    half = 2 * tok
    width = inputs.shape[1]
    own_rows = w_qkv.shape[0]
    head_width = w_qkv.shape[2]
    heads = head_width // HD
    padded = -(-head_width // LANES) * LANES
    extra = padded - head_width
    own_bias = bias_qkv.shape[0]

    w_parts = w_qkv.astype(BF16)
    small = jnp.concatenate(
        [
            vectors.astype(BF16),
            bias_up.astype(BF16)[:, None],
            jnp.pad(bias_qkv.astype(BF16), ((0, own_rows - own_bias), (0, 0))),
        ],
        axis=1,
    )
    small = jnp.pad(small, ((0, 0), (0, extra - small.shape[1])))
    packed = 3 * head_width + extra
    w_cols = jnp.concatenate(
        [
            w_parts[:, 0],
            small,
            w_parts[:, 1],
            w_parts[:, 2],
            jnp.pad(w_out.astype(BF16), ((0, 0), (0, extra))),
        ],
        axis=1,
    )
    first_slots = dp_send(w_cols, True)
    x_far = after(swap(inputs, "tensor", 2), *first_slots[2:7:4])
    x_rows = jnp.concatenate(
        [inputs, swap(inputs, "tensor", 1), x_far, swap(x_far, "tensor", 1)], axis=0
    )
    first_slots[-1], x_rows = tie([first_slots[-1], x_rows])
    cot_rows = tensor_gather(cotangent)
    wq, wo = dp_place(first_slots, ((0, packed), (packed, packed + padded)))
    w_down_low = after(w_down.astype(BF16), *first_slots)
    wd = lax.all_gather(w_down_low, "dp", axis=0, tiled=True)
    w_up_low = after(w_up.astype(BF16), *first_slots)
    up_slots = dp_send(w_up_low)
    smalls = jnp.transpose(wq[:, head_width : head_width + 16].astype(F32))
    vec_rows = smalls[:8]
    bu = smalls[6:7]
    bq = smalls[7:9].reshape(2, dp_size, own_rows)[:, :, :own_bias].reshape(2, head_width)
    qkv_bias = jnp.concatenate(
        [bq[0:1], jnp.zeros((1, padded), F32), bq[1:2]], axis=1
    )

    me = lax.axis_index("tensor")
    place = jnp.concatenate([(me ^ s) * tok + jnp.arange(tok, dtype=jnp.int32) for s in range(4)])
    key_bias = jnp.where(place < lengths[0], 0.0, MASKED).astype(F32)[:, None]

    attn_in, qkv = qkv_call(x_rows, vec_rows, wq, qkv_bias, tok)
    up_line = up_slots[4:8:2] + up_slots[2:3] if len(up_slots) == 8 else up_slots * 3
    att, lse, *sent = attn_call(
        heads, ("pieces",), after(qkv, up_line[0]), key_bias, wo, tok, 3 * tok
    )
    att, lse, part_two = attn_call(
        heads, ("own",), after(qkv, up_line[1]), key_bias, wo, tok, 2 * tok, (att, lse)
    )
    total = pair_pieces(part_two, swap_all(sent, "tensor", 1))
    far = swap(total, "tensor", 2)
    att, lse, mine, *sent = attn_call(
        heads,
        ("own", "pieces"),
        after(qkv, total, up_line[2]),
        key_bias,
        wo,
        tok,
        0,
        (att, lse),
    )
    near = swap_all(sent, "tensor", 1)
    residual, mlp_in = row_call(
        residual_body, (inputs, mine, far), near, vec_rows, (F32, BF16), 0, "residual"
    )

    near = swap(mlp_in, "tensor", 1)
    far = swap(mlp_in, "tensor", 2)
    d_hidden = mm(after(cot_rows, mlp_in), wd)
    (wu,) = dp_place([*up_slots[:-1], after(up_slots[-1], d_hidden)], ((0, w_up.shape[1]),))
    hidden, d_pre, bu_sums, mine, *sent = mlp_call(
        ("own", "pieces"), [mlp_in, near], wu, bu, d_hidden, 0, frames
    )
    near_parts = swap_all(sent, "tensor", 1)
    far = after(far, mine)
    slots = [mlp_in, near, far, swap(far, "tensor", 1)]
    hidden, d_pre, sums, *sent = mlp_call(
        ("pieces",), slots[3:], wu, bu, d_hidden, 3 * tok, frames, (hidden, d_pre)
    )
    bu_sums = bu_sums + sums
    hidden, d_pre, sums, part_two = mlp_call(
        ("own",), slots[2:3], wu, bu, d_hidden, 2 * tok, frames, (hidden, d_pre)
    )
    bu_sums = bu_sums + sums
    total = pair_pieces(part_two, swap_all(sent, "tensor", 1))
    far = swap(total, "tensor", 2)
    hidden_later, d_pre_later = tie([hidden, d_pre], total)
    raw_wd = mm(cot_rows, hidden_later, TN).astype(BF16)
    raw_wu = mm(jnp.concatenate(slots, axis=0), after(d_pre_later, raw_wd), TN).astype(BF16)
    near_parts = tie(near_parts, raw_wd, raw_wu)
    grad_wd, grad_wu = dp_scatter_plain(raw_wd), dp_scatter_plain(raw_wu)
    d_residual, d_out, sums_two = row_call(
        second_back_body,
        (residual, mine, far, cotangent),
        near_parts,
        vec_rows,
        (F32, BF16),
        1,
        "second_back",
    )
    block = tok * 2 // 3
    near = swap(d_out, "tensor", 1)
    far = swap(d_out, "tensor", 2)
    out_mine = jnp.concatenate([d_out, near], axis=0)
    carried = attn_back_call(
        heads, out_mine, wo, att, qkv, key_bias, lse, block, 0
    )
    far = after(far, carried[1])
    out_far = jnp.concatenate([far, swap(far, "tensor", 1)], axis=0)
    raw_wo = (mm(out_mine, att[:half], TN) + mm(out_far, att[half:], TN)).astype(BF16)
    out_later = after(out_far, raw_wo)
    d_qkv, bias_sums = attn_back_call(
        heads, out_later, wo, att, qkv, key_bias, lse, block, half, carried
    )
    raw_wq = mm(attn_in, d_qkv, TN).astype(BF16)
    d_qkv, raw_wq, raw_wo = tie([d_qkv, raw_wq, raw_wo])
    raw_first = jnp.concatenate([raw_wq, raw_wo], axis=1)
    owns, crossed = dp_cross(raw_first)
    first_far = mm(d_qkv[half:], wq, NT).astype(BF16)
    far = swap(pair_sum(first_far[:tok], first_far[tok:]), "tensor", 2)
    first_mine = mm(after(d_qkv[:half], first_far, crossed[0]), wq, NT).astype(BF16)
    hidden = after(hidden, first_mine)
    down_far = mm(hidden[half:], wd, NT).astype(BF16)
    output_far = swap(pair_sum(down_far[:tok], down_far[tok:]), "tensor", 2)
    down_mine = mm(hidden[:half], wd, NT).astype(BF16)
    output_near = swap(down_mine[tok:], "tensor", 1)
    quarter = tok // PIECES
    sent = [first_mine[tok + k * quarter : tok + k * quarter + quarter] for k in range(PIECES)]
    near = swap_all(sent, "tensor", 1)
    lined = dp_line(owns, crossed)
    grad_wd = after(grad_wd, first_mine, lined[0], far)
    grad_wu = after(grad_wu, *lined[:2], output_far, output_near)
    output = (
        residual
        + (down_mine[:tok].astype(F32) + output_near.astype(F32) + output_far.astype(F32))
        + vec_rows[5]
    )
    input_grad, sums_one = row_call(
        first_back_body,
        (inputs, first_mine[:tok], far, d_residual),
        near,
        vec_rows,
        (F32,),
        1,
        "first_back",
    )

    vec_sums = tensor_sum(sums_one + sums_two)
    rows_of = jnp.concatenate(
        [
            vec_sums[:6],
            bu_sums[0:1],
            jnp.pad(bias_sums[:2], ((0, 0), (0, width - padded))),
        ],
        axis=0,
    )
    rows_of = dp_sum(rows_of)
    own_cols = lax.dynamic_slice(rows_of, (0, dp_index * own_rows), (7, own_rows))
    vec_grad = jnp.transpose(own_cols[:6])
    bu_grad = own_cols[6]
    bq_grad = jnp.transpose(
        lax.dynamic_slice(rows_of, (7, dp_index * own_bias), (2, own_bias))
    )

    mom_down_new, update_down = momentum(mom_down, grad_wd.astype(F32))
    mom_up_new, update_up = momentum(mom_up, grad_wu.astype(F32))
    early = polar_call(tensor_sum(gram_of(update_down)[None]))
    new_w_down = applied(w_down, early[0], update_down, STEP_DOWN)
    gram_up = gram_of(update_up)
    lined = tie(lined, new_w_down, gram_up, input_grad)
    grad_first = dp_total(lined)
    grad_wq, grad_wo = grad_first[:, :packed], grad_first[:, packed : packed + head_width]
    mom_out_new, update_out = momentum(mom_out, grad_wo)
    spots = (0, padded, padded + head_width)
    grad_parts = jnp.stack([grad_wq[:, spot : spot + head_width] for spot in spots], axis=1)
    mom_qkv_new, update_qkv = momentum(mom_qkv, grad_parts)
    flat = jnp.concatenate(
        [update_qkv[:, 0], jnp.zeros((own_rows, extra), F32), update_qkv[:, 1], update_qkv[:, 2]], axis=1
    )
    late = tensor_sum(jnp.stack([gram_of(update_out), gram_of(flat), gram_up]))
    late = polar_call(after(late, vec_sums))
    new_w_out = applied(w_out, late[0], update_out, STEP_OUT)
    new_w_up = applied(w_up, late[2], update_up, STEP_UP)
    polar_qkv = jnp.dot(late[1], flat, precision=HIGHEST)
    new_w_qkv = w_qkv - STEP_QKV * jnp.stack(
        [polar_qkv[:, spot : spot + head_width] for spot in spots], axis=1
    )

    vec_rate = VEC_RATE / math.sqrt(tokens)
    new_mom_vectors = VEC_DECAY * mom_vectors + vec_grad
    new_mom_bias_qkv = VEC_DECAY * mom_bias_qkv + bq_grad
    new_mom_bias_up = VEC_DECAY * mom_bias_up + bu_grad
    new_vectors = vectors - vec_rate * new_mom_vectors
    new_bias_qkv = bias_qkv - vec_rate * new_mom_bias_qkv
    new_bias_up = bias_up - vec_rate * new_mom_bias_up
    return (
        output,
        input_grad,
        new_w_qkv,
        new_w_out,
        new_w_up,
        new_w_down,
        new_vectors,
        new_bias_qkv,
        new_bias_up,
        mom_qkv_new,
        mom_out_new,
        mom_up_new,
        mom_down_new,
        new_mom_vectors,
        new_mom_bias_qkv,
        new_mom_bias_up,
    )


def solution(mesh):
    in_specs = (
        P(("dp", "tensor"), None),
        P("dp"),
        P(("dp", "tensor"), None),
        P("dp", None, "tensor"),
        P("dp", "tensor"),
        P("dp", "tensor"),
        P("dp", "tensor"),
        P("dp", None),
        P(("tensor", "dp"), None),
        P(("tensor", "dp")),
        P("dp", None, "tensor"),
        P("dp", "tensor"),
        P("dp", "tensor"),
        P("dp", "tensor"),
        P("dp", None),
        P(("tensor", "dp"), None),
        P(("tensor", "dp")),
    )
    out_specs = (
        P(("dp", "tensor"), None),
        P(("dp", "tensor"), None),
        P("dp", None, "tensor"),
        P("dp", "tensor"),
        P("dp", "tensor"),
        P("dp", "tensor"),
        P("dp", None),
        P(("tensor", "dp"), None),
        P(("tensor", "dp")),
        P("dp", None, "tensor"),
        P("dp", "tensor"),
        P("dp", "tensor"),
        P("dp", "tensor"),
        P("dp", None),
        P(("tensor", "dp"), None),
        P(("tensor", "dp")),
    )
    return jax.shard_map(local, mesh=mesh, in_specs=in_specs, out_specs=out_specs, check_vma=False)
```

```python
from functools import partial
import math

import jax
import jax.numpy as jnp
from jax import lax
from jax.experimental import pallas as pl
from jax.experimental.pallas import tpu as pltpu
from jax.sharding import PartitionSpec as P

HD = 80
SWEEPS = 5
LANES = 128
WINDOW = 256
BIAS_LANE = WINDOW - 1
VMEM_LIMIT = 58 * 1024 * 1024

HIGHEST = lax.Precision.HIGHEST
NORM_EPS = 1e-05
POLAR_EPS = 1e-07
MASKED = -1e30
QUINTIC_A = 3.4445
QUINTIC_B = -4.775
QUINTIC_C = 2.0315
MUON_DECAY = 0.95
VEC_DECAY = 0.9
VEC_RATE = 0.1
STEP_QKV = 0.5 * math.sqrt(3.0)
STEP_OUT = 2.0
STEP_UP = 1.0
STEP_DOWN = 0.5
LOG2E = math.log2(math.e)
SCORE_SCALE = 1.0 / math.sqrt(HD)
F32 = jnp.float32
BF16 = jnp.bfloat16
LITTLE = pl.CostEstimate(flops=1_000_000, bytes_accessed=100_000, transcendentals=0)
NN = (((1,), (0,)), ((), ()))
NT = (((1,), (1,)), ((), ()))
TN = (((0,), (0,)), ((), ()))


def mm(left, right, dims=NN):
    return lax.dot_general(left, right, dims, preferred_element_type=F32)


def norm_parts(values):
    center = values - jnp.mean(values, axis=-1, keepdims=True)
    spread = jnp.mean(center * center, axis=-1, keepdims=True)
    scale = lax.rsqrt(spread + NORM_EPS)
    return center * scale, scale


def norm_back(grad, gain, unit, scale):
    inner = grad * gain
    mean_grad = jnp.mean(inner, axis=-1, keepdims=True)
    mean_unit = jnp.mean(inner * unit, axis=-1, keepdims=True)
    return scale * (inner - mean_grad - unit * mean_unit)


def params(*semantics):
    return pltpu.CompilerParams(
        dimension_semantics=semantics or None, vmem_limit_bytes=VMEM_LIMIT
    )


def swap(value, axis, mask):
    size = lax.axis_size(axis)
    return lax.ppermute(value, axis, [(i, i ^ mask) for i in range(size)])


def tensor_slots(own):
    near = swap(own, "tensor", 1)
    far = swap(own, "tensor", 2)
    return [own, near, far, swap(far, "tensor", 1)]


def tensor_gather(own):
    return jnp.concatenate(tensor_slots(own), axis=0)


def tensor_sum(value):
    value = value + swap(value, "tensor", 1)
    return value + swap(value, "tensor", 2)


def pair_sum(own, sent):
    arrived = swap(sent, "tensor", 1)
    return (own.astype(F32) + arrived.astype(F32)).astype(BF16)


def after(value, *others):
    return lax.optimization_barrier((value, *others))[0]


def tie(values, *others):
    return list(lax.optimization_barrier((*values, *others))[: len(values)])


def qkv_body(x_ref, vec_ref, w_ref, bias_ref, attn_ref, qkv_ref):
    unit, _ = norm_parts(x_ref[...].astype(F32))
    attn_in = (unit * vec_ref[0:1, :] + vec_ref[1:2, :]).astype(BF16)
    attn_ref[...] = attn_in
    qkv_ref[...] = (mm(attn_in, w_ref[...]) + bias_ref[0:1, :]).astype(BF16)


def qkv_call(x_rows, vec_rows, weight, bias, block):
    rows, width = x_rows.shape
    columns = weight.shape[1]
    return pl.pallas_call(
        qkv_body,
        grid=(rows // block,),
        in_specs=[
            pl.BlockSpec((block, width), lambda i: (i, 0)),
            pl.BlockSpec(vec_rows.shape, lambda i: (0, 0)),
            pl.BlockSpec(weight.shape, lambda i: (0, 0)),
            pl.BlockSpec(bias.shape, lambda i: (0, 0)),
        ],
        out_specs=[
            pl.BlockSpec((block, width), lambda i: (i, 0)),
            pl.BlockSpec((block, columns), lambda i: (i, 0)),
        ],
        out_shape=[
            jax.ShapeDtypeStruct((rows, width), BF16),
            jax.ShapeDtypeStruct((rows, columns), BF16),
        ],
        compiler_params=params("arbitrary"),
        cost_estimate=LITTLE,
        name="norm_qkv",
    )(x_rows, vec_rows, weight, bias)


PIECES = 4


def part_shapes(emits, rows, width):
    shapes = []
    for kind in emits:
        count = PIECES if kind == "pieces" else 1
        shapes += [jax.ShapeDtypeStruct((rows // count, width), BF16)] * count
    return shapes, [pl.BlockSpec(shape.shape, lambda i: (0, 0)) for shape in shapes]


def part_store(emits, refs, value):
    spot = 0
    for index, kind in enumerate(emits):
        count = PIECES if kind == "pieces" else 1
        group = refs[spot : spot + count]
        spot += count

        @pl.when(pl.program_id(0) == index)
        def _():
            rows = value.shape[0] // count
            for piece, ref in enumerate(group):
                ref[...] = value[piece * rows : piece * rows + rows].astype(BF16)


def swap_all(values, axis, mask):
    return [swap(value, axis, mask) for value in values]


def pair_body(own_ref, *rest):
    pieces, out_ref = rest[:-1], rest[-1]
    for index, piece in enumerate(pieces):

        @pl.when(pl.program_id(0) == index)
        def _():
            out_ref[...] = (own_ref[...].astype(F32) + piece[...].astype(F32)).astype(BF16)


def pair_pieces(own, pieces):
    rows, width = own.shape
    spec = pl.BlockSpec((rows // PIECES, width), lambda i: (i, 0))
    return pl.pallas_call(
        pair_body,
        grid=(PIECES,),
        in_specs=[spec] + [pl.BlockSpec(pieces[0].shape, lambda i: (0, 0))] * PIECES,
        out_specs=spec,
        out_shape=jax.ShapeDtypeStruct(own.shape, BF16),
        compiler_params=params("arbitrary"),
        cost_estimate=LITTLE,
        name="pair_sum",
    )(own, *pieces)


def head_place(head):
    start = 0 if head * HD + HD <= BIAS_LANE else LANES
    return start, head * HD - start


def lane_mask(rows, head):
    _, offset = head_place(head)
    lane = lax.broadcasted_iota(jnp.int32, (rows, WINDOW), 1)
    return (lane >= offset) & (lane < offset + HD), lane == BIAS_LANE


def window(value, head):
    start, _ = head_place(head)
    return value[:, start : start + WINDOW].astype(F32)


def key_columns(qkv_ref):
    third = (qkv_ref.shape[1] + LANES) // 3
    return qkv_ref[:, third : 2 * third]


def value_columns(qkv_ref):
    third = (qkv_ref.shape[1] + LANES) // 3
    tail = qkv_ref[:, qkv_ref.shape[1] - third :].astype(F32)
    return pltpu.roll(tail, third - LANES // 2, 1)


def fill_keys(qkv_ref, bias_ref, keys_out, heads):
    columns = key_columns(qkv_ref)
    for head in range(heads):
        inside, last = lane_mask(columns.shape[0], head)
        picked = jnp.where(inside, window(columns, head), 0.0)
        keys_out[head] = jnp.where(last, bias_ref[...], picked).astype(BF16)


def join_windows(parts):
    low, high = None, None
    for head, part in enumerate(parts):
        if head_place(head)[0] == 0:
            low = part if low is None else low + part
        else:
            high = part if high is None else high + part
    return jnp.concatenate(
        [low[:, :LANES], low[:, LANES:] + high[:, :LANES], high[:, LANES:]], axis=1
    )


def attn_body(heads, emits, skip, q_ref, qkv_ref, bias_ref, wo_ref, *rest):
    (att_ref, lse_ref), parts, (keys, vals) = rest[skip : skip + 2], rest[skip + 2 : -2], rest[-2:]
    block = q_ref.shape[0]
    frames = qkv_ref.shape[0]

    @pl.when(pl.program_id(0) == 0)
    def _():
        fill_keys(qkv_ref, bias_ref, keys, heads)
        columns = value_columns(qkv_ref)
        for head in range(heads):
            inside, _ = lane_mask(frames, head)
            vals[head] = jnp.where(inside, window(columns, head), 0.0).astype(BF16)

    log_scale = SCORE_SCALE * LOG2E
    outs = []
    lane = lax.broadcasted_iota(jnp.int32, (block, LANES), 1)
    lse_cols = jnp.zeros((block, LANES), F32)
    for head in range(heads):
        _, last = lane_mask(block, head)
        query = jnp.where(last, 1.0, window(q_ref, head)).astype(BF16)
        scores = mm(query, keys[head], NT)
        row_max = jnp.max(scores, axis=1, keepdims=True)
        powers = jnp.exp2((scores - row_max) * log_scale)
        totals = jnp.sum(powers, axis=1, keepdims=True)
        outs.append(mm(powers.astype(BF16), vals[head]) * (1.0 / totals))
        lse_cols = jnp.where(lane == head, row_max * log_scale + jnp.log2(totals), lse_cols)
    attended = join_windows(outs).astype(BF16)
    att_ref[...] = attended
    lse_ref[...] = jnp.transpose(lse_cols)[:8]
    part_store(emits, parts, mm(attended, wo_ref[...], NT))


def attn_call(heads, emits, qkv, key_bias, wo, block, first, earlier=None):
    count = block * len(emits)
    frames = qkv.shape[0]
    part_width = wo.shape[1]
    width = wo.shape[0]
    held = [] if earlier is None else list(earlier)
    base = first // block
    shapes, specs = part_shapes(emits, block, width)
    return pl.pallas_call(
        partial(attn_body, heads, emits, len(held)),
        grid=(count // block,),
        in_specs=[
            pl.BlockSpec((block, part_width), lambda i: (i + base, 0)),
            pl.BlockSpec(qkv.shape, lambda i: (0, 0)),
            pl.BlockSpec(key_bias.shape, lambda i: (0, 0)),
            pl.BlockSpec(wo.shape, lambda i: (0, 0)),
        ]
        + [pl.BlockSpec(memory_space=pl.ANY)] * len(held),
        out_specs=[
            pl.BlockSpec((block, part_width), lambda i: (i + base, 0)),
            pl.BlockSpec((8, block), lambda i: (0, i + base)),
        ]
        + specs,
        out_shape=[
            jax.ShapeDtypeStruct((frames, part_width), BF16),
            jax.ShapeDtypeStruct((8, frames), F32),
        ]
        + shapes,
        scratch_shapes=[
            pltpu.VMEM((heads, frames, WINDOW), BF16),
            pltpu.VMEM((heads, frames, WINDOW), BF16),
        ],
        input_output_aliases={} if earlier is None else {4: 0, 5: 1},
        compiler_params=params("arbitrary"),
        cost_estimate=LITTLE,
        name="attn_fwd",
    )(qkv, qkv, key_bias, wo, *held)


def attn_back_body(heads, last_part, first, dout_ref, wo_ref, att_ref, q_ref, qkv_ref, bias_ref, lse_ref, *rest):
    if last_part:
        dkey_in, dval_in, sums_in, _, dqkv_ref, sums_ref, keys, vals, d_query, d_key, d_val, packed, sems = rest
    else:
        dqkv_ref, sums_ref, d_key, d_val, keys, vals, d_query, sems = rest
    step = pl.program_id(0)
    block, part_width = q_ref.shape
    count = d_query.shape[0]

    @pl.when(step == 0)
    def _():
        fill_keys(qkv_ref, bias_ref, keys, heads)
        vals[...] = value_columns(qkv_ref).astype(BF16)
        if last_part:
            d_key[...] = dkey_in[...]
            d_val[...] = dval_in[...]
            sums_ref[...] = sums_in[...]
        else:
            d_key[...] = jnp.zeros_like(d_key)
            d_val[...] = jnp.zeros_like(d_val)
            sums_ref[...] = jnp.zeros_like(sums_ref)

    log_scale = SCORE_SCALE * LOG2E
    d_att = mm(dout_ref[...], wo_ref[...]).astype(BF16)
    inner_cols = jnp.transpose(d_att.astype(F32) * att_ref[...].astype(F32))
    outs = []
    for head in range(heads):
        start, _ = head_place(head)
        inside, last = lane_mask(block, head)
        q_window = window(q_ref, head)
        query = jnp.where(last, 1.0, q_window).astype(BF16)
        q_only = jnp.where(inside, q_window, 0.0).astype(BF16)
        d_only = jnp.where(inside, window(d_att, head), 0.0).astype(BF16)
        inner = jnp.sum(inner_cols[head * HD : head * HD + HD], axis=0, keepdims=True)
        scores = mm(keys[head], query, NT)
        probs = jnp.exp2(scores * log_scale - lse_ref[head : head + 1, :])
        d_probs = mm(vals[:, start : start + WINDOW], d_only, NT)
        d_scores = (probs * (d_probs - inner)).astype(BF16)
        d_val[:, start : start + WINDOW] += mm(probs.astype(BF16), d_only)
        d_key[:, start : start + WINDOW] += mm(d_scores, q_only)
        outs.append(mm(d_scores, keys[head], TN))
    low = (join_windows(outs) * SCORE_SCALE).astype(BF16)
    d_query[pl.ds(pl.multiple_of(step * block, block), block), :] = low
    sums_ref[0:1, :] += jnp.sum(low.astype(F32), axis=0, keepdims=True)

    @pl.when(step == pl.num_programs(0) - 1)
    def _():
        copies = [
            pltpu.make_async_copy(
                d_query, dqkv_ref.at[pl.ds(first, count), pl.ds(0, part_width)], sems.at[0]
            )
        ]
        copies[0].start()
        if last_part:
            key_low = d_key[...] * SCORE_SCALE
            value_low = d_val[...]
            sums_ref[1:2, :] = jnp.sum(value_low.astype(BF16).astype(F32), axis=0, keepdims=True)
            value_low = pltpu.roll(value_low, LANES // 2, 1)
            whole = part_width - LANES
            packed[:, :whole] = key_low[:, :whole].astype(BF16)
            packed[:, whole:part_width] = (key_low[:, whole:] + value_low[:, :LANES]).astype(BF16)
            packed[:, part_width:] = value_low[:, LANES:].astype(BF16)
            copies.append(
                pltpu.make_async_copy(
                    packed,
                    dqkv_ref.at[pl.ds(0, packed.shape[0]), pl.ds(part_width, packed.shape[1])],
                    sems.at[1],
                )
            )
            copies[1].start()
        for copy in copies:
            copy.wait()


def attn_back_call(heads, d_out, wo, attended, qkv, key_bias, lse, block, first, earlier=None):
    count, width = d_out.shape
    frames = qkv.shape[0]
    part_width = wo.shape[1]
    base = first // block
    last_part = earlier is not None
    whole = pl.BlockSpec((frames, part_width), lambda i: (0, 0))
    sums_spec = pl.BlockSpec((8, part_width), lambda i: (0, 0))
    anywhere = pl.BlockSpec(memory_space=pl.ANY)
    out_shape = [
        jax.ShapeDtypeStruct(qkv.shape, BF16),
        jax.ShapeDtypeStruct((8, part_width), F32),
    ]
    out_specs = [anywhere, sums_spec]
    scratch = [
        pltpu.VMEM((heads, frames, WINDOW), BF16),
        pltpu.VMEM((frames, part_width), BF16),
        pltpu.VMEM((count, part_width), BF16),
    ]
    held = []
    if last_part:
        d_qkv, sums, d_key, d_val = earlier
        held = [d_key, d_val, sums, d_qkv]
        scratch += [pltpu.VMEM((frames, part_width), F32)] * 2
        scratch += [pltpu.VMEM((frames, qkv.shape[1] - part_width), BF16)]
    else:
        out_shape += [jax.ShapeDtypeStruct((frames, part_width), F32)] * 2
        out_specs += [whole, whole]
    return pl.pallas_call(
        partial(attn_back_body, heads, last_part, first),
        grid=(count // block,),
        in_specs=[
            pl.BlockSpec((block, width), lambda i: (i, 0)),
            pl.BlockSpec(wo.shape, lambda i: (0, 0)),
            pl.BlockSpec((block, part_width), lambda i: (i + base, 0)),
            pl.BlockSpec((block, part_width), lambda i: (i + base, 0)),
            pl.BlockSpec(qkv.shape, lambda i: (0, 0)),
            pl.BlockSpec(key_bias.shape, lambda i: (0, 0)),
            pl.BlockSpec((8, block), lambda i: (0, i + base)),
        ]
        + [whole, whole, sums_spec, anywhere][: len(held)],
        out_specs=out_specs,
        out_shape=out_shape,
        scratch_shapes=scratch + [pltpu.SemaphoreType.DMA((2,))],
        input_output_aliases={10: 0} if last_part else {},
        compiler_params=params("arbitrary"),
        cost_estimate=LITTLE,
        name="attn_bwd",
    )(d_out, wo, attended, qkv, qkv, key_bias, lse, *held)


def gelu_parts(values):
    size = jnp.abs(values)
    bell = jnp.exp2(values * values * (-0.5 * LOG2E))
    inv = 1.0 / (1.0 + (0.3275911 * math.sqrt(0.5)) * size)
    tail = inv * (
        0.5 * 0.254829592
        + inv
        * (
            0.5 * -0.284496736
            + inv * (0.5 * 1.421413741 + inv * (0.5 * -1.453152027 + inv * (0.5 * 1.061405429)))
        )
    )
    tail = tail * bell
    share = jnp.where(values < 0.0, tail, 1.0 - tail)
    return share, share + values * bell * (1.0 / math.sqrt(2.0 * math.pi))


def mlp_body(chunk, emits, skip, *refs):
    slot_refs, (w_ref, bias_ref, dhid_ref) = refs[: len(emits)], refs[len(emits) : len(emits) + 3]
    outs = refs[len(emits) + 3 + skip :]
    hid_ref, dpre_ref, sums_ref, parts, in_ref = *outs[:3], outs[3:-1], outs[-1]
    for index, slot_ref in enumerate(slot_refs):

        @pl.when(pl.program_id(0) == index)
        def _():
            in_ref[...] = slot_ref[...]

    @pl.when(pl.program_id(0) == 0)
    def _():
        sums_ref[...] = jnp.zeros_like(sums_ref)

    for start in range(0, w_ref.shape[1], chunk):
        cols = slice(start, start + chunk)
        pre = mm(in_ref[...], w_ref[:, cols]) + bias_ref[0:1, cols]
        share, slope = gelu_parts(pre)
        hid_ref[:, cols] = (pre * share).astype(BF16)
        d_pre = (dhid_ref[:, cols] * slope).astype(BF16)
        dpre_ref[:, cols] = d_pre
        sums_ref[0:1, cols] += jnp.sum(d_pre.astype(F32), axis=0, keepdims=True)
    part_store(emits, parts, mm(dpre_ref[...], w_ref[...], NT))


def mlp_call(emits, slots, weight, bias, d_hidden, first, frames, earlier=None):
    block, width = slots[0].shape
    count = block * len(slots)
    hidden_width = weight.shape[1]
    held = [] if earlier is None else list(earlier)
    base = first // block
    shapes, specs = part_shapes(emits, block, width)
    return pl.pallas_call(
        partial(mlp_body, min(256, hidden_width), emits, len(held)),
        grid=(count // block,),
        in_specs=[pl.BlockSpec((block, width), lambda i: (0, 0))] * len(slots)
        + [
            pl.BlockSpec(weight.shape, lambda i: (0, 0)),
            pl.BlockSpec(bias.shape, lambda i: (0, 0)),
            pl.BlockSpec((block, hidden_width), lambda i: (i + base, 0)),
        ]
        + [pl.BlockSpec(memory_space=pl.ANY)] * len(held),
        out_specs=[
            pl.BlockSpec((block, hidden_width), lambda i: (i + base, 0)),
            pl.BlockSpec((block, hidden_width), lambda i: (i + base, 0)),
            pl.BlockSpec((8, hidden_width), lambda i: (0, 0)),
        ]
        + specs,
        out_shape=[
            jax.ShapeDtypeStruct((frames, hidden_width), BF16),
            jax.ShapeDtypeStruct((frames, hidden_width), BF16),
            jax.ShapeDtypeStruct((8, hidden_width), F32),
        ]
        + shapes,
        scratch_shapes=[pltpu.VMEM((block, width), BF16)],
        input_output_aliases=(
            {} if earlier is None else {len(slots) + 3: 0, len(slots) + 4: 1}
        ),
        compiler_params=params("arbitrary"),
        cost_estimate=LITTLE,
        name="mlp_up",
    )(*slots, weight, bias, d_hidden, *held)


def residual_body(x_ref, mine_ref, far_ref, near_ref, vec_ref, res_ref, in_ref):
    total = mine_ref[...].astype(F32) + near_ref[...].astype(F32) + far_ref[...].astype(F32)
    residual = x_ref[...].astype(F32) + total + vec_ref[2:3, :]
    res_ref[...] = residual
    unit, _ = norm_parts(residual)
    in_ref[...] = (unit * vec_ref[3:4, :] + vec_ref[4:5, :]).astype(BF16)


def second_back_body(
    res_ref, mine_ref, far_ref, cot_ref, near_ref, vec_ref, dres_ref, low_ref, sums_ref
):
    @pl.when(pl.program_id(0) == 0)
    def _():
        sums_ref[...] = jnp.zeros_like(sums_ref)

    grad = mine_ref[...].astype(F32) + near_ref[...].astype(F32) + far_ref[...].astype(F32)
    unit, scale = norm_parts(res_ref[...])
    cot = cot_ref[...].astype(F32)
    d_res = norm_back(grad, vec_ref[3:4, :], unit, scale) + cot
    dres_ref[...] = d_res
    low_ref[...] = d_res.astype(BF16)
    sums_ref[2:3, :] += jnp.sum(d_res, axis=0, keepdims=True)
    sums_ref[3:4, :] += jnp.sum(grad * unit, axis=0, keepdims=True)
    sums_ref[4:5, :] += jnp.sum(grad, axis=0, keepdims=True)
    sums_ref[5:6, :] += jnp.sum(cot, axis=0, keepdims=True)


def first_back_body(x_ref, mine_ref, far_ref, dres_ref, near_ref, vec_ref, out_ref, sums_ref):
    @pl.when(pl.program_id(0) == 0)
    def _():
        sums_ref[...] = jnp.zeros_like(sums_ref)

    grad = mine_ref[...].astype(F32) + near_ref[...].astype(F32) + far_ref[...].astype(F32)
    unit, scale = norm_parts(x_ref[...].astype(F32))
    out_ref[...] = norm_back(grad, vec_ref[0:1, :], unit, scale) + dres_ref[...]
    sums_ref[0:1, :] += jnp.sum(grad * unit, axis=0, keepdims=True)
    sums_ref[1:2, :] += jnp.sum(grad, axis=0, keepdims=True)


def row_body(body, count, *refs):
    row_refs, pieces, vec_ref = refs[:count], refs[count : count + PIECES], refs[count + PIECES]
    near_ref = refs[-1]
    for index, piece in enumerate(pieces):

        @pl.when(pl.program_id(0) == index)
        def _():
            near_ref[...] = piece[...]

    body(*row_refs, near_ref, vec_ref, *refs[count + PIECES + 1 : -1])


def row_call(body, rows_in, near, vec_rows, out_types, with_sums, name):
    rows, width = rows_in[0].shape
    block = rows // PIECES
    row_spec = pl.BlockSpec((block, width), lambda i: (i, 0))
    whole = pl.BlockSpec((8, width), lambda i: (0, 0))
    return pl.pallas_call(
        partial(row_body, body, len(rows_in)),
        grid=(PIECES,),
        in_specs=[row_spec] * len(rows_in)
        + [pl.BlockSpec((block, width), lambda i: (0, 0))] * PIECES
        + [whole],
        out_specs=[row_spec] * len(out_types) + [whole] * with_sums,
        out_shape=[jax.ShapeDtypeStruct((rows, width), kind) for kind in out_types]
        + [jax.ShapeDtypeStruct((8, width), F32)] * with_sums,
        scratch_shapes=[pltpu.VMEM((block, width), BF16)],
        compiler_params=params("arbitrary"),
        cost_estimate=LITTLE,
        name=name,
    )(*rows_in, *near, vec_rows)


def polar_factors(grams, eye):
    def high(left, right):
        return jnp.dot(left, right, precision=HIGHEST, preferred_element_type=F32)

    scales = [1.0 / (jnp.sqrt(jnp.sum(gram * eye, keepdims=True)) + POLAR_EPS) for gram in grams]
    grams = [gram * scale * scale for gram, scale in zip(grams, scales)]
    factors = None
    for sweep in range(SWEEPS):
        squares = [high(gram, gram) for gram in grams]
        steps = [
            QUINTIC_A * eye + QUINTIC_B * gram + QUINTIC_C * square
            for gram, square in zip(grams, squares)
        ]
        if sweep < SWEEPS - 1:
            halves = [high(step, gram) for step, gram in zip(steps, grams)]
        if factors is None:
            factors = steps
        else:
            factors = [high(step, factor) for step, factor in zip(steps, factors)]
        if sweep < SWEEPS - 1:
            grams = [high(step, part) for step, part in zip(steps, halves)]
    return [factor * scale for factor, scale in zip(factors, scales)]


def polar_body(gram_ref, out_ref):
    count, rows, _ = gram_ref.shape
    row = lax.broadcasted_iota(jnp.int32, (rows, rows), 0)
    col = lax.broadcasted_iota(jnp.int32, (rows, rows), 1)
    eye = jnp.where(row == col, 1.0, 0.0)
    for index, factor in enumerate(polar_factors([gram_ref[i] for i in range(count)], eye)):
        out_ref[index] = factor


def polar_call(grams):
    count, rows, _ = grams.shape
    if rows % 32:
        return jnp.stack(polar_factors([grams[i] for i in range(count)], jnp.eye(rows, dtype=F32)))
    return pl.pallas_call(
        polar_body,
        out_shape=jax.ShapeDtypeStruct(grams.shape, F32),
        compiler_params=params(),
        name="polar",
    )(grams)


def gram_of(update):
    return lax.dot_general(update, update, NT, precision=HIGHEST, preferred_element_type=F32)


def momentum(moment, gradient):
    moved = MUON_DECAY * moment + gradient
    return moved, gradient + MUON_DECAY * moved


def applied(weight, factor, update, rate):
    return weight - rate * jnp.dot(factor, update, precision=HIGHEST)


def place_body(splits, narrow, me_ref, *refs):
    slots, outs = refs[:8], refs[8:]
    rows = slots[0].shape[0]
    for mask, slot in enumerate(slots):
        start = pl.multiple_of((me_ref[0] ^ mask) * rows, rows)
        for (low, high), out in zip(splits, outs):
            out[pl.ds(start, rows), :] = slot[:, low:high]
    if narrow is not None:
        tile = narrow // LANES * LANES
        turned = jnp.transpose(outs[0][:, tile : tile + LANES].astype(F32))
        outs[-1][...] = turned[narrow - tile : narrow - tile + 16]


def place_rows(slots, splits, narrow):
    rows = slots[0].shape[0]
    shapes = [jax.ShapeDtypeStruct((8 * rows, high - low), slots[0].dtype) for low, high in splits]
    if narrow is not None:
        shapes.append(jax.ShapeDtypeStruct((16, 8 * rows), F32))
    return pl.pallas_call(
        partial(place_body, splits, narrow),
        in_specs=[pl.BlockSpec(memory_space=pltpu.SMEM)]
        + [pl.BlockSpec(memory_space=pltpu.VMEM)] * 8,
        out_specs=[pl.BlockSpec(memory_space=pltpu.VMEM)] * len(shapes),
        out_shape=shapes,
        compiler_params=params(),
        cost_estimate=LITTLE,
        name="place_rows",
    )(lax.axis_index("dp").astype(jnp.int32)[None], *slots)


def dp_slots(own, ordered=False):
    line = {mask: swap(own, "dp", mask) for mask in (6, 2, 4)}
    slots = [own, swap(own, "dp", 1)] + [None] * 6
    for mask in (6, 2, 4):
        arrived = line[mask]
        if ordered:
            held = [slots[1]] if mask == 2 else [slots[3], slots[7]] if mask == 4 else []
            arrived = after(arrived, *held)
        slots[mask] = arrived
        slots[mask + 1] = swap(arrived, "dp", 1)
    return slots


def dp_send(own, ordered=False):
    if lax.axis_size("dp") != 8:
        return [lax.all_gather(own, "dp", axis=0, tiled=True)]
    return dp_slots(own, ordered)


def dp_place(slots, splits, narrow=None):
    if len(slots) > 1:
        return place_rows(slots, splits, narrow)
    parts = [slots[0][:, low:high] for low, high in splits]
    if narrow is not None:
        parts.append(jnp.transpose(slots[0][:, narrow : narrow + 16].astype(F32)))
    return parts


LINE = (4, 6, 2, 0)


def dp_cross(part):
    size = lax.axis_size("dp")
    if size != 8:
        return [], [dp_scatter_plain(part)]
    rows = part.shape[0] // size
    me = lax.axis_index("dp")

    def block(mask):
        return lax.dynamic_slice(part, ((me ^ mask) * rows, 0), (rows, part.shape[1]))

    return [block(mask) for mask in LINE], [swap(block(mask + 1), "dp", 1) for mask in LINE]


def dp_line(owns, arrivals):
    if not owns:
        return arrivals
    sums, pair = [], None
    for mask, own, arrived in zip(LINE, owns, arrivals):
        arrived = arrived if pair is None else after(arrived, pair)
        pair = own.astype(F32) + arrived.astype(F32)
        sums.append(swap(pair.astype(BF16), "dp", mask) if mask else pair)
    return sums


def dp_total(sums):
    total = sums[-1].astype(F32)
    for value in sums[:-1]:
        total = total + value.astype(F32)
    return total


def dp_scatter_plain(part):
    return lax.psum_scatter(part, "dp", scatter_dimension=0, tiled=True)


def dp_sum(value):
    if lax.axis_size("dp") != 8:
        return lax.psum(value, "dp")
    for mask in (1, 2, 4):
        value = value + swap(value, "dp", mask)
    return value


def local(
    inputs,
    lengths,
    cotangent,
    w_qkv,
    w_out,
    w_up,
    w_down,
    vectors,
    bias_qkv,
    bias_up,
    mom_qkv,
    mom_out,
    mom_up,
    mom_down,
    mom_vectors,
    mom_bias_qkv,
    mom_bias_up,
):
    dp_size = lax.axis_size("dp")
    tensor_size = lax.axis_size("tensor")
    dp_index = lax.axis_index("dp")
    tok = inputs.shape[0]
    frames = tok * tensor_size
    tokens = frames * dp_size
    half = 2 * tok
    width = inputs.shape[1]
    own_rows = w_qkv.shape[0]
    head_width = w_qkv.shape[2]
    heads = head_width // HD
    padded = -(-head_width // LANES) * LANES
    extra = padded - head_width
    own_bias = bias_qkv.shape[0]

    w_parts = w_qkv.astype(BF16)
    small = jnp.concatenate(
        [
            vectors.astype(BF16),
            bias_up.astype(BF16)[:, None],
            jnp.pad(bias_qkv.astype(BF16), ((0, own_rows - own_bias), (0, 0))),
        ],
        axis=1,
    )
    small = jnp.pad(small, ((0, 0), (0, extra - small.shape[1])))
    packed = 3 * head_width + extra
    w_cols = jnp.concatenate(
        [
            w_parts[:, 0],
            small,
            w_parts[:, 1],
            w_parts[:, 2],
            jnp.pad(w_out.astype(BF16), ((0, 0), (0, extra))),
        ],
        axis=1,
    )
    first_slots = dp_send(w_cols, True)
    x_far = after(swap(inputs, "tensor", 2), *first_slots[2:7:4])
    x_rows = jnp.concatenate(
        [inputs, swap(inputs, "tensor", 1), x_far, swap(x_far, "tensor", 1)], axis=0
    )
    cot_far = after(swap(cotangent, "tensor", 2), *first_slots[4:5])
    cot_rows = jnp.concatenate(
        [cotangent, swap(cotangent, "tensor", 1), cot_far, swap(cot_far, "tensor", 1)], axis=0
    )
    first_slots[-1], x_rows, cot_rows = tie([first_slots[-1], x_rows, cot_rows])
    wq, wo, smalls = dp_place(
        first_slots, ((0, packed), (packed, packed + padded)), head_width
    )
    wd = lax.all_gather(w_down.astype(BF16), "dp", axis=0, tiled=True)
    w_up_low = after(w_up.astype(BF16), *first_slots)
    up_slots = dp_send(w_up_low)
    vec_rows = smalls[:8]
    bu = smalls[6:7]
    bq = smalls[7:9].reshape(2, dp_size, own_rows)[:, :, :own_bias].reshape(2, head_width)
    qkv_bias = jnp.concatenate(
        [bq[0:1], jnp.zeros((1, padded), F32), bq[1:2]], axis=1
    )

    me = lax.axis_index("tensor")
    place = jnp.concatenate([(me ^ s) * tok + jnp.arange(tok, dtype=jnp.int32) for s in range(4)])
    key_bias = jnp.where(place < lengths[0], 0.0, MASKED).astype(F32)[:, None]

    attn_in, qkv = qkv_call(x_rows, vec_rows, wq, qkv_bias, tok)
    up_line = up_slots[4:8:2] + up_slots[2:3] if len(up_slots) == 8 else up_slots * 3
    att, lse, *sent = attn_call(
        heads, ("pieces",), qkv, key_bias, wo, tok, 3 * tok
    )
    att, lse, part_two = attn_call(
        heads, ("own",), after(qkv, up_line[0]), key_bias, wo, tok, 2 * tok, (att, lse)
    )
    total = pair_pieces(after(part_two, up_line[1]), swap_all(sent, "tensor", 1))
    far = swap(total, "tensor", 2)
    att, lse, mine, *sent = attn_call(
        heads,
        ("own", "pieces"),
        after(qkv, total),
        key_bias,
        wo,
        tok,
        0,
        (att, lse),
    )
    near = swap_all(sent, "tensor", 1)
    residual, mlp_in = row_call(
        residual_body, (inputs, mine, after(far, up_line[2], wd, *up_slots[1:6:4])), near, vec_rows, (F32, BF16), 0, "residual"
    )

    near = swap(mlp_in, "tensor", 1)
    far = swap(mlp_in, "tensor", 2)
    d_hidden = mm(after(cot_rows, mlp_in), wd)
    (wu,) = dp_place([*up_slots[:-1], after(up_slots[-1], d_hidden)], ((0, w_up.shape[1]),))
    hidden, d_pre, bu_sums, mine, *sent = mlp_call(
        ("own", "pieces"), [mlp_in, near], wu, bu, d_hidden, 0, frames
    )
    near_parts = swap_all(sent, "tensor", 1)
    far = after(far, mine)
    slots = [mlp_in, near, far, swap(far, "tensor", 1)]
    hidden, d_pre, sums, *sent = mlp_call(
        ("pieces",), slots[3:], wu, bu, d_hidden, 3 * tok, frames, (hidden, d_pre)
    )
    bu_sums = bu_sums + sums
    hidden, d_pre, sums, part_two = mlp_call(
        ("own",), slots[2:3], wu, bu, d_hidden, 2 * tok, frames, (hidden, d_pre)
    )
    bu_sums = bu_sums + sums
    total = pair_pieces(part_two, swap_all(sent, "tensor", 1))
    far = swap(total, "tensor", 2)
    hidden_later, d_pre_later = tie([hidden, d_pre], total)
    raw_wd = mm(cot_rows, hidden_later, TN).astype(BF16)
    raw_wu = mm(jnp.concatenate(slots, axis=0), after(d_pre_later, raw_wd), TN).astype(BF16)
    hidden = after(hidden, raw_wu)
    down_far = mm(hidden[half:], wd, NT).astype(BF16)
    down_mine = mm(hidden[:half], wd, NT).astype(BF16)
    near_parts = tie(near_parts, raw_wd, raw_wu, down_far, down_mine)
    grad_wd, grad_wu = dp_scatter_plain(raw_wd), dp_scatter_plain(raw_wu)
    d_residual, d_out, sums_two = row_call(
        second_back_body,
        (residual, mine, far, cotangent),
        near_parts,
        vec_rows,
        (F32, BF16),
        1,
        "second_back",
    )
    block = tok * 2 // 3
    near = swap(d_out, "tensor", 1)
    far = swap(d_out, "tensor", 2)
    out_mine = jnp.concatenate([d_out, near], axis=0)
    carried = attn_back_call(
        heads, out_mine, wo, att, qkv, key_bias, lse, block, 0
    )
    far = after(far, carried[1])
    output_far = swap(after(pair_sum(down_far[:tok], down_far[tok:]), far), "tensor", 2)
    output_near = swap(down_mine[tok:], "tensor", 1)
    out_far = jnp.concatenate([far, swap(far, "tensor", 1)], axis=0)
    raw_wo = (mm(out_mine, att[:half], TN) + mm(out_far, att[half:], TN)).astype(BF16)
    out_later = after(out_far, raw_wo)
    d_qkv, bias_sums = attn_back_call(
        heads, out_later, wo, att, qkv, key_bias, lse, block, half, carried
    )
    raw_wq = mm(attn_in, after(d_qkv, grad_wd, output_far, output_near), TN).astype(BF16)
    d_qkv, raw_wq, raw_wo = tie([d_qkv, raw_wq, raw_wo])
    raw_first = jnp.concatenate([raw_wq, raw_wo], axis=1)
    owns, crossed = dp_cross(raw_first)
    first_far = mm(d_qkv[half:], wq, NT).astype(BF16)
    far = swap(pair_sum(first_far[:tok], first_far[tok:]), "tensor", 2)
    lined = dp_line(owns, crossed)
    grad_wd = after(grad_wd, first_far, *crossed[:2])
    mom_down_new, update_down = momentum(mom_down, grad_wd.astype(F32))
    early = polar_call(tensor_sum(gram_of(update_down)[None]))
    new_w_down = applied(w_down, early[0], update_down, STEP_DOWN)
    first_gate = (first_far, far, new_w_down, grad_wu, *crossed, *lined[:1])
    first_mine = mm(after(d_qkv[:half], *first_gate), wq, NT).astype(BF16)
    quarter = tok // PIECES
    sent = [first_mine[tok + k * quarter : tok + k * quarter + quarter] for k in range(PIECES)]
    near = swap_all(sent, "tensor", 1)
    grad_wu = after(grad_wu, first_mine, lined[0])
    output = (
        residual
        + (down_mine[:tok].astype(F32) + output_near.astype(F32) + output_far.astype(F32))
        + vec_rows[5]
    )
    input_grad, sums_one = row_call(
        first_back_body,
        (inputs, first_mine[:tok], far, d_residual),
        near,
        vec_rows,
        (F32,),
        1,
        "first_back",
    )

    vec_sums = tensor_sum(sums_one + sums_two)
    rows_of = jnp.concatenate(
        [
            vec_sums[:6],
            bu_sums[0:1],
            jnp.pad(bias_sums[:2], ((0, 0), (0, width - padded))),
        ],
        axis=0,
    )
    rows_of = dp_sum(rows_of)
    own_cols = lax.dynamic_slice(rows_of, (0, dp_index * own_rows), (7, own_rows))
    vec_grad = jnp.transpose(own_cols[:6])
    bu_grad = own_cols[6]
    bq_grad = jnp.transpose(
        lax.dynamic_slice(rows_of, (7, dp_index * own_bias), (2, own_bias))
    )

    mom_up_new, update_up = momentum(mom_up, grad_wu.astype(F32))
    gram_up = gram_of(update_up)
    lined = tie(lined, gram_up, input_grad)
    grad_first = dp_total(lined)
    grad_wq, grad_wo = grad_first[:, :packed], grad_first[:, packed : packed + head_width]
    mom_out_new, update_out = momentum(mom_out, grad_wo)
    spots = (0, padded, padded + head_width)
    grad_parts = jnp.stack([grad_wq[:, spot : spot + head_width] for spot in spots], axis=1)
    mom_qkv_new, update_qkv = momentum(mom_qkv, grad_parts)
    flat = jnp.concatenate(
        [update_qkv[:, 0], jnp.zeros((own_rows, extra), F32), update_qkv[:, 1], update_qkv[:, 2]], axis=1
    )
    late = tensor_sum(jnp.stack([gram_of(update_out), gram_of(flat), gram_up]))
    late = polar_call(after(late, vec_sums))
    new_w_out = applied(w_out, late[0], update_out, STEP_OUT)
    new_w_up = applied(w_up, late[2], update_up, STEP_UP)
    polar_qkv = jnp.dot(late[1], flat, precision=HIGHEST)
    new_w_qkv = w_qkv - STEP_QKV * jnp.stack(
        [polar_qkv[:, spot : spot + head_width] for spot in spots], axis=1
    )

    vec_rate = VEC_RATE / math.sqrt(tokens)
    new_mom_vectors = VEC_DECAY * mom_vectors + vec_grad
    new_mom_bias_qkv = VEC_DECAY * mom_bias_qkv + bq_grad
    new_mom_bias_up = VEC_DECAY * mom_bias_up + bu_grad
    new_vectors = vectors - vec_rate * new_mom_vectors
    new_bias_qkv = bias_qkv - vec_rate * new_mom_bias_qkv
    new_bias_up = bias_up - vec_rate * new_mom_bias_up
    return (
        output,
        input_grad,
        new_w_qkv,
        new_w_out,
        new_w_up,
        new_w_down,
        new_vectors,
        new_bias_qkv,
        new_bias_up,
        mom_qkv_new,
        mom_out_new,
        mom_up_new,
        mom_down_new,
        new_mom_vectors,
        new_mom_bias_qkv,
        new_mom_bias_up,
    )


def solution(mesh):
    in_specs = (
        P(("dp", "tensor"), None),
        P("dp"),
        P(("dp", "tensor"), None),
        P("dp", None, "tensor"),
        P("dp", "tensor"),
        P("dp", "tensor"),
        P("dp", "tensor"),
        P("dp", None),
        P(("tensor", "dp"), None),
        P(("tensor", "dp")),
        P("dp", None, "tensor"),
        P("dp", "tensor"),
        P("dp", "tensor"),
        P("dp", "tensor"),
        P("dp", None),
        P(("tensor", "dp"), None),
        P(("tensor", "dp")),
    )
    out_specs = (
        P(("dp", "tensor"), None),
        P(("dp", "tensor"), None),
        P("dp", None, "tensor"),
        P("dp", "tensor"),
        P("dp", "tensor"),
        P("dp", "tensor"),
        P("dp", None),
        P(("tensor", "dp"), None),
        P(("tensor", "dp")),
        P("dp", None, "tensor"),
        P("dp", "tensor"),
        P("dp", "tensor"),
        P("dp", "tensor"),
        P("dp", None),
        P(("tensor", "dp"), None),
        P(("tensor", "dp")),
    )
    return jax.shard_map(local, mesh=mesh, in_specs=in_specs, out_specs=out_specs, check_vma=False)
```

```python
from functools import partial
import math

import jax
import jax.numpy as jnp
from jax import lax
from jax.experimental import pallas as pl
from jax.experimental.pallas import tpu as pltpu
from jax.sharding import PartitionSpec as P

HD = 80
SWEEPS = 5
LANES = 128
WINDOW = 256
BIAS_LANE = WINDOW - 1
VMEM_LIMIT = 58 * 1024 * 1024

HIGHEST = lax.Precision.HIGHEST
NORM_EPS = 1e-05
POLAR_EPS = 1e-07
MASKED = -1e30
QUINTIC_A = 3.4445
QUINTIC_B = -4.775
QUINTIC_C = 2.0315
MUON_DECAY = 0.95
VEC_DECAY = 0.9
VEC_RATE = 0.1
STEP_QKV = 0.5 * math.sqrt(3.0)
STEP_OUT = 2.0
STEP_UP = 1.0
STEP_DOWN = 0.5
LOG2E = math.log2(math.e)
SCORE_SCALE = 1.0 / math.sqrt(HD)
F32 = jnp.float32
BF16 = jnp.bfloat16
LITTLE = pl.CostEstimate(flops=1_000_000, bytes_accessed=100_000, transcendentals=0)
NN = (((1,), (0,)), ((), ()))
NT = (((1,), (1,)), ((), ()))
TN = (((0,), (0,)), ((), ()))


def mm(left, right, dims=NN):
    return lax.dot_general(left, right, dims, preferred_element_type=F32)


def norm_parts(values):
    center = values - jnp.mean(values, axis=-1, keepdims=True)
    spread = jnp.mean(center * center, axis=-1, keepdims=True)
    scale = lax.rsqrt(spread + NORM_EPS)
    return center * scale, scale


def norm_back(grad, gain, unit, scale):
    inner = grad * gain
    mean_grad = jnp.mean(inner, axis=-1, keepdims=True)
    mean_unit = jnp.mean(inner * unit, axis=-1, keepdims=True)
    return scale * (inner - mean_grad - unit * mean_unit)


def params(*semantics):
    return pltpu.CompilerParams(
        dimension_semantics=semantics or None, vmem_limit_bytes=VMEM_LIMIT
    )


def swap(value, axis, mask):
    size = lax.axis_size(axis)
    return lax.ppermute(value, axis, [(i, i ^ mask) for i in range(size)])


def tensor_slots(own):
    near = swap(own, "tensor", 1)
    far = swap(own, "tensor", 2)
    return [own, near, far, swap(far, "tensor", 1)]


def tensor_gather(own):
    return jnp.concatenate(tensor_slots(own), axis=0)


def tensor_sum(value):
    value = value + swap(value, "tensor", 1)
    return value + swap(value, "tensor", 2)


def pair_sum(own, sent):
    arrived = swap(sent, "tensor", 1)
    return (own.astype(F32) + arrived.astype(F32)).astype(BF16)


def after(value, *others):
    return lax.optimization_barrier((value, *others))[0]


def tie(values, *others):
    return list(lax.optimization_barrier((*values, *others))[: len(values)])


def qkv_body(x_ref, vec_ref, w_ref, bias_ref, attn_ref, qkv_ref):
    unit, _ = norm_parts(x_ref[...].astype(F32))
    attn_in = (unit * vec_ref[0:1, :] + vec_ref[1:2, :]).astype(BF16)
    attn_ref[...] = attn_in
    qkv_ref[...] = (mm(attn_in, w_ref[...]) + bias_ref[0:1, :]).astype(BF16)


def qkv_call(x_rows, vec_rows, weight, bias, block):
    rows, width = x_rows.shape
    columns = weight.shape[1]
    return pl.pallas_call(
        qkv_body,
        grid=(rows // block,),
        in_specs=[
            pl.BlockSpec((block, width), lambda i: (i, 0)),
            pl.BlockSpec(vec_rows.shape, lambda i: (0, 0)),
            pl.BlockSpec(weight.shape, lambda i: (0, 0)),
            pl.BlockSpec(bias.shape, lambda i: (0, 0)),
        ],
        out_specs=[
            pl.BlockSpec((block, width), lambda i: (i, 0)),
            pl.BlockSpec((block, columns), lambda i: (i, 0)),
        ],
        out_shape=[
            jax.ShapeDtypeStruct((rows, width), BF16),
            jax.ShapeDtypeStruct((rows, columns), BF16),
        ],
        compiler_params=params("arbitrary"),
        cost_estimate=LITTLE,
        name="norm_qkv",
    )(x_rows, vec_rows, weight, bias)


PIECES = 4


def part_shapes(emits, rows, width):
    shapes = []
    for kind in emits:
        count = PIECES if kind == "pieces" else 1
        shapes += [jax.ShapeDtypeStruct((rows // count, width), BF16)] * count
    return shapes, [pl.BlockSpec(shape.shape, lambda i: (0, 0)) for shape in shapes]


def part_store(emits, refs, value):
    spot = 0
    for index, kind in enumerate(emits):
        count = PIECES if kind == "pieces" else 1
        group = refs[spot : spot + count]
        spot += count

        @pl.when(pl.program_id(0) == index)
        def _():
            rows = value.shape[0] // count
            for piece, ref in enumerate(group):
                ref[...] = value[piece * rows : piece * rows + rows].astype(BF16)


def swap_all(values, axis, mask):
    return [swap(value, axis, mask) for value in values]


def pair_body(own_ref, *rest):
    pieces, out_ref = rest[:-1], rest[-1]
    rows = pieces[0].shape[0]
    for index, piece in enumerate(pieces):
        part = slice(index * rows, index * rows + rows)
        out_ref[part, :] = (own_ref[part, :].astype(F32) + piece[...].astype(F32)).astype(BF16)


def pair_pieces(own, pieces):
    return pl.pallas_call(
        pair_body,
        out_shape=jax.ShapeDtypeStruct(own.shape, BF16),
        compiler_params=params(),
        cost_estimate=LITTLE,
        name="pair_sum",
    )(own, *pieces)


def head_place(head):
    start = 0 if head * HD + HD <= BIAS_LANE else LANES
    return start, head * HD - start


def lane_mask(rows, head):
    _, offset = head_place(head)
    lane = lax.broadcasted_iota(jnp.int32, (rows, WINDOW), 1)
    return (lane >= offset) & (lane < offset + HD), lane == BIAS_LANE


def window(value, head):
    start, _ = head_place(head)
    return value[:, start : start + WINDOW].astype(F32)


def key_columns(qkv_ref):
    third = (qkv_ref.shape[1] + LANES) // 3
    return qkv_ref[:, third : 2 * third]


def value_columns(qkv_ref):
    third = (qkv_ref.shape[1] + LANES) // 3
    tail = qkv_ref[:, qkv_ref.shape[1] - third :].astype(F32)
    return pltpu.roll(tail, third - LANES // 2, 1)


def fill_keys(qkv_ref, bias_ref, keys_out, heads):
    columns = key_columns(qkv_ref)
    for head in range(heads):
        inside, last = lane_mask(columns.shape[0], head)
        picked = jnp.where(inside, window(columns, head), 0.0)
        keys_out[head] = jnp.where(last, bias_ref[...], picked).astype(BF16)


def join_windows(parts):
    low, high = None, None
    for head, part in enumerate(parts):
        if head_place(head)[0] == 0:
            low = part if low is None else low + part
        else:
            high = part if high is None else high + part
    return jnp.concatenate(
        [low[:, :LANES], low[:, LANES:] + high[:, :LANES], high[:, LANES:]], axis=1
    )


def attn_body(heads, emits, skip, q_ref, qkv_ref, bias_ref, wo_ref, *rest):
    (att_ref, lse_ref), parts, (keys, vals) = rest[skip : skip + 2], rest[skip + 2 : -2], rest[-2:]
    block = q_ref.shape[0]
    frames = qkv_ref.shape[0]

    @pl.when(pl.program_id(0) == 0)
    def _():
        fill_keys(qkv_ref, bias_ref, keys, heads)
        columns = value_columns(qkv_ref)
        for head in range(heads):
            inside, _ = lane_mask(frames, head)
            vals[head] = jnp.where(inside, window(columns, head), 0.0).astype(BF16)

    log_scale = SCORE_SCALE * LOG2E
    outs = []
    lane = lax.broadcasted_iota(jnp.int32, (block, LANES), 1)
    lse_cols = jnp.zeros((block, LANES), F32)
    for head in range(heads):
        _, last = lane_mask(block, head)
        query = jnp.where(last, 1.0, window(q_ref, head)).astype(BF16)
        scores = mm(query, keys[head], NT)
        row_max = jnp.max(scores, axis=1, keepdims=True)
        powers = jnp.exp2((scores - row_max) * log_scale)
        totals = jnp.sum(powers, axis=1, keepdims=True)
        outs.append(mm(powers.astype(BF16), vals[head]) * (1.0 / totals))
        lse_cols = jnp.where(lane == head, row_max * log_scale + jnp.log2(totals), lse_cols)
    attended = join_windows(outs).astype(BF16)
    att_ref[...] = attended
    lse_ref[...] = jnp.transpose(lse_cols)[:8]
    part_store(emits, parts, mm(attended, wo_ref[...], NT))


def attn_call(heads, emits, qkv, key_bias, wo, block, first, earlier=None):
    count = block * len(emits)
    frames = qkv.shape[0]
    part_width = wo.shape[1]
    width = wo.shape[0]
    held = [] if earlier is None else list(earlier)
    base = first // block
    shapes, specs = part_shapes(emits, block, width)
    return pl.pallas_call(
        partial(attn_body, heads, emits, len(held)),
        grid=(count // block,),
        in_specs=[
            pl.BlockSpec((block, part_width), lambda i: (i + base, 0)),
            pl.BlockSpec(qkv.shape, lambda i: (0, 0)),
            pl.BlockSpec(key_bias.shape, lambda i: (0, 0)),
            pl.BlockSpec(wo.shape, lambda i: (0, 0)),
        ]
        + [pl.BlockSpec(memory_space=pl.ANY)] * len(held),
        out_specs=[
            pl.BlockSpec((block, part_width), lambda i: (i + base, 0)),
            pl.BlockSpec((8, block), lambda i: (0, i + base)),
        ]
        + specs,
        out_shape=[
            jax.ShapeDtypeStruct((frames, part_width), BF16),
            jax.ShapeDtypeStruct((8, frames), F32),
        ]
        + shapes,
        scratch_shapes=[
            pltpu.VMEM((heads, frames, WINDOW), BF16),
            pltpu.VMEM((heads, frames, WINDOW), BF16),
        ],
        input_output_aliases={} if earlier is None else {4: 0, 5: 1},
        compiler_params=params("arbitrary"),
        cost_estimate=LITTLE,
        name="attn_fwd",
    )(qkv, qkv, key_bias, wo, *held)


def attn_back_body(heads, last_part, first, dout_ref, wo_ref, att_ref, q_ref, qkv_ref, bias_ref, lse_ref, *rest):
    if last_part:
        dkey_in, dval_in, sums_in, _, dqkv_ref, sums_ref, keys, vals, d_query, d_key, d_val, packed, sems = rest
    else:
        dqkv_ref, sums_ref, d_key, d_val, keys, vals, d_query, sems = rest
    step = pl.program_id(0)
    block, part_width = q_ref.shape
    count = d_query.shape[0]

    @pl.when(step == 0)
    def _():
        fill_keys(qkv_ref, bias_ref, keys, heads)
        vals[...] = value_columns(qkv_ref).astype(BF16)
        if last_part:
            d_key[...] = dkey_in[...]
            d_val[...] = dval_in[...]
            sums_ref[...] = sums_in[...]
        else:
            d_key[...] = jnp.zeros_like(d_key)
            d_val[...] = jnp.zeros_like(d_val)
            sums_ref[...] = jnp.zeros_like(sums_ref)

    log_scale = SCORE_SCALE * LOG2E
    d_att = mm(dout_ref[...], wo_ref[...]).astype(BF16)
    inner_cols = jnp.transpose(d_att.astype(F32) * att_ref[...].astype(F32))
    outs = []
    for head in range(heads):
        start, _ = head_place(head)
        inside, last = lane_mask(block, head)
        q_window = window(q_ref, head)
        query = jnp.where(last, 1.0, q_window).astype(BF16)
        q_only = jnp.where(inside, q_window, 0.0).astype(BF16)
        d_only = jnp.where(inside, window(d_att, head), 0.0).astype(BF16)
        inner = jnp.sum(inner_cols[head * HD : head * HD + HD], axis=0, keepdims=True)
        scores = mm(keys[head], query, NT)
        probs = jnp.exp2(scores * log_scale - lse_ref[head : head + 1, :])
        d_probs = mm(vals[:, start : start + WINDOW], d_only, NT)
        d_scores = (probs * (d_probs - inner)).astype(BF16)
        d_val[:, start : start + WINDOW] += mm(probs.astype(BF16), d_only)
        d_key[:, start : start + WINDOW] += mm(d_scores, q_only)
        outs.append(mm(d_scores, keys[head], TN))
    low = (join_windows(outs) * SCORE_SCALE).astype(BF16)
    d_query[pl.ds(pl.multiple_of(step * block, block), block), :] = low
    sums_ref[0:1, :] += jnp.sum(low.astype(F32), axis=0, keepdims=True)

    @pl.when(step == pl.num_programs(0) - 1)
    def _():
        copies = [
            pltpu.make_async_copy(
                d_query, dqkv_ref.at[pl.ds(first, count), pl.ds(0, part_width)], sems.at[0]
            )
        ]
        copies[0].start()
        if last_part:
            key_low = d_key[...] * SCORE_SCALE
            value_low = d_val[...]
            sums_ref[1:2, :] = jnp.sum(value_low.astype(BF16).astype(F32), axis=0, keepdims=True)
            value_low = pltpu.roll(value_low, LANES // 2, 1)
            whole = part_width - LANES
            packed[:, :whole] = key_low[:, :whole].astype(BF16)
            packed[:, whole:part_width] = (key_low[:, whole:] + value_low[:, :LANES]).astype(BF16)
            packed[:, part_width:] = value_low[:, LANES:].astype(BF16)
            copies.append(
                pltpu.make_async_copy(
                    packed,
                    dqkv_ref.at[pl.ds(0, packed.shape[0]), pl.ds(part_width, packed.shape[1])],
                    sems.at[1],
                )
            )
            copies[1].start()
        for copy in copies:
            copy.wait()


def attn_back_call(heads, d_out, wo, attended, qkv, key_bias, lse, block, first, earlier=None):
    count, width = d_out.shape
    frames = qkv.shape[0]
    part_width = wo.shape[1]
    base = first // block
    last_part = earlier is not None
    whole = pl.BlockSpec((frames, part_width), lambda i: (0, 0))
    sums_spec = pl.BlockSpec((8, part_width), lambda i: (0, 0))
    anywhere = pl.BlockSpec(memory_space=pl.ANY)
    out_shape = [
        jax.ShapeDtypeStruct(qkv.shape, BF16),
        jax.ShapeDtypeStruct((8, part_width), F32),
    ]
    out_specs = [anywhere, sums_spec]
    scratch = [
        pltpu.VMEM((heads, frames, WINDOW), BF16),
        pltpu.VMEM((frames, part_width), BF16),
        pltpu.VMEM((count, part_width), BF16),
    ]
    held = []
    if last_part:
        d_qkv, sums, d_key, d_val = earlier
        held = [d_key, d_val, sums, d_qkv]
        scratch += [pltpu.VMEM((frames, part_width), F32)] * 2
        scratch += [pltpu.VMEM((frames, qkv.shape[1] - part_width), BF16)]
    else:
        out_shape += [jax.ShapeDtypeStruct((frames, part_width), F32)] * 2
        out_specs += [whole, whole]
    return pl.pallas_call(
        partial(attn_back_body, heads, last_part, first),
        grid=(count // block,),
        in_specs=[
            pl.BlockSpec((block, width), lambda i: (i, 0)),
            pl.BlockSpec(wo.shape, lambda i: (0, 0)),
            pl.BlockSpec((block, part_width), lambda i: (i + base, 0)),
            pl.BlockSpec((block, part_width), lambda i: (i + base, 0)),
            pl.BlockSpec(qkv.shape, lambda i: (0, 0)),
            pl.BlockSpec(key_bias.shape, lambda i: (0, 0)),
            pl.BlockSpec((8, block), lambda i: (0, i + base)),
        ]
        + [whole, whole, sums_spec, anywhere][: len(held)],
        out_specs=out_specs,
        out_shape=out_shape,
        scratch_shapes=scratch + [pltpu.SemaphoreType.DMA((2,))],
        input_output_aliases={10: 0} if last_part else {},
        compiler_params=params("arbitrary"),
        cost_estimate=LITTLE,
        name="attn_bwd",
    )(d_out, wo, attended, qkv, qkv, key_bias, lse, *held)


def gelu_parts(values):
    size = jnp.abs(values)
    bell = jnp.exp2(values * values * (-0.5 * LOG2E))
    inv = 1.0 / (1.0 + (0.3275911 * math.sqrt(0.5)) * size)
    tail = inv * (
        0.5 * 0.254829592
        + inv
        * (
            0.5 * -0.284496736
            + inv * (0.5 * 1.421413741 + inv * (0.5 * -1.453152027 + inv * (0.5 * 1.061405429)))
        )
    )
    tail = tail * bell
    share = jnp.where(values < 0.0, tail, 1.0 - tail)
    return share, share + values * bell * (1.0 / math.sqrt(2.0 * math.pi))


def mlp_body(chunk, emits, skip, *refs):
    slot_refs, (w_ref, bias_ref, dhid_ref) = refs[: len(emits)], refs[len(emits) : len(emits) + 3]
    outs = refs[len(emits) + 3 + skip :]
    hid_ref, dpre_ref, sums_ref, parts, in_ref = *outs[:3], outs[3:-1], outs[-1]
    for index, slot_ref in enumerate(slot_refs):

        @pl.when(pl.program_id(0) == index)
        def _():
            in_ref[...] = slot_ref[...]

    @pl.when(pl.program_id(0) == 0)
    def _():
        sums_ref[...] = jnp.zeros_like(sums_ref)

    for start in range(0, w_ref.shape[1], chunk):
        cols = slice(start, start + chunk)
        pre = mm(in_ref[...], w_ref[:, cols]) + bias_ref[0:1, cols]
        share, slope = gelu_parts(pre)
        hid_ref[:, cols] = (pre * share).astype(BF16)
        d_pre = (dhid_ref[:, cols] * slope).astype(BF16)
        dpre_ref[:, cols] = d_pre
        sums_ref[0:1, cols] += jnp.sum(d_pre.astype(F32), axis=0, keepdims=True)
    part_store(emits, parts, mm(dpre_ref[...], w_ref[...], NT))


def mlp_call(emits, slots, weight, bias, d_hidden, first, frames, earlier=None):
    block, width = slots[0].shape
    count = block * len(slots)
    hidden_width = weight.shape[1]
    held = [] if earlier is None else list(earlier)
    base = first // block
    shapes, specs = part_shapes(emits, block, width)
    return pl.pallas_call(
        partial(mlp_body, min(256, hidden_width), emits, len(held)),
        grid=(count // block,),
        in_specs=[pl.BlockSpec((block, width), lambda i: (0, 0))] * len(slots)
        + [
            pl.BlockSpec(weight.shape, lambda i: (0, 0)),
            pl.BlockSpec(bias.shape, lambda i: (0, 0)),
            pl.BlockSpec((block, hidden_width), lambda i: (i + base, 0)),
        ]
        + [pl.BlockSpec(memory_space=pl.ANY)] * len(held),
        out_specs=[
            pl.BlockSpec((block, hidden_width), lambda i: (i + base, 0)),
            pl.BlockSpec((block, hidden_width), lambda i: (i + base, 0)),
            pl.BlockSpec((8, hidden_width), lambda i: (0, 0)),
        ]
        + specs,
        out_shape=[
            jax.ShapeDtypeStruct((frames, hidden_width), BF16),
            jax.ShapeDtypeStruct((frames, hidden_width), BF16),
            jax.ShapeDtypeStruct((8, hidden_width), F32),
        ]
        + shapes,
        scratch_shapes=[pltpu.VMEM((block, width), BF16)],
        input_output_aliases=(
            {} if earlier is None else {len(slots) + 3: 0, len(slots) + 4: 1}
        ),
        compiler_params=params("arbitrary"),
        cost_estimate=LITTLE,
        name="mlp_up",
    )(*slots, weight, bias, d_hidden, *held)


def residual_body(x_ref, mine_ref, far_ref, near_ref, vec_ref, res_ref, in_ref):
    total = mine_ref[...].astype(F32) + near_ref[...].astype(F32) + far_ref[...].astype(F32)
    residual = x_ref[...].astype(F32) + total + vec_ref[2:3, :]
    res_ref[...] = residual
    unit, _ = norm_parts(residual)
    in_ref[...] = (unit * vec_ref[3:4, :] + vec_ref[4:5, :]).astype(BF16)


def second_back_body(
    res_ref, mine_ref, far_ref, cot_ref, near_ref, vec_ref, dres_ref, low_ref, sums_ref
):
    @pl.when(pl.program_id(0) == 0)
    def _():
        sums_ref[...] = jnp.zeros_like(sums_ref)

    grad = mine_ref[...].astype(F32) + near_ref[...].astype(F32) + far_ref[...].astype(F32)
    unit, scale = norm_parts(res_ref[...])
    cot = cot_ref[...].astype(F32)
    d_res = norm_back(grad, vec_ref[3:4, :], unit, scale) + cot
    dres_ref[...] = d_res
    low_ref[...] = d_res.astype(BF16)
    sums_ref[2:3, :] += jnp.sum(d_res, axis=0, keepdims=True)
    sums_ref[3:4, :] += jnp.sum(grad * unit, axis=0, keepdims=True)
    sums_ref[4:5, :] += jnp.sum(grad, axis=0, keepdims=True)
    sums_ref[5:6, :] += jnp.sum(cot, axis=0, keepdims=True)


def first_back_body(x_ref, mine_ref, far_ref, dres_ref, near_ref, vec_ref, out_ref, sums_ref):
    @pl.when(pl.program_id(0) == 0)
    def _():
        sums_ref[...] = jnp.zeros_like(sums_ref)

    grad = mine_ref[...].astype(F32) + near_ref[...].astype(F32) + far_ref[...].astype(F32)
    unit, scale = norm_parts(x_ref[...].astype(F32))
    out_ref[...] = norm_back(grad, vec_ref[0:1, :], unit, scale) + dres_ref[...]
    sums_ref[0:1, :] += jnp.sum(grad * unit, axis=0, keepdims=True)
    sums_ref[1:2, :] += jnp.sum(grad, axis=0, keepdims=True)


def row_body(body, count, *refs):
    row_refs, pieces, vec_ref = refs[:count], refs[count : count + PIECES], refs[count + PIECES]
    near_ref = refs[-1]
    for index, piece in enumerate(pieces):

        @pl.when(pl.program_id(0) == index)
        def _():
            near_ref[...] = piece[...]

    body(*row_refs, near_ref, vec_ref, *refs[count + PIECES + 1 : -1])


def row_call(body, rows_in, near, vec_rows, out_types, with_sums, name):
    rows, width = rows_in[0].shape
    block = rows // PIECES
    row_spec = pl.BlockSpec((block, width), lambda i: (i, 0))
    whole = pl.BlockSpec((8, width), lambda i: (0, 0))
    return pl.pallas_call(
        partial(row_body, body, len(rows_in)),
        grid=(PIECES,),
        in_specs=[row_spec] * len(rows_in)
        + [pl.BlockSpec((block, width), lambda i: (0, 0))] * PIECES
        + [whole],
        out_specs=[row_spec] * len(out_types) + [whole] * with_sums,
        out_shape=[jax.ShapeDtypeStruct((rows, width), kind) for kind in out_types]
        + [jax.ShapeDtypeStruct((8, width), F32)] * with_sums,
        scratch_shapes=[pltpu.VMEM((block, width), BF16)],
        compiler_params=params("arbitrary"),
        cost_estimate=LITTLE,
        name=name,
    )(*rows_in, *near, vec_rows)


def polar_factors(grams, eye):
    def high(left, right):
        return jnp.dot(left, right, precision=HIGHEST, preferred_element_type=F32)

    scales = [1.0 / (jnp.sqrt(jnp.sum(gram * eye, keepdims=True)) + POLAR_EPS) for gram in grams]
    grams = [gram * scale * scale for gram, scale in zip(grams, scales)]
    factors = None
    for sweep in range(SWEEPS):
        squares = [high(gram, gram) for gram in grams]
        steps = [
            QUINTIC_A * eye + QUINTIC_B * gram + QUINTIC_C * square
            for gram, square in zip(grams, squares)
        ]
        if sweep < SWEEPS - 1:
            halves = [high(step, gram) for step, gram in zip(steps, grams)]
        if factors is None:
            factors = steps
        else:
            factors = [high(step, factor) for step, factor in zip(steps, factors)]
        if sweep < SWEEPS - 1:
            grams = [high(step, part) for step, part in zip(steps, halves)]
    return [factor * scale for factor, scale in zip(factors, scales)]


def polar_body(gram_ref, out_ref):
    count, rows, _ = gram_ref.shape
    row = lax.broadcasted_iota(jnp.int32, (rows, rows), 0)
    col = lax.broadcasted_iota(jnp.int32, (rows, rows), 1)
    eye = jnp.where(row == col, 1.0, 0.0)
    for index, factor in enumerate(polar_factors([gram_ref[i] for i in range(count)], eye)):
        out_ref[index] = factor


def polar_call(grams):
    count, rows, _ = grams.shape
    if rows % 32:
        return jnp.stack(polar_factors([grams[i] for i in range(count)], jnp.eye(rows, dtype=F32)))
    return pl.pallas_call(
        polar_body,
        out_shape=jax.ShapeDtypeStruct(grams.shape, F32),
        compiler_params=params(),
        name="polar",
    )(grams)


def gram_of(update):
    return lax.dot_general(update, update, NT, precision=HIGHEST, preferred_element_type=F32)


def momentum(moment, gradient):
    moved = MUON_DECAY * moment + gradient
    return moved, gradient + MUON_DECAY * moved


def applied(weight, factor, update, rate):
    return weight - rate * jnp.dot(factor, update, precision=HIGHEST)


def place_body(splits, narrow, me_ref, *refs):
    slots, outs = refs[:8], refs[8:]
    rows = slots[0].shape[0]
    for mask, slot in enumerate(slots):
        start = pl.multiple_of((me_ref[0] ^ mask) * rows, rows)
        for (low, high), out in zip(splits, outs):
            out[pl.ds(start, rows), :] = slot[:, low:high]
    if narrow is not None:
        tile = narrow // LANES * LANES
        turned = jnp.transpose(outs[0][:, tile : tile + LANES].astype(F32))
        outs[-1][...] = turned[narrow - tile : narrow - tile + 16]


def place_rows(slots, splits, narrow):
    rows = slots[0].shape[0]
    shapes = [jax.ShapeDtypeStruct((8 * rows, high - low), slots[0].dtype) for low, high in splits]
    if narrow is not None:
        shapes.append(jax.ShapeDtypeStruct((16, 8 * rows), F32))
    return pl.pallas_call(
        partial(place_body, splits, narrow),
        in_specs=[pl.BlockSpec(memory_space=pltpu.SMEM)]
        + [pl.BlockSpec(memory_space=pltpu.VMEM)] * 8,
        out_specs=[pl.BlockSpec(memory_space=pltpu.VMEM)] * len(shapes),
        out_shape=shapes,
        compiler_params=params(),
        cost_estimate=LITTLE,
        name="place_rows",
    )(lax.axis_index("dp").astype(jnp.int32)[None], *slots)


def dp_slots(own, ordered=False):
    line = {mask: swap(own, "dp", mask) for mask in (6, 2, 4)}
    slots = [own, swap(own, "dp", 1)] + [None] * 6
    for mask in (6, 2, 4):
        arrived = line[mask]
        if ordered:
            held = [slots[1]] if mask == 2 else [slots[3], slots[7]] if mask == 4 else []
            arrived = after(arrived, *held)
        slots[mask] = arrived
        slots[mask + 1] = swap(arrived, "dp", 1)
    return slots


def dp_send(own, ordered=False):
    if lax.axis_size("dp") != 8:
        return [lax.all_gather(own, "dp", axis=0, tiled=True)]
    return dp_slots(own, ordered)


def dp_place(slots, splits, narrow=None):
    if len(slots) > 1:
        return place_rows(slots, splits, narrow)
    parts = [slots[0][:, low:high] for low, high in splits]
    if narrow is not None:
        parts.append(jnp.transpose(slots[0][:, narrow : narrow + 16].astype(F32)))
    return parts


LINE = (4, 6, 2, 0)


def dp_cross(part):
    size = lax.axis_size("dp")
    if size != 8:
        return [], [dp_scatter_plain(part)]
    rows = part.shape[0] // size
    me = lax.axis_index("dp")

    def block(mask):
        return lax.dynamic_slice(part, ((me ^ mask) * rows, 0), (rows, part.shape[1]))

    return [block(mask) for mask in LINE], [swap(block(mask + 1), "dp", 1) for mask in LINE]


def dp_line(owns, arrivals):
    if not owns:
        return arrivals
    sums = []
    for mask, own, arrived in zip(LINE, owns, arrivals):
        pair = own.astype(F32) + arrived.astype(F32)
        sums.append(swap(pair.astype(BF16), "dp", mask) if mask else pair)
    return sums


def dp_total(sums):
    total = sums[-1].astype(F32)
    for value in sums[:-1]:
        total = total + value.astype(F32)
    return total


def dp_scatter_plain(part):
    return lax.psum_scatter(part, "dp", scatter_dimension=0, tiled=True)


def dp_sum(value):
    if lax.axis_size("dp") != 8:
        return lax.psum(value, "dp")
    for mask in (1, 2, 4):
        value = value + swap(value, "dp", mask)
    return value


def local(
    inputs,
    lengths,
    cotangent,
    w_qkv,
    w_out,
    w_up,
    w_down,
    vectors,
    bias_qkv,
    bias_up,
    mom_qkv,
    mom_out,
    mom_up,
    mom_down,
    mom_vectors,
    mom_bias_qkv,
    mom_bias_up,
):
    dp_size = lax.axis_size("dp")
    tensor_size = lax.axis_size("tensor")
    dp_index = lax.axis_index("dp")
    tok = inputs.shape[0]
    frames = tok * tensor_size
    tokens = frames * dp_size
    half = 2 * tok
    width = inputs.shape[1]
    own_rows = w_qkv.shape[0]
    head_width = w_qkv.shape[2]
    heads = head_width // HD
    padded = -(-head_width // LANES) * LANES
    extra = padded - head_width
    own_bias = bias_qkv.shape[0]

    w_parts = w_qkv.astype(BF16)
    small = jnp.concatenate(
        [
            vectors.astype(BF16),
            bias_up.astype(BF16)[:, None],
            jnp.pad(bias_qkv.astype(BF16), ((0, own_rows - own_bias), (0, 0))),
        ],
        axis=1,
    )
    small = jnp.pad(small, ((0, 0), (0, extra - small.shape[1])))
    packed = 3 * head_width + extra
    w_cols = jnp.concatenate(
        [
            w_parts[:, 0],
            small,
            w_parts[:, 1],
            w_parts[:, 2],
            jnp.pad(w_out.astype(BF16), ((0, 0), (0, extra))),
        ],
        axis=1,
    )
    first_slots = dp_send(w_cols, True)
    x_far = after(swap(inputs, "tensor", 2), *first_slots[2:7:4])
    x_rows = jnp.concatenate(
        [inputs, swap(inputs, "tensor", 1), x_far, swap(x_far, "tensor", 1)], axis=0
    )
    cot_far = after(swap(cotangent, "tensor", 2), *first_slots[4:5])
    cot_rows = jnp.concatenate(
        [cotangent, swap(cotangent, "tensor", 1), cot_far, swap(cot_far, "tensor", 1)], axis=0
    )
    first_slots[-1], x_rows, cot_rows = tie([first_slots[-1], x_rows, cot_rows])
    wq, wo, smalls = dp_place(
        first_slots, ((0, packed), (packed, packed + padded)), head_width
    )
    wd = lax.all_gather(w_down.astype(BF16), "dp", axis=0, tiled=True)
    wu = lax.all_gather(w_up.astype(BF16), "dp", axis=0, tiled=True)
    vec_rows = smalls[:8]
    bu = smalls[6:7]
    bq = smalls[7:9].reshape(2, dp_size, own_rows)[:, :, :own_bias].reshape(2, head_width)
    qkv_bias = jnp.concatenate(
        [bq[0:1], jnp.zeros((1, padded), F32), bq[1:2]], axis=1
    )

    me = lax.axis_index("tensor")
    place = jnp.concatenate([(me ^ s) * tok + jnp.arange(tok, dtype=jnp.int32) for s in range(4)])
    key_bias = jnp.where(place < lengths[0], 0.0, MASKED).astype(F32)[:, None]

    attn_in, qkv = qkv_call(x_rows, vec_rows, wq, qkv_bias, tok)
    att, lse, *sent = attn_call(
        heads, ("pieces",), qkv, key_bias, wo, tok, 3 * tok
    )
    att, lse, part_two = attn_call(
        heads, ("own",), qkv, key_bias, wo, tok, 2 * tok, (att, lse)
    )
    total = pair_pieces(part_two, swap_all(sent, "tensor", 1))
    far = swap(total, "tensor", 2)
    att, lse, mine, *sent = attn_call(
        heads,
        ("own", "pieces"),
        after(qkv, total),
        key_bias,
        wo,
        tok,
        0,
        (att, lse),
    )
    near = swap_all(sent, "tensor", 1)
    residual, mlp_in = row_call(
        residual_body, (inputs, mine, after(far, wd)), near, vec_rows, (F32, BF16), 0, "residual"
    )

    near = swap(mlp_in, "tensor", 1)
    far = swap(mlp_in, "tensor", 2)
    d_hidden = mm(after(cot_rows, mlp_in, wu), wd)
    hidden, d_pre, bu_sums, mine, *sent = mlp_call(
        ("own", "pieces"), [mlp_in, near], wu, bu, d_hidden, 0, frames
    )
    near_parts = swap_all(sent, "tensor", 1)
    far = after(far, mine)
    slots = [mlp_in, near, far, swap(far, "tensor", 1)]
    hidden, d_pre, sums, *sent = mlp_call(
        ("pieces",), slots[3:], wu, bu, d_hidden, 3 * tok, frames, (hidden, d_pre)
    )
    bu_sums = bu_sums + sums
    hidden, d_pre, sums, part_two = mlp_call(
        ("own",), slots[2:3], wu, bu, d_hidden, 2 * tok, frames, (hidden, d_pre)
    )
    bu_sums = bu_sums + sums
    total = pair_pieces(part_two, swap_all(sent, "tensor", 1))
    far = swap(total, "tensor", 2)
    hidden_later, d_pre_later = tie([hidden, d_pre], total)
    raw_wd = mm(cot_rows, hidden_later, TN).astype(BF16)
    raw_wu = mm(jnp.concatenate(slots, axis=0), after(d_pre_later, raw_wd), TN).astype(BF16)
    hidden = after(hidden, raw_wu)
    down_far = mm(hidden[half:], wd, NT).astype(BF16)
    down_mine = mm(hidden[:half], wd, NT).astype(BF16)
    near_parts = tie(near_parts, raw_wd, raw_wu, down_far, down_mine)
    grad_wd, grad_wu = dp_scatter_plain(raw_wd), dp_scatter_plain(raw_wu)
    d_residual, d_out, sums_two = row_call(
        second_back_body,
        (residual, mine, far, cotangent),
        near_parts,
        vec_rows,
        (F32, BF16),
        1,
        "second_back",
    )
    block = tok * 2 // 3
    near = swap(d_out, "tensor", 1)
    far = swap(d_out, "tensor", 2)
    out_mine = jnp.concatenate([d_out, near], axis=0)
    carried = attn_back_call(
        heads, out_mine, wo, att, qkv, key_bias, lse, block, 0
    )
    far = after(far, carried[1])
    output_far = swap(after(pair_sum(down_far[:tok], down_far[tok:]), far), "tensor", 2)
    output_near = swap(down_mine[tok:], "tensor", 1)
    out_far = jnp.concatenate([far, swap(far, "tensor", 1)], axis=0)
    raw_wo = (mm(out_mine, att[:half], TN) + mm(out_far, att[half:], TN)).astype(BF16)
    out_later = after(out_far, raw_wo)
    d_qkv, bias_sums = attn_back_call(
        heads, out_later, wo, att, qkv, key_bias, lse, block, half, carried
    )
    raw_wq = mm(attn_in, after(d_qkv, grad_wd, output_far, output_near), TN).astype(BF16)
    d_qkv, raw_wq, raw_wo = tie([d_qkv, raw_wq, raw_wo])
    raw_first = jnp.concatenate([raw_wq, raw_wo], axis=1)
    owns, crossed = dp_cross(raw_first)
    first_far = mm(d_qkv[half:], wq, NT).astype(BF16)
    far = swap(pair_sum(first_far[:tok], first_far[tok:]), "tensor", 2)
    lined = dp_line(owns, crossed)
    first_mine = mm(after(d_qkv[:half], first_far), wq, NT).astype(BF16)
    grad_wd = after(grad_wd, first_mine, *crossed)
    mom_down_new, update_down = momentum(mom_down, grad_wd.astype(F32))
    early = polar_call(tensor_sum(gram_of(update_down)[None]))
    new_w_down = applied(w_down, early[0], update_down, STEP_DOWN)
    quarter = tok // PIECES
    sent = [first_mine[tok + k * quarter : tok + k * quarter + quarter] for k in range(PIECES)]
    near = swap_all(sent, "tensor", 1)
    grad_wu = after(after(grad_wu, first_mine, *crossed), *lined[:2])
    output = (
        residual
        + (down_mine[:tok].astype(F32) + output_near.astype(F32) + output_far.astype(F32))
        + vec_rows[5]
    )
    input_grad, sums_one = row_call(
        first_back_body,
        (inputs, first_mine[:tok], far, d_residual),
        near,
        vec_rows,
        (F32,),
        1,
        "first_back",
    )

    vec_sums = tensor_sum(sums_one + sums_two)
    rows_of = jnp.concatenate(
        [
            vec_sums[:6],
            bu_sums[0:1],
            jnp.pad(bias_sums[:2], ((0, 0), (0, width - padded))),
        ],
        axis=0,
    )
    rows_of = dp_sum(rows_of)
    own_cols = lax.dynamic_slice(rows_of, (0, dp_index * own_rows), (7, own_rows))
    vec_grad = jnp.transpose(own_cols[:6])
    bu_grad = own_cols[6]
    bq_grad = jnp.transpose(
        lax.dynamic_slice(rows_of, (7, dp_index * own_bias), (2, own_bias))
    )

    mom_up_new, update_up = momentum(mom_up, grad_wu.astype(F32))
    middle = polar_call(tensor_sum(gram_of(update_up)[None]))
    new_w_up = applied(w_up, middle[0], update_up, STEP_UP)
    lined = tie(lined, new_w_up, new_w_down, rows_of)
    grad_first = dp_total(lined)
    grad_wq, grad_wo = grad_first[:, :packed], grad_first[:, packed : packed + head_width]
    mom_out_new, update_out = momentum(mom_out, grad_wo)
    spots = (0, padded, padded + head_width)
    grad_parts = jnp.stack([grad_wq[:, spot : spot + head_width] for spot in spots], axis=1)
    mom_qkv_new, update_qkv = momentum(mom_qkv, grad_parts)
    flat = jnp.concatenate(
        [update_qkv[:, 0], jnp.zeros((own_rows, extra), F32), update_qkv[:, 1], update_qkv[:, 2]], axis=1
    )
    late = tensor_sum(jnp.stack([gram_of(update_out), gram_of(flat)]))
    late = polar_call(late)
    new_w_out = applied(w_out, late[0], update_out, STEP_OUT)
    polar_qkv = jnp.dot(late[1], flat, precision=HIGHEST)
    new_w_qkv = w_qkv - STEP_QKV * jnp.stack(
        [polar_qkv[:, spot : spot + head_width] for spot in spots], axis=1
    )

    vec_rate = VEC_RATE / math.sqrt(tokens)
    new_mom_vectors = VEC_DECAY * mom_vectors + vec_grad
    new_mom_bias_qkv = VEC_DECAY * mom_bias_qkv + bq_grad
    new_mom_bias_up = VEC_DECAY * mom_bias_up + bu_grad
    new_vectors = vectors - vec_rate * new_mom_vectors
    new_bias_qkv = bias_qkv - vec_rate * new_mom_bias_qkv
    new_bias_up = bias_up - vec_rate * new_mom_bias_up
    return (
        output,
        input_grad,
        new_w_qkv,
        new_w_out,
        new_w_up,
        new_w_down,
        new_vectors,
        new_bias_qkv,
        new_bias_up,
        mom_qkv_new,
        mom_out_new,
        mom_up_new,
        mom_down_new,
        new_mom_vectors,
        new_mom_bias_qkv,
        new_mom_bias_up,
    )


def solution(mesh):
    in_specs = (
        P(("dp", "tensor"), None),
        P("dp"),
        P(("dp", "tensor"), None),
        P("dp", None, "tensor"),
        P("dp", "tensor"),
        P("dp", "tensor"),
        P("dp", "tensor"),
        P("dp", None),
        P(("tensor", "dp"), None),
        P(("tensor", "dp")),
        P("dp", None, "tensor"),
        P("dp", "tensor"),
        P("dp", "tensor"),
        P("dp", "tensor"),
        P("dp", None),
        P(("tensor", "dp"), None),
        P(("tensor", "dp")),
    )
    out_specs = (
        P(("dp", "tensor"), None),
        P(("dp", "tensor"), None),
        P("dp", None, "tensor"),
        P("dp", "tensor"),
        P("dp", "tensor"),
        P("dp", "tensor"),
        P("dp", None),
        P(("tensor", "dp"), None),
        P(("tensor", "dp")),
        P("dp", None, "tensor"),
        P("dp", "tensor"),
        P("dp", "tensor"),
        P("dp", "tensor"),
        P("dp", None),
        P(("tensor", "dp"), None),
        P(("tensor", "dp")),
    )
    return jax.shard_map(local, mesh=mesh, in_specs=in_specs, out_specs=out_specs, check_vma=False)
```

```python
from functools import partial
import math

import jax
import jax.numpy as jnp
from jax import lax
from jax.experimental import pallas as pl
from jax.experimental.pallas import tpu as pltpu
from jax.sharding import PartitionSpec as P

HD = 80
SWEEPS = 5
LANES = 128
WINDOW = 256
BIAS_LANE = WINDOW - 1
VMEM_LIMIT = 58 * 1024 * 1024

HIGHEST = lax.Precision.HIGHEST
NORM_EPS = 1e-05
POLAR_EPS = 1e-07
MASKED = -1e30
QUINTIC_A = 3.4445
QUINTIC_B = -4.775
QUINTIC_C = 2.0315
MUON_DECAY = 0.95
VEC_DECAY = 0.9
VEC_RATE = 0.1
STEP_QKV = 0.5 * math.sqrt(3.0)
STEP_OUT = 2.0
STEP_UP = 1.0
STEP_DOWN = 0.5
LOG2E = math.log2(math.e)
SCORE_SCALE = 1.0 / math.sqrt(HD)
F32 = jnp.float32
BF16 = jnp.bfloat16
LITTLE = pl.CostEstimate(flops=1_000_000, bytes_accessed=100_000, transcendentals=0)
NN = (((1,), (0,)), ((), ()))
NT = (((1,), (1,)), ((), ()))
TN = (((0,), (0,)), ((), ()))


def mm(left, right, dims=NN):
    return lax.dot_general(left, right, dims, preferred_element_type=F32)


def norm_parts(values):
    center = values - jnp.mean(values, axis=-1, keepdims=True)
    spread = jnp.mean(center * center, axis=-1, keepdims=True)
    scale = lax.rsqrt(spread + NORM_EPS)
    return center * scale, scale


def norm_back(grad, gain, unit, scale):
    inner = grad * gain
    mean_grad = jnp.mean(inner, axis=-1, keepdims=True)
    mean_unit = jnp.mean(inner * unit, axis=-1, keepdims=True)
    return scale * (inner - mean_grad - unit * mean_unit)


def params(*semantics):
    return pltpu.CompilerParams(
        dimension_semantics=semantics or None, vmem_limit_bytes=VMEM_LIMIT
    )


def swap(value, axis, mask):
    size = lax.axis_size(axis)
    return lax.ppermute(value, axis, [(i, i ^ mask) for i in range(size)])


def tensor_slots(own):
    near = swap(own, "tensor", 1)
    far = swap(own, "tensor", 2)
    return [own, near, far, swap(far, "tensor", 1)]


def tensor_gather(own):
    return jnp.concatenate(tensor_slots(own), axis=0)


def tensor_sum(value):
    value = value + swap(value, "tensor", 1)
    return value + swap(value, "tensor", 2)


def pair_sum(own, sent):
    arrived = swap(sent, "tensor", 1)
    return (own.astype(F32) + arrived.astype(F32)).astype(BF16)


def after(value, *others):
    return lax.optimization_barrier((value, *others))[0]


def tie(values, *others):
    return list(lax.optimization_barrier((*values, *others))[: len(values)])


def qkv_body(x_ref, vec_ref, w_ref, bias_ref, attn_ref, qkv_ref):
    unit, _ = norm_parts(x_ref[...].astype(F32))
    attn_in = (unit * vec_ref[0:1, :] + vec_ref[1:2, :]).astype(BF16)
    attn_ref[...] = attn_in
    qkv_ref[...] = (mm(attn_in, w_ref[...]) + bias_ref[0:1, :]).astype(BF16)


def qkv_call(x_rows, vec_rows, weight, bias, block):
    rows, width = x_rows.shape
    columns = weight.shape[1]
    return pl.pallas_call(
        qkv_body,
        grid=(rows // block,),
        in_specs=[
            pl.BlockSpec((block, width), lambda i: (i, 0)),
            pl.BlockSpec(vec_rows.shape, lambda i: (0, 0)),
            pl.BlockSpec(weight.shape, lambda i: (0, 0)),
            pl.BlockSpec(bias.shape, lambda i: (0, 0)),
        ],
        out_specs=[
            pl.BlockSpec((block, width), lambda i: (i, 0)),
            pl.BlockSpec((block, columns), lambda i: (i, 0)),
        ],
        out_shape=[
            jax.ShapeDtypeStruct((rows, width), BF16),
            jax.ShapeDtypeStruct((rows, columns), BF16),
        ],
        compiler_params=params("arbitrary"),
        cost_estimate=LITTLE,
        name="norm_qkv",
    )(x_rows, vec_rows, weight, bias)


PIECES = 4


def part_shapes(emits, rows, width):
    shapes = []
    for kind in emits:
        count = PIECES if kind == "pieces" else 1
        shapes += [jax.ShapeDtypeStruct((rows // count, width), BF16)] * count
    return shapes, [pl.BlockSpec(shape.shape, lambda i: (0, 0)) for shape in shapes]


def part_store(emits, refs, value):
    spot = 0
    for index, kind in enumerate(emits):
        count = PIECES if kind == "pieces" else 1
        group = refs[spot : spot + count]
        spot += count

        @pl.when(pl.program_id(0) == index)
        def _():
            rows = value.shape[0] // count
            for piece, ref in enumerate(group):
                ref[...] = value[piece * rows : piece * rows + rows].astype(BF16)


def swap_all(values, axis, mask):
    return [swap(value, axis, mask) for value in values]


def pair_body(own_ref, *rest):
    pieces, out_ref = rest[:-1], rest[-1]
    rows = pieces[0].shape[0]
    for index, piece in enumerate(pieces):
        part = slice(index * rows, index * rows + rows)
        out_ref[part, :] = (own_ref[part, :].astype(F32) + piece[...].astype(F32)).astype(BF16)


def pair_pieces(own, pieces):
    return pl.pallas_call(
        pair_body,
        out_shape=jax.ShapeDtypeStruct(own.shape, BF16),
        compiler_params=params(),
        cost_estimate=LITTLE,
        name="pair_sum",
    )(own, *pieces)


def head_place(head):
    start = 0 if head * HD + HD <= BIAS_LANE else LANES
    return start, head * HD - start


def lane_mask(rows, head):
    _, offset = head_place(head)
    lane = lax.broadcasted_iota(jnp.int32, (rows, WINDOW), 1)
    return (lane >= offset) & (lane < offset + HD), lane == BIAS_LANE


def window(value, head):
    start, _ = head_place(head)
    return value[:, start : start + WINDOW].astype(F32)


def key_columns(qkv_ref):
    third = (qkv_ref.shape[1] + LANES) // 3
    return qkv_ref[:, third : 2 * third]


def value_columns(qkv_ref):
    third = (qkv_ref.shape[1] + LANES) // 3
    tail = qkv_ref[:, qkv_ref.shape[1] - third :].astype(F32)
    return pltpu.roll(tail, third - LANES // 2, 1)


def fill_keys(qkv_ref, bias_ref, keys_out, heads):
    columns = key_columns(qkv_ref)
    for head in range(heads):
        inside, last = lane_mask(columns.shape[0], head)
        picked = jnp.where(inside, window(columns, head), 0.0)
        keys_out[head] = jnp.where(last, bias_ref[...], picked).astype(BF16)


def join_windows(parts):
    low, high = None, None
    for head, part in enumerate(parts):
        if head_place(head)[0] == 0:
            low = part if low is None else low + part
        else:
            high = part if high is None else high + part
    return jnp.concatenate(
        [low[:, :LANES], low[:, LANES:] + high[:, :LANES], high[:, LANES:]], axis=1
    )


def attn_body(heads, emits, skip, q_ref, qkv_ref, bias_ref, wo_ref, *rest):
    (att_ref, lse_ref), parts, (keys, vals) = rest[skip : skip + 2], rest[skip + 2 : -2], rest[-2:]
    block = q_ref.shape[0]
    frames = qkv_ref.shape[0]

    @pl.when(pl.program_id(0) == 0)
    def _():
        fill_keys(qkv_ref, bias_ref, keys, heads)
        columns = value_columns(qkv_ref)
        for head in range(heads):
            inside, _ = lane_mask(frames, head)
            vals[head] = jnp.where(inside, window(columns, head), 0.0).astype(BF16)

    log_scale = SCORE_SCALE * LOG2E
    outs = []
    lane = lax.broadcasted_iota(jnp.int32, (block, LANES), 1)
    lse_cols = jnp.zeros((block, LANES), F32)
    for head in range(heads):
        _, last = lane_mask(block, head)
        query = jnp.where(last, 1.0, window(q_ref, head)).astype(BF16)
        scores = mm(query, keys[head], NT)
        row_max = jnp.max(scores, axis=1, keepdims=True)
        powers = jnp.exp2((scores - row_max) * log_scale)
        totals = jnp.sum(powers, axis=1, keepdims=True)
        outs.append(mm(powers.astype(BF16), vals[head]) * (1.0 / totals))
        lse_cols = jnp.where(lane == head, row_max * log_scale + jnp.log2(totals), lse_cols)
    attended = join_windows(outs).astype(BF16)
    att_ref[...] = attended
    lse_ref[...] = jnp.transpose(lse_cols)[:8]
    part_store(emits, parts, mm(attended, wo_ref[...], NT))


def attn_call(heads, emits, qkv, key_bias, wo, block, first, earlier=None):
    count = block * len(emits)
    frames = qkv.shape[0]
    part_width = wo.shape[1]
    width = wo.shape[0]
    held = [] if earlier is None else list(earlier)
    base = first // block
    shapes, specs = part_shapes(emits, block, width)
    return pl.pallas_call(
        partial(attn_body, heads, emits, len(held)),
        grid=(count // block,),
        in_specs=[
            pl.BlockSpec((block, part_width), lambda i: (i + base, 0)),
            pl.BlockSpec(qkv.shape, lambda i: (0, 0)),
            pl.BlockSpec(key_bias.shape, lambda i: (0, 0)),
            pl.BlockSpec(wo.shape, lambda i: (0, 0)),
        ]
        + [pl.BlockSpec(memory_space=pl.ANY)] * len(held),
        out_specs=[
            pl.BlockSpec((block, part_width), lambda i: (i + base, 0)),
            pl.BlockSpec((8, block), lambda i: (0, i + base)),
        ]
        + specs,
        out_shape=[
            jax.ShapeDtypeStruct((frames, part_width), BF16),
            jax.ShapeDtypeStruct((8, frames), F32),
        ]
        + shapes,
        scratch_shapes=[
            pltpu.VMEM((heads, frames, WINDOW), BF16),
            pltpu.VMEM((heads, frames, WINDOW), BF16),
        ],
        input_output_aliases={} if earlier is None else {4: 0, 5: 1},
        compiler_params=params("arbitrary"),
        cost_estimate=LITTLE,
        name="attn_fwd",
    )(qkv, qkv, key_bias, wo, *held)


def attn_back_body(heads, last_part, first, dout_ref, wo_ref, att_ref, q_ref, qkv_ref, bias_ref, lse_ref, *rest):
    if last_part:
        dkey_in, dval_in, sums_in, _, dqkv_ref, sums_ref, keys, vals, d_query, d_key, d_val, packed, sems = rest
    else:
        dqkv_ref, sums_ref, d_key, d_val, keys, vals, d_query, sems = rest
    step = pl.program_id(0)
    block, part_width = q_ref.shape
    count = d_query.shape[0]

    @pl.when(step == 0)
    def _():
        fill_keys(qkv_ref, bias_ref, keys, heads)
        vals[...] = value_columns(qkv_ref).astype(BF16)
        if last_part:
            d_key[...] = dkey_in[...]
            d_val[...] = dval_in[...]
            sums_ref[...] = sums_in[...]
        else:
            d_key[...] = jnp.zeros_like(d_key)
            d_val[...] = jnp.zeros_like(d_val)
            sums_ref[...] = jnp.zeros_like(sums_ref)

    log_scale = SCORE_SCALE * LOG2E
    d_att = mm(dout_ref[...], wo_ref[...]).astype(BF16)
    inner_cols = jnp.transpose(d_att.astype(F32) * att_ref[...].astype(F32))
    outs = []
    for head in range(heads):
        start, _ = head_place(head)
        inside, last = lane_mask(block, head)
        q_window = window(q_ref, head)
        query = jnp.where(last, 1.0, q_window).astype(BF16)
        q_only = jnp.where(inside, q_window, 0.0).astype(BF16)
        d_only = jnp.where(inside, window(d_att, head), 0.0).astype(BF16)
        inner = jnp.sum(inner_cols[head * HD : head * HD + HD], axis=0, keepdims=True)
        scores = mm(keys[head], query, NT)
        probs = jnp.exp2(scores * log_scale - lse_ref[head : head + 1, :])
        d_probs = mm(vals[:, start : start + WINDOW], d_only, NT)
        d_scores = (probs * (d_probs - inner)).astype(BF16)
        d_val[:, start : start + WINDOW] += mm(probs.astype(BF16), d_only)
        d_key[:, start : start + WINDOW] += mm(d_scores, q_only)
        outs.append(mm(d_scores, keys[head], TN))
    low = (join_windows(outs) * SCORE_SCALE).astype(BF16)
    d_query[pl.ds(pl.multiple_of(step * block, block), block), :] = low
    sums_ref[0:1, :] += jnp.sum(low.astype(F32), axis=0, keepdims=True)

    @pl.when(step == pl.num_programs(0) - 1)
    def _():
        copies = [
            pltpu.make_async_copy(
                d_query, dqkv_ref.at[pl.ds(first, count), pl.ds(0, part_width)], sems.at[0]
            )
        ]
        copies[0].start()
        if last_part:
            key_low = d_key[...] * SCORE_SCALE
            value_low = d_val[...]
            sums_ref[1:2, :] = jnp.sum(value_low.astype(BF16).astype(F32), axis=0, keepdims=True)
            value_low = pltpu.roll(value_low, LANES // 2, 1)
            whole = part_width - LANES
            packed[:, :whole] = key_low[:, :whole].astype(BF16)
            packed[:, whole:part_width] = (key_low[:, whole:] + value_low[:, :LANES]).astype(BF16)
            packed[:, part_width:] = value_low[:, LANES:].astype(BF16)
            copies.append(
                pltpu.make_async_copy(
                    packed,
                    dqkv_ref.at[pl.ds(0, packed.shape[0]), pl.ds(part_width, packed.shape[1])],
                    sems.at[1],
                )
            )
            copies[1].start()
        for copy in copies:
            copy.wait()


def attn_back_call(heads, d_out, wo, attended, qkv, key_bias, lse, block, first, earlier=None):
    count, width = d_out.shape
    frames = qkv.shape[0]
    part_width = wo.shape[1]
    base = first // block
    last_part = earlier is not None
    whole = pl.BlockSpec((frames, part_width), lambda i: (0, 0))
    sums_spec = pl.BlockSpec((8, part_width), lambda i: (0, 0))
    anywhere = pl.BlockSpec(memory_space=pl.ANY)
    out_shape = [
        jax.ShapeDtypeStruct(qkv.shape, BF16),
        jax.ShapeDtypeStruct((8, part_width), F32),
    ]
    out_specs = [anywhere, sums_spec]
    scratch = [
        pltpu.VMEM((heads, frames, WINDOW), BF16),
        pltpu.VMEM((frames, part_width), BF16),
        pltpu.VMEM((count, part_width), BF16),
    ]
    held = []
    if last_part:
        d_qkv, sums, d_key, d_val = earlier
        held = [d_key, d_val, sums, d_qkv]
        scratch += [pltpu.VMEM((frames, part_width), F32)] * 2
        scratch += [pltpu.VMEM((frames, qkv.shape[1] - part_width), BF16)]
    else:
        out_shape += [jax.ShapeDtypeStruct((frames, part_width), F32)] * 2
        out_specs += [whole, whole]
    return pl.pallas_call(
        partial(attn_back_body, heads, last_part, first),
        grid=(count // block,),
        in_specs=[
            pl.BlockSpec((block, width), lambda i: (i, 0)),
            pl.BlockSpec(wo.shape, lambda i: (0, 0)),
            pl.BlockSpec((block, part_width), lambda i: (i + base, 0)),
            pl.BlockSpec((block, part_width), lambda i: (i + base, 0)),
            pl.BlockSpec(qkv.shape, lambda i: (0, 0)),
            pl.BlockSpec(key_bias.shape, lambda i: (0, 0)),
            pl.BlockSpec((8, block), lambda i: (0, i + base)),
        ]
        + [whole, whole, sums_spec, anywhere][: len(held)],
        out_specs=out_specs,
        out_shape=out_shape,
        scratch_shapes=scratch + [pltpu.SemaphoreType.DMA((2,))],
        input_output_aliases={10: 0} if last_part else {},
        compiler_params=params("arbitrary"),
        cost_estimate=LITTLE,
        name="attn_bwd",
    )(d_out, wo, attended, qkv, qkv, key_bias, lse, *held)


def gelu_parts(values):
    size = jnp.abs(values)
    bell = jnp.exp2(values * values * (-0.5 * LOG2E))
    inv = 1.0 / (1.0 + (0.3275911 * math.sqrt(0.5)) * size)
    tail = inv * (
        0.5 * 0.254829592
        + inv
        * (
            0.5 * -0.284496736
            + inv * (0.5 * 1.421413741 + inv * (0.5 * -1.453152027 + inv * (0.5 * 1.061405429)))
        )
    )
    tail = tail * bell
    share = jnp.where(values < 0.0, tail, 1.0 - tail)
    return share, share + values * bell * (1.0 / math.sqrt(2.0 * math.pi))


def mlp_body(chunk, emits, skip, *refs):
    slot_refs, (w_ref, bias_ref, dhid_ref) = refs[: len(emits)], refs[len(emits) : len(emits) + 3]
    outs = refs[len(emits) + 3 + skip :]
    hid_ref, dpre_ref, sums_ref, parts, in_ref = *outs[:3], outs[3:-1], outs[-1]
    for index, slot_ref in enumerate(slot_refs):

        @pl.when(pl.program_id(0) == index)
        def _():
            in_ref[...] = slot_ref[...]

    @pl.when(pl.program_id(0) == 0)
    def _():
        sums_ref[...] = jnp.zeros_like(sums_ref)

    for start in range(0, w_ref.shape[1], chunk):
        cols = slice(start, start + chunk)
        pre = mm(in_ref[...], w_ref[:, cols]) + bias_ref[0:1, cols]
        share, slope = gelu_parts(pre)
        hid_ref[:, cols] = (pre * share).astype(BF16)
        d_pre = (dhid_ref[:, cols] * slope).astype(BF16)
        dpre_ref[:, cols] = d_pre
        sums_ref[0:1, cols] += jnp.sum(d_pre.astype(F32), axis=0, keepdims=True)
    part_store(emits, parts, mm(dpre_ref[...], w_ref[...], NT))


def mlp_call(emits, slots, weight, bias, d_hidden, first, frames, earlier=None):
    block, width = slots[0].shape
    count = block * len(slots)
    hidden_width = weight.shape[1]
    held = [] if earlier is None else list(earlier)
    base = first // block
    shapes, specs = part_shapes(emits, block, width)
    return pl.pallas_call(
        partial(mlp_body, min(256, hidden_width), emits, len(held)),
        grid=(count // block,),
        in_specs=[pl.BlockSpec((block, width), lambda i: (0, 0))] * len(slots)
        + [
            pl.BlockSpec(weight.shape, lambda i: (0, 0)),
            pl.BlockSpec(bias.shape, lambda i: (0, 0)),
            pl.BlockSpec((block, hidden_width), lambda i: (i + base, 0)),
        ]
        + [pl.BlockSpec(memory_space=pl.ANY)] * len(held),
        out_specs=[
            pl.BlockSpec((block, hidden_width), lambda i: (i + base, 0)),
            pl.BlockSpec((block, hidden_width), lambda i: (i + base, 0)),
            pl.BlockSpec((8, hidden_width), lambda i: (0, 0)),
        ]
        + specs,
        out_shape=[
            jax.ShapeDtypeStruct((frames, hidden_width), BF16),
            jax.ShapeDtypeStruct((frames, hidden_width), BF16),
            jax.ShapeDtypeStruct((8, hidden_width), F32),
        ]
        + shapes,
        scratch_shapes=[pltpu.VMEM((block, width), BF16)],
        input_output_aliases=(
            {} if earlier is None else {len(slots) + 3: 0, len(slots) + 4: 1}
        ),
        compiler_params=params("arbitrary"),
        cost_estimate=LITTLE,
        name="mlp_up",
    )(*slots, weight, bias, d_hidden, *held)


def residual_body(x_ref, mine_ref, far_ref, near_ref, vec_ref, res_ref, in_ref):
    total = mine_ref[...].astype(F32) + near_ref[...].astype(F32) + far_ref[...].astype(F32)
    residual = x_ref[...].astype(F32) + total + vec_ref[2:3, :]
    res_ref[...] = residual
    unit, _ = norm_parts(residual)
    in_ref[...] = (unit * vec_ref[3:4, :] + vec_ref[4:5, :]).astype(BF16)


def second_back_body(
    res_ref, mine_ref, far_ref, cot_ref, near_ref, vec_ref, dres_ref, low_ref, sums_ref
):
    @pl.when(pl.program_id(0) == 0)
    def _():
        sums_ref[...] = jnp.zeros_like(sums_ref)

    grad = mine_ref[...].astype(F32) + near_ref[...].astype(F32) + far_ref[...].astype(F32)
    unit, scale = norm_parts(res_ref[...])
    cot = cot_ref[...].astype(F32)
    d_res = norm_back(grad, vec_ref[3:4, :], unit, scale) + cot
    dres_ref[...] = d_res
    low_ref[...] = d_res.astype(BF16)
    sums_ref[2:3, :] += jnp.sum(d_res, axis=0, keepdims=True)
    sums_ref[3:4, :] += jnp.sum(grad * unit, axis=0, keepdims=True)
    sums_ref[4:5, :] += jnp.sum(grad, axis=0, keepdims=True)
    sums_ref[5:6, :] += jnp.sum(cot, axis=0, keepdims=True)


def first_back_body(x_ref, mine_ref, far_ref, dres_ref, near_ref, vec_ref, out_ref, sums_ref):
    @pl.when(pl.program_id(0) == 0)
    def _():
        sums_ref[...] = jnp.zeros_like(sums_ref)

    grad = mine_ref[...].astype(F32) + near_ref[...].astype(F32) + far_ref[...].astype(F32)
    unit, scale = norm_parts(x_ref[...].astype(F32))
    out_ref[...] = norm_back(grad, vec_ref[0:1, :], unit, scale) + dres_ref[...]
    sums_ref[0:1, :] += jnp.sum(grad * unit, axis=0, keepdims=True)
    sums_ref[1:2, :] += jnp.sum(grad, axis=0, keepdims=True)


def row_body(body, count, *refs):
    row_refs, pieces, vec_ref = refs[:count], refs[count : count + PIECES], refs[count + PIECES]
    near_ref = refs[-1]
    for index, piece in enumerate(pieces):

        @pl.when(pl.program_id(0) == index)
        def _():
            near_ref[...] = piece[...]

    body(*row_refs, near_ref, vec_ref, *refs[count + PIECES + 1 : -1])


def row_call(body, rows_in, near, vec_rows, out_types, with_sums, name):
    rows, width = rows_in[0].shape
    block = rows // PIECES
    row_spec = pl.BlockSpec((block, width), lambda i: (i, 0))
    whole = pl.BlockSpec((8, width), lambda i: (0, 0))
    return pl.pallas_call(
        partial(row_body, body, len(rows_in)),
        grid=(PIECES,),
        in_specs=[row_spec] * len(rows_in)
        + [pl.BlockSpec((block, width), lambda i: (0, 0))] * PIECES
        + [whole],
        out_specs=[row_spec] * len(out_types) + [whole] * with_sums,
        out_shape=[jax.ShapeDtypeStruct((rows, width), kind) for kind in out_types]
        + [jax.ShapeDtypeStruct((8, width), F32)] * with_sums,
        scratch_shapes=[pltpu.VMEM((block, width), BF16)],
        compiler_params=params("arbitrary"),
        cost_estimate=LITTLE,
        name=name,
    )(*rows_in, *near, vec_rows)


def polar_factors(grams, eye):
    def high(left, right):
        return jnp.dot(left, right, precision=HIGHEST, preferred_element_type=F32)

    scales = [1.0 / (jnp.sqrt(jnp.sum(gram * eye, keepdims=True)) + POLAR_EPS) for gram in grams]
    grams = [gram * scale * scale for gram, scale in zip(grams, scales)]
    factors = None
    for sweep in range(SWEEPS):
        squares = [high(gram, gram) for gram in grams]
        steps = [
            QUINTIC_A * eye + QUINTIC_B * gram + QUINTIC_C * square
            for gram, square in zip(grams, squares)
        ]
        if sweep < SWEEPS - 1:
            halves = [high(step, gram) for step, gram in zip(steps, grams)]
        if factors is None:
            factors = steps
        else:
            factors = [high(step, factor) for step, factor in zip(steps, factors)]
        if sweep < SWEEPS - 1:
            grams = [high(step, part) for step, part in zip(steps, halves)]
    return [factor * scale for factor, scale in zip(factors, scales)]


def polar_body(gram_ref, out_ref):
    count, rows, _ = gram_ref.shape
    row = lax.broadcasted_iota(jnp.int32, (rows, rows), 0)
    col = lax.broadcasted_iota(jnp.int32, (rows, rows), 1)
    eye = jnp.where(row == col, 1.0, 0.0)
    for index, factor in enumerate(polar_factors([gram_ref[i] for i in range(count)], eye)):
        out_ref[index] = factor


def polar_call(grams):
    count, rows, _ = grams.shape
    if rows % 32:
        return jnp.stack(polar_factors([grams[i] for i in range(count)], jnp.eye(rows, dtype=F32)))
    return pl.pallas_call(
        polar_body,
        out_shape=jax.ShapeDtypeStruct(grams.shape, F32),
        compiler_params=params(),
        name="polar",
    )(grams)


def gram_of(update):
    return lax.dot_general(update, update, NT, precision=HIGHEST, preferred_element_type=F32)


def momentum(moment, gradient):
    moved = MUON_DECAY * moment + gradient
    return moved, gradient + MUON_DECAY * moved


def applied(weight, factor, update, rate):
    return weight - rate * jnp.dot(factor, update, precision=HIGHEST)


def place_body(splits, narrow, me_ref, *refs):
    slots, outs = refs[:8], refs[8:]
    rows = slots[0].shape[0]
    for mask, slot in enumerate(slots):
        start = pl.multiple_of((me_ref[0] ^ mask) * rows, rows)
        for (low, high), out in zip(splits, outs):
            out[pl.ds(start, rows), :] = slot[:, low:high]
    if narrow is not None:
        tile = narrow // LANES * LANES
        turned = jnp.transpose(outs[0][:, tile : tile + LANES].astype(F32))
        outs[-1][...] = turned[narrow - tile : narrow - tile + 16]


def place_rows(slots, splits, narrow):
    rows = slots[0].shape[0]
    shapes = [jax.ShapeDtypeStruct((8 * rows, high - low), slots[0].dtype) for low, high in splits]
    if narrow is not None:
        shapes.append(jax.ShapeDtypeStruct((16, 8 * rows), F32))
    return pl.pallas_call(
        partial(place_body, splits, narrow),
        in_specs=[pl.BlockSpec(memory_space=pltpu.SMEM)]
        + [pl.BlockSpec(memory_space=pltpu.VMEM)] * 8,
        out_specs=[pl.BlockSpec(memory_space=pltpu.VMEM)] * len(shapes),
        out_shape=shapes,
        compiler_params=params(),
        cost_estimate=LITTLE,
        name="place_rows",
    )(lax.axis_index("dp").astype(jnp.int32)[None], *slots)


def dp_slots(own, ordered=False):
    line = {mask: swap(own, "dp", mask) for mask in (6, 2, 4)}
    slots = [own, swap(own, "dp", 1)] + [None] * 6
    for mask in (6, 2, 4):
        arrived = line[mask]
        if ordered:
            held = [slots[1]] if mask == 2 else [slots[3], slots[7]] if mask == 4 else []
            arrived = after(arrived, *held)
        slots[mask] = arrived
        slots[mask + 1] = swap(arrived, "dp", 1)
    return slots


def dp_send(own, ordered=False):
    if lax.axis_size("dp") != 8:
        return [lax.all_gather(own, "dp", axis=0, tiled=True)]
    return dp_slots(own, ordered)


def dp_place(slots, splits, narrow=None):
    if len(slots) > 1:
        return place_rows(slots, splits, narrow)
    parts = [slots[0][:, low:high] for low, high in splits]
    if narrow is not None:
        parts.append(jnp.transpose(slots[0][:, narrow : narrow + 16].astype(F32)))
    return parts


LINE = (4, 6, 2, 0)


def dp_cross(part):
    size = lax.axis_size("dp")
    if size != 8:
        return [], [dp_scatter_plain(part)]
    rows = part.shape[0] // size
    me = lax.axis_index("dp")

    def block(mask):
        return lax.dynamic_slice(part, ((me ^ mask) * rows, 0), (rows, part.shape[1]))

    return [block(mask) for mask in LINE], [swap(block(mask + 1), "dp", 1) for mask in LINE]


def dp_line(owns, arrivals):
    if not owns:
        return arrivals
    sums = []
    for mask, own, arrived in zip(LINE, owns, arrivals):
        pair = own.astype(F32) + arrived.astype(F32)
        sums.append(swap(pair.astype(BF16), "dp", mask) if mask else pair)
    return sums


def dp_total(sums):
    total = sums[-1].astype(F32)
    for value in sums[:-1]:
        total = total + value.astype(F32)
    return total


def dp_scatter_plain(part):
    return lax.psum_scatter(part, "dp", scatter_dimension=0, tiled=True)


def dp_sum(value):
    if lax.axis_size("dp") != 8:
        return lax.psum(value, "dp")
    for mask in (1, 2, 4):
        value = value + swap(value, "dp", mask)
    return value


def local(
    inputs,
    lengths,
    cotangent,
    w_qkv,
    w_out,
    w_up,
    w_down,
    vectors,
    bias_qkv,
    bias_up,
    mom_qkv,
    mom_out,
    mom_up,
    mom_down,
    mom_vectors,
    mom_bias_qkv,
    mom_bias_up,
):
    dp_size = lax.axis_size("dp")
    tensor_size = lax.axis_size("tensor")
    dp_index = lax.axis_index("dp")
    tok = inputs.shape[0]
    frames = tok * tensor_size
    tokens = frames * dp_size
    half = 2 * tok
    width = inputs.shape[1]
    own_rows = w_qkv.shape[0]
    head_width = w_qkv.shape[2]
    heads = head_width // HD
    padded = -(-head_width // LANES) * LANES
    extra = padded - head_width
    own_bias = bias_qkv.shape[0]

    w_parts = w_qkv.astype(BF16)
    small = jnp.concatenate(
        [
            vectors.astype(BF16),
            bias_up.astype(BF16)[:, None],
            jnp.pad(bias_qkv.astype(BF16), ((0, own_rows - own_bias), (0, 0))),
        ],
        axis=1,
    )
    small = jnp.pad(small, ((0, 0), (0, extra - small.shape[1])))
    packed = 3 * head_width + extra
    w_cols = jnp.concatenate(
        [
            w_parts[:, 0],
            small,
            w_parts[:, 1],
            w_parts[:, 2],
            jnp.pad(w_out.astype(BF16), ((0, 0), (0, extra))),
        ],
        axis=1,
    )
    first_slots = dp_send(w_cols, True)
    x_far = after(swap(inputs, "tensor", 2), *first_slots[2:7:4])
    x_rows = jnp.concatenate(
        [inputs, swap(inputs, "tensor", 1), x_far, swap(x_far, "tensor", 1)], axis=0
    )
    cot_far = after(swap(cotangent, "tensor", 2), *first_slots[4:5])
    cot_rows = jnp.concatenate(
        [cotangent, swap(cotangent, "tensor", 1), cot_far, swap(cot_far, "tensor", 1)], axis=0
    )
    first_slots[-1], x_rows, cot_rows = tie([first_slots[-1], x_rows, cot_rows])
    wq, wo, smalls = dp_place(
        first_slots, ((0, packed), (packed, packed + padded)), head_width
    )
    wd = lax.all_gather(w_down.astype(BF16), "dp", axis=0, tiled=True)
    wu = lax.all_gather(w_up.astype(BF16), "dp", axis=0, tiled=True)
    vec_rows = smalls[:8]
    bu = smalls[6:7]
    bq = smalls[7:9].reshape(2, dp_size, own_rows)[:, :, :own_bias].reshape(2, head_width)
    qkv_bias = jnp.concatenate(
        [bq[0:1], jnp.zeros((1, padded), F32), bq[1:2]], axis=1
    )

    me = lax.axis_index("tensor")
    place = jnp.concatenate([(me ^ s) * tok + jnp.arange(tok, dtype=jnp.int32) for s in range(4)])
    key_bias = jnp.where(place < lengths[0], 0.0, MASKED).astype(F32)[:, None]

    attn_in, qkv = qkv_call(x_rows, vec_rows, wq, qkv_bias, tok)
    att, lse, *sent = attn_call(
        heads, ("pieces",), qkv, key_bias, wo, tok, 3 * tok
    )
    att, lse, part_two = attn_call(
        heads, ("own",), qkv, key_bias, wo, tok, 2 * tok, (att, lse)
    )
    total = pair_pieces(part_two, swap_all(sent, "tensor", 1))
    far = swap(total, "tensor", 2)
    att, lse, mine, *sent = attn_call(
        heads,
        ("own", "pieces"),
        after(qkv, total),
        key_bias,
        wo,
        tok,
        0,
        (att, lse),
    )
    near = swap_all(sent, "tensor", 1)
    residual, mlp_in = row_call(
        residual_body, (inputs, mine, after(far, wd)), near, vec_rows, (F32, BF16), 0, "residual"
    )

    near = swap(mlp_in, "tensor", 1)
    far = swap(mlp_in, "tensor", 2)
    d_hidden = mm(after(cot_rows, mlp_in, wu), wd)
    hidden, d_pre, bu_sums, mine, *sent = mlp_call(
        ("own", "pieces"), [mlp_in, near], wu, bu, d_hidden, 0, frames
    )
    near_parts = swap_all(sent, "tensor", 1)
    far = after(far, mine)
    slots = [mlp_in, near, far, swap(far, "tensor", 1)]
    hidden, d_pre, sums, *sent = mlp_call(
        ("pieces",), slots[3:], wu, bu, d_hidden, 3 * tok, frames, (hidden, d_pre)
    )
    bu_sums = bu_sums + sums
    hidden, d_pre, sums, part_two = mlp_call(
        ("own",), slots[2:3], wu, bu, d_hidden, 2 * tok, frames, (hidden, d_pre)
    )
    bu_sums = bu_sums + sums
    total = pair_pieces(part_two, swap_all(sent, "tensor", 1))
    far = swap(total, "tensor", 2)
    hidden_later, d_pre_later = tie([hidden, d_pre], total)
    raw_wd = mm(cot_rows, hidden_later, TN).astype(BF16)
    raw_wu = mm(jnp.concatenate(slots, axis=0), after(d_pre_later, raw_wd), TN).astype(BF16)
    hidden = after(hidden, raw_wu)
    down_far = mm(hidden[half:], wd, NT).astype(BF16)
    down_mine = mm(hidden[:half], wd, NT).astype(BF16)
    near_parts = tie(near_parts, raw_wd, raw_wu, down_far, down_mine)
    grad_wd, grad_wu = dp_scatter_plain(raw_wd), dp_scatter_plain(raw_wu)
    d_residual, d_out, sums_two = row_call(
        second_back_body,
        (residual, mine, far, cotangent),
        near_parts,
        vec_rows,
        (F32, BF16),
        1,
        "second_back",
    )
    block = tok * 2 // 3
    near = swap(d_out, "tensor", 1)
    far = swap(d_out, "tensor", 2)
    out_mine = jnp.concatenate([d_out, near], axis=0)
    carried = attn_back_call(
        heads, out_mine, wo, att, qkv, key_bias, lse, half, 0
    )
    far = after(far, carried[1])
    output_far = swap(after(pair_sum(down_far[:tok], down_far[tok:]), far), "tensor", 2)
    output_near = swap(down_mine[tok:], "tensor", 1)
    out_far = jnp.concatenate([far, swap(far, "tensor", 1)], axis=0)
    raw_wo = (mm(out_mine, att[:half], TN) + mm(out_far, att[half:], TN)).astype(BF16)
    out_later = after(out_far, raw_wo)
    d_qkv, bias_sums = attn_back_call(
        heads, out_later, wo, att, qkv, key_bias, lse, half, half, carried
    )
    raw_wq = mm(attn_in, after(d_qkv, output_far, output_near), TN).astype(BF16)
    d_qkv, raw_wq, raw_wo = tie([d_qkv, raw_wq, raw_wo])
    raw_first = jnp.concatenate([raw_wq, raw_wo], axis=1)
    owns, crossed = dp_cross(raw_first)
    first_far = mm(after(d_qkv[half:], grad_wd), wq, NT).astype(BF16)
    far = swap(pair_sum(first_far[:tok], first_far[tok:]), "tensor", 2)
    lined = dp_line(owns, crossed)
    first_mine = mm(after(d_qkv[:half], first_far), wq, NT).astype(BF16)
    grad_wd = after(grad_wd, first_mine, *crossed[:2])
    mom_down_new, update_down = momentum(mom_down, grad_wd.astype(F32))
    early = polar_call(tensor_sum(gram_of(update_down)[None]))
    new_w_down = applied(w_down, early[0], update_down, STEP_DOWN)
    quarter = tok // PIECES
    sent = [first_mine[tok + k * quarter : tok + k * quarter + quarter] for k in range(PIECES)]
    near = swap_all(sent, "tensor", 1)
    grad_wu = after(after(grad_wu, first_mine, *crossed), *lined[:3])
    output = (
        residual
        + (down_mine[:tok].astype(F32) + output_near.astype(F32) + output_far.astype(F32))
        + vec_rows[5]
    )
    input_grad, sums_one = row_call(
        first_back_body,
        (inputs, first_mine[:tok], far, d_residual),
        near,
        vec_rows,
        (F32,),
        1,
        "first_back",
    )

    mom_up_new, update_up = momentum(mom_up, grad_wu.astype(F32))
    gram_up = gram_of(update_up)
    lined = tie(lined, gram_up, new_w_down, input_grad)
    grad_first = dp_total(lined)
    grad_wq, grad_wo = grad_first[:, :packed], grad_first[:, packed : packed + head_width]
    mom_out_new, update_out = momentum(mom_out, grad_wo)
    spots = (0, padded, padded + head_width)
    grad_parts = jnp.stack([grad_wq[:, spot : spot + head_width] for spot in spots], axis=1)
    mom_qkv_new, update_qkv = momentum(mom_qkv, grad_parts)
    flat = jnp.concatenate(
        [update_qkv[:, 0], jnp.zeros((own_rows, extra), F32), update_qkv[:, 1], update_qkv[:, 2]], axis=1
    )
    vec_tail = (sums_one + sums_two).reshape(-1, own_rows)
    late = tensor_sum(
        jnp.concatenate([gram_of(update_out), gram_of(flat), gram_up, vec_tail], axis=0)
    )
    vec_sums = late[3 * own_rows :].reshape(8, width)
    late = polar_call(late[: 3 * own_rows].reshape(3, own_rows, own_rows))
    new_w_up = applied(w_up, late[2], update_up, STEP_UP)
    new_w_out = applied(w_out, late[0], update_out, STEP_OUT)
    polar_qkv = jnp.dot(late[1], flat, precision=HIGHEST)
    new_w_qkv = w_qkv - STEP_QKV * jnp.stack(
        [polar_qkv[:, spot : spot + head_width] for spot in spots], axis=1
    )

    rows_of = jnp.concatenate(
        [
            vec_sums[:6],
            bu_sums[0:1],
            jnp.pad(bias_sums[:2], ((0, 0), (0, width - padded))),
        ],
        axis=0,
    )
    rows_of = dp_sum(rows_of)
    own_cols = lax.dynamic_slice(rows_of, (0, dp_index * own_rows), (7, own_rows))
    vec_grad = jnp.transpose(own_cols[:6])
    bu_grad = own_cols[6]
    bq_grad = jnp.transpose(
        lax.dynamic_slice(rows_of, (7, dp_index * own_bias), (2, own_bias))
    )

    vec_rate = VEC_RATE / math.sqrt(tokens)
    new_mom_vectors = VEC_DECAY * mom_vectors + vec_grad
    new_mom_bias_qkv = VEC_DECAY * mom_bias_qkv + bq_grad
    new_mom_bias_up = VEC_DECAY * mom_bias_up + bu_grad
    new_vectors = vectors - vec_rate * new_mom_vectors
    new_bias_qkv = bias_qkv - vec_rate * new_mom_bias_qkv
    new_bias_up = bias_up - vec_rate * new_mom_bias_up
    return (
        output,
        input_grad,
        new_w_qkv,
        new_w_out,
        new_w_up,
        new_w_down,
        new_vectors,
        new_bias_qkv,
        new_bias_up,
        mom_qkv_new,
        mom_out_new,
        mom_up_new,
        mom_down_new,
        new_mom_vectors,
        new_mom_bias_qkv,
        new_mom_bias_up,
    )


def solution(mesh):
    in_specs = (
        P(("dp", "tensor"), None),
        P("dp"),
        P(("dp", "tensor"), None),
        P("dp", None, "tensor"),
        P("dp", "tensor"),
        P("dp", "tensor"),
        P("dp", "tensor"),
        P("dp", None),
        P(("tensor", "dp"), None),
        P(("tensor", "dp")),
        P("dp", None, "tensor"),
        P("dp", "tensor"),
        P("dp", "tensor"),
        P("dp", "tensor"),
        P("dp", None),
        P(("tensor", "dp"), None),
        P(("tensor", "dp")),
    )
    out_specs = (
        P(("dp", "tensor"), None),
        P(("dp", "tensor"), None),
        P("dp", None, "tensor"),
        P("dp", "tensor"),
        P("dp", "tensor"),
        P("dp", "tensor"),
        P("dp", None),
        P(("tensor", "dp"), None),
        P(("tensor", "dp")),
        P("dp", None, "tensor"),
        P("dp", "tensor"),
        P("dp", "tensor"),
        P("dp", "tensor"),
        P("dp", None),
        P(("tensor", "dp"), None),
        P(("tensor", "dp")),
    )
    return jax.shard_map(local, mesh=mesh, in_specs=in_specs, out_specs=out_specs, check_vma=False)
```

```python
from functools import partial
import math

import jax
import jax.numpy as jnp
from jax import lax
from jax.experimental import pallas as pl
from jax.experimental.pallas import tpu as pltpu
from jax.sharding import PartitionSpec as P

HD = 80
SWEEPS = 5
LANES = 128
WINDOW = 256
BIAS_LANE = WINDOW - 1
VMEM_LIMIT = 58 * 1024 * 1024

HIGHEST = lax.Precision.HIGHEST
NORM_EPS = 1e-05
POLAR_EPS = 1e-07
MASKED = -1e30
QUINTIC_A = 3.4445
QUINTIC_B = -4.775
QUINTIC_C = 2.0315
MUON_DECAY = 0.95
VEC_DECAY = 0.9
VEC_RATE = 0.1
STEP_QKV = 0.5 * math.sqrt(3.0)
STEP_OUT = 2.0
STEP_UP = 1.0
STEP_DOWN = 0.5
LOG2E = math.log2(math.e)
SCORE_SCALE = 1.0 / math.sqrt(HD)
F32 = jnp.float32
BF16 = jnp.bfloat16
LITTLE = pl.CostEstimate(flops=1_000_000, bytes_accessed=100_000, transcendentals=0)
NN = (((1,), (0,)), ((), ()))
NT = (((1,), (1,)), ((), ()))
TN = (((0,), (0,)), ((), ()))


def mm(left, right, dims=NN):
    return lax.dot_general(left, right, dims, preferred_element_type=F32)


def norm_parts(values):
    center = values - jnp.mean(values, axis=-1, keepdims=True)
    spread = jnp.mean(center * center, axis=-1, keepdims=True)
    scale = lax.rsqrt(spread + NORM_EPS)
    return center * scale, scale


def norm_back(grad, gain, unit, scale):
    inner = grad * gain
    mean_grad = jnp.mean(inner, axis=-1, keepdims=True)
    mean_unit = jnp.mean(inner * unit, axis=-1, keepdims=True)
    return scale * (inner - mean_grad - unit * mean_unit)


def params(*semantics):
    return pltpu.CompilerParams(
        dimension_semantics=semantics or None, vmem_limit_bytes=VMEM_LIMIT
    )


def swap(value, axis, mask):
    size = lax.axis_size(axis)
    return lax.ppermute(value, axis, [(i, i ^ mask) for i in range(size)])


def tensor_slots(own):
    near = swap(own, "tensor", 1)
    far = swap(own, "tensor", 2)
    return [own, near, far, swap(far, "tensor", 1)]


def tensor_gather(own):
    return jnp.concatenate(tensor_slots(own), axis=0)


def tensor_sum(value):
    value = value + swap(value, "tensor", 1)
    return value + swap(value, "tensor", 2)


def pair_sum(own, sent):
    arrived = swap(sent, "tensor", 1)
    return (own.astype(F32) + arrived.astype(F32)).astype(BF16)


def after(value, *others):
    return lax.optimization_barrier((value, *others))[0]


def tie(values, *others):
    return list(lax.optimization_barrier((*values, *others))[: len(values)])


def qkv_body(x_ref, vec_ref, w_ref, bias_ref, attn_ref, qkv_ref):
    unit, _ = norm_parts(x_ref[...].astype(F32))
    attn_in = (unit * vec_ref[0:1, :] + vec_ref[1:2, :]).astype(BF16)
    attn_ref[...] = attn_in
    qkv_ref[...] = (mm(attn_in, w_ref[...]) + bias_ref[0:1, :]).astype(BF16)


def qkv_call(x_rows, vec_rows, weight, bias, block):
    rows, width = x_rows.shape
    columns = weight.shape[1]
    return pl.pallas_call(
        qkv_body,
        grid=(rows // block,),
        in_specs=[
            pl.BlockSpec((block, width), lambda i: (i, 0)),
            pl.BlockSpec(vec_rows.shape, lambda i: (0, 0)),
            pl.BlockSpec(weight.shape, lambda i: (0, 0)),
            pl.BlockSpec(bias.shape, lambda i: (0, 0)),
        ],
        out_specs=[
            pl.BlockSpec((block, width), lambda i: (i, 0)),
            pl.BlockSpec((block, columns), lambda i: (i, 0)),
        ],
        out_shape=[
            jax.ShapeDtypeStruct((rows, width), BF16),
            jax.ShapeDtypeStruct((rows, columns), BF16),
        ],
        compiler_params=params("arbitrary"),
        cost_estimate=LITTLE,
        name="norm_qkv",
    )(x_rows, vec_rows, weight, bias)


PIECES = 4


def part_shapes(emits, rows, width):
    shapes = []
    for kind in emits:
        count = PIECES if kind == "pieces" else 1
        shapes += [jax.ShapeDtypeStruct((rows // count, width), BF16)] * count
    return shapes, [pl.BlockSpec(shape.shape, lambda i: (0, 0)) for shape in shapes]


def part_store(emits, refs, value):
    spot = 0
    for index, kind in enumerate(emits):
        count = PIECES if kind == "pieces" else 1
        group = refs[spot : spot + count]
        spot += count

        @pl.when(pl.program_id(0) == index)
        def _():
            rows = value.shape[0] // count
            for piece, ref in enumerate(group):
                ref[...] = value[piece * rows : piece * rows + rows].astype(BF16)


def swap_all(values, axis, mask):
    return [swap(value, axis, mask) for value in values]


def pair_body(own_ref, *rest):
    pieces, out_ref = rest[:-1], rest[-1]
    rows = pieces[0].shape[0]
    for index, piece in enumerate(pieces):
        part = slice(index * rows, index * rows + rows)
        out_ref[part, :] = (own_ref[part, :].astype(F32) + piece[...].astype(F32)).astype(BF16)


def pair_pieces(own, pieces):
    return pl.pallas_call(
        pair_body,
        out_shape=jax.ShapeDtypeStruct(own.shape, BF16),
        compiler_params=params(),
        cost_estimate=LITTLE,
        name="pair_sum",
    )(own, *pieces)


def head_place(head):
    start = 0 if head * HD + HD <= BIAS_LANE else LANES
    return start, head * HD - start


def lane_mask(rows, head):
    _, offset = head_place(head)
    lane = lax.broadcasted_iota(jnp.int32, (rows, WINDOW), 1)
    return (lane >= offset) & (lane < offset + HD), lane == BIAS_LANE


def window(value, head):
    start, _ = head_place(head)
    return value[:, start : start + WINDOW].astype(F32)


def key_columns(qkv_ref):
    third = (qkv_ref.shape[1] + LANES) // 3
    return qkv_ref[:, third : 2 * third]


def value_columns(qkv_ref):
    third = (qkv_ref.shape[1] + LANES) // 3
    tail = qkv_ref[:, qkv_ref.shape[1] - third :].astype(F32)
    return pltpu.roll(tail, third - LANES // 2, 1)


def fill_keys(qkv_ref, bias_ref, keys_out, heads):
    columns = key_columns(qkv_ref)
    for head in range(heads):
        inside, last = lane_mask(columns.shape[0], head)
        picked = jnp.where(inside, window(columns, head), 0.0)
        keys_out[head] = jnp.where(last, bias_ref[...], picked).astype(BF16)


def join_windows(parts):
    low, high = None, None
    for head, part in enumerate(parts):
        if head_place(head)[0] == 0:
            low = part if low is None else low + part
        else:
            high = part if high is None else high + part
    return jnp.concatenate(
        [low[:, :LANES], low[:, LANES:] + high[:, :LANES], high[:, LANES:]], axis=1
    )


def attn_body(heads, emits, skip, q_ref, qkv_ref, bias_ref, wo_ref, *rest):
    (att_ref, lse_ref), parts, (keys, vals) = rest[skip : skip + 2], rest[skip + 2 : -2], rest[-2:]
    block = q_ref.shape[0]
    frames = qkv_ref.shape[0]

    @pl.when(pl.program_id(0) == 0)
    def _():
        fill_keys(qkv_ref, bias_ref, keys, heads)
        columns = value_columns(qkv_ref)
        for head in range(heads):
            inside, _ = lane_mask(frames, head)
            vals[head] = jnp.where(inside, window(columns, head), 0.0).astype(BF16)

    log_scale = SCORE_SCALE * LOG2E
    outs = []
    lane = lax.broadcasted_iota(jnp.int32, (block, LANES), 1)
    lse_cols = jnp.zeros((block, LANES), F32)
    for head in range(heads):
        _, last = lane_mask(block, head)
        query = jnp.where(last, 1.0, window(q_ref, head)).astype(BF16)
        scores = mm(query, keys[head], NT)
        row_max = jnp.max(scores, axis=1, keepdims=True)
        powers = jnp.exp2((scores - row_max) * log_scale)
        totals = jnp.sum(powers, axis=1, keepdims=True)
        outs.append(mm(powers.astype(BF16), vals[head]) * (1.0 / totals))
        lse_cols = jnp.where(lane == head, row_max * log_scale + jnp.log2(totals), lse_cols)
    attended = join_windows(outs).astype(BF16)
    att_ref[...] = attended
    lse_ref[...] = jnp.transpose(lse_cols)[:8]
    part_store(emits, parts, mm(attended, wo_ref[...], NT))


def attn_call(heads, emits, qkv, key_bias, wo, block, first, earlier=None):
    count = block * len(emits)
    frames = qkv.shape[0]
    part_width = wo.shape[1]
    width = wo.shape[0]
    held = [] if earlier is None else list(earlier)
    base = first // block
    shapes, specs = part_shapes(emits, block, width)
    return pl.pallas_call(
        partial(attn_body, heads, emits, len(held)),
        grid=(count // block,),
        in_specs=[
            pl.BlockSpec((block, part_width), lambda i: (i + base, 0)),
            pl.BlockSpec(qkv.shape, lambda i: (0, 0)),
            pl.BlockSpec(key_bias.shape, lambda i: (0, 0)),
            pl.BlockSpec(wo.shape, lambda i: (0, 0)),
        ]
        + [pl.BlockSpec(memory_space=pl.ANY)] * len(held),
        out_specs=[
            pl.BlockSpec((block, part_width), lambda i: (i + base, 0)),
            pl.BlockSpec((8, block), lambda i: (0, i + base)),
        ]
        + specs,
        out_shape=[
            jax.ShapeDtypeStruct((frames, part_width), BF16),
            jax.ShapeDtypeStruct((8, frames), F32),
        ]
        + shapes,
        scratch_shapes=[
            pltpu.VMEM((heads, frames, WINDOW), BF16),
            pltpu.VMEM((heads, frames, WINDOW), BF16),
        ],
        input_output_aliases={} if earlier is None else {4: 0, 5: 1},
        compiler_params=params("arbitrary"),
        cost_estimate=LITTLE,
        name="attn_fwd",
    )(qkv, qkv, key_bias, wo, *held)


def attn_back_body(heads, last_part, first, dout_ref, wo_ref, att_ref, q_ref, qkv_ref, bias_ref, lse_ref, *rest):
    if last_part:
        dkey_in, dval_in, sums_in, _, dqkv_ref, sums_ref, keys, vals, d_query, d_key, d_val, packed, sems = rest
    else:
        dqkv_ref, sums_ref, d_key, d_val, keys, vals, d_query, sems = rest
    step = pl.program_id(0)
    block, part_width = q_ref.shape
    count = d_query.shape[0]

    @pl.when(step == 0)
    def _():
        fill_keys(qkv_ref, bias_ref, keys, heads)
        vals[...] = value_columns(qkv_ref).astype(BF16)
        if last_part:
            d_key[...] = dkey_in[...]
            d_val[...] = dval_in[...]
            sums_ref[...] = sums_in[...]
        else:
            d_key[...] = jnp.zeros_like(d_key)
            d_val[...] = jnp.zeros_like(d_val)
            sums_ref[...] = jnp.zeros_like(sums_ref)

    log_scale = SCORE_SCALE * LOG2E
    d_att = mm(dout_ref[...], wo_ref[...]).astype(BF16)
    inner_cols = jnp.transpose(d_att.astype(F32) * att_ref[...].astype(F32))
    outs = []
    for head in range(heads):
        start, _ = head_place(head)
        inside, last = lane_mask(block, head)
        q_window = window(q_ref, head)
        query = jnp.where(last, 1.0, q_window).astype(BF16)
        q_only = jnp.where(inside, q_window, 0.0).astype(BF16)
        d_only = jnp.where(inside, window(d_att, head), 0.0).astype(BF16)
        inner = jnp.sum(inner_cols[head * HD : head * HD + HD], axis=0, keepdims=True)
        scores = mm(keys[head], query, NT)
        probs = jnp.exp2(scores * log_scale - lse_ref[head : head + 1, :])
        d_probs = mm(vals[:, start : start + WINDOW], d_only, NT)
        d_scores = (probs * (d_probs - inner)).astype(BF16)
        d_val[:, start : start + WINDOW] += mm(probs.astype(BF16), d_only)
        d_key[:, start : start + WINDOW] += mm(d_scores, q_only)
        outs.append(mm(d_scores, keys[head], TN))
    low = (join_windows(outs) * SCORE_SCALE).astype(BF16)
    d_query[pl.ds(pl.multiple_of(step * block, block), block), :] = low
    sums_ref[0:1, :] += jnp.sum(low.astype(F32), axis=0, keepdims=True)

    @pl.when(step == pl.num_programs(0) - 1)
    def _():
        copies = [
            pltpu.make_async_copy(
                d_query, dqkv_ref.at[pl.ds(first, count), pl.ds(0, part_width)], sems.at[0]
            )
        ]
        copies[0].start()
        if last_part:
            key_low = d_key[...] * SCORE_SCALE
            value_low = d_val[...]
            sums_ref[1:2, :] = jnp.sum(value_low.astype(BF16).astype(F32), axis=0, keepdims=True)
            value_low = pltpu.roll(value_low, LANES // 2, 1)
            whole = part_width - LANES
            packed[:, :whole] = key_low[:, :whole].astype(BF16)
            packed[:, whole:part_width] = (key_low[:, whole:] + value_low[:, :LANES]).astype(BF16)
            packed[:, part_width:] = value_low[:, LANES:].astype(BF16)
            copies.append(
                pltpu.make_async_copy(
                    packed,
                    dqkv_ref.at[pl.ds(0, packed.shape[0]), pl.ds(part_width, packed.shape[1])],
                    sems.at[1],
                )
            )
            copies[1].start()
        for copy in copies:
            copy.wait()


def attn_back_call(heads, d_out, wo, attended, qkv, key_bias, lse, block, first, earlier=None):
    count, width = d_out.shape
    frames = qkv.shape[0]
    part_width = wo.shape[1]
    base = first // block
    last_part = earlier is not None
    whole = pl.BlockSpec((frames, part_width), lambda i: (0, 0))
    sums_spec = pl.BlockSpec((8, part_width), lambda i: (0, 0))
    anywhere = pl.BlockSpec(memory_space=pl.ANY)
    out_shape = [
        jax.ShapeDtypeStruct(qkv.shape, BF16),
        jax.ShapeDtypeStruct((8, part_width), F32),
    ]
    out_specs = [anywhere, sums_spec]
    scratch = [
        pltpu.VMEM((heads, frames, WINDOW), BF16),
        pltpu.VMEM((frames, part_width), BF16),
        pltpu.VMEM((count, part_width), BF16),
    ]
    held = []
    if last_part:
        d_qkv, sums, d_key, d_val = earlier
        held = [d_key, d_val, sums, d_qkv]
        scratch += [pltpu.VMEM((frames, part_width), F32)] * 2
        scratch += [pltpu.VMEM((frames, qkv.shape[1] - part_width), BF16)]
    else:
        out_shape += [jax.ShapeDtypeStruct((frames, part_width), F32)] * 2
        out_specs += [whole, whole]
    return pl.pallas_call(
        partial(attn_back_body, heads, last_part, first),
        grid=(count // block,),
        in_specs=[
            pl.BlockSpec((block, width), lambda i: (i, 0)),
            pl.BlockSpec(wo.shape, lambda i: (0, 0)),
            pl.BlockSpec((block, part_width), lambda i: (i + base, 0)),
            pl.BlockSpec((block, part_width), lambda i: (i + base, 0)),
            pl.BlockSpec(qkv.shape, lambda i: (0, 0)),
            pl.BlockSpec(key_bias.shape, lambda i: (0, 0)),
            pl.BlockSpec((8, block), lambda i: (0, i + base)),
        ]
        + [whole, whole, sums_spec, anywhere][: len(held)],
        out_specs=out_specs,
        out_shape=out_shape,
        scratch_shapes=scratch + [pltpu.SemaphoreType.DMA((2,))],
        input_output_aliases={10: 0} if last_part else {},
        compiler_params=params("arbitrary"),
        cost_estimate=LITTLE,
        name="attn_bwd",
    )(d_out, wo, attended, qkv, qkv, key_bias, lse, *held)


def gelu_parts(values):
    size = jnp.abs(values)
    bell = jnp.exp2(values * values * (-0.5 * LOG2E))
    inv = 1.0 / (1.0 + (0.3275911 * math.sqrt(0.5)) * size)
    tail = inv * (
        0.5 * 0.254829592
        + inv
        * (
            0.5 * -0.284496736
            + inv * (0.5 * 1.421413741 + inv * (0.5 * -1.453152027 + inv * (0.5 * 1.061405429)))
        )
    )
    tail = tail * bell
    share = jnp.where(values < 0.0, tail, 1.0 - tail)
    return share, share + values * bell * (1.0 / math.sqrt(2.0 * math.pi))


def mlp_body(chunk, emits, skip, *refs):
    slot_refs, (w_ref, bias_ref, dhid_ref) = refs[: len(emits)], refs[len(emits) : len(emits) + 3]
    outs = refs[len(emits) + 3 + skip :]
    hid_ref, dpre_ref, sums_ref, parts, in_ref = *outs[:3], outs[3:-1], outs[-1]
    for index, slot_ref in enumerate(slot_refs):

        @pl.when(pl.program_id(0) == index)
        def _():
            in_ref[...] = slot_ref[...]

    @pl.when(pl.program_id(0) == 0)
    def _():
        sums_ref[...] = jnp.zeros_like(sums_ref)

    for start in range(0, w_ref.shape[1], chunk):
        cols = slice(start, start + chunk)
        pre = mm(in_ref[...], w_ref[:, cols]) + bias_ref[0:1, cols]
        share, slope = gelu_parts(pre)
        hid_ref[:, cols] = (pre * share).astype(BF16)
        d_pre = (dhid_ref[:, cols] * slope).astype(BF16)
        dpre_ref[:, cols] = d_pre
        sums_ref[0:1, cols] += jnp.sum(d_pre.astype(F32), axis=0, keepdims=True)
    part_store(emits, parts, mm(dpre_ref[...], w_ref[...], NT))


def mlp_call(emits, slots, weight, bias, d_hidden, first, frames, earlier=None):
    block, width = slots[0].shape
    count = block * len(slots)
    hidden_width = weight.shape[1]
    held = [] if earlier is None else list(earlier)
    base = first // block
    shapes, specs = part_shapes(emits, block, width)
    return pl.pallas_call(
        partial(mlp_body, min(256, hidden_width), emits, len(held)),
        grid=(count // block,),
        in_specs=[pl.BlockSpec((block, width), lambda i: (0, 0))] * len(slots)
        + [
            pl.BlockSpec(weight.shape, lambda i: (0, 0)),
            pl.BlockSpec(bias.shape, lambda i: (0, 0)),
            pl.BlockSpec((block, hidden_width), lambda i: (i + base, 0)),
        ]
        + [pl.BlockSpec(memory_space=pl.ANY)] * len(held),
        out_specs=[
            pl.BlockSpec((block, hidden_width), lambda i: (i + base, 0)),
            pl.BlockSpec((block, hidden_width), lambda i: (i + base, 0)),
            pl.BlockSpec((8, hidden_width), lambda i: (0, 0)),
        ]
        + specs,
        out_shape=[
            jax.ShapeDtypeStruct((frames, hidden_width), BF16),
            jax.ShapeDtypeStruct((frames, hidden_width), BF16),
            jax.ShapeDtypeStruct((8, hidden_width), F32),
        ]
        + shapes,
        scratch_shapes=[pltpu.VMEM((block, width), BF16)],
        input_output_aliases=(
            {} if earlier is None else {len(slots) + 3: 0, len(slots) + 4: 1}
        ),
        compiler_params=params("arbitrary"),
        cost_estimate=LITTLE,
        name="mlp_up",
    )(*slots, weight, bias, d_hidden, *held)


def residual_body(x_ref, mine_ref, far_ref, near_ref, vec_ref, res_ref, in_ref):
    total = mine_ref[...].astype(F32) + near_ref[...].astype(F32) + far_ref[...].astype(F32)
    residual = x_ref[...].astype(F32) + total + vec_ref[2:3, :]
    res_ref[...] = residual
    unit, _ = norm_parts(residual)
    in_ref[...] = (unit * vec_ref[3:4, :] + vec_ref[4:5, :]).astype(BF16)


def second_back_body(
    res_ref, mine_ref, far_ref, cot_ref, near_ref, vec_ref, dres_ref, low_ref, sums_ref
):
    @pl.when(pl.program_id(0) == 0)
    def _():
        sums_ref[...] = jnp.zeros_like(sums_ref)

    grad = mine_ref[...].astype(F32) + near_ref[...].astype(F32) + far_ref[...].astype(F32)
    unit, scale = norm_parts(res_ref[...])
    cot = cot_ref[...].astype(F32)
    d_res = norm_back(grad, vec_ref[3:4, :], unit, scale) + cot
    dres_ref[...] = d_res
    low_ref[...] = d_res.astype(BF16)
    sums_ref[2:3, :] += jnp.sum(d_res, axis=0, keepdims=True)
    sums_ref[3:4, :] += jnp.sum(grad * unit, axis=0, keepdims=True)
    sums_ref[4:5, :] += jnp.sum(grad, axis=0, keepdims=True)
    sums_ref[5:6, :] += jnp.sum(cot, axis=0, keepdims=True)


def first_back_body(x_ref, mine_ref, far_ref, dres_ref, near_ref, vec_ref, out_ref, sums_ref):
    @pl.when(pl.program_id(0) == 0)
    def _():
        sums_ref[...] = jnp.zeros_like(sums_ref)

    grad = mine_ref[...].astype(F32) + near_ref[...].astype(F32) + far_ref[...].astype(F32)
    unit, scale = norm_parts(x_ref[...].astype(F32))
    out_ref[...] = norm_back(grad, vec_ref[0:1, :], unit, scale) + dres_ref[...]
    sums_ref[0:1, :] += jnp.sum(grad * unit, axis=0, keepdims=True)
    sums_ref[1:2, :] += jnp.sum(grad, axis=0, keepdims=True)


def row_body(body, count, *refs):
    row_refs, pieces, vec_ref = refs[:count], refs[count : count + PIECES], refs[count + PIECES]
    near_ref = refs[-1]
    for index, piece in enumerate(pieces):

        @pl.when(pl.program_id(0) == index)
        def _():
            near_ref[...] = piece[...]

    body(*row_refs, near_ref, vec_ref, *refs[count + PIECES + 1 : -1])


def row_call(body, rows_in, near, vec_rows, out_types, with_sums, name):
    rows, width = rows_in[0].shape
    block = rows // PIECES
    row_spec = pl.BlockSpec((block, width), lambda i: (i, 0))
    whole = pl.BlockSpec((8, width), lambda i: (0, 0))
    return pl.pallas_call(
        partial(row_body, body, len(rows_in)),
        grid=(PIECES,),
        in_specs=[row_spec] * len(rows_in)
        + [pl.BlockSpec((block, width), lambda i: (0, 0))] * PIECES
        + [whole],
        out_specs=[row_spec] * len(out_types) + [whole] * with_sums,
        out_shape=[jax.ShapeDtypeStruct((rows, width), kind) for kind in out_types]
        + [jax.ShapeDtypeStruct((8, width), F32)] * with_sums,
        scratch_shapes=[pltpu.VMEM((block, width), BF16)],
        compiler_params=params("arbitrary"),
        cost_estimate=LITTLE,
        name=name,
    )(*rows_in, *near, vec_rows)


def polar_factors(grams, eye):
    def high(left, right):
        return jnp.dot(left, right, precision=HIGHEST, preferred_element_type=F32)

    scales = [1.0 / (jnp.sqrt(jnp.sum(gram * eye, keepdims=True)) + POLAR_EPS) for gram in grams]
    grams = [gram * scale * scale for gram, scale in zip(grams, scales)]
    factors = None
    for sweep in range(SWEEPS):
        squares = [high(gram, gram) for gram in grams]
        steps = [
            QUINTIC_A * eye + QUINTIC_B * gram + QUINTIC_C * square
            for gram, square in zip(grams, squares)
        ]
        if sweep < SWEEPS - 1:
            halves = [high(step, gram) for step, gram in zip(steps, grams)]
        if factors is None:
            factors = steps
        else:
            factors = [high(step, factor) for step, factor in zip(steps, factors)]
        if sweep < SWEEPS - 1:
            grams = [high(step, part) for step, part in zip(steps, halves)]
    return [factor * scale for factor, scale in zip(factors, scales)]


def polar_body(gram_ref, out_ref):
    count, rows, _ = gram_ref.shape
    row = lax.broadcasted_iota(jnp.int32, (rows, rows), 0)
    col = lax.broadcasted_iota(jnp.int32, (rows, rows), 1)
    eye = jnp.where(row == col, 1.0, 0.0)
    for index, factor in enumerate(polar_factors([gram_ref[i] for i in range(count)], eye)):
        out_ref[index] = factor


def polar_call(grams):
    count, rows, _ = grams.shape
    if rows % 32:
        return jnp.stack(polar_factors([grams[i] for i in range(count)], jnp.eye(rows, dtype=F32)))
    return pl.pallas_call(
        polar_body,
        out_shape=jax.ShapeDtypeStruct(grams.shape, F32),
        compiler_params=params(),
        name="polar",
    )(grams)


def gram_of(update):
    return lax.dot_general(update, update, NT, precision=HIGHEST, preferred_element_type=F32)


def momentum(moment, gradient):
    moved = MUON_DECAY * moment + gradient
    return moved, gradient + MUON_DECAY * moved


def applied(weight, factor, update, rate):
    return weight - rate * jnp.dot(factor, update, precision=HIGHEST)


def place_body(splits, narrow, me_ref, *refs):
    slots, outs = refs[:8], refs[8:]
    rows = slots[0].shape[0]
    for mask, slot in enumerate(slots):
        start = pl.multiple_of((me_ref[0] ^ mask) * rows, rows)
        for (low, high), out in zip(splits, outs):
            out[pl.ds(start, rows), :] = slot[:, low:high]
    if narrow is not None:
        tile = narrow // LANES * LANES
        turned = jnp.transpose(outs[0][:, tile : tile + LANES].astype(F32))
        outs[-1][...] = turned[narrow - tile : narrow - tile + 16]


def place_rows(slots, splits, narrow):
    rows = slots[0].shape[0]
    shapes = [jax.ShapeDtypeStruct((8 * rows, high - low), slots[0].dtype) for low, high in splits]
    if narrow is not None:
        shapes.append(jax.ShapeDtypeStruct((16, 8 * rows), F32))
    return pl.pallas_call(
        partial(place_body, splits, narrow),
        in_specs=[pl.BlockSpec(memory_space=pltpu.SMEM)]
        + [pl.BlockSpec(memory_space=pltpu.VMEM)] * 8,
        out_specs=[pl.BlockSpec(memory_space=pltpu.VMEM)] * len(shapes),
        out_shape=shapes,
        compiler_params=params(),
        cost_estimate=LITTLE,
        name="place_rows",
    )(lax.axis_index("dp").astype(jnp.int32)[None], *slots)


def dp_slots(own, ordered=False):
    line = {mask: swap(own, "dp", mask) for mask in (6, 2, 4)}
    slots = [own, swap(own, "dp", 1)] + [None] * 6
    for mask in (6, 2, 4):
        arrived = line[mask]
        if ordered:
            held = [slots[1]] if mask == 2 else [slots[3], slots[7]] if mask == 4 else []
            arrived = after(arrived, *held)
        slots[mask] = arrived
        slots[mask + 1] = swap(arrived, "dp", 1)
    return slots


def dp_send(own, ordered=False):
    if lax.axis_size("dp") != 8:
        return [lax.all_gather(own, "dp", axis=0, tiled=True)]
    return dp_slots(own, ordered)


def dp_place(slots, splits, narrow=None):
    if len(slots) > 1:
        return place_rows(slots, splits, narrow)
    parts = [slots[0][:, low:high] for low, high in splits]
    if narrow is not None:
        parts.append(jnp.transpose(slots[0][:, narrow : narrow + 16].astype(F32)))
    return parts


LINE = (4, 6, 2, 0)


def dp_cross(part):
    size = lax.axis_size("dp")
    if size != 8:
        return [], [dp_scatter_plain(part)]
    rows = part.shape[0] // size
    me = lax.axis_index("dp")

    def block(mask):
        return lax.dynamic_slice(part, ((me ^ mask) * rows, 0), (rows, part.shape[1]))

    return [block(mask) for mask in LINE], [swap(block(mask + 1), "dp", 1) for mask in LINE]


def dp_line(owns, arrivals):
    if not owns:
        return arrivals
    sums = []
    for mask, own, arrived in zip(LINE, owns, arrivals):
        pair = own.astype(F32) + arrived.astype(F32)
        sums.append(swap(pair.astype(BF16), "dp", mask) if mask else pair)
    return sums


def dp_total(sums):
    total = sums[-1].astype(F32)
    for value in sums[:-1]:
        total = total + value.astype(F32)
    return total


def dp_scatter_plain(part):
    return lax.psum_scatter(part, "dp", scatter_dimension=0, tiled=True)


def dp_sum(value):
    if lax.axis_size("dp") != 8:
        return lax.psum(value, "dp")
    for mask in (1, 2, 4):
        value = value + swap(value, "dp", mask)
    return value


def local(
    inputs,
    lengths,
    cotangent,
    w_qkv,
    w_out,
    w_up,
    w_down,
    vectors,
    bias_qkv,
    bias_up,
    mom_qkv,
    mom_out,
    mom_up,
    mom_down,
    mom_vectors,
    mom_bias_qkv,
    mom_bias_up,
):
    dp_size = lax.axis_size("dp")
    tensor_size = lax.axis_size("tensor")
    dp_index = lax.axis_index("dp")
    tok = inputs.shape[0]
    frames = tok * tensor_size
    tokens = frames * dp_size
    half = 2 * tok
    width = inputs.shape[1]
    own_rows = w_qkv.shape[0]
    head_width = w_qkv.shape[2]
    heads = head_width // HD
    padded = -(-head_width // LANES) * LANES
    extra = padded - head_width
    own_bias = bias_qkv.shape[0]

    w_parts = w_qkv.astype(BF16)
    small = jnp.concatenate(
        [
            vectors.astype(BF16),
            bias_up.astype(BF16)[:, None],
            jnp.pad(bias_qkv.astype(BF16), ((0, own_rows - own_bias), (0, 0))),
        ],
        axis=1,
    )
    small = jnp.pad(small, ((0, 0), (0, extra - small.shape[1])))
    packed = 3 * head_width + extra
    w_cols = jnp.concatenate(
        [
            w_parts[:, 0],
            small,
            w_parts[:, 1],
            w_parts[:, 2],
            jnp.pad(w_out.astype(BF16), ((0, 0), (0, extra))),
        ],
        axis=1,
    )
    first_slots = dp_send(w_cols, True)
    x_far = after(swap(inputs, "tensor", 2), *first_slots[2:7:4])
    x_rows = jnp.concatenate(
        [inputs, swap(inputs, "tensor", 1), x_far, swap(x_far, "tensor", 1)], axis=0
    )
    cot_far = after(swap(cotangent, "tensor", 2), *first_slots[4:5])
    cot_rows = jnp.concatenate(
        [cotangent, swap(cotangent, "tensor", 1), cot_far, swap(cot_far, "tensor", 1)], axis=0
    )
    first_slots[-1], x_rows, cot_rows = tie([first_slots[-1], x_rows, cot_rows])
    wq, wo, smalls = dp_place(
        first_slots, ((0, packed), (packed, packed + padded)), head_width
    )
    wd = lax.all_gather(w_down.astype(BF16), "dp", axis=0, tiled=True)
    wu = lax.all_gather(w_up.astype(BF16), "dp", axis=0, tiled=True)
    vec_rows = smalls[:8]
    bu = smalls[6:7]
    bq = smalls[7:9].reshape(2, dp_size, own_rows)[:, :, :own_bias].reshape(2, head_width)
    qkv_bias = jnp.concatenate(
        [bq[0:1], jnp.zeros((1, padded), F32), bq[1:2]], axis=1
    )

    me = lax.axis_index("tensor")
    place = jnp.concatenate([(me ^ s) * tok + jnp.arange(tok, dtype=jnp.int32) for s in range(4)])
    key_bias = jnp.where(place < lengths[0], 0.0, MASKED).astype(F32)[:, None]

    attn_in, qkv = qkv_call(x_rows, vec_rows, wq, qkv_bias, tok)
    att, lse, *sent = attn_call(
        heads, ("pieces",), qkv, key_bias, wo, tok, 3 * tok
    )
    att, lse, part_two = attn_call(
        heads, ("own",), qkv, key_bias, wo, tok, 2 * tok, (att, lse)
    )
    total = pair_pieces(part_two, swap_all(sent, "tensor", 1))
    far = swap(total, "tensor", 2)
    att, lse, mine, *sent = attn_call(
        heads,
        ("own", "pieces"),
        after(qkv, total),
        key_bias,
        wo,
        tok,
        0,
        (att, lse),
    )
    near = swap_all(sent, "tensor", 1)
    residual, mlp_in = row_call(
        residual_body, (inputs, mine, after(far, wd)), near, vec_rows, (F32, BF16), 0, "residual"
    )

    near = swap(mlp_in, "tensor", 1)
    far = swap(mlp_in, "tensor", 2)
    d_hidden = mm(after(cot_rows, mlp_in, wu), wd)
    hidden, d_pre, bu_sums, mine, *sent = mlp_call(
        ("own", "pieces"), [mlp_in, near], wu, bu, d_hidden, 0, frames
    )
    near_parts = swap_all(sent, "tensor", 1)
    far = after(far, mine)
    slots = [mlp_in, near, far, swap(far, "tensor", 1)]
    hidden, d_pre, sums, *sent = mlp_call(
        ("pieces",), slots[3:], wu, bu, d_hidden, 3 * tok, frames, (hidden, d_pre)
    )
    bu_sums = bu_sums + sums
    hidden, d_pre, sums, part_two = mlp_call(
        ("own",), slots[2:3], wu, bu, d_hidden, 2 * tok, frames, (hidden, d_pre)
    )
    bu_sums = bu_sums + sums
    total = pair_pieces(part_two, swap_all(sent, "tensor", 1))
    far = swap(total, "tensor", 2)
    hidden_later, d_pre_later = tie([hidden, d_pre], total)
    raw_wd = mm(cot_rows, hidden_later, TN).astype(BF16)
    raw_wu = mm(jnp.concatenate(slots, axis=0), after(d_pre_later, raw_wd), TN).astype(BF16)
    hidden = after(hidden, raw_wu)
    down_far = mm(hidden[half:], wd, NT).astype(BF16)
    down_mine = mm(hidden[:half], wd, NT).astype(BF16)
    near_parts = tie(near_parts, raw_wd, raw_wu, down_far, down_mine)
    grad_wd, grad_wu = dp_scatter_plain(raw_wd), dp_scatter_plain(raw_wu)
    d_residual, d_out, sums_two = row_call(
        second_back_body,
        (residual, mine, far, cotangent),
        near_parts,
        vec_rows,
        (F32, BF16),
        1,
        "second_back",
    )
    near = swap(d_out, "tensor", 1)
    far = swap(d_out, "tensor", 2)
    out_mine = jnp.concatenate([d_out, near], axis=0)
    carried = attn_back_call(
        heads, out_mine, wo, att, qkv, key_bias, lse, half, 0
    )
    far = after(far, carried[1])
    output_far = swap(after(pair_sum(down_far[:tok], down_far[tok:]), far), "tensor", 2)
    output_near = swap(down_mine[tok:], "tensor", 1)
    out_far = jnp.concatenate([far, swap(far, "tensor", 1)], axis=0)
    raw_wo = (mm(out_mine, att[:half], TN) + mm(out_far, att[half:], TN)).astype(BF16)
    out_later = after(out_far, raw_wo)
    d_qkv, bias_sums = attn_back_call(
        heads, out_later, wo, att, qkv, key_bias, lse, half, half, carried
    )
    d_qkv = after(d_qkv, output_far, output_near)
    first_far = mm(d_qkv[half:], wq, NT).astype(BF16)
    raw_wq = mm(attn_in, after(d_qkv, grad_wd, first_far), TN).astype(BF16)
    first_total = pair_sum(first_far[:tok], first_far[tok:])
    far = swap(first_total, "tensor", 2)
    d_qkv, raw_wq, raw_wo = tie([d_qkv, raw_wq, raw_wo])
    owns, crossed = dp_cross(jnp.concatenate([raw_wq, raw_wo], axis=1))
    first_mine = mm(after(d_qkv[:half], first_total), wq, NT).astype(BF16)
    quarter = tok // PIECES
    sent = [first_mine[tok + k * quarter : tok + k * quarter + quarter] for k in range(PIECES)]
    near = swap_all(sent, "tensor", 1)
    output = (
        residual
        + (down_mine[:tok].astype(F32) + output_near.astype(F32) + output_far.astype(F32))
        + vec_rows[5]
    )
    input_grad, sums_one = row_call(
        first_back_body,
        (inputs, first_mine[:tok], far, d_residual),
        near,
        vec_rows,
        (F32,),
        1,
        "first_back",
    )

    vec_sums = tensor_sum(sums_one + sums_two)
    rows_of = jnp.concatenate(
        [
            vec_sums[:6],
            bu_sums[0:1],
            jnp.pad(bias_sums[:2], ((0, 0), (0, width - padded))),
        ],
        axis=0,
    )
    rows_of = dp_sum(rows_of)
    own_cols = lax.dynamic_slice(rows_of, (0, dp_index * own_rows), (7, own_rows))
    vec_grad = jnp.transpose(own_cols[:6])
    bu_grad = own_cols[6]
    bq_grad = jnp.transpose(
        lax.dynamic_slice(rows_of, (7, dp_index * own_bias), (2, own_bias))
    )

    lined = dp_line(owns, tie(crossed, input_grad))
    grad_wd = after(grad_wd, first_mine, lined[-1])
    mom_down_new, update_down = momentum(mom_down, grad_wd.astype(F32))
    early = polar_call(tensor_sum(gram_of(update_down)[None]))
    new_w_down = applied(w_down, early[0], update_down, STEP_DOWN)
    grad_wu = after(after(grad_wu, first_mine, *crossed), *lined[:3])

    mom_up_new, update_up = momentum(mom_up, grad_wu.astype(F32))
    gram_up = gram_of(update_up)
    lined = tie(lined, gram_up, new_w_down, rows_of)
    grad_first = dp_total(lined)
    grad_wq, grad_wo = grad_first[:, :packed], grad_first[:, packed : packed + head_width]
    mom_out_new, update_out = momentum(mom_out, grad_wo)
    spots = (0, padded, padded + head_width)
    grad_parts = jnp.stack([grad_wq[:, spot : spot + head_width] for spot in spots], axis=1)
    mom_qkv_new, update_qkv = momentum(mom_qkv, grad_parts)
    flat = jnp.concatenate(
        [update_qkv[:, 0], jnp.zeros((own_rows, extra), F32), update_qkv[:, 1], update_qkv[:, 2]], axis=1
    )
    late = tensor_sum(jnp.stack([gram_of(update_out), gram_of(flat), gram_up]))
    late = polar_call(late)
    new_w_out = applied(w_out, late[0], update_out, STEP_OUT)
    new_w_up = applied(w_up, late[2], update_up, STEP_UP)
    polar_qkv = jnp.dot(late[1], flat, precision=HIGHEST)
    new_w_qkv = w_qkv - STEP_QKV * jnp.stack(
        [polar_qkv[:, spot : spot + head_width] for spot in spots], axis=1
    )

    vec_rate = VEC_RATE / math.sqrt(tokens)
    new_mom_vectors = VEC_DECAY * mom_vectors + vec_grad
    new_mom_bias_qkv = VEC_DECAY * mom_bias_qkv + bq_grad
    new_mom_bias_up = VEC_DECAY * mom_bias_up + bu_grad
    new_vectors = vectors - vec_rate * new_mom_vectors
    new_bias_qkv = bias_qkv - vec_rate * new_mom_bias_qkv
    new_bias_up = bias_up - vec_rate * new_mom_bias_up
    return (
        output,
        input_grad,
        new_w_qkv,
        new_w_out,
        new_w_up,
        new_w_down,
        new_vectors,
        new_bias_qkv,
        new_bias_up,
        mom_qkv_new,
        mom_out_new,
        mom_up_new,
        mom_down_new,
        new_mom_vectors,
        new_mom_bias_qkv,
        new_mom_bias_up,
    )


def solution(mesh):
    in_specs = (
        P(("dp", "tensor"), None),
        P("dp"),
        P(("dp", "tensor"), None),
        P("dp", None, "tensor"),
        P("dp", "tensor"),
        P("dp", "tensor"),
        P("dp", "tensor"),
        P("dp", None),
        P(("tensor", "dp"), None),
        P(("tensor", "dp")),
        P("dp", None, "tensor"),
        P("dp", "tensor"),
        P("dp", "tensor"),
        P("dp", "tensor"),
        P("dp", None),
        P(("tensor", "dp"), None),
        P(("tensor", "dp")),
    )
    out_specs = (
        P(("dp", "tensor"), None),
        P(("dp", "tensor"), None),
        P("dp", None, "tensor"),
        P("dp", "tensor"),
        P("dp", "tensor"),
        P("dp", "tensor"),
        P("dp", None),
        P(("tensor", "dp"), None),
        P(("tensor", "dp")),
        P("dp", None, "tensor"),
        P("dp", "tensor"),
        P("dp", "tensor"),
        P("dp", "tensor"),
        P("dp", None),
        P(("tensor", "dp"), None),
        P(("tensor", "dp")),
    )
    return jax.shard_map(local, mesh=mesh, in_specs=in_specs, out_specs=out_specs, check_vma=False)
```

```python
from functools import partial
import math

import jax
import jax.numpy as jnp
from jax import lax
from jax.experimental import pallas as pl
from jax.experimental.pallas import tpu as pltpu
from jax.sharding import PartitionSpec as P

HD = 80
SWEEPS = 5
LANES = 128
WINDOW = 256
BIAS_LANE = WINDOW - 1
VMEM_LIMIT = 58 * 1024 * 1024

HIGHEST = lax.Precision.HIGHEST
NORM_EPS = 1e-05
POLAR_EPS = 1e-07
MASKED = -1e30
QUINTIC_A = 3.4445
QUINTIC_B = -4.775
QUINTIC_C = 2.0315
MUON_DECAY = 0.95
VEC_DECAY = 0.9
VEC_RATE = 0.1
STEP_QKV = 0.5 * math.sqrt(3.0)
STEP_OUT = 2.0
STEP_UP = 1.0
STEP_DOWN = 0.5
LOG2E = math.log2(math.e)
SCORE_SCALE = 1.0 / math.sqrt(HD)
F32 = jnp.float32
BF16 = jnp.bfloat16
LITTLE = pl.CostEstimate(flops=1_000_000, bytes_accessed=100_000, transcendentals=0)
NN = (((1,), (0,)), ((), ()))
NT = (((1,), (1,)), ((), ()))
TN = (((0,), (0,)), ((), ()))


def mm(left, right, dims=NN):
    return lax.dot_general(left, right, dims, preferred_element_type=F32)


def norm_parts(values):
    center = values - jnp.mean(values, axis=-1, keepdims=True)
    spread = jnp.mean(center * center, axis=-1, keepdims=True)
    scale = lax.rsqrt(spread + NORM_EPS)
    return center * scale, scale


def norm_back(grad, gain, unit, scale):
    inner = grad * gain
    mean_grad = jnp.mean(inner, axis=-1, keepdims=True)
    mean_unit = jnp.mean(inner * unit, axis=-1, keepdims=True)
    return scale * (inner - mean_grad - unit * mean_unit)


def params(*semantics):
    return pltpu.CompilerParams(
        dimension_semantics=semantics or None, vmem_limit_bytes=VMEM_LIMIT
    )


def swap(value, axis, mask):
    size = lax.axis_size(axis)
    return lax.ppermute(value, axis, [(i, i ^ mask) for i in range(size)])


def tensor_slots(own):
    near = swap(own, "tensor", 1)
    far = swap(own, "tensor", 2)
    return [own, near, far, swap(far, "tensor", 1)]


def tensor_gather(own):
    return jnp.concatenate(tensor_slots(own), axis=0)


def tensor_sum(value):
    value = value + swap(value, "tensor", 1)
    return value + swap(value, "tensor", 2)


def pair_sum(own, sent):
    arrived = swap(sent, "tensor", 1)
    return (own.astype(F32) + arrived.astype(F32)).astype(BF16)


def after(value, *others):
    return lax.optimization_barrier((value, *others))[0]


def tie(values, *others):
    return list(lax.optimization_barrier((*values, *others))[: len(values)])


def qkv_body(x_ref, vec_ref, w_ref, bias_ref, attn_ref, qkv_ref):
    unit, _ = norm_parts(x_ref[...].astype(F32))
    attn_in = (unit * vec_ref[0:1, :] + vec_ref[1:2, :]).astype(BF16)
    attn_ref[...] = attn_in
    qkv_ref[...] = (mm(attn_in, w_ref[...]) + bias_ref[0:1, :]).astype(BF16)


def qkv_call(x_rows, vec_rows, weight, bias, block):
    rows, width = x_rows.shape
    columns = weight.shape[1]
    return pl.pallas_call(
        qkv_body,
        grid=(rows // block,),
        in_specs=[
            pl.BlockSpec((block, width), lambda i: (i, 0)),
            pl.BlockSpec(vec_rows.shape, lambda i: (0, 0)),
            pl.BlockSpec(weight.shape, lambda i: (0, 0)),
            pl.BlockSpec(bias.shape, lambda i: (0, 0)),
        ],
        out_specs=[
            pl.BlockSpec((block, width), lambda i: (i, 0)),
            pl.BlockSpec((block, columns), lambda i: (i, 0)),
        ],
        out_shape=[
            jax.ShapeDtypeStruct((rows, width), BF16),
            jax.ShapeDtypeStruct((rows, columns), BF16),
        ],
        compiler_params=params("arbitrary"),
        cost_estimate=LITTLE,
        name="norm_qkv",
    )(x_rows, vec_rows, weight, bias)


PIECES = 4


def part_shapes(emits, rows, width):
    shapes = []
    for kind in emits:
        count = PIECES if kind == "pieces" else 1
        shapes += [jax.ShapeDtypeStruct((rows // count, width), BF16)] * count
    return shapes, [pl.BlockSpec(shape.shape, lambda i: (0, 0)) for shape in shapes]


def part_store(emits, refs, value):
    spot = 0
    for index, kind in enumerate(emits):
        count = PIECES if kind == "pieces" else 1
        group = refs[spot : spot + count]
        spot += count

        @pl.when(pl.program_id(0) == index)
        def _():
            rows = value.shape[0] // count
            for piece, ref in enumerate(group):
                ref[...] = value[piece * rows : piece * rows + rows].astype(BF16)


def swap_all(values, axis, mask):
    return [swap(value, axis, mask) for value in values]


def pair_body(own_ref, *rest):
    pieces, out_ref = rest[:-1], rest[-1]
    rows = pieces[0].shape[0]
    for index, piece in enumerate(pieces):
        part = slice(index * rows, index * rows + rows)
        out_ref[part, :] = (own_ref[part, :].astype(F32) + piece[...].astype(F32)).astype(BF16)


def pair_pieces(own, pieces):
    return pl.pallas_call(
        pair_body,
        out_shape=jax.ShapeDtypeStruct(own.shape, BF16),
        compiler_params=params(),
        cost_estimate=LITTLE,
        name="pair_sum",
    )(own, *pieces)


def head_place(head):
    start = 0 if head * HD + HD <= BIAS_LANE else LANES
    return start, head * HD - start


def lane_mask(rows, head):
    _, offset = head_place(head)
    lane = lax.broadcasted_iota(jnp.int32, (rows, WINDOW), 1)
    return (lane >= offset) & (lane < offset + HD), lane == BIAS_LANE


def window(value, head):
    start, _ = head_place(head)
    return value[:, start : start + WINDOW].astype(F32)


def key_columns(qkv_ref):
    third = (qkv_ref.shape[1] + LANES) // 3
    return qkv_ref[:, third : 2 * third]


def value_columns(qkv_ref):
    third = (qkv_ref.shape[1] + LANES) // 3
    tail = qkv_ref[:, qkv_ref.shape[1] - third :].astype(F32)
    return pltpu.roll(tail, third - LANES // 2, 1)


def fill_keys(qkv_ref, bias_ref, keys_out, heads):
    columns = key_columns(qkv_ref)
    for head in range(heads):
        inside, last = lane_mask(columns.shape[0], head)
        picked = jnp.where(inside, window(columns, head), 0.0)
        keys_out[head] = jnp.where(last, bias_ref[...], picked).astype(BF16)


def join_windows(parts):
    low, high = None, None
    for head, part in enumerate(parts):
        if head_place(head)[0] == 0:
            low = part if low is None else low + part
        else:
            high = part if high is None else high + part
    return jnp.concatenate(
        [low[:, :LANES], low[:, LANES:] + high[:, :LANES], high[:, LANES:]], axis=1
    )


def attn_body(heads, emits, skip, q_ref, qkv_ref, bias_ref, wo_ref, *rest):
    (att_ref, lse_ref), parts, (keys, vals) = rest[skip : skip + 2], rest[skip + 2 : -2], rest[-2:]
    block = q_ref.shape[0]
    frames = qkv_ref.shape[0]

    @pl.when(pl.program_id(0) == 0)
    def _():
        fill_keys(qkv_ref, bias_ref, keys, heads)
        columns = value_columns(qkv_ref)
        for head in range(heads):
            inside, _ = lane_mask(frames, head)
            vals[head] = jnp.where(inside, window(columns, head), 0.0).astype(BF16)

    log_scale = SCORE_SCALE * LOG2E
    outs = []
    lane = lax.broadcasted_iota(jnp.int32, (block, LANES), 1)
    lse_cols = jnp.zeros((block, LANES), F32)
    for head in range(heads):
        _, last = lane_mask(block, head)
        query = jnp.where(last, 1.0, window(q_ref, head)).astype(BF16)
        scores = mm(query, keys[head], NT)
        row_max = jnp.max(scores, axis=1, keepdims=True)
        powers = jnp.exp2((scores - row_max) * log_scale)
        totals = jnp.sum(powers, axis=1, keepdims=True)
        outs.append(mm(powers.astype(BF16), vals[head]) * (1.0 / totals))
        lse_cols = jnp.where(lane == head, row_max * log_scale + jnp.log2(totals), lse_cols)
    attended = join_windows(outs).astype(BF16)
    att_ref[...] = attended
    lse_ref[...] = jnp.transpose(lse_cols)[:8]
    part_store(emits, parts, mm(attended, wo_ref[...], NT))


def attn_call(heads, emits, qkv, key_bias, wo, block, first, earlier=None):
    count = block * len(emits)
    frames = qkv.shape[0]
    part_width = wo.shape[1]
    width = wo.shape[0]
    held = [] if earlier is None else list(earlier)
    base = first // block
    shapes, specs = part_shapes(emits, block, width)
    return pl.pallas_call(
        partial(attn_body, heads, emits, len(held)),
        grid=(count // block,),
        in_specs=[
            pl.BlockSpec((block, part_width), lambda i: (i + base, 0)),
            pl.BlockSpec(qkv.shape, lambda i: (0, 0)),
            pl.BlockSpec(key_bias.shape, lambda i: (0, 0)),
            pl.BlockSpec(wo.shape, lambda i: (0, 0)),
        ]
        + [pl.BlockSpec(memory_space=pl.ANY)] * len(held),
        out_specs=[
            pl.BlockSpec((block, part_width), lambda i: (i + base, 0)),
            pl.BlockSpec((8, block), lambda i: (0, i + base)),
        ]
        + specs,
        out_shape=[
            jax.ShapeDtypeStruct((frames, part_width), BF16),
            jax.ShapeDtypeStruct((8, frames), F32),
        ]
        + shapes,
        scratch_shapes=[
            pltpu.VMEM((heads, frames, WINDOW), BF16),
            pltpu.VMEM((heads, frames, WINDOW), BF16),
        ],
        input_output_aliases={} if earlier is None else {4: 0, 5: 1},
        compiler_params=params("arbitrary"),
        cost_estimate=LITTLE,
        name="attn_fwd",
    )(qkv, qkv, key_bias, wo, *held)


def attn_back_body(heads, last_part, first, dout_ref, wo_ref, att_ref, q_ref, qkv_ref, bias_ref, lse_ref, *rest):
    if last_part:
        dkey_in, dval_in, sums_in, _, dqkv_ref, sums_ref, keys, vals, d_query, d_key, d_val, packed, sems = rest
    else:
        dqkv_ref, sums_ref, d_key, d_val, keys, vals, d_query, sems = rest
    step = pl.program_id(0)
    block, part_width = q_ref.shape
    count = d_query.shape[0]

    @pl.when(step == 0)
    def _():
        fill_keys(qkv_ref, bias_ref, keys, heads)
        vals[...] = value_columns(qkv_ref).astype(BF16)
        if last_part:
            d_key[...] = dkey_in[...]
            d_val[...] = dval_in[...]
            sums_ref[...] = sums_in[...]
        else:
            d_key[...] = jnp.zeros_like(d_key)
            d_val[...] = jnp.zeros_like(d_val)
            sums_ref[...] = jnp.zeros_like(sums_ref)

    log_scale = SCORE_SCALE * LOG2E
    d_att = mm(dout_ref[...], wo_ref[...]).astype(BF16)
    inner_cols = jnp.transpose(d_att.astype(F32) * att_ref[...].astype(F32))
    outs = []
    for head in range(heads):
        start, _ = head_place(head)
        inside, last = lane_mask(block, head)
        q_window = window(q_ref, head)
        query = jnp.where(last, 1.0, q_window).astype(BF16)
        q_only = jnp.where(inside, q_window, 0.0).astype(BF16)
        d_only = jnp.where(inside, window(d_att, head), 0.0).astype(BF16)
        inner = jnp.sum(inner_cols[head * HD : head * HD + HD], axis=0, keepdims=True)
        scores = mm(keys[head], query, NT)
        probs = jnp.exp2(scores * log_scale - lse_ref[head : head + 1, :])
        d_probs = mm(vals[:, start : start + WINDOW], d_only, NT)
        d_scores = (probs * (d_probs - inner)).astype(BF16)
        d_val[:, start : start + WINDOW] += mm(probs.astype(BF16), d_only)
        d_key[:, start : start + WINDOW] += mm(d_scores, q_only)
        outs.append(mm(d_scores, keys[head], TN))
    low = (join_windows(outs) * SCORE_SCALE).astype(BF16)
    d_query[pl.ds(pl.multiple_of(step * block, block), block), :] = low
    sums_ref[0:1, :] += jnp.sum(low.astype(F32), axis=0, keepdims=True)

    @pl.when(step == pl.num_programs(0) - 1)
    def _():
        copies = [
            pltpu.make_async_copy(
                d_query, dqkv_ref.at[pl.ds(first, count), pl.ds(0, part_width)], sems.at[0]
            )
        ]
        copies[0].start()
        if last_part:
            key_low = d_key[...] * SCORE_SCALE
            value_low = d_val[...]
            sums_ref[1:2, :] = jnp.sum(value_low.astype(BF16).astype(F32), axis=0, keepdims=True)
            value_low = pltpu.roll(value_low, LANES // 2, 1)
            whole = part_width - LANES
            packed[:, :whole] = key_low[:, :whole].astype(BF16)
            packed[:, whole:part_width] = (key_low[:, whole:] + value_low[:, :LANES]).astype(BF16)
            packed[:, part_width:] = value_low[:, LANES:].astype(BF16)
            copies.append(
                pltpu.make_async_copy(
                    packed,
                    dqkv_ref.at[pl.ds(0, packed.shape[0]), pl.ds(part_width, packed.shape[1])],
                    sems.at[1],
                )
            )
            copies[1].start()
        for copy in copies:
            copy.wait()


def attn_back_call(heads, d_out, wo, attended, qkv, key_bias, lse, block, first, earlier=None):
    count, width = d_out.shape
    frames = qkv.shape[0]
    part_width = wo.shape[1]
    base = first // block
    last_part = earlier is not None
    whole = pl.BlockSpec((frames, part_width), lambda i: (0, 0))
    sums_spec = pl.BlockSpec((8, part_width), lambda i: (0, 0))
    anywhere = pl.BlockSpec(memory_space=pl.ANY)
    out_shape = [
        jax.ShapeDtypeStruct(qkv.shape, BF16),
        jax.ShapeDtypeStruct((8, part_width), F32),
    ]
    out_specs = [anywhere, sums_spec]
    scratch = [
        pltpu.VMEM((heads, frames, WINDOW), BF16),
        pltpu.VMEM((frames, part_width), BF16),
        pltpu.VMEM((count, part_width), BF16),
    ]
    held = []
    if last_part:
        d_qkv, sums, d_key, d_val = earlier
        held = [d_key, d_val, sums, d_qkv]
        scratch += [pltpu.VMEM((frames, part_width), F32)] * 2
        scratch += [pltpu.VMEM((frames, qkv.shape[1] - part_width), BF16)]
    else:
        out_shape += [jax.ShapeDtypeStruct((frames, part_width), F32)] * 2
        out_specs += [whole, whole]
    return pl.pallas_call(
        partial(attn_back_body, heads, last_part, first),
        grid=(count // block,),
        in_specs=[
            pl.BlockSpec((block, width), lambda i: (i, 0)),
            pl.BlockSpec(wo.shape, lambda i: (0, 0)),
            pl.BlockSpec((block, part_width), lambda i: (i + base, 0)),
            pl.BlockSpec((block, part_width), lambda i: (i + base, 0)),
            pl.BlockSpec(qkv.shape, lambda i: (0, 0)),
            pl.BlockSpec(key_bias.shape, lambda i: (0, 0)),
            pl.BlockSpec((8, block), lambda i: (0, i + base)),
        ]
        + [whole, whole, sums_spec, anywhere][: len(held)],
        out_specs=out_specs,
        out_shape=out_shape,
        scratch_shapes=scratch + [pltpu.SemaphoreType.DMA((2,))],
        input_output_aliases={10: 0} if last_part else {},
        compiler_params=params("arbitrary"),
        cost_estimate=LITTLE,
        name="attn_bwd",
    )(d_out, wo, attended, qkv, qkv, key_bias, lse, *held)


def gelu_parts(values):
    size = jnp.abs(values)
    bell = jnp.exp2(values * values * (-0.5 * LOG2E))
    inv = 1.0 / (1.0 + (0.3275911 * math.sqrt(0.5)) * size)
    tail = inv * (
        0.5 * 0.254829592
        + inv
        * (
            0.5 * -0.284496736
            + inv * (0.5 * 1.421413741 + inv * (0.5 * -1.453152027 + inv * (0.5 * 1.061405429)))
        )
    )
    tail = tail * bell
    share = jnp.where(values < 0.0, tail, 1.0 - tail)
    return share, share + values * bell * (1.0 / math.sqrt(2.0 * math.pi))


def mlp_body(chunk, emits, skip, *refs):
    slot_refs, (w_ref, bias_ref, dhid_ref) = refs[: len(emits)], refs[len(emits) : len(emits) + 3]
    outs = refs[len(emits) + 3 + skip :]
    hid_ref, dpre_ref, sums_ref, parts, in_ref = *outs[:3], outs[3:-1], outs[-1]
    for index, slot_ref in enumerate(slot_refs):

        @pl.when(pl.program_id(0) == index)
        def _():
            in_ref[...] = slot_ref[...]

    @pl.when(pl.program_id(0) == 0)
    def _():
        sums_ref[...] = jnp.zeros_like(sums_ref)

    for start in range(0, w_ref.shape[1], chunk):
        cols = slice(start, start + chunk)
        pre = mm(in_ref[...], w_ref[:, cols]) + bias_ref[0:1, cols]
        share, slope = gelu_parts(pre)
        hid_ref[:, cols] = (pre * share).astype(BF16)
        d_pre = (dhid_ref[:, cols] * slope).astype(BF16)
        dpre_ref[:, cols] = d_pre
        sums_ref[0:1, cols] += jnp.sum(d_pre.astype(F32), axis=0, keepdims=True)
    part_store(emits, parts, mm(dpre_ref[...], w_ref[...], NT))


def mlp_call(emits, slots, weight, bias, d_hidden, first, frames, earlier=None):
    block, width = slots[0].shape
    count = block * len(slots)
    hidden_width = weight.shape[1]
    held = [] if earlier is None else list(earlier)
    base = first // block
    shapes, specs = part_shapes(emits, block, width)
    return pl.pallas_call(
        partial(mlp_body, min(256, hidden_width), emits, len(held)),
        grid=(count // block,),
        in_specs=[pl.BlockSpec((block, width), lambda i: (0, 0))] * len(slots)
        + [
            pl.BlockSpec(weight.shape, lambda i: (0, 0)),
            pl.BlockSpec(bias.shape, lambda i: (0, 0)),
            pl.BlockSpec((block, hidden_width), lambda i: (i + base, 0)),
        ]
        + [pl.BlockSpec(memory_space=pl.ANY)] * len(held),
        out_specs=[
            pl.BlockSpec((block, hidden_width), lambda i: (i + base, 0)),
            pl.BlockSpec((block, hidden_width), lambda i: (i + base, 0)),
            pl.BlockSpec((8, hidden_width), lambda i: (0, 0)),
        ]
        + specs,
        out_shape=[
            jax.ShapeDtypeStruct((frames, hidden_width), BF16),
            jax.ShapeDtypeStruct((frames, hidden_width), BF16),
            jax.ShapeDtypeStruct((8, hidden_width), F32),
        ]
        + shapes,
        scratch_shapes=[pltpu.VMEM((block, width), BF16)],
        input_output_aliases=(
            {} if earlier is None else {len(slots) + 3: 0, len(slots) + 4: 1}
        ),
        compiler_params=params("arbitrary"),
        cost_estimate=LITTLE,
        name="mlp_up",
    )(*slots, weight, bias, d_hidden, *held)


def residual_body(x_ref, mine_ref, far_ref, near_ref, vec_ref, res_ref, in_ref):
    total = mine_ref[...].astype(F32) + near_ref[...].astype(F32) + far_ref[...].astype(F32)
    residual = x_ref[...].astype(F32) + total + vec_ref[2:3, :]
    res_ref[...] = residual
    unit, _ = norm_parts(residual)
    in_ref[...] = (unit * vec_ref[3:4, :] + vec_ref[4:5, :]).astype(BF16)


def second_back_body(
    res_ref, mine_ref, far_ref, cot_ref, near_ref, vec_ref, dres_ref, low_ref, sums_ref
):
    @pl.when(pl.program_id(0) == 0)
    def _():
        sums_ref[...] = jnp.zeros_like(sums_ref)

    grad = mine_ref[...].astype(F32) + near_ref[...].astype(F32) + far_ref[...].astype(F32)
    unit, scale = norm_parts(res_ref[...])
    cot = cot_ref[...].astype(F32)
    d_res = norm_back(grad, vec_ref[3:4, :], unit, scale) + cot
    dres_ref[...] = d_res
    low_ref[...] = d_res.astype(BF16)
    sums_ref[2:3, :] += jnp.sum(d_res, axis=0, keepdims=True)
    sums_ref[3:4, :] += jnp.sum(grad * unit, axis=0, keepdims=True)
    sums_ref[4:5, :] += jnp.sum(grad, axis=0, keepdims=True)
    sums_ref[5:6, :] += jnp.sum(cot, axis=0, keepdims=True)


def first_back_body(x_ref, mine_ref, far_ref, dres_ref, near_ref, vec_ref, out_ref, sums_ref):
    @pl.when(pl.program_id(0) == 0)
    def _():
        sums_ref[...] = jnp.zeros_like(sums_ref)

    grad = mine_ref[...].astype(F32) + near_ref[...].astype(F32) + far_ref[...].astype(F32)
    unit, scale = norm_parts(x_ref[...].astype(F32))
    out_ref[...] = norm_back(grad, vec_ref[0:1, :], unit, scale) + dres_ref[...]
    sums_ref[0:1, :] += jnp.sum(grad * unit, axis=0, keepdims=True)
    sums_ref[1:2, :] += jnp.sum(grad, axis=0, keepdims=True)


def row_body(body, count, *refs):
    row_refs, pieces, vec_ref = refs[:count], refs[count : count + PIECES], refs[count + PIECES]
    near_ref = refs[-1]
    for index, piece in enumerate(pieces):

        @pl.when(pl.program_id(0) == index)
        def _():
            near_ref[...] = piece[...]

    body(*row_refs, near_ref, vec_ref, *refs[count + PIECES + 1 : -1])


def row_call(body, rows_in, near, vec_rows, out_types, with_sums, name):
    rows, width = rows_in[0].shape
    block = rows // PIECES
    row_spec = pl.BlockSpec((block, width), lambda i: (i, 0))
    whole = pl.BlockSpec((8, width), lambda i: (0, 0))
    return pl.pallas_call(
        partial(row_body, body, len(rows_in)),
        grid=(PIECES,),
        in_specs=[row_spec] * len(rows_in)
        + [pl.BlockSpec((block, width), lambda i: (0, 0))] * PIECES
        + [whole],
        out_specs=[row_spec] * len(out_types) + [whole] * with_sums,
        out_shape=[jax.ShapeDtypeStruct((rows, width), kind) for kind in out_types]
        + [jax.ShapeDtypeStruct((8, width), F32)] * with_sums,
        scratch_shapes=[pltpu.VMEM((block, width), BF16)],
        compiler_params=params("arbitrary"),
        cost_estimate=LITTLE,
        name=name,
    )(*rows_in, *near, vec_rows)


def polar_factors(grams, eye):
    def high(left, right):
        return jnp.dot(left, right, precision=HIGHEST, preferred_element_type=F32)

    scales = [1.0 / (jnp.sqrt(jnp.sum(gram * eye, keepdims=True)) + POLAR_EPS) for gram in grams]
    grams = [gram * scale * scale for gram, scale in zip(grams, scales)]
    factors = None
    for sweep in range(SWEEPS):
        squares = [high(gram, gram) for gram in grams]
        steps = [
            QUINTIC_A * eye + QUINTIC_B * gram + QUINTIC_C * square
            for gram, square in zip(grams, squares)
        ]
        if sweep < SWEEPS - 1:
            halves = [high(step, gram) for step, gram in zip(steps, grams)]
        if factors is None:
            factors = steps
        else:
            factors = [high(step, factor) for step, factor in zip(steps, factors)]
        if sweep < SWEEPS - 1:
            grams = [high(step, part) for step, part in zip(steps, halves)]
    return [factor * scale for factor, scale in zip(factors, scales)]


def polar_body(gram_ref, out_ref):
    count, rows, _ = gram_ref.shape
    row = lax.broadcasted_iota(jnp.int32, (rows, rows), 0)
    col = lax.broadcasted_iota(jnp.int32, (rows, rows), 1)
    eye = jnp.where(row == col, 1.0, 0.0)
    for index, factor in enumerate(polar_factors([gram_ref[i] for i in range(count)], eye)):
        out_ref[index] = factor


def polar_call(grams):
    count, rows, _ = grams.shape
    if rows % 32:
        return jnp.stack(polar_factors([grams[i] for i in range(count)], jnp.eye(rows, dtype=F32)))
    return pl.pallas_call(
        polar_body,
        out_shape=jax.ShapeDtypeStruct(grams.shape, F32),
        compiler_params=params(),
        name="polar",
    )(grams)


def gram_of(update):
    return lax.dot_general(update, update, NT, precision=HIGHEST, preferred_element_type=F32)


def momentum(moment, gradient):
    moved = MUON_DECAY * moment + gradient
    return moved, gradient + MUON_DECAY * moved


def applied(weight, factor, update, rate):
    return weight - rate * jnp.dot(factor, update, precision=HIGHEST)


def place_body(splits, narrow, me_ref, *refs):
    slots, outs = refs[:8], refs[8:]
    rows = slots[0].shape[0]
    for mask, slot in enumerate(slots):
        start = pl.multiple_of((me_ref[0] ^ mask) * rows, rows)
        for (low, high), out in zip(splits, outs):
            out[pl.ds(start, rows), :] = slot[:, low:high]
    if narrow is not None:
        tile = narrow // LANES * LANES
        turned = jnp.transpose(outs[0][:, tile : tile + LANES].astype(F32))
        outs[-1][...] = turned[narrow - tile : narrow - tile + 16]


def place_rows(slots, splits, narrow):
    rows = slots[0].shape[0]
    shapes = [jax.ShapeDtypeStruct((8 * rows, high - low), slots[0].dtype) for low, high in splits]
    if narrow is not None:
        shapes.append(jax.ShapeDtypeStruct((16, 8 * rows), F32))
    return pl.pallas_call(
        partial(place_body, splits, narrow),
        in_specs=[pl.BlockSpec(memory_space=pltpu.SMEM)]
        + [pl.BlockSpec(memory_space=pltpu.VMEM)] * 8,
        out_specs=[pl.BlockSpec(memory_space=pltpu.VMEM)] * len(shapes),
        out_shape=shapes,
        compiler_params=params(),
        cost_estimate=LITTLE,
        name="place_rows",
    )(lax.axis_index("dp").astype(jnp.int32)[None], *slots)


def dp_slots(own, ordered=False):
    line = {mask: swap(own, "dp", mask) for mask in (6, 2, 4)}
    slots = [own, swap(own, "dp", 1)] + [None] * 6
    for mask in (6, 2, 4):
        arrived = line[mask]
        if ordered:
            held = [slots[1]] if mask == 2 else [slots[3], slots[7]] if mask == 4 else []
            arrived = after(arrived, *held)
        slots[mask] = arrived
        slots[mask + 1] = swap(arrived, "dp", 1)
    return slots


def dp_send(own, ordered=False):
    if lax.axis_size("dp") != 8:
        return [lax.all_gather(own, "dp", axis=0, tiled=True)]
    return dp_slots(own, ordered)


def dp_place(slots, splits, narrow=None):
    if len(slots) > 1:
        return place_rows(slots, splits, narrow)
    parts = [slots[0][:, low:high] for low, high in splits]
    if narrow is not None:
        parts.append(jnp.transpose(slots[0][:, narrow : narrow + 16].astype(F32)))
    return parts


LINE = (4, 6, 2, 0)


def dp_cross(part):
    size = lax.axis_size("dp")
    if size != 8:
        return [], [dp_scatter_plain(part)]
    rows = part.shape[0] // size
    me = lax.axis_index("dp")

    def block(mask):
        return lax.dynamic_slice(part, ((me ^ mask) * rows, 0), (rows, part.shape[1]))

    return [block(mask) for mask in LINE], [swap(block(mask + 1), "dp", 1) for mask in LINE]


def dp_line(owns, arrivals):
    if not owns:
        return arrivals
    sums = []
    for mask, own, arrived in zip(LINE, owns, arrivals):
        pair = own.astype(F32) + arrived.astype(F32)
        sums.append(swap(pair.astype(BF16), "dp", mask) if mask else pair)
    return sums


def dp_total(sums):
    total = sums[-1].astype(F32)
    for value in sums[:-1]:
        total = total + value.astype(F32)
    return total


def dp_scatter_plain(part):
    return lax.psum_scatter(part, "dp", scatter_dimension=0, tiled=True)


def dp_sum(value):
    if lax.axis_size("dp") != 8:
        return lax.psum(value, "dp")
    for mask in (1, 2, 4):
        value = value + swap(value, "dp", mask)
    return value


def local(
    inputs,
    lengths,
    cotangent,
    w_qkv,
    w_out,
    w_up,
    w_down,
    vectors,
    bias_qkv,
    bias_up,
    mom_qkv,
    mom_out,
    mom_up,
    mom_down,
    mom_vectors,
    mom_bias_qkv,
    mom_bias_up,
):
    dp_size = lax.axis_size("dp")
    tensor_size = lax.axis_size("tensor")
    dp_index = lax.axis_index("dp")
    tok = inputs.shape[0]
    frames = tok * tensor_size
    tokens = frames * dp_size
    half = 2 * tok
    width = inputs.shape[1]
    own_rows = w_qkv.shape[0]
    head_width = w_qkv.shape[2]
    heads = head_width // HD
    padded = -(-head_width // LANES) * LANES
    extra = padded - head_width
    own_bias = bias_qkv.shape[0]

    w_parts = w_qkv.astype(BF16)
    small = jnp.concatenate(
        [
            vectors.astype(BF16),
            bias_up.astype(BF16)[:, None],
            jnp.pad(bias_qkv.astype(BF16), ((0, own_rows - own_bias), (0, 0))),
        ],
        axis=1,
    )
    small = jnp.pad(small, ((0, 0), (0, extra - small.shape[1])))
    packed = 3 * head_width + extra
    w_cols = jnp.concatenate(
        [
            w_parts[:, 0],
            small,
            w_parts[:, 1],
            w_parts[:, 2],
            jnp.pad(w_out.astype(BF16), ((0, 0), (0, extra))),
        ],
        axis=1,
    )
    first_slots = dp_send(w_cols, True)
    x_far = after(swap(inputs, "tensor", 2), *first_slots[2:7:4])
    x_rows = jnp.concatenate(
        [inputs, swap(inputs, "tensor", 1), x_far, swap(x_far, "tensor", 1)], axis=0
    )
    cot_far = after(swap(cotangent, "tensor", 2), *first_slots[4:5])
    cot_rows = jnp.concatenate(
        [cotangent, swap(cotangent, "tensor", 1), cot_far, swap(cot_far, "tensor", 1)], axis=0
    )
    first_slots[-1], x_rows, cot_rows = tie([first_slots[-1], x_rows, cot_rows])
    wq, wo, smalls = dp_place(
        first_slots, ((0, packed), (packed, packed + padded)), head_width
    )
    wd = lax.all_gather(w_down.astype(BF16), "dp", axis=0, tiled=True)
    wu = lax.all_gather(w_up.astype(BF16), "dp", axis=0, tiled=True)
    vec_rows = smalls[:8]
    bu = smalls[6:7]
    bq = smalls[7:9].reshape(2, dp_size, own_rows)[:, :, :own_bias].reshape(2, head_width)
    qkv_bias = jnp.concatenate(
        [bq[0:1], jnp.zeros((1, padded), F32), bq[1:2]], axis=1
    )

    me = lax.axis_index("tensor")
    place = jnp.concatenate([(me ^ s) * tok + jnp.arange(tok, dtype=jnp.int32) for s in range(4)])
    key_bias = jnp.where(place < lengths[0], 0.0, MASKED).astype(F32)[:, None]

    attn_in, qkv = qkv_call(x_rows, vec_rows, wq, qkv_bias, tok)
    att, lse, *sent = attn_call(
        heads, ("pieces",), qkv, key_bias, wo, tok, 3 * tok
    )
    att, lse, part_two = attn_call(
        heads, ("own",), qkv, key_bias, wo, tok, 2 * tok, (att, lse)
    )
    total = pair_pieces(part_two, swap_all(sent, "tensor", 1))
    far = swap(total, "tensor", 2)
    att, lse, mine, *sent = attn_call(
        heads,
        ("own", "pieces"),
        after(qkv, total),
        key_bias,
        wo,
        tok,
        0,
        (att, lse),
    )
    near = swap_all(sent, "tensor", 1)
    residual, mlp_in = row_call(
        residual_body, (inputs, mine, after(far, wd)), near, vec_rows, (F32, BF16), 0, "residual"
    )

    near = swap(mlp_in, "tensor", 1)
    far = swap(mlp_in, "tensor", 2)
    d_hidden = mm(after(cot_rows, mlp_in, wu), wd)
    hidden, d_pre, bu_sums, mine, *sent = mlp_call(
        ("own", "pieces"), [mlp_in, near], wu, bu, d_hidden, 0, frames
    )
    near_parts = swap_all(sent, "tensor", 1)
    far = after(far, mine)
    slots = [mlp_in, near, far, swap(far, "tensor", 1)]
    hidden, d_pre, sums, *sent = mlp_call(
        ("pieces",), slots[3:], wu, bu, d_hidden, 3 * tok, frames, (hidden, d_pre)
    )
    bu_sums = bu_sums + sums
    hidden, d_pre, sums, part_two = mlp_call(
        ("own",), slots[2:3], wu, bu, d_hidden, 2 * tok, frames, (hidden, d_pre)
    )
    bu_sums = bu_sums + sums
    total = pair_pieces(part_two, swap_all(sent, "tensor", 1))
    far = swap(total, "tensor", 2)
    hidden_later, d_pre_later = tie([hidden, d_pre], total)
    raw_wd = mm(cot_rows, hidden_later, TN).astype(BF16)
    raw_wu = mm(jnp.concatenate(slots, axis=0), after(d_pre_later, raw_wd), TN).astype(BF16)
    hidden = after(hidden, raw_wu)
    down_far = mm(hidden[half:], wd, NT).astype(BF16)
    down_mine = mm(hidden[:half], wd, NT).astype(BF16)
    near_parts = tie(near_parts, raw_wd, raw_wu, down_far, down_mine)
    grad_wd, grad_wu = dp_scatter_plain(raw_wd), dp_scatter_plain(raw_wu)
    d_residual, d_out, sums_two = row_call(
        second_back_body,
        (residual, mine, far, cotangent),
        near_parts,
        vec_rows,
        (F32, BF16),
        1,
        "second_back",
    )
    near = swap(d_out, "tensor", 1)
    far = swap(d_out, "tensor", 2)
    out_mine = jnp.concatenate([d_out, near], axis=0)
    carried = attn_back_call(
        heads, out_mine, wo, att, qkv, key_bias, lse, half, 0
    )
    far = after(far, carried[1])
    output_far = swap(after(pair_sum(down_far[:tok], down_far[tok:]), far), "tensor", 2)
    output_near = swap(down_mine[tok:], "tensor", 1)
    out_far = jnp.concatenate([far, swap(far, "tensor", 1)], axis=0)
    raw_wo = (mm(out_mine, att[:half], TN) + mm(out_far, att[half:], TN)).astype(BF16)
    out_later = after(out_far, raw_wo)
    d_qkv, bias_sums = attn_back_call(
        heads, out_later, wo, att, qkv, key_bias, lse, half, half, carried
    )
    d_qkv = after(d_qkv, output_far, output_near)
    first_far = mm(d_qkv[half:], wq, NT).astype(BF16)
    raw_wq = mm(attn_in, after(d_qkv, grad_wd, first_far), TN).astype(BF16)
    first_total = pair_sum(first_far[:tok], first_far[tok:])
    far = swap(first_total, "tensor", 2)
    d_qkv, raw_wq, raw_wo = tie([d_qkv, raw_wq, raw_wo])
    owns, crossed = dp_cross(jnp.concatenate([raw_wq, raw_wo], axis=1))
    first_mine = mm(after(d_qkv[:half], first_total, *crossed[:1]), wq, NT).astype(BF16)
    lined = dp_line(owns, tie(crossed, far))
    far = after(far, lined[-1])
    quarter = tok // PIECES
    sent = [first_mine[tok + k * quarter : tok + k * quarter + quarter] for k in range(PIECES)]
    near = swap_all(sent, "tensor", 1)
    output = (
        residual
        + (down_mine[:tok].astype(F32) + output_near.astype(F32) + output_far.astype(F32))
        + vec_rows[5]
    )
    input_grad, sums_one = row_call(
        first_back_body,
        (inputs, first_mine[:tok], far, d_residual),
        near,
        vec_rows,
        (F32,),
        1,
        "first_back",
    )

    vec_sums = tensor_sum(sums_one + sums_two)
    grad_wd = after(grad_wd, first_mine, lined[-1])
    mom_down_new, update_down = momentum(mom_down, grad_wd.astype(F32))
    early = polar_call(tensor_sum(gram_of(update_down)[None]))
    early = after(early, *lined[:2])
    new_w_down = applied(w_down, early[0], update_down, STEP_DOWN)
    grad_wu = after(after(grad_wu, first_mine, *crossed), *lined[:3])

    rows_of = jnp.concatenate(
        [
            vec_sums[:6],
            bu_sums[0:1],
            jnp.pad(bias_sums[:2], ((0, 0), (0, width - padded))),
        ],
        axis=0,
    )
    rows_of = dp_sum(after(rows_of, new_w_down))
    own_cols = lax.dynamic_slice(rows_of, (0, dp_index * own_rows), (7, own_rows))
    vec_grad = jnp.transpose(own_cols[:6])
    bu_grad = own_cols[6]
    bq_grad = jnp.transpose(
        lax.dynamic_slice(rows_of, (7, dp_index * own_bias), (2, own_bias))
    )

    mom_up_new, update_up = momentum(mom_up, grad_wu.astype(F32))
    gram_up = gram_of(update_up)
    lined = tie(lined, gram_up, new_w_down, rows_of)
    grad_first = dp_total(lined)
    grad_wq, grad_wo = grad_first[:, :packed], grad_first[:, packed : packed + head_width]
    mom_out_new, update_out = momentum(mom_out, grad_wo)
    spots = (0, padded, padded + head_width)
    grad_parts = jnp.stack([grad_wq[:, spot : spot + head_width] for spot in spots], axis=1)
    mom_qkv_new, update_qkv = momentum(mom_qkv, grad_parts)
    flat = jnp.concatenate(
        [update_qkv[:, 0], jnp.zeros((own_rows, extra), F32), update_qkv[:, 1], update_qkv[:, 2]], axis=1
    )
    late = tensor_sum(jnp.stack([gram_of(update_out), gram_of(flat), gram_up]))
    late = polar_call(late)
    new_w_out = applied(w_out, late[0], update_out, STEP_OUT)
    new_w_up = applied(w_up, late[2], update_up, STEP_UP)
    polar_qkv = jnp.dot(late[1], flat, precision=HIGHEST)
    new_w_qkv = w_qkv - STEP_QKV * jnp.stack(
        [polar_qkv[:, spot : spot + head_width] for spot in spots], axis=1
    )

    vec_rate = VEC_RATE / math.sqrt(tokens)
    new_mom_vectors = VEC_DECAY * mom_vectors + vec_grad
    new_mom_bias_qkv = VEC_DECAY * mom_bias_qkv + bq_grad
    new_mom_bias_up = VEC_DECAY * mom_bias_up + bu_grad
    new_vectors = vectors - vec_rate * new_mom_vectors
    new_bias_qkv = bias_qkv - vec_rate * new_mom_bias_qkv
    new_bias_up = bias_up - vec_rate * new_mom_bias_up
    return (
        output,
        input_grad,
        new_w_qkv,
        new_w_out,
        new_w_up,
        new_w_down,
        new_vectors,
        new_bias_qkv,
        new_bias_up,
        mom_qkv_new,
        mom_out_new,
        mom_up_new,
        mom_down_new,
        new_mom_vectors,
        new_mom_bias_qkv,
        new_mom_bias_up,
    )


def solution(mesh):
    in_specs = (
        P(("dp", "tensor"), None),
        P("dp"),
        P(("dp", "tensor"), None),
        P("dp", None, "tensor"),
        P("dp", "tensor"),
        P("dp", "tensor"),
        P("dp", "tensor"),
        P("dp", None),
        P(("tensor", "dp"), None),
        P(("tensor", "dp")),
        P("dp", None, "tensor"),
        P("dp", "tensor"),
        P("dp", "tensor"),
        P("dp", "tensor"),
        P("dp", None),
        P(("tensor", "dp"), None),
        P(("tensor", "dp")),
    )
    out_specs = (
        P(("dp", "tensor"), None),
        P(("dp", "tensor"), None),
        P("dp", None, "tensor"),
        P("dp", "tensor"),
        P("dp", "tensor"),
        P("dp", "tensor"),
        P("dp", None),
        P(("tensor", "dp"), None),
        P(("tensor", "dp")),
        P("dp", None, "tensor"),
        P("dp", "tensor"),
        P("dp", "tensor"),
        P("dp", "tensor"),
        P("dp", None),
        P(("tensor", "dp"), None),
        P(("tensor", "dp")),
    )
    return jax.shard_map(local, mesh=mesh, in_specs=in_specs, out_specs=out_specs, check_vma=False)
```

```python
from functools import partial
import math

import jax
import jax.numpy as jnp
from jax import lax
from jax.experimental import pallas as pl
from jax.experimental.pallas import tpu as pltpu
from jax.sharding import PartitionSpec as P

HD = 80
SWEEPS = 5
LANES = 128
WINDOW = 256
BIAS_LANE = WINDOW - 1
VMEM_LIMIT = 58 * 1024 * 1024

HIGHEST = lax.Precision.HIGHEST
NORM_EPS = 1e-05
POLAR_EPS = 1e-07
MASKED = -1e30
QUINTIC_A = 3.4445
QUINTIC_B = -4.775
QUINTIC_C = 2.0315
MUON_DECAY = 0.95
VEC_DECAY = 0.9
VEC_RATE = 0.1
STEP_QKV = 0.5 * math.sqrt(3.0)
STEP_OUT = 2.0
STEP_UP = 1.0
STEP_DOWN = 0.5
LOG2E = math.log2(math.e)
SCORE_SCALE = 1.0 / math.sqrt(HD)
F32 = jnp.float32
BF16 = jnp.bfloat16
LITTLE = pl.CostEstimate(flops=1_000_000, bytes_accessed=100_000, transcendentals=0)
NN = (((1,), (0,)), ((), ()))
NT = (((1,), (1,)), ((), ()))
TN = (((0,), (0,)), ((), ()))


def mm(left, right, dims=NN):
    return lax.dot_general(left, right, dims, preferred_element_type=F32)


def norm_parts(values):
    center = values - jnp.mean(values, axis=-1, keepdims=True)
    spread = jnp.mean(center * center, axis=-1, keepdims=True)
    scale = lax.rsqrt(spread + NORM_EPS)
    return center * scale, scale


def norm_back(grad, gain, unit, scale):
    inner = grad * gain
    mean_grad = jnp.mean(inner, axis=-1, keepdims=True)
    mean_unit = jnp.mean(inner * unit, axis=-1, keepdims=True)
    return scale * (inner - mean_grad - unit * mean_unit)


def params(*semantics):
    return pltpu.CompilerParams(
        dimension_semantics=semantics or None, vmem_limit_bytes=VMEM_LIMIT
    )


def swap(value, axis, mask):
    size = lax.axis_size(axis)
    return lax.ppermute(value, axis, [(i, i ^ mask) for i in range(size)])


def tensor_slots(own):
    near = swap(own, "tensor", 1)
    far = swap(own, "tensor", 2)
    return [own, near, far, swap(far, "tensor", 1)]


def tensor_gather(own):
    return jnp.concatenate(tensor_slots(own), axis=0)


def tensor_sum(value):
    value = value + swap(value, "tensor", 1)
    return value + swap(value, "tensor", 2)


def pair_sum(own, sent):
    arrived = swap(sent, "tensor", 1)
    return (own.astype(F32) + arrived.astype(F32)).astype(BF16)


def after(value, *others):
    return lax.optimization_barrier((value, *others))[0]


def tie(values, *others):
    return list(lax.optimization_barrier((*values, *others))[: len(values)])


def qkv_body(x_ref, vec_ref, w_ref, bias_ref, attn_ref, qkv_ref):
    unit, _ = norm_parts(x_ref[...].astype(F32))
    attn_in = (unit * vec_ref[0:1, :] + vec_ref[1:2, :]).astype(BF16)
    attn_ref[...] = attn_in
    qkv_ref[...] = (mm(attn_in, w_ref[...]) + bias_ref[0:1, :]).astype(BF16)


def qkv_call(x_rows, vec_rows, weight, bias, block):
    rows, width = x_rows.shape
    columns = weight.shape[1]
    return pl.pallas_call(
        qkv_body,
        grid=(rows // block,),
        in_specs=[
            pl.BlockSpec((block, width), lambda i: (i, 0)),
            pl.BlockSpec(vec_rows.shape, lambda i: (0, 0)),
            pl.BlockSpec(weight.shape, lambda i: (0, 0)),
            pl.BlockSpec(bias.shape, lambda i: (0, 0)),
        ],
        out_specs=[
            pl.BlockSpec((block, width), lambda i: (i, 0)),
            pl.BlockSpec((block, columns), lambda i: (i, 0)),
        ],
        out_shape=[
            jax.ShapeDtypeStruct((rows, width), BF16),
            jax.ShapeDtypeStruct((rows, columns), BF16),
        ],
        compiler_params=params("arbitrary"),
        cost_estimate=LITTLE,
        name="norm_qkv",
    )(x_rows, vec_rows, weight, bias)


PIECES = 4


def part_shapes(emits, rows, width):
    shapes = []
    for kind in emits:
        count = PIECES if kind == "pieces" else 1
        shapes += [jax.ShapeDtypeStruct((rows // count, width), BF16)] * count
    return shapes, [pl.BlockSpec(shape.shape, lambda i: (0, 0)) for shape in shapes]


def part_store(emits, refs, value):
    spot = 0
    for index, kind in enumerate(emits):
        count = PIECES if kind == "pieces" else 1
        group = refs[spot : spot + count]
        spot += count

        @pl.when(pl.program_id(0) == index)
        def _():
            rows = value.shape[0] // count
            for piece, ref in enumerate(group):
                ref[...] = value[piece * rows : piece * rows + rows].astype(BF16)


def swap_all(values, axis, mask):
    return [swap(value, axis, mask) for value in values]


def pair_body(own_ref, *rest):
    pieces, out_ref = rest[:-1], rest[-1]
    rows = pieces[0].shape[0]
    for index, piece in enumerate(pieces):
        part = slice(index * rows, index * rows + rows)
        out_ref[part, :] = (own_ref[part, :].astype(F32) + piece[...].astype(F32)).astype(BF16)


def pair_pieces(own, pieces):
    return pl.pallas_call(
        pair_body,
        out_shape=jax.ShapeDtypeStruct(own.shape, BF16),
        compiler_params=params(),
        cost_estimate=LITTLE,
        name="pair_sum",
    )(own, *pieces)


def head_place(head):
    start = 0 if head * HD + HD <= BIAS_LANE else LANES
    return start, head * HD - start


def lane_mask(rows, head):
    _, offset = head_place(head)
    lane = lax.broadcasted_iota(jnp.int32, (rows, WINDOW), 1)
    return (lane >= offset) & (lane < offset + HD), lane == BIAS_LANE


def window(value, head):
    start, _ = head_place(head)
    return value[:, start : start + WINDOW].astype(F32)


def key_columns(qkv_ref):
    third = (qkv_ref.shape[1] + LANES) // 3
    return qkv_ref[:, third : 2 * third]


def value_columns(qkv_ref):
    third = (qkv_ref.shape[1] + LANES) // 3
    tail = qkv_ref[:, qkv_ref.shape[1] - third :].astype(F32)
    return pltpu.roll(tail, third - LANES // 2, 1)


def fill_keys(qkv_ref, bias_ref, keys_out, heads):
    columns = key_columns(qkv_ref)
    for head in range(heads):
        inside, last = lane_mask(columns.shape[0], head)
        picked = jnp.where(inside, window(columns, head), 0.0)
        keys_out[head] = jnp.where(last, bias_ref[...], picked).astype(BF16)


def join_windows(parts):
    low, high = None, None
    for head, part in enumerate(parts):
        if head_place(head)[0] == 0:
            low = part if low is None else low + part
        else:
            high = part if high is None else high + part
    return jnp.concatenate(
        [low[:, :LANES], low[:, LANES:] + high[:, :LANES], high[:, LANES:]], axis=1
    )


def attn_body(heads, emits, skip, q_ref, qkv_ref, bias_ref, wo_ref, *rest):
    (att_ref, lse_ref), parts, (keys, vals) = rest[skip : skip + 2], rest[skip + 2 : -2], rest[-2:]
    block = q_ref.shape[0]
    frames = qkv_ref.shape[0]

    @pl.when(pl.program_id(0) == 0)
    def _():
        fill_keys(qkv_ref, bias_ref, keys, heads)
        columns = value_columns(qkv_ref)
        for head in range(heads):
            inside, _ = lane_mask(frames, head)
            vals[head] = jnp.where(inside, window(columns, head), 0.0).astype(BF16)

    log_scale = SCORE_SCALE * LOG2E
    outs = []
    lane = lax.broadcasted_iota(jnp.int32, (block, LANES), 1)
    lse_cols = jnp.zeros((block, LANES), F32)
    for head in range(heads):
        _, last = lane_mask(block, head)
        query = jnp.where(last, 1.0, window(q_ref, head)).astype(BF16)
        scores = mm(query, keys[head], NT)
        row_max = jnp.max(scores, axis=1, keepdims=True)
        powers = jnp.exp2((scores - row_max) * log_scale)
        totals = jnp.sum(powers, axis=1, keepdims=True)
        outs.append(mm(powers.astype(BF16), vals[head]) * (1.0 / totals))
        lse_cols = jnp.where(lane == head, row_max * log_scale + jnp.log2(totals), lse_cols)
    attended = join_windows(outs).astype(BF16)
    att_ref[...] = attended
    lse_ref[...] = jnp.transpose(lse_cols)[:8]
    part_store(emits, parts, mm(attended, wo_ref[...], NT))


def attn_call(heads, emits, qkv, key_bias, wo, block, first, earlier=None):
    count = block * len(emits)
    frames = qkv.shape[0]
    part_width = wo.shape[1]
    width = wo.shape[0]
    held = [] if earlier is None else list(earlier)
    base = first // block
    shapes, specs = part_shapes(emits, block, width)
    return pl.pallas_call(
        partial(attn_body, heads, emits, len(held)),
        grid=(count // block,),
        in_specs=[
            pl.BlockSpec((block, part_width), lambda i: (i + base, 0)),
            pl.BlockSpec(qkv.shape, lambda i: (0, 0)),
            pl.BlockSpec(key_bias.shape, lambda i: (0, 0)),
            pl.BlockSpec(wo.shape, lambda i: (0, 0)),
        ]
        + [pl.BlockSpec(memory_space=pl.ANY)] * len(held),
        out_specs=[
            pl.BlockSpec((block, part_width), lambda i: (i + base, 0)),
            pl.BlockSpec((8, block), lambda i: (0, i + base)),
        ]
        + specs,
        out_shape=[
            jax.ShapeDtypeStruct((frames, part_width), BF16),
            jax.ShapeDtypeStruct((8, frames), F32),
        ]
        + shapes,
        scratch_shapes=[
            pltpu.VMEM((heads, frames, WINDOW), BF16),
            pltpu.VMEM((heads, frames, WINDOW), BF16),
        ],
        input_output_aliases={} if earlier is None else {4: 0, 5: 1},
        compiler_params=params("arbitrary"),
        cost_estimate=LITTLE,
        name="attn_fwd",
    )(qkv, qkv, key_bias, wo, *held)


def attn_back_body(heads, last_part, first, dout_ref, wo_ref, att_ref, q_ref, qkv_ref, bias_ref, lse_ref, *rest):
    if last_part:
        dkey_in, dval_in, sums_in, _, dqkv_ref, sums_ref, keys, vals, d_query, d_key, d_val, packed, sems = rest
    else:
        dqkv_ref, sums_ref, d_key, d_val, keys, vals, d_query, sems = rest
    step = pl.program_id(0)
    block, part_width = q_ref.shape
    count = d_query.shape[0]

    @pl.when(step == 0)
    def _():
        fill_keys(qkv_ref, bias_ref, keys, heads)
        vals[...] = value_columns(qkv_ref).astype(BF16)
        if last_part:
            d_key[...] = dkey_in[...]
            d_val[...] = dval_in[...]
            sums_ref[...] = sums_in[...]
        else:
            d_key[...] = jnp.zeros_like(d_key)
            d_val[...] = jnp.zeros_like(d_val)
            sums_ref[...] = jnp.zeros_like(sums_ref)

    log_scale = SCORE_SCALE * LOG2E
    d_att = mm(dout_ref[...], wo_ref[...]).astype(BF16)
    inner_cols = jnp.transpose(d_att.astype(F32) * att_ref[...].astype(F32))
    outs = []
    for head in range(heads):
        start, _ = head_place(head)
        inside, last = lane_mask(block, head)
        q_window = window(q_ref, head)
        query = jnp.where(last, 1.0, q_window).astype(BF16)
        q_only = jnp.where(inside, q_window, 0.0).astype(BF16)
        d_only = jnp.where(inside, window(d_att, head), 0.0).astype(BF16)
        inner = jnp.sum(inner_cols[head * HD : head * HD + HD], axis=0, keepdims=True)
        scores = mm(keys[head], query, NT)
        probs = jnp.exp2(scores * log_scale - lse_ref[head : head + 1, :])
        d_probs = mm(vals[:, start : start + WINDOW], d_only, NT)
        d_scores = (probs * (d_probs - inner)).astype(BF16)
        d_val[:, start : start + WINDOW] += mm(probs.astype(BF16), d_only)
        d_key[:, start : start + WINDOW] += mm(d_scores, q_only)
        outs.append(mm(d_scores, keys[head], TN))
    low = (join_windows(outs) * SCORE_SCALE).astype(BF16)
    d_query[pl.ds(pl.multiple_of(step * block, block), block), :] = low
    sums_ref[0:1, :] += jnp.sum(low.astype(F32), axis=0, keepdims=True)

    @pl.when(step == pl.num_programs(0) - 1)
    def _():
        copies = [
            pltpu.make_async_copy(
                d_query, dqkv_ref.at[pl.ds(first, count), pl.ds(0, part_width)], sems.at[0]
            )
        ]
        copies[0].start()
        if last_part:
            key_low = d_key[...] * SCORE_SCALE
            value_low = d_val[...]
            sums_ref[1:2, :] = jnp.sum(value_low.astype(BF16).astype(F32), axis=0, keepdims=True)
            value_low = pltpu.roll(value_low, LANES // 2, 1)
            whole = part_width - LANES
            packed[:, :whole] = key_low[:, :whole].astype(BF16)
            packed[:, whole:part_width] = (key_low[:, whole:] + value_low[:, :LANES]).astype(BF16)
            packed[:, part_width:] = value_low[:, LANES:].astype(BF16)
            copies.append(
                pltpu.make_async_copy(
                    packed,
                    dqkv_ref.at[pl.ds(0, packed.shape[0]), pl.ds(part_width, packed.shape[1])],
                    sems.at[1],
                )
            )
            copies[1].start()
        for copy in copies:
            copy.wait()


def attn_back_call(heads, d_out, wo, attended, qkv, key_bias, lse, block, first, earlier=None):
    count, width = d_out.shape
    frames = qkv.shape[0]
    part_width = wo.shape[1]
    base = first // block
    last_part = earlier is not None
    whole = pl.BlockSpec((frames, part_width), lambda i: (0, 0))
    sums_spec = pl.BlockSpec((8, part_width), lambda i: (0, 0))
    anywhere = pl.BlockSpec(memory_space=pl.ANY)
    out_shape = [
        jax.ShapeDtypeStruct(qkv.shape, BF16),
        jax.ShapeDtypeStruct((8, part_width), F32),
    ]
    out_specs = [anywhere, sums_spec]
    scratch = [
        pltpu.VMEM((heads, frames, WINDOW), BF16),
        pltpu.VMEM((frames, part_width), BF16),
        pltpu.VMEM((count, part_width), BF16),
    ]
    held = []
    if last_part:
        d_qkv, sums, d_key, d_val = earlier
        held = [d_key, d_val, sums, d_qkv]
        scratch += [pltpu.VMEM((frames, part_width), F32)] * 2
        scratch += [pltpu.VMEM((frames, qkv.shape[1] - part_width), BF16)]
    else:
        out_shape += [jax.ShapeDtypeStruct((frames, part_width), F32)] * 2
        out_specs += [whole, whole]
    return pl.pallas_call(
        partial(attn_back_body, heads, last_part, first),
        grid=(count // block,),
        in_specs=[
            pl.BlockSpec((block, width), lambda i: (i, 0)),
            pl.BlockSpec(wo.shape, lambda i: (0, 0)),
            pl.BlockSpec((block, part_width), lambda i: (i + base, 0)),
            pl.BlockSpec((block, part_width), lambda i: (i + base, 0)),
            pl.BlockSpec(qkv.shape, lambda i: (0, 0)),
            pl.BlockSpec(key_bias.shape, lambda i: (0, 0)),
            pl.BlockSpec((8, block), lambda i: (0, i + base)),
        ]
        + [whole, whole, sums_spec, anywhere][: len(held)],
        out_specs=out_specs,
        out_shape=out_shape,
        scratch_shapes=scratch + [pltpu.SemaphoreType.DMA((2,))],
        input_output_aliases={10: 0} if last_part else {},
        compiler_params=params("arbitrary"),
        cost_estimate=LITTLE,
        name="attn_bwd",
    )(d_out, wo, attended, qkv, qkv, key_bias, lse, *held)


def gelu_parts(values):
    size = jnp.abs(values)
    bell = jnp.exp2(values * values * (-0.5 * LOG2E))
    inv = 1.0 / (1.0 + (0.3275911 * math.sqrt(0.5)) * size)
    tail = inv * (
        0.5 * 0.254829592
        + inv
        * (
            0.5 * -0.284496736
            + inv * (0.5 * 1.421413741 + inv * (0.5 * -1.453152027 + inv * (0.5 * 1.061405429)))
        )
    )
    tail = tail * bell
    share = jnp.where(values < 0.0, tail, 1.0 - tail)
    return share, share + values * bell * (1.0 / math.sqrt(2.0 * math.pi))


def mlp_body(chunk, emits, skip, *refs):
    slot_refs, (w_ref, bias_ref, dhid_ref) = refs[: len(emits)], refs[len(emits) : len(emits) + 3]
    outs = refs[len(emits) + 3 + skip :]
    hid_ref, dpre_ref, sums_ref, parts, in_ref = *outs[:3], outs[3:-1], outs[-1]
    for index, slot_ref in enumerate(slot_refs):

        @pl.when(pl.program_id(0) == index)
        def _():
            in_ref[...] = slot_ref[...]

    @pl.when(pl.program_id(0) == 0)
    def _():
        sums_ref[...] = jnp.zeros_like(sums_ref)

    for start in range(0, w_ref.shape[1], chunk):
        cols = slice(start, start + chunk)
        pre = mm(in_ref[...], w_ref[:, cols]) + bias_ref[0:1, cols]
        share, slope = gelu_parts(pre)
        hid_ref[:, cols] = (pre * share).astype(BF16)
        d_pre = (dhid_ref[:, cols] * slope).astype(BF16)
        dpre_ref[:, cols] = d_pre
        sums_ref[0:1, cols] += jnp.sum(d_pre.astype(F32), axis=0, keepdims=True)
    part_store(emits, parts, mm(dpre_ref[...], w_ref[...], NT))


def mlp_call(emits, slots, weight, bias, d_hidden, first, frames, earlier=None):
    block, width = slots[0].shape
    count = block * len(slots)
    hidden_width = weight.shape[1]
    held = [] if earlier is None else list(earlier)
    base = first // block
    shapes, specs = part_shapes(emits, block, width)
    return pl.pallas_call(
        partial(mlp_body, min(256, hidden_width), emits, len(held)),
        grid=(count // block,),
        in_specs=[pl.BlockSpec((block, width), lambda i: (0, 0))] * len(slots)
        + [
            pl.BlockSpec(weight.shape, lambda i: (0, 0)),
            pl.BlockSpec(bias.shape, lambda i: (0, 0)),
            pl.BlockSpec((block, hidden_width), lambda i: (i + base, 0)),
        ]
        + [pl.BlockSpec(memory_space=pl.ANY)] * len(held),
        out_specs=[
            pl.BlockSpec((block, hidden_width), lambda i: (i + base, 0)),
            pl.BlockSpec((block, hidden_width), lambda i: (i + base, 0)),
            pl.BlockSpec((8, hidden_width), lambda i: (0, 0)),
        ]
        + specs,
        out_shape=[
            jax.ShapeDtypeStruct((frames, hidden_width), BF16),
            jax.ShapeDtypeStruct((frames, hidden_width), BF16),
            jax.ShapeDtypeStruct((8, hidden_width), F32),
        ]
        + shapes,
        scratch_shapes=[pltpu.VMEM((block, width), BF16)],
        input_output_aliases=(
            {} if earlier is None else {len(slots) + 3: 0, len(slots) + 4: 1}
        ),
        compiler_params=params("arbitrary"),
        cost_estimate=LITTLE,
        name="mlp_up",
    )(*slots, weight, bias, d_hidden, *held)


def residual_body(x_ref, mine_ref, far_ref, near_ref, vec_ref, res_ref, in_ref):
    total = mine_ref[...].astype(F32) + near_ref[...].astype(F32) + far_ref[...].astype(F32)
    residual = x_ref[...].astype(F32) + total + vec_ref[2:3, :]
    res_ref[...] = residual
    unit, _ = norm_parts(residual)
    in_ref[...] = (unit * vec_ref[3:4, :] + vec_ref[4:5, :]).astype(BF16)


def second_back_body(
    res_ref, mine_ref, far_ref, cot_ref, near_ref, vec_ref, dres_ref, low_ref, sums_ref
):
    @pl.when(pl.program_id(0) == 0)
    def _():
        sums_ref[...] = jnp.zeros_like(sums_ref)

    grad = mine_ref[...].astype(F32) + near_ref[...].astype(F32) + far_ref[...].astype(F32)
    unit, scale = norm_parts(res_ref[...])
    cot = cot_ref[...].astype(F32)
    d_res = norm_back(grad, vec_ref[3:4, :], unit, scale) + cot
    dres_ref[...] = d_res
    low_ref[...] = d_res.astype(BF16)
    sums_ref[2:3, :] += jnp.sum(d_res, axis=0, keepdims=True)
    sums_ref[3:4, :] += jnp.sum(grad * unit, axis=0, keepdims=True)
    sums_ref[4:5, :] += jnp.sum(grad, axis=0, keepdims=True)
    sums_ref[5:6, :] += jnp.sum(cot, axis=0, keepdims=True)


def first_back_body(x_ref, mine_ref, far_ref, dres_ref, near_ref, vec_ref, out_ref, sums_ref):
    @pl.when(pl.program_id(0) == 0)
    def _():
        sums_ref[...] = jnp.zeros_like(sums_ref)

    grad = mine_ref[...].astype(F32) + near_ref[...].astype(F32) + far_ref[...].astype(F32)
    unit, scale = norm_parts(x_ref[...].astype(F32))
    out_ref[...] = norm_back(grad, vec_ref[0:1, :], unit, scale) + dres_ref[...]
    sums_ref[0:1, :] += jnp.sum(grad * unit, axis=0, keepdims=True)
    sums_ref[1:2, :] += jnp.sum(grad, axis=0, keepdims=True)


def row_body(body, count, *refs):
    row_refs, pieces, vec_ref = refs[:count], refs[count : count + PIECES], refs[count + PIECES]
    near_ref = refs[-1]
    for index, piece in enumerate(pieces):

        @pl.when(pl.program_id(0) == index)
        def _():
            near_ref[...] = piece[...]

    body(*row_refs, near_ref, vec_ref, *refs[count + PIECES + 1 : -1])


def row_call(body, rows_in, near, vec_rows, out_types, with_sums, name):
    rows, width = rows_in[0].shape
    block = rows // PIECES
    row_spec = pl.BlockSpec((block, width), lambda i: (i, 0))
    whole = pl.BlockSpec((8, width), lambda i: (0, 0))
    return pl.pallas_call(
        partial(row_body, body, len(rows_in)),
        grid=(PIECES,),
        in_specs=[row_spec] * len(rows_in)
        + [pl.BlockSpec((block, width), lambda i: (0, 0))] * PIECES
        + [whole],
        out_specs=[row_spec] * len(out_types) + [whole] * with_sums,
        out_shape=[jax.ShapeDtypeStruct((rows, width), kind) for kind in out_types]
        + [jax.ShapeDtypeStruct((8, width), F32)] * with_sums,
        scratch_shapes=[pltpu.VMEM((block, width), BF16)],
        compiler_params=params("arbitrary"),
        cost_estimate=LITTLE,
        name=name,
    )(*rows_in, *near, vec_rows)


def polar_factors(grams, eye):
    def high(left, right):
        return jnp.dot(left, right, precision=HIGHEST, preferred_element_type=F32)

    scales = [1.0 / (jnp.sqrt(jnp.sum(gram * eye, keepdims=True)) + POLAR_EPS) for gram in grams]
    grams = [gram * scale * scale for gram, scale in zip(grams, scales)]
    factors = None
    for sweep in range(SWEEPS):
        squares = [high(gram, gram) for gram in grams]
        steps = [
            QUINTIC_A * eye + QUINTIC_B * gram + QUINTIC_C * square
            for gram, square in zip(grams, squares)
        ]
        if sweep < SWEEPS - 1:
            halves = [high(step, gram) for step, gram in zip(steps, grams)]
        if factors is None:
            factors = steps
        else:
            factors = [high(step, factor) for step, factor in zip(steps, factors)]
        if sweep < SWEEPS - 1:
            grams = [high(step, part) for step, part in zip(steps, halves)]
    return [factor * scale for factor, scale in zip(factors, scales)]


def polar_body(gram_ref, out_ref):
    count, rows, _ = gram_ref.shape
    row = lax.broadcasted_iota(jnp.int32, (rows, rows), 0)
    col = lax.broadcasted_iota(jnp.int32, (rows, rows), 1)
    eye = jnp.where(row == col, 1.0, 0.0)
    for index, factor in enumerate(polar_factors([gram_ref[i] for i in range(count)], eye)):
        out_ref[index] = factor


def polar_call(grams):
    count, rows, _ = grams.shape
    if rows % 32:
        return jnp.stack(polar_factors([grams[i] for i in range(count)], jnp.eye(rows, dtype=F32)))
    return pl.pallas_call(
        polar_body,
        out_shape=jax.ShapeDtypeStruct(grams.shape, F32),
        compiler_params=params(),
        name="polar",
    )(grams)


def gram_of(update):
    return lax.dot_general(update, update, NT, precision=HIGHEST, preferred_element_type=F32)


def momentum(moment, gradient):
    moved = MUON_DECAY * moment + gradient
    return moved, gradient + MUON_DECAY * moved


def applied(weight, factor, update, rate):
    return weight - rate * jnp.dot(factor, update, precision=HIGHEST)


def place_body(splits, narrow, me_ref, *refs):
    slots, outs = refs[:8], refs[8:]
    rows = slots[0].shape[0]
    for mask, slot in enumerate(slots):
        start = pl.multiple_of((me_ref[0] ^ mask) * rows, rows)
        for (low, high), out in zip(splits, outs):
            out[pl.ds(start, rows), :] = slot[:, low:high]
    if narrow is not None:
        tile = narrow // LANES * LANES
        turned = jnp.transpose(outs[0][:, tile : tile + LANES].astype(F32))
        outs[-1][...] = turned[narrow - tile : narrow - tile + 16]


def place_rows(slots, splits, narrow):
    rows = slots[0].shape[0]
    shapes = [jax.ShapeDtypeStruct((8 * rows, high - low), slots[0].dtype) for low, high in splits]
    if narrow is not None:
        shapes.append(jax.ShapeDtypeStruct((16, 8 * rows), F32))
    return pl.pallas_call(
        partial(place_body, splits, narrow),
        in_specs=[pl.BlockSpec(memory_space=pltpu.SMEM)]
        + [pl.BlockSpec(memory_space=pltpu.VMEM)] * 8,
        out_specs=[pl.BlockSpec(memory_space=pltpu.VMEM)] * len(shapes),
        out_shape=shapes,
        compiler_params=params(),
        cost_estimate=LITTLE,
        name="place_rows",
    )(lax.axis_index("dp").astype(jnp.int32)[None], *slots)


def dp_slots(own, ordered=False):
    line = {mask: swap(own, "dp", mask) for mask in (6, 2, 4)}
    slots = [own, swap(own, "dp", 1)] + [None] * 6
    for mask in (6, 2, 4):
        arrived = line[mask]
        if ordered:
            held = [slots[1]] if mask == 2 else [slots[3], slots[7]] if mask == 4 else []
            arrived = after(arrived, *held)
        slots[mask] = arrived
        slots[mask + 1] = swap(arrived, "dp", 1)
    return slots


def dp_send(own, ordered=False):
    if lax.axis_size("dp") != 8:
        return [lax.all_gather(own, "dp", axis=0, tiled=True)]
    return dp_slots(own, ordered)


def dp_place(slots, splits, narrow=None):
    if len(slots) > 1:
        return place_rows(slots, splits, narrow)
    parts = [slots[0][:, low:high] for low, high in splits]
    if narrow is not None:
        parts.append(jnp.transpose(slots[0][:, narrow : narrow + 16].astype(F32)))
    return parts


LINE = (4, 6, 2, 0)


def dp_cross(part):
    size = lax.axis_size("dp")
    if size != 8:
        return [], [dp_scatter_plain(part)]
    rows = part.shape[0] // size
    me = lax.axis_index("dp")

    def block(mask):
        return lax.dynamic_slice(part, ((me ^ mask) * rows, 0), (rows, part.shape[1]))

    return [block(mask) for mask in LINE], [swap(block(mask + 1), "dp", 1) for mask in LINE]


def dp_line(owns, arrivals):
    if not owns:
        return arrivals
    sums = []
    for mask, own, arrived in zip(LINE, owns, arrivals):
        pair = own.astype(F32) + arrived.astype(F32)
        sums.append(swap(pair.astype(BF16), "dp", mask) if mask else pair)
    return sums


def dp_total(sums):
    total = sums[-1].astype(F32)
    for value in sums[:-1]:
        total = total + value.astype(F32)
    return total


def dp_scatter_plain(part):
    return lax.psum_scatter(part, "dp", scatter_dimension=0, tiled=True)


def dp_sum(value):
    if lax.axis_size("dp") != 8:
        return lax.psum(value, "dp")
    for mask in (1, 2, 4):
        value = value + swap(value, "dp", mask)
    return value


def local(
    inputs,
    lengths,
    cotangent,
    w_qkv,
    w_out,
    w_up,
    w_down,
    vectors,
    bias_qkv,
    bias_up,
    mom_qkv,
    mom_out,
    mom_up,
    mom_down,
    mom_vectors,
    mom_bias_qkv,
    mom_bias_up,
):
    dp_size = lax.axis_size("dp")
    tensor_size = lax.axis_size("tensor")
    dp_index = lax.axis_index("dp")
    tok = inputs.shape[0]
    frames = tok * tensor_size
    tokens = frames * dp_size
    half = 2 * tok
    width = inputs.shape[1]
    own_rows = w_qkv.shape[0]
    head_width = w_qkv.shape[2]
    heads = head_width // HD
    padded = -(-head_width // LANES) * LANES
    extra = padded - head_width
    own_bias = bias_qkv.shape[0]

    w_parts = w_qkv.astype(BF16)
    small = jnp.concatenate(
        [
            vectors.astype(BF16),
            bias_up.astype(BF16)[:, None],
            jnp.pad(bias_qkv.astype(BF16), ((0, own_rows - own_bias), (0, 0))),
        ],
        axis=1,
    )
    small = jnp.pad(small, ((0, 0), (0, extra - small.shape[1])))
    packed = 3 * head_width + extra
    w_cols = jnp.concatenate(
        [
            w_parts[:, 0],
            small,
            w_parts[:, 1],
            w_parts[:, 2],
            jnp.pad(w_out.astype(BF16), ((0, 0), (0, extra))),
        ],
        axis=1,
    )
    first_slots = dp_send(w_cols, True)
    x_far = after(swap(inputs, "tensor", 2), *first_slots[2:7:4])
    x_rows = jnp.concatenate(
        [inputs, swap(inputs, "tensor", 1), x_far, swap(x_far, "tensor", 1)], axis=0
    )
    cot_far = after(swap(cotangent, "tensor", 2), *first_slots[4:5])
    cot_rows = jnp.concatenate(
        [cotangent, swap(cotangent, "tensor", 1), cot_far, swap(cot_far, "tensor", 1)], axis=0
    )
    first_slots[-1], x_rows, cot_rows = tie([first_slots[-1], x_rows, cot_rows])
    wq, wo, smalls = dp_place(
        first_slots, ((0, packed), (packed, packed + padded)), head_width
    )
    wd = lax.all_gather(w_down.astype(BF16), "dp", axis=0, tiled=True)
    wu = lax.all_gather(w_up.astype(BF16), "dp", axis=0, tiled=True)
    vec_rows = smalls[:8]
    bu = smalls[6:7]
    bq = smalls[7:9].reshape(2, dp_size, own_rows)[:, :, :own_bias].reshape(2, head_width)
    qkv_bias = jnp.concatenate(
        [bq[0:1], jnp.zeros((1, padded), F32), bq[1:2]], axis=1
    )

    me = lax.axis_index("tensor")
    place = jnp.concatenate([(me ^ s) * tok + jnp.arange(tok, dtype=jnp.int32) for s in range(4)])
    key_bias = jnp.where(place < lengths[0], 0.0, MASKED).astype(F32)[:, None]

    attn_in, qkv = qkv_call(x_rows, vec_rows, wq, qkv_bias, tok)
    att, lse, *sent = attn_call(
        heads, ("pieces",), qkv, key_bias, wo, tok, 3 * tok
    )
    att, lse, part_two = attn_call(
        heads, ("own",), qkv, key_bias, wo, tok, 2 * tok, (att, lse)
    )
    total = pair_pieces(part_two, swap_all(sent, "tensor", 1))
    far = swap(total, "tensor", 2)
    att, lse, mine, *sent = attn_call(
        heads,
        ("own", "pieces"),
        after(qkv, total),
        key_bias,
        wo,
        tok,
        0,
        (att, lse),
    )
    near = swap_all(sent, "tensor", 1)
    residual, mlp_in = row_call(
        residual_body, (inputs, mine, after(far, wd)), near, vec_rows, (F32, BF16), 0, "residual"
    )

    near = swap(mlp_in, "tensor", 1)
    far = swap(mlp_in, "tensor", 2)
    d_hidden = mm(after(cot_rows, mlp_in, wu), wd)
    hidden, d_pre, bu_sums, mine, *sent = mlp_call(
        ("own", "pieces"), [mlp_in, near], wu, bu, d_hidden, 0, frames
    )
    near_parts = swap_all(sent, "tensor", 1)
    far = after(far, mine)
    slots = [mlp_in, near, far, swap(far, "tensor", 1)]
    hidden, d_pre, sums, *sent = mlp_call(
        ("pieces",), slots[3:], wu, bu, d_hidden, 3 * tok, frames, (hidden, d_pre)
    )
    bu_sums = bu_sums + sums
    hidden, d_pre, sums, part_two = mlp_call(
        ("own",), slots[2:3], wu, bu, d_hidden, 2 * tok, frames, (hidden, d_pre)
    )
    bu_sums = bu_sums + sums
    total = pair_pieces(part_two, swap_all(sent, "tensor", 1))
    far = swap(total, "tensor", 2)
    hidden_later, d_pre_later = tie([hidden, d_pre], total)
    raw_wd = mm(cot_rows, hidden_later, TN).astype(BF16)
    raw_wu = mm(jnp.concatenate(slots, axis=0), after(d_pre_later, raw_wd), TN).astype(BF16)
    hidden = after(hidden, raw_wu)
    down_far = mm(hidden[half:], wd, NT).astype(BF16)
    down_mine = mm(hidden[:half], wd, NT).astype(BF16)
    near_parts = tie(near_parts, raw_wd, raw_wu, down_far, down_mine)
    grad_wd, grad_wu = dp_scatter_plain(raw_wd), dp_scatter_plain(raw_wu)
    d_residual, d_out, sums_two = row_call(
        second_back_body,
        (residual, mine, far, cotangent),
        near_parts,
        vec_rows,
        (F32, BF16),
        1,
        "second_back",
    )
    near = swap(d_out, "tensor", 1)
    far = swap(d_out, "tensor", 2)
    out_mine = jnp.concatenate([d_out, near], axis=0)
    carried = attn_back_call(
        heads, out_mine, wo, att, qkv, key_bias, lse, half, 0
    )
    far = after(far, carried[1])
    output_far = swap(after(pair_sum(down_far[:tok], down_far[tok:]), far), "tensor", 2)
    output_near = swap(down_mine[tok:], "tensor", 1)
    out_far = jnp.concatenate([far, swap(far, "tensor", 1)], axis=0)
    raw_wo = (mm(out_mine, att[:half], TN) + mm(out_far, att[half:], TN)).astype(BF16)
    out_later = after(out_far, raw_wo)
    d_qkv, bias_sums = attn_back_call(
        heads, out_later, wo, att, qkv, key_bias, lse, half, half, carried
    )
    d_qkv = after(d_qkv, output_far, output_near)
    first_far = mm(d_qkv[half:], wq, NT).astype(BF16)
    raw_wq = mm(attn_in, after(d_qkv, grad_wd, first_far), TN).astype(BF16)
    first_total = pair_sum(first_far[:tok], first_far[tok:])
    far = swap(first_total, "tensor", 2)
    d_qkv, raw_wq, raw_wo = tie([d_qkv, raw_wq, raw_wo])
    owns, crossed = dp_cross(jnp.concatenate([raw_wq, raw_wo], axis=1))
    first_mine = mm(after(d_qkv[:half], first_total, *crossed[:1]), wq, NT).astype(BF16)
    lined = dp_line(owns, tie(crossed, far))
    far = after(far, lined[-1])
    quarter = tok // PIECES
    sent = [first_mine[tok + k * quarter : tok + k * quarter + quarter] for k in range(PIECES)]
    near = swap_all(sent, "tensor", 1)
    output = (
        residual
        + (down_mine[:tok].astype(F32) + output_near.astype(F32) + output_far.astype(F32))
        + vec_rows[5]
    )
    input_grad, sums_one = row_call(
        first_back_body,
        (inputs, first_mine[:tok], far, d_residual),
        near,
        vec_rows,
        (F32,),
        1,
        "first_back",
    )

    vec_sums = tensor_sum(sums_one + sums_two)
    grad_wd = after(grad_wd, first_mine, lined[-1])
    mom_down_new, update_down = momentum(mom_down, grad_wd.astype(F32))
    early = polar_call(tensor_sum(gram_of(update_down)[None]))
    early = after(early, *lined[:2])
    new_w_down = applied(w_down, early[0], update_down, STEP_DOWN)
    grad_wu = after(after(grad_wu, first_mine, *crossed), *lined[:3])

    rows_of = jnp.concatenate(
        [
            vec_sums[:6],
            bu_sums[0:1],
            jnp.pad(bias_sums[:2], ((0, 0), (0, width - padded))),
        ],
        axis=0,
    )
    rows_of = dp_sum(after(rows_of, new_w_down))
    own_cols = lax.dynamic_slice(rows_of, (0, dp_index * own_rows), (7, own_rows))
    vec_grad = jnp.transpose(own_cols[:6])
    bu_grad = own_cols[6]
    bq_grad = jnp.transpose(
        lax.dynamic_slice(rows_of, (7, dp_index * own_bias), (2, own_bias))
    )

    mom_up_new, update_up = momentum(mom_up, grad_wu.astype(F32))
    gram_up = gram_of(update_up)
    lined = tie(lined, gram_up, new_w_down, vec_sums)
    grad_first = dp_total(lined)
    grad_wq, grad_wo = grad_first[:, :packed], grad_first[:, packed : packed + head_width]
    mom_out_new, update_out = momentum(mom_out, grad_wo)
    spots = (0, padded, padded + head_width)
    grad_parts = jnp.stack([grad_wq[:, spot : spot + head_width] for spot in spots], axis=1)
    mom_qkv_new, update_qkv = momentum(mom_qkv, grad_parts)
    flat = jnp.concatenate(
        [update_qkv[:, 0], jnp.zeros((own_rows, extra), F32), update_qkv[:, 1], update_qkv[:, 2]], axis=1
    )
    late = tensor_sum(jnp.stack([gram_of(update_out), gram_of(flat), gram_up]))
    late = polar_call(late)
    new_w_out = applied(w_out, late[0], update_out, STEP_OUT)
    new_w_up = applied(w_up, late[2], update_up, STEP_UP)
    polar_qkv = jnp.dot(late[1], flat, precision=HIGHEST)
    new_w_qkv = w_qkv - STEP_QKV * jnp.stack(
        [polar_qkv[:, spot : spot + head_width] for spot in spots], axis=1
    )

    vec_rate = VEC_RATE / math.sqrt(tokens)
    new_mom_vectors = VEC_DECAY * mom_vectors + vec_grad
    new_mom_bias_qkv = VEC_DECAY * mom_bias_qkv + bq_grad
    new_mom_bias_up = VEC_DECAY * mom_bias_up + bu_grad
    new_vectors = vectors - vec_rate * new_mom_vectors
    new_bias_qkv = bias_qkv - vec_rate * new_mom_bias_qkv
    new_bias_up = bias_up - vec_rate * new_mom_bias_up
    return (
        output,
        input_grad,
        new_w_qkv,
        new_w_out,
        new_w_up,
        new_w_down,
        new_vectors,
        new_bias_qkv,
        new_bias_up,
        mom_qkv_new,
        mom_out_new,
        mom_up_new,
        mom_down_new,
        new_mom_vectors,
        new_mom_bias_qkv,
        new_mom_bias_up,
    )


def solution(mesh):
    in_specs = (
        P(("dp", "tensor"), None),
        P("dp"),
        P(("dp", "tensor"), None),
        P("dp", None, "tensor"),
        P("dp", "tensor"),
        P("dp", "tensor"),
        P("dp", "tensor"),
        P("dp", None),
        P(("tensor", "dp"), None),
        P(("tensor", "dp")),
        P("dp", None, "tensor"),
        P("dp", "tensor"),
        P("dp", "tensor"),
        P("dp", "tensor"),
        P("dp", None),
        P(("tensor", "dp"), None),
        P(("tensor", "dp")),
    )
    out_specs = (
        P(("dp", "tensor"), None),
        P(("dp", "tensor"), None),
        P("dp", None, "tensor"),
        P("dp", "tensor"),
        P("dp", "tensor"),
        P("dp", "tensor"),
        P("dp", None),
        P(("tensor", "dp"), None),
        P(("tensor", "dp")),
        P("dp", None, "tensor"),
        P("dp", "tensor"),
        P("dp", "tensor"),
        P("dp", "tensor"),
        P("dp", None),
        P(("tensor", "dp"), None),
        P(("tensor", "dp")),
    )
    return jax.shard_map(local, mesh=mesh, in_specs=in_specs, out_specs=out_specs, check_vma=False)
```

```python
from functools import partial
import math

import jax
import jax.numpy as jnp
from jax import lax
from jax.experimental import pallas as pl
from jax.experimental.pallas import tpu as pltpu
from jax.sharding import PartitionSpec as P

HD = 80
SWEEPS = 5
LANES = 128
WINDOW = 256
BIAS_LANE = WINDOW - 1
VMEM_LIMIT = 58 * 1024 * 1024

HIGHEST = lax.Precision.HIGHEST
NORM_EPS = 1e-05
POLAR_EPS = 1e-07
MASKED = -1e30
QUINTIC_A = 3.4445
QUINTIC_B = -4.775
QUINTIC_C = 2.0315
MUON_DECAY = 0.95
VEC_DECAY = 0.9
VEC_RATE = 0.1
STEP_QKV = 0.5 * math.sqrt(3.0)
STEP_OUT = 2.0
STEP_UP = 1.0
STEP_DOWN = 0.5
LOG2E = math.log2(math.e)
SCORE_SCALE = 1.0 / math.sqrt(HD)
F32 = jnp.float32
BF16 = jnp.bfloat16
LITTLE = pl.CostEstimate(flops=1_000_000, bytes_accessed=100_000, transcendentals=0)
NN = (((1,), (0,)), ((), ()))
NT = (((1,), (1,)), ((), ()))
TN = (((0,), (0,)), ((), ()))


def mm(left, right, dims=NN):
    return lax.dot_general(left, right, dims, preferred_element_type=F32)


def norm_parts(values):
    center = values - jnp.mean(values, axis=-1, keepdims=True)
    spread = jnp.mean(center * center, axis=-1, keepdims=True)
    scale = lax.rsqrt(spread + NORM_EPS)
    return center * scale, scale


def norm_back(grad, gain, unit, scale):
    inner = grad * gain
    mean_grad = jnp.mean(inner, axis=-1, keepdims=True)
    mean_unit = jnp.mean(inner * unit, axis=-1, keepdims=True)
    return scale * (inner - mean_grad - unit * mean_unit)


def params(*semantics):
    return pltpu.CompilerParams(
        dimension_semantics=semantics or None, vmem_limit_bytes=VMEM_LIMIT
    )


def swap(value, axis, mask):
    size = lax.axis_size(axis)
    return lax.ppermute(value, axis, [(i, i ^ mask) for i in range(size)])


def tensor_slots(own):
    near = swap(own, "tensor", 1)
    far = swap(own, "tensor", 2)
    return [own, near, far, swap(far, "tensor", 1)]


def tensor_gather(own):
    return jnp.concatenate(tensor_slots(own), axis=0)


def tensor_sum(value):
    value = value + swap(value, "tensor", 1)
    return value + swap(value, "tensor", 2)


def pair_sum(own, sent):
    arrived = swap(sent, "tensor", 1)
    return (own.astype(F32) + arrived.astype(F32)).astype(BF16)


def after(value, *others):
    return lax.optimization_barrier((value, *others))[0]


def tie(values, *others):
    return list(lax.optimization_barrier((*values, *others))[: len(values)])


def qkv_body(x_ref, vec_ref, w_ref, bias_ref, attn_ref, qkv_ref):
    unit, _ = norm_parts(x_ref[...].astype(F32))
    attn_in = (unit * vec_ref[0:1, :] + vec_ref[1:2, :]).astype(BF16)
    attn_ref[...] = attn_in
    qkv_ref[...] = (mm(attn_in, w_ref[...]) + bias_ref[0:1, :]).astype(BF16)


def qkv_call(x_rows, vec_rows, weight, bias, block):
    rows, width = x_rows.shape
    columns = weight.shape[1]
    return pl.pallas_call(
        qkv_body,
        grid=(rows // block,),
        in_specs=[
            pl.BlockSpec((block, width), lambda i: (i, 0)),
            pl.BlockSpec(vec_rows.shape, lambda i: (0, 0)),
            pl.BlockSpec(weight.shape, lambda i: (0, 0)),
            pl.BlockSpec(bias.shape, lambda i: (0, 0)),
        ],
        out_specs=[
            pl.BlockSpec((block, width), lambda i: (i, 0)),
            pl.BlockSpec((block, columns), lambda i: (i, 0)),
        ],
        out_shape=[
            jax.ShapeDtypeStruct((rows, width), BF16),
            jax.ShapeDtypeStruct((rows, columns), BF16),
        ],
        compiler_params=params("arbitrary"),
        cost_estimate=LITTLE,
        name="norm_qkv",
    )(x_rows, vec_rows, weight, bias)


PIECES = 4


def part_shapes(emits, rows, width):
    shapes = []
    for kind in emits:
        count = PIECES if kind == "pieces" else 1
        shapes += [jax.ShapeDtypeStruct((rows // count, width), BF16)] * count
    return shapes, [pl.BlockSpec(shape.shape, lambda i: (0, 0)) for shape in shapes]


def part_store(emits, refs, value):
    spot = 0
    for index, kind in enumerate(emits):
        count = PIECES if kind == "pieces" else 1
        group = refs[spot : spot + count]
        spot += count

        @pl.when(pl.program_id(0) == index)
        def _():
            rows = value.shape[0] // count
            for piece, ref in enumerate(group):
                ref[...] = value[piece * rows : piece * rows + rows].astype(BF16)


def swap_all(values, axis, mask):
    return [swap(value, axis, mask) for value in values]


def pair_body(own_ref, *rest):
    pieces, out_ref = rest[:-1], rest[-1]
    rows = pieces[0].shape[0]
    for index, piece in enumerate(pieces):
        part = slice(index * rows, index * rows + rows)
        out_ref[part, :] = (own_ref[part, :].astype(F32) + piece[...].astype(F32)).astype(BF16)


def pair_pieces(own, pieces):
    return pl.pallas_call(
        pair_body,
        out_shape=jax.ShapeDtypeStruct(own.shape, BF16),
        compiler_params=params(),
        cost_estimate=LITTLE,
        name="pair_sum",
    )(own, *pieces)


def head_place(head):
    start = 0 if head * HD + HD <= BIAS_LANE else LANES
    return start, head * HD - start


def lane_mask(rows, head):
    _, offset = head_place(head)
    lane = lax.broadcasted_iota(jnp.int32, (rows, WINDOW), 1)
    return (lane >= offset) & (lane < offset + HD), lane == BIAS_LANE


def window(value, head):
    start, _ = head_place(head)
    return value[:, start : start + WINDOW].astype(F32)


def key_columns(qkv_ref):
    third = (qkv_ref.shape[1] + LANES) // 3
    return qkv_ref[:, third : 2 * third]


def value_columns(qkv_ref):
    third = (qkv_ref.shape[1] + LANES) // 3
    tail = qkv_ref[:, qkv_ref.shape[1] - third :].astype(F32)
    return pltpu.roll(tail, third - LANES // 2, 1)


def fill_keys(qkv_ref, bias_ref, keys_out, heads):
    columns = key_columns(qkv_ref)
    for head in range(heads):
        inside, last = lane_mask(columns.shape[0], head)
        picked = jnp.where(inside, window(columns, head), 0.0)
        keys_out[head] = jnp.where(last, bias_ref[...], picked).astype(BF16)


def join_windows(parts):
    low, high = None, None
    for head, part in enumerate(parts):
        if head_place(head)[0] == 0:
            low = part if low is None else low + part
        else:
            high = part if high is None else high + part
    return jnp.concatenate(
        [low[:, :LANES], low[:, LANES:] + high[:, :LANES], high[:, LANES:]], axis=1
    )


def attn_body(heads, emits, skip, q_ref, qkv_ref, bias_ref, wo_ref, *rest):
    (att_ref, lse_ref), parts, (keys, vals) = rest[skip : skip + 2], rest[skip + 2 : -2], rest[-2:]
    block = q_ref.shape[0]
    frames = qkv_ref.shape[0]

    @pl.when(pl.program_id(0) == 0)
    def _():
        fill_keys(qkv_ref, bias_ref, keys, heads)
        columns = value_columns(qkv_ref)
        for head in range(heads):
            inside, _ = lane_mask(frames, head)
            vals[head] = jnp.where(inside, window(columns, head), 0.0).astype(BF16)

    log_scale = SCORE_SCALE * LOG2E
    outs = []
    lane = lax.broadcasted_iota(jnp.int32, (block, LANES), 1)
    lse_cols = jnp.zeros((block, LANES), F32)
    for head in range(heads):
        _, last = lane_mask(block, head)
        query = jnp.where(last, 1.0, window(q_ref, head)).astype(BF16)
        scores = mm(query, keys[head], NT)
        row_max = jnp.max(scores, axis=1, keepdims=True)
        powers = jnp.exp2((scores - row_max) * log_scale)
        totals = jnp.sum(powers, axis=1, keepdims=True)
        outs.append(mm(powers.astype(BF16), vals[head]) * (1.0 / totals))
        lse_cols = jnp.where(lane == head, row_max * log_scale + jnp.log2(totals), lse_cols)
    attended = join_windows(outs).astype(BF16)
    att_ref[...] = attended
    lse_ref[...] = jnp.transpose(lse_cols)[:8]
    part_store(emits, parts, mm(attended, wo_ref[...], NT))


def attn_call(heads, emits, qkv, key_bias, wo, block, first, earlier=None):
    count = block * len(emits)
    frames = qkv.shape[0]
    part_width = wo.shape[1]
    width = wo.shape[0]
    held = [] if earlier is None else list(earlier)
    base = first // block
    shapes, specs = part_shapes(emits, block, width)
    return pl.pallas_call(
        partial(attn_body, heads, emits, len(held)),
        grid=(count // block,),
        in_specs=[
            pl.BlockSpec((block, part_width), lambda i: (i + base, 0)),
            pl.BlockSpec(qkv.shape, lambda i: (0, 0)),
            pl.BlockSpec(key_bias.shape, lambda i: (0, 0)),
            pl.BlockSpec(wo.shape, lambda i: (0, 0)),
        ]
        + [pl.BlockSpec(memory_space=pl.ANY)] * len(held),
        out_specs=[
            pl.BlockSpec((block, part_width), lambda i: (i + base, 0)),
            pl.BlockSpec((8, block), lambda i: (0, i + base)),
        ]
        + specs,
        out_shape=[
            jax.ShapeDtypeStruct((frames, part_width), BF16),
            jax.ShapeDtypeStruct((8, frames), F32),
        ]
        + shapes,
        scratch_shapes=[
            pltpu.VMEM((heads, frames, WINDOW), BF16),
            pltpu.VMEM((heads, frames, WINDOW), BF16),
        ],
        input_output_aliases={} if earlier is None else {4: 0, 5: 1},
        compiler_params=params("arbitrary"),
        cost_estimate=LITTLE,
        name="attn_fwd",
    )(qkv, qkv, key_bias, wo, *held)


def attn_back_body(heads, last_part, first, dout_ref, wo_ref, att_ref, q_ref, qkv_ref, bias_ref, lse_ref, *rest):
    if last_part:
        dkey_in, dval_in, sums_in, _, dqkv_ref, sums_ref, keys, vals, d_query, d_key, d_val, packed, sems = rest
    else:
        dqkv_ref, sums_ref, d_key, d_val, keys, vals, d_query, sems = rest
    step = pl.program_id(0)
    block, part_width = q_ref.shape
    count = d_query.shape[0]

    @pl.when(step == 0)
    def _():
        fill_keys(qkv_ref, bias_ref, keys, heads)
        vals[...] = value_columns(qkv_ref).astype(BF16)
        if last_part:
            d_key[...] = dkey_in[...]
            d_val[...] = dval_in[...]
            sums_ref[...] = sums_in[...]
        else:
            d_key[...] = jnp.zeros_like(d_key)
            d_val[...] = jnp.zeros_like(d_val)
            sums_ref[...] = jnp.zeros_like(sums_ref)

    log_scale = SCORE_SCALE * LOG2E
    d_att = mm(dout_ref[...], wo_ref[...]).astype(BF16)
    inner_cols = jnp.transpose(d_att.astype(F32) * att_ref[...].astype(F32))
    outs = []
    for head in range(heads):
        start, _ = head_place(head)
        inside, last = lane_mask(block, head)
        q_window = window(q_ref, head)
        query = jnp.where(last, 1.0, q_window).astype(BF16)
        q_only = jnp.where(inside, q_window, 0.0).astype(BF16)
        d_only = jnp.where(inside, window(d_att, head), 0.0).astype(BF16)
        inner = jnp.sum(inner_cols[head * HD : head * HD + HD], axis=0, keepdims=True)
        scores = mm(keys[head], query, NT)
        probs = jnp.exp2(scores * log_scale - lse_ref[head : head + 1, :])
        d_probs = mm(vals[:, start : start + WINDOW], d_only, NT)
        d_scores = (probs * (d_probs - inner)).astype(BF16)
        d_val[:, start : start + WINDOW] += mm(probs.astype(BF16), d_only)
        d_key[:, start : start + WINDOW] += mm(d_scores, q_only)
        outs.append(mm(d_scores, keys[head], TN))
    low = (join_windows(outs) * SCORE_SCALE).astype(BF16)
    d_query[pl.ds(pl.multiple_of(step * block, block), block), :] = low
    sums_ref[0:1, :] += jnp.sum(low.astype(F32), axis=0, keepdims=True)

    @pl.when(step == pl.num_programs(0) - 1)
    def _():
        copies = [
            pltpu.make_async_copy(
                d_query, dqkv_ref.at[pl.ds(first, count), pl.ds(0, part_width)], sems.at[0]
            )
        ]
        copies[0].start()
        if last_part:
            key_low = d_key[...] * SCORE_SCALE
            value_low = d_val[...]
            sums_ref[1:2, :] = jnp.sum(value_low.astype(BF16).astype(F32), axis=0, keepdims=True)
            value_low = pltpu.roll(value_low, LANES // 2, 1)
            whole = part_width - LANES
            packed[:, :whole] = key_low[:, :whole].astype(BF16)
            packed[:, whole:part_width] = (key_low[:, whole:] + value_low[:, :LANES]).astype(BF16)
            packed[:, part_width:] = value_low[:, LANES:].astype(BF16)
            copies.append(
                pltpu.make_async_copy(
                    packed,
                    dqkv_ref.at[pl.ds(0, packed.shape[0]), pl.ds(part_width, packed.shape[1])],
                    sems.at[1],
                )
            )
            copies[1].start()
        for copy in copies:
            copy.wait()


def attn_back_call(heads, d_out, wo, attended, qkv, key_bias, lse, block, first, earlier=None):
    count, width = d_out.shape
    frames = qkv.shape[0]
    part_width = wo.shape[1]
    base = first // block
    last_part = earlier is not None
    whole = pl.BlockSpec((frames, part_width), lambda i: (0, 0))
    sums_spec = pl.BlockSpec((8, part_width), lambda i: (0, 0))
    anywhere = pl.BlockSpec(memory_space=pl.ANY)
    out_shape = [
        jax.ShapeDtypeStruct(qkv.shape, BF16),
        jax.ShapeDtypeStruct((8, part_width), F32),
    ]
    out_specs = [anywhere, sums_spec]
    scratch = [
        pltpu.VMEM((heads, frames, WINDOW), BF16),
        pltpu.VMEM((frames, part_width), BF16),
        pltpu.VMEM((count, part_width), BF16),
    ]
    held = []
    if last_part:
        d_qkv, sums, d_key, d_val = earlier
        held = [d_key, d_val, sums, d_qkv]
        scratch += [pltpu.VMEM((frames, part_width), F32)] * 2
        scratch += [pltpu.VMEM((frames, qkv.shape[1] - part_width), BF16)]
    else:
        out_shape += [jax.ShapeDtypeStruct((frames, part_width), F32)] * 2
        out_specs += [whole, whole]
    return pl.pallas_call(
        partial(attn_back_body, heads, last_part, first),
        grid=(count // block,),
        in_specs=[
            pl.BlockSpec((block, width), lambda i: (i, 0)),
            pl.BlockSpec(wo.shape, lambda i: (0, 0)),
            pl.BlockSpec((block, part_width), lambda i: (i + base, 0)),
            pl.BlockSpec((block, part_width), lambda i: (i + base, 0)),
            pl.BlockSpec(qkv.shape, lambda i: (0, 0)),
            pl.BlockSpec(key_bias.shape, lambda i: (0, 0)),
            pl.BlockSpec((8, block), lambda i: (0, i + base)),
        ]
        + [whole, whole, sums_spec, anywhere][: len(held)],
        out_specs=out_specs,
        out_shape=out_shape,
        scratch_shapes=scratch + [pltpu.SemaphoreType.DMA((2,))],
        input_output_aliases={10: 0} if last_part else {},
        compiler_params=params("arbitrary"),
        cost_estimate=LITTLE,
        name="attn_bwd",
    )(d_out, wo, attended, qkv, qkv, key_bias, lse, *held)


def gelu_parts(values):
    size = jnp.abs(values)
    bell = jnp.exp2(values * values * (-0.5 * LOG2E))
    inv = 1.0 / (1.0 + (0.3275911 * math.sqrt(0.5)) * size)
    tail = inv * (
        0.5 * 0.254829592
        + inv
        * (
            0.5 * -0.284496736
            + inv * (0.5 * 1.421413741 + inv * (0.5 * -1.453152027 + inv * (0.5 * 1.061405429)))
        )
    )
    tail = tail * bell
    share = jnp.where(values < 0.0, tail, 1.0 - tail)
    return share, share + values * bell * (1.0 / math.sqrt(2.0 * math.pi))


def mlp_body(chunk, emits, skip, *refs):
    slot_refs, (w_ref, bias_ref, dhid_ref) = refs[: len(emits)], refs[len(emits) : len(emits) + 3]
    outs = refs[len(emits) + 3 + skip :]
    hid_ref, dpre_ref, sums_ref, parts, in_ref = *outs[:3], outs[3:-1], outs[-1]
    for index, slot_ref in enumerate(slot_refs):

        @pl.when(pl.program_id(0) == index)
        def _():
            in_ref[...] = slot_ref[...]

    @pl.when(pl.program_id(0) == 0)
    def _():
        sums_ref[...] = jnp.zeros_like(sums_ref)

    for start in range(0, w_ref.shape[1], chunk):
        cols = slice(start, start + chunk)
        pre = mm(in_ref[...], w_ref[:, cols]) + bias_ref[0:1, cols]
        share, slope = gelu_parts(pre)
        hid_ref[:, cols] = (pre * share).astype(BF16)
        d_pre = (dhid_ref[:, cols] * slope).astype(BF16)
        dpre_ref[:, cols] = d_pre
        sums_ref[0:1, cols] += jnp.sum(d_pre.astype(F32), axis=0, keepdims=True)
    part_store(emits, parts, mm(dpre_ref[...], w_ref[...], NT))


def mlp_call(emits, slots, weight, bias, d_hidden, first, frames, earlier=None):
    block, width = slots[0].shape
    count = block * len(slots)
    hidden_width = weight.shape[1]
    held = [] if earlier is None else list(earlier)
    base = first // block
    shapes, specs = part_shapes(emits, block, width)
    return pl.pallas_call(
        partial(mlp_body, min(256, hidden_width), emits, len(held)),
        grid=(count // block,),
        in_specs=[pl.BlockSpec((block, width), lambda i: (0, 0))] * len(slots)
        + [
            pl.BlockSpec(weight.shape, lambda i: (0, 0)),
            pl.BlockSpec(bias.shape, lambda i: (0, 0)),
            pl.BlockSpec((block, hidden_width), lambda i: (i + base, 0)),
        ]
        + [pl.BlockSpec(memory_space=pl.ANY)] * len(held),
        out_specs=[
            pl.BlockSpec((block, hidden_width), lambda i: (i + base, 0)),
            pl.BlockSpec((block, hidden_width), lambda i: (i + base, 0)),
            pl.BlockSpec((8, hidden_width), lambda i: (0, 0)),
        ]
        + specs,
        out_shape=[
            jax.ShapeDtypeStruct((frames, hidden_width), BF16),
            jax.ShapeDtypeStruct((frames, hidden_width), BF16),
            jax.ShapeDtypeStruct((8, hidden_width), F32),
        ]
        + shapes,
        scratch_shapes=[pltpu.VMEM((block, width), BF16)],
        input_output_aliases=(
            {} if earlier is None else {len(slots) + 3: 0, len(slots) + 4: 1}
        ),
        compiler_params=params("arbitrary"),
        cost_estimate=LITTLE,
        name="mlp_up",
    )(*slots, weight, bias, d_hidden, *held)


def residual_body(x_ref, mine_ref, far_ref, near_ref, vec_ref, res_ref, in_ref):
    total = mine_ref[...].astype(F32) + near_ref[...].astype(F32) + far_ref[...].astype(F32)
    residual = x_ref[...].astype(F32) + total + vec_ref[2:3, :]
    res_ref[...] = residual
    unit, _ = norm_parts(residual)
    in_ref[...] = (unit * vec_ref[3:4, :] + vec_ref[4:5, :]).astype(BF16)


def second_back_body(
    res_ref, mine_ref, far_ref, cot_ref, near_ref, vec_ref, dres_ref, low_ref, sums_ref
):
    @pl.when(pl.program_id(0) == 0)
    def _():
        sums_ref[...] = jnp.zeros_like(sums_ref)

    grad = mine_ref[...].astype(F32) + near_ref[...].astype(F32) + far_ref[...].astype(F32)
    unit, scale = norm_parts(res_ref[...])
    cot = cot_ref[...].astype(F32)
    d_res = norm_back(grad, vec_ref[3:4, :], unit, scale) + cot
    dres_ref[...] = d_res
    low_ref[...] = d_res.astype(BF16)
    sums_ref[2:3, :] += jnp.sum(d_res, axis=0, keepdims=True)
    sums_ref[3:4, :] += jnp.sum(grad * unit, axis=0, keepdims=True)
    sums_ref[4:5, :] += jnp.sum(grad, axis=0, keepdims=True)
    sums_ref[5:6, :] += jnp.sum(cot, axis=0, keepdims=True)


def first_back_body(x_ref, mine_ref, far_ref, dres_ref, near_ref, vec_ref, out_ref, sums_ref):
    @pl.when(pl.program_id(0) == 0)
    def _():
        sums_ref[...] = jnp.zeros_like(sums_ref)

    grad = mine_ref[...].astype(F32) + near_ref[...].astype(F32) + far_ref[...].astype(F32)
    unit, scale = norm_parts(x_ref[...].astype(F32))
    out_ref[...] = norm_back(grad, vec_ref[0:1, :], unit, scale) + dres_ref[...]
    sums_ref[0:1, :] += jnp.sum(grad * unit, axis=0, keepdims=True)
    sums_ref[1:2, :] += jnp.sum(grad, axis=0, keepdims=True)


def row_body(body, count, *refs):
    row_refs, pieces, vec_ref = refs[:count], refs[count : count + PIECES], refs[count + PIECES]
    near_ref = refs[-1]
    for index, piece in enumerate(pieces):

        @pl.when(pl.program_id(0) == index)
        def _():
            near_ref[...] = piece[...]

    body(*row_refs, near_ref, vec_ref, *refs[count + PIECES + 1 : -1])


def row_call(body, rows_in, near, vec_rows, out_types, with_sums, name):
    rows, width = rows_in[0].shape
    block = rows // PIECES
    row_spec = pl.BlockSpec((block, width), lambda i: (i, 0))
    whole = pl.BlockSpec((8, width), lambda i: (0, 0))
    return pl.pallas_call(
        partial(row_body, body, len(rows_in)),
        grid=(PIECES,),
        in_specs=[row_spec] * len(rows_in)
        + [pl.BlockSpec((block, width), lambda i: (0, 0))] * PIECES
        + [whole],
        out_specs=[row_spec] * len(out_types) + [whole] * with_sums,
        out_shape=[jax.ShapeDtypeStruct((rows, width), kind) for kind in out_types]
        + [jax.ShapeDtypeStruct((8, width), F32)] * with_sums,
        scratch_shapes=[pltpu.VMEM((block, width), BF16)],
        compiler_params=params("arbitrary"),
        cost_estimate=LITTLE,
        name=name,
    )(*rows_in, *near, vec_rows)


def polar_factors(grams, eye):
    def high(left, right):
        return jnp.dot(left, right, precision=HIGHEST, preferred_element_type=F32)

    scales = [1.0 / (jnp.sqrt(jnp.sum(gram * eye, keepdims=True)) + POLAR_EPS) for gram in grams]
    grams = [gram * scale * scale for gram, scale in zip(grams, scales)]
    factors = None
    for sweep in range(SWEEPS):
        squares = [high(gram, gram) for gram in grams]
        steps = [
            QUINTIC_A * eye + QUINTIC_B * gram + QUINTIC_C * square
            for gram, square in zip(grams, squares)
        ]
        if sweep < SWEEPS - 1:
            halves = [high(step, gram) for step, gram in zip(steps, grams)]
        if factors is None:
            factors = steps
        else:
            factors = [high(step, factor) for step, factor in zip(steps, factors)]
        if sweep < SWEEPS - 1:
            grams = [high(step, part) for step, part in zip(steps, halves)]
    return [factor * scale for factor, scale in zip(factors, scales)]


def polar_body(gram_ref, out_ref):
    count, rows, _ = gram_ref.shape
    row = lax.broadcasted_iota(jnp.int32, (rows, rows), 0)
    col = lax.broadcasted_iota(jnp.int32, (rows, rows), 1)
    eye = jnp.where(row == col, 1.0, 0.0)
    for index, factor in enumerate(polar_factors([gram_ref[i] for i in range(count)], eye)):
        out_ref[index] = factor


def polar_call(grams):
    count, rows, _ = grams.shape
    if rows % 32:
        return jnp.stack(polar_factors([grams[i] for i in range(count)], jnp.eye(rows, dtype=F32)))
    return pl.pallas_call(
        polar_body,
        out_shape=jax.ShapeDtypeStruct(grams.shape, F32),
        compiler_params=params(),
        name="polar",
    )(grams)


def gram_of(update):
    return lax.dot_general(update, update, NT, precision=HIGHEST, preferred_element_type=F32)


def momentum(moment, gradient):
    moved = MUON_DECAY * moment + gradient
    return moved, gradient + MUON_DECAY * moved


def applied(weight, factor, update, rate):
    return weight - rate * jnp.dot(factor, update, precision=HIGHEST)


def place_body(splits, narrow, me_ref, *refs):
    slots, outs = refs[:8], refs[8:]
    rows = slots[0].shape[0]
    for mask, slot in enumerate(slots):
        start = pl.multiple_of((me_ref[0] ^ mask) * rows, rows)
        for (low, high), out in zip(splits, outs):
            out[pl.ds(start, rows), :] = slot[:, low:high]
    if narrow is not None:
        tile = narrow // LANES * LANES
        turned = jnp.transpose(outs[0][:, tile : tile + LANES].astype(F32))
        outs[-1][...] = turned[narrow - tile : narrow - tile + 16]


def place_rows(slots, splits, narrow):
    rows = slots[0].shape[0]
    shapes = [jax.ShapeDtypeStruct((8 * rows, high - low), slots[0].dtype) for low, high in splits]
    if narrow is not None:
        shapes.append(jax.ShapeDtypeStruct((16, 8 * rows), F32))
    return pl.pallas_call(
        partial(place_body, splits, narrow),
        in_specs=[pl.BlockSpec(memory_space=pltpu.SMEM)]
        + [pl.BlockSpec(memory_space=pltpu.VMEM)] * 8,
        out_specs=[pl.BlockSpec(memory_space=pltpu.VMEM)] * len(shapes),
        out_shape=shapes,
        compiler_params=params(),
        cost_estimate=LITTLE,
        name="place_rows",
    )(lax.axis_index("dp").astype(jnp.int32)[None], *slots)


def dp_slots(own, ordered=False):
    line = {mask: swap(own, "dp", mask) for mask in (6, 2, 4)}
    slots = [own, swap(own, "dp", 1)] + [None] * 6
    for mask in (6, 2, 4):
        arrived = line[mask]
        if ordered:
            held = [slots[1]] if mask == 2 else [slots[3], slots[7]] if mask == 4 else []
            arrived = after(arrived, *held)
        slots[mask] = arrived
        slots[mask + 1] = swap(arrived, "dp", 1)
    return slots


def dp_send(own, ordered=False):
    if lax.axis_size("dp") != 8:
        return [lax.all_gather(own, "dp", axis=0, tiled=True)]
    return dp_slots(own, ordered)


def dp_place(slots, splits, narrow=None):
    if len(slots) > 1:
        return place_rows(slots, splits, narrow)
    parts = [slots[0][:, low:high] for low, high in splits]
    if narrow is not None:
        parts.append(jnp.transpose(slots[0][:, narrow : narrow + 16].astype(F32)))
    return parts


LINE = (4, 6, 2, 0)


def dp_cross(part):
    size = lax.axis_size("dp")
    if size != 8:
        return [], [dp_scatter_plain(part)]
    rows = part.shape[0] // size
    me = lax.axis_index("dp")

    def block(mask):
        return lax.dynamic_slice(part, ((me ^ mask) * rows, 0), (rows, part.shape[1]))

    return [block(mask) for mask in LINE], [swap(block(mask + 1), "dp", 1) for mask in LINE]


def dp_line(owns, arrivals):
    if not owns:
        return arrivals
    sums = []
    for mask, own, arrived in zip(LINE, owns, arrivals):
        pair = own.astype(F32) + arrived.astype(F32)
        sums.append(swap(pair.astype(BF16), "dp", mask) if mask else pair)
    return sums


def dp_total(sums):
    total = sums[-1].astype(F32)
    for value in sums[:-1]:
        total = total + value.astype(F32)
    return total


def dp_scatter_plain(part):
    return lax.psum_scatter(part, "dp", scatter_dimension=0, tiled=True)


def dp_sum(value):
    if lax.axis_size("dp") != 8:
        return lax.psum(value, "dp")
    for mask in (1, 2, 4):
        value = value + swap(value, "dp", mask)
    return value


def local(
    inputs,
    lengths,
    cotangent,
    w_qkv,
    w_out,
    w_up,
    w_down,
    vectors,
    bias_qkv,
    bias_up,
    mom_qkv,
    mom_out,
    mom_up,
    mom_down,
    mom_vectors,
    mom_bias_qkv,
    mom_bias_up,
):
    dp_size = lax.axis_size("dp")
    tensor_size = lax.axis_size("tensor")
    dp_index = lax.axis_index("dp")
    tok = inputs.shape[0]
    frames = tok * tensor_size
    tokens = frames * dp_size
    half = 2 * tok
    width = inputs.shape[1]
    own_rows = w_qkv.shape[0]
    head_width = w_qkv.shape[2]
    heads = head_width // HD
    padded = -(-head_width // LANES) * LANES
    extra = padded - head_width
    own_bias = bias_qkv.shape[0]

    w_parts = w_qkv.astype(BF16)
    small = jnp.concatenate(
        [
            vectors.astype(BF16),
            bias_up.astype(BF16)[:, None],
            jnp.pad(bias_qkv.astype(BF16), ((0, own_rows - own_bias), (0, 0))),
        ],
        axis=1,
    )
    small = jnp.pad(small, ((0, 0), (0, extra - small.shape[1])))
    packed = 3 * head_width + extra
    w_cols = jnp.concatenate(
        [
            w_parts[:, 0],
            small,
            w_parts[:, 1],
            w_parts[:, 2],
            jnp.pad(w_out.astype(BF16), ((0, 0), (0, extra))),
        ],
        axis=1,
    )
    first_slots = dp_send(w_cols, True)
    x_far = after(swap(inputs, "tensor", 2), *first_slots[2:7:4])
    x_rows = jnp.concatenate(
        [inputs, swap(inputs, "tensor", 1), x_far, swap(x_far, "tensor", 1)], axis=0
    )
    cot_far = after(swap(cotangent, "tensor", 2), *first_slots[4:5])
    cot_rows = jnp.concatenate(
        [cotangent, swap(cotangent, "tensor", 1), cot_far, swap(cot_far, "tensor", 1)], axis=0
    )
    first_slots[-1], x_rows, cot_rows = tie([first_slots[-1], x_rows, cot_rows])
    wq, wo, smalls = dp_place(
        first_slots, ((0, packed), (packed, packed + padded)), head_width
    )
    wd = lax.all_gather(w_down.astype(BF16), "dp", axis=0, tiled=True)
    wu = lax.all_gather(w_up.astype(BF16), "dp", axis=0, tiled=True)
    vec_rows = smalls[:8]
    bu = smalls[6:7]
    bq = smalls[7:9].reshape(2, dp_size, own_rows)[:, :, :own_bias].reshape(2, head_width)
    qkv_bias = jnp.concatenate(
        [bq[0:1], jnp.zeros((1, padded), F32), bq[1:2]], axis=1
    )

    me = lax.axis_index("tensor")
    place = jnp.concatenate([(me ^ s) * tok + jnp.arange(tok, dtype=jnp.int32) for s in range(4)])
    key_bias = jnp.where(place < lengths[0], 0.0, MASKED).astype(F32)[:, None]

    attn_in, qkv = qkv_call(x_rows, vec_rows, wq, qkv_bias, tok)
    att, lse, *sent = attn_call(
        heads, ("pieces",), qkv, key_bias, wo, tok, 3 * tok
    )
    att, lse, part_two = attn_call(
        heads, ("own",), qkv, key_bias, wo, tok, 2 * tok, (att, lse)
    )
    total = pair_pieces(part_two, swap_all(sent, "tensor", 1))
    far = swap(total, "tensor", 2)
    att, lse, mine, *sent = attn_call(
        heads,
        ("own", "pieces"),
        after(qkv, total),
        key_bias,
        wo,
        tok,
        0,
        (att, lse),
    )
    near = swap_all(sent, "tensor", 1)
    residual, mlp_in = row_call(
        residual_body, (inputs, mine, after(far, wd)), near, vec_rows, (F32, BF16), 0, "residual"
    )

    near = swap(mlp_in, "tensor", 1)
    far = swap(mlp_in, "tensor", 2)
    d_hidden = mm(after(cot_rows, mlp_in, wu), wd)
    hidden, d_pre, bu_sums, mine, *sent = mlp_call(
        ("own", "pieces"), [mlp_in, near], wu, bu, d_hidden, 0, frames
    )
    near_parts = swap_all(sent, "tensor", 1)
    far = after(far, mine)
    slots = [mlp_in, near, far, swap(far, "tensor", 1)]
    hidden, d_pre, sums, *sent = mlp_call(
        ("pieces",), slots[3:], wu, bu, d_hidden, 3 * tok, frames, (hidden, d_pre)
    )
    bu_sums = bu_sums + sums
    hidden, d_pre, sums, part_two = mlp_call(
        ("own",), slots[2:3], wu, bu, d_hidden, 2 * tok, frames, (hidden, d_pre)
    )
    bu_sums = bu_sums + sums
    total = pair_pieces(part_two, swap_all(sent, "tensor", 1))
    far = swap(total, "tensor", 2)
    hidden_later, d_pre_later = tie([hidden, d_pre], total)
    raw_wd = mm(cot_rows, hidden_later, TN).astype(BF16)
    raw_wu = mm(jnp.concatenate(slots, axis=0), after(d_pre_later, raw_wd), TN).astype(BF16)
    hidden = after(hidden, raw_wu)
    down_far = mm(hidden[half:], wd, NT).astype(BF16)
    down_mine = mm(hidden[:half], wd, NT).astype(BF16)
    near_parts = tie(near_parts, raw_wd, raw_wu, down_far, down_mine)
    grad_wd, grad_wu = dp_scatter_plain(raw_wd), dp_scatter_plain(raw_wu)
    d_residual, d_out, sums_two = row_call(
        second_back_body,
        (residual, mine, far, cotangent),
        near_parts,
        vec_rows,
        (F32, BF16),
        1,
        "second_back",
    )
    near = swap(d_out, "tensor", 1)
    far = swap(d_out, "tensor", 2)
    out_mine = jnp.concatenate([d_out, near], axis=0)
    carried = attn_back_call(
        heads, out_mine, wo, att, qkv, key_bias, lse, half, 0
    )
    far = after(far, carried[1])
    output_far = swap(after(pair_sum(down_far[:tok], down_far[tok:]), far), "tensor", 2)
    output_near = swap(down_mine[tok:], "tensor", 1)
    out_far = jnp.concatenate([far, swap(far, "tensor", 1)], axis=0)
    raw_wo = (mm(out_mine, att[:half], TN) + mm(out_far, att[half:], TN)).astype(BF16)
    out_later = after(out_far, raw_wo)
    d_qkv, bias_sums = attn_back_call(
        heads, out_later, wo, att, qkv, key_bias, lse, half, half, carried
    )
    d_qkv = after(d_qkv, output_far, output_near)
    first_far = mm(d_qkv[half:], wq, NT).astype(BF16)
    raw_wq = mm(attn_in, after(d_qkv, grad_wd, first_far), TN).astype(BF16)
    first_total = pair_sum(first_far[:tok], first_far[tok:])
    far = swap(first_total, "tensor", 2)
    d_qkv, raw_wq, raw_wo = tie([d_qkv, raw_wq, raw_wo])
    owns, crossed = dp_cross(jnp.concatenate([raw_wq, raw_wo], axis=1))
    first_mine = mm(after(d_qkv[:half], first_total, *crossed[:1]), wq, NT).astype(BF16)
    lined = dp_line(owns, tie(crossed, far))
    far = after(far, lined[-1])
    quarter = tok // PIECES
    sent = [first_mine[tok + k * quarter : tok + k * quarter + quarter] for k in range(PIECES)]
    near = swap_all(sent, "tensor", 1)
    output = (
        residual
        + (down_mine[:tok].astype(F32) + output_near.astype(F32) + output_far.astype(F32))
        + vec_rows[5]
    )
    input_grad, sums_one = row_call(
        first_back_body,
        (inputs, first_mine[:tok], far, d_residual),
        near,
        vec_rows,
        (F32,),
        1,
        "first_back",
    )

    vec_sums = tensor_sum(sums_one + sums_two)
    grad_wd = after(grad_wd, first_mine, lined[-1])
    mom_down_new, update_down = momentum(mom_down, grad_wd.astype(F32))
    early = polar_call(tensor_sum(gram_of(update_down)[None]))
    early = after(early, *lined[:2])
    new_w_down = applied(w_down, early[0], update_down, STEP_DOWN)
    grad_wu = after(after(grad_wu, first_mine, *crossed), *lined[:3])

    mom_up_new, update_up = momentum(mom_up, grad_wu.astype(F32))
    gram_up = gram_of(update_up)
    lined = tie(lined, gram_up, new_w_down, vec_sums)
    grad_first = dp_total(lined)
    grad_wq, grad_wo = grad_first[:, :packed], grad_first[:, packed : packed + head_width]
    mom_out_new, update_out = momentum(mom_out, grad_wo)
    spots = (0, padded, padded + head_width)
    grad_parts = jnp.stack([grad_wq[:, spot : spot + head_width] for spot in spots], axis=1)
    mom_qkv_new, update_qkv = momentum(mom_qkv, grad_parts)
    flat = jnp.concatenate(
        [update_qkv[:, 0], jnp.zeros((own_rows, extra), F32), update_qkv[:, 1], update_qkv[:, 2]], axis=1
    )
    late = tensor_sum(jnp.stack([gram_of(update_out), gram_of(flat), gram_up]))
    rows_of = jnp.concatenate(
        [
            vec_sums[:6],
            bu_sums[0:1],
            jnp.pad(bias_sums[:2], ((0, 0), (0, width - padded))),
        ],
        axis=0,
    )
    rows_of = dp_sum(after(rows_of, late))
    own_cols = lax.dynamic_slice(rows_of, (0, dp_index * own_rows), (7, own_rows))
    vec_grad = jnp.transpose(own_cols[:6])
    bu_grad = own_cols[6]
    bq_grad = jnp.transpose(
        lax.dynamic_slice(rows_of, (7, dp_index * own_bias), (2, own_bias))
    )

    late = polar_call(late)
    new_w_out = applied(w_out, late[0], update_out, STEP_OUT)
    new_w_up = applied(w_up, late[2], update_up, STEP_UP)
    polar_qkv = jnp.dot(late[1], flat, precision=HIGHEST)
    new_w_qkv = w_qkv - STEP_QKV * jnp.stack(
        [polar_qkv[:, spot : spot + head_width] for spot in spots], axis=1
    )

    vec_rate = VEC_RATE / math.sqrt(tokens)
    new_mom_vectors = VEC_DECAY * mom_vectors + vec_grad
    new_mom_bias_qkv = VEC_DECAY * mom_bias_qkv + bq_grad
    new_mom_bias_up = VEC_DECAY * mom_bias_up + bu_grad
    new_vectors = vectors - vec_rate * new_mom_vectors
    new_bias_qkv = bias_qkv - vec_rate * new_mom_bias_qkv
    new_bias_up = bias_up - vec_rate * new_mom_bias_up
    return (
        output,
        input_grad,
        new_w_qkv,
        new_w_out,
        new_w_up,
        new_w_down,
        new_vectors,
        new_bias_qkv,
        new_bias_up,
        mom_qkv_new,
        mom_out_new,
        mom_up_new,
        mom_down_new,
        new_mom_vectors,
        new_mom_bias_qkv,
        new_mom_bias_up,
    )


def solution(mesh):
    in_specs = (
        P(("dp", "tensor"), None),
        P("dp"),
        P(("dp", "tensor"), None),
        P("dp", None, "tensor"),
        P("dp", "tensor"),
        P("dp", "tensor"),
        P("dp", "tensor"),
        P("dp", None),
        P(("tensor", "dp"), None),
        P(("tensor", "dp")),
        P("dp", None, "tensor"),
        P("dp", "tensor"),
        P("dp", "tensor"),
        P("dp", "tensor"),
        P("dp", None),
        P(("tensor", "dp"), None),
        P(("tensor", "dp")),
    )
    out_specs = (
        P(("dp", "tensor"), None),
        P(("dp", "tensor"), None),
        P("dp", None, "tensor"),
        P("dp", "tensor"),
        P("dp", "tensor"),
        P("dp", "tensor"),
        P("dp", None),
        P(("tensor", "dp"), None),
        P(("tensor", "dp")),
        P("dp", None, "tensor"),
        P("dp", "tensor"),
        P("dp", "tensor"),
        P("dp", "tensor"),
        P("dp", None),
        P(("tensor", "dp"), None),
        P(("tensor", "dp")),
    )
    return jax.shard_map(local, mesh=mesh, in_specs=in_specs, out_specs=out_specs, check_vma=False)
```

```python
from functools import partial
import math

import jax
import jax.numpy as jnp
from jax import lax
from jax.experimental import pallas as pl
from jax.experimental.pallas import tpu as pltpu
from jax.sharding import PartitionSpec as P

HD = 80
SWEEPS = 5
LANES = 128
WINDOW = 256
BIAS_LANE = WINDOW - 1
VMEM_LIMIT = 58 * 1024 * 1024

HIGHEST = lax.Precision.HIGHEST
NORM_EPS = 1e-05
POLAR_EPS = 1e-07
MASKED = -1e30
QUINTIC_A = 3.4445
QUINTIC_B = -4.775
QUINTIC_C = 2.0315
MUON_DECAY = 0.95
VEC_DECAY = 0.9
VEC_RATE = 0.1
STEP_QKV = 0.5 * math.sqrt(3.0)
STEP_OUT = 2.0
STEP_UP = 1.0
STEP_DOWN = 0.5
LOG2E = math.log2(math.e)
SCORE_SCALE = 1.0 / math.sqrt(HD)
F32 = jnp.float32
BF16 = jnp.bfloat16
LITTLE = pl.CostEstimate(flops=1_000_000, bytes_accessed=100_000, transcendentals=0)
NN = (((1,), (0,)), ((), ()))
NT = (((1,), (1,)), ((), ()))
TN = (((0,), (0,)), ((), ()))


def mm(left, right, dims=NN):
    return lax.dot_general(left, right, dims, preferred_element_type=F32)


def norm_parts(values):
    center = values - jnp.mean(values, axis=-1, keepdims=True)
    spread = jnp.mean(center * center, axis=-1, keepdims=True)
    scale = lax.rsqrt(spread + NORM_EPS)
    return center * scale, scale


def norm_back(grad, gain, unit, scale):
    inner = grad * gain
    mean_grad = jnp.mean(inner, axis=-1, keepdims=True)
    mean_unit = jnp.mean(inner * unit, axis=-1, keepdims=True)
    return scale * (inner - mean_grad - unit * mean_unit)


def params(*semantics):
    return pltpu.CompilerParams(
        dimension_semantics=semantics or None, vmem_limit_bytes=VMEM_LIMIT
    )


def swap(value, axis, mask):
    size = lax.axis_size(axis)
    return lax.ppermute(value, axis, [(i, i ^ mask) for i in range(size)])


def tensor_slots(own):
    near = swap(own, "tensor", 1)
    far = swap(own, "tensor", 2)
    return [own, near, far, swap(far, "tensor", 1)]


def tensor_gather(own):
    return jnp.concatenate(tensor_slots(own), axis=0)


def tensor_sum(value):
    value = value + swap(value, "tensor", 1)
    return value + swap(value, "tensor", 2)


def pair_sum(own, sent):
    arrived = swap(sent, "tensor", 1)
    return (own.astype(F32) + arrived.astype(F32)).astype(BF16)


def after(value, *others):
    return lax.optimization_barrier((value, *others))[0]


def tie(values, *others):
    return list(lax.optimization_barrier((*values, *others))[: len(values)])


def qkv_body(x_ref, vec_ref, w_ref, bias_ref, attn_ref, qkv_ref):
    unit, _ = norm_parts(x_ref[...].astype(F32))
    attn_in = (unit * vec_ref[0:1, :] + vec_ref[1:2, :]).astype(BF16)
    attn_ref[...] = attn_in
    qkv_ref[...] = (mm(attn_in, w_ref[...]) + bias_ref[0:1, :]).astype(BF16)


def qkv_call(x_rows, vec_rows, weight, bias, block):
    rows, width = x_rows.shape
    columns = weight.shape[1]
    return pl.pallas_call(
        qkv_body,
        grid=(rows // block,),
        in_specs=[
            pl.BlockSpec((block, width), lambda i: (i, 0)),
            pl.BlockSpec(vec_rows.shape, lambda i: (0, 0)),
            pl.BlockSpec(weight.shape, lambda i: (0, 0)),
            pl.BlockSpec(bias.shape, lambda i: (0, 0)),
        ],
        out_specs=[
            pl.BlockSpec((block, width), lambda i: (i, 0)),
            pl.BlockSpec((block, columns), lambda i: (i, 0)),
        ],
        out_shape=[
            jax.ShapeDtypeStruct((rows, width), BF16),
            jax.ShapeDtypeStruct((rows, columns), BF16),
        ],
        compiler_params=params("arbitrary"),
        cost_estimate=LITTLE,
        name="norm_qkv",
    )(x_rows, vec_rows, weight, bias)


PIECES = 4


def part_shapes(emits, rows, width):
    shapes = []
    for kind in emits:
        count = PIECES if kind == "pieces" else 1
        shapes += [jax.ShapeDtypeStruct((rows // count, width), BF16)] * count
    return shapes, [pl.BlockSpec(shape.shape, lambda i: (0, 0)) for shape in shapes]


def part_store(emits, refs, value):
    spot = 0
    for index, kind in enumerate(emits):
        count = PIECES if kind == "pieces" else 1
        group = refs[spot : spot + count]
        spot += count

        @pl.when(pl.program_id(0) == index)
        def _():
            rows = value.shape[0] // count
            for piece, ref in enumerate(group):
                ref[...] = value[piece * rows : piece * rows + rows].astype(BF16)


def swap_all(values, axis, mask):
    return [swap(value, axis, mask) for value in values]


def pair_body(own_ref, *rest):
    pieces, out_ref = rest[:-1], rest[-1]
    rows = pieces[0].shape[0]
    for index, piece in enumerate(pieces):
        part = slice(index * rows, index * rows + rows)
        out_ref[part, :] = (own_ref[part, :].astype(F32) + piece[...].astype(F32)).astype(BF16)


def pair_pieces(own, pieces):
    return pl.pallas_call(
        pair_body,
        out_shape=jax.ShapeDtypeStruct(own.shape, BF16),
        compiler_params=params(),
        cost_estimate=LITTLE,
        name="pair_sum",
    )(own, *pieces)


def head_place(head):
    start = 0 if head * HD + HD <= BIAS_LANE else LANES
    return start, head * HD - start


def lane_mask(rows, head):
    _, offset = head_place(head)
    lane = lax.broadcasted_iota(jnp.int32, (rows, WINDOW), 1)
    return (lane >= offset) & (lane < offset + HD), lane == BIAS_LANE


def window(value, head):
    start, _ = head_place(head)
    return value[:, start : start + WINDOW].astype(F32)


def key_columns(qkv_ref):
    third = (qkv_ref.shape[1] + LANES) // 3
    return qkv_ref[:, third : 2 * third]


def value_columns(qkv_ref):
    third = (qkv_ref.shape[1] + LANES) // 3
    tail = qkv_ref[:, qkv_ref.shape[1] - third :].astype(F32)
    return pltpu.roll(tail, third - LANES // 2, 1)


def fill_keys(qkv_ref, bias_ref, keys_out, heads):
    columns = key_columns(qkv_ref)
    for head in range(heads):
        inside, last = lane_mask(columns.shape[0], head)
        picked = jnp.where(inside, window(columns, head), 0.0)
        keys_out[head] = jnp.where(last, bias_ref[...], picked).astype(BF16)


def join_windows(parts):
    low, high = None, None
    for head, part in enumerate(parts):
        if head_place(head)[0] == 0:
            low = part if low is None else low + part
        else:
            high = part if high is None else high + part
    return jnp.concatenate(
        [low[:, :LANES], low[:, LANES:] + high[:, :LANES], high[:, LANES:]], axis=1
    )


def attn_body(heads, emits, skip, q_ref, qkv_ref, bias_ref, wo_ref, *rest):
    (att_ref, lse_ref), parts, (keys, vals) = rest[skip : skip + 2], rest[skip + 2 : -2], rest[-2:]
    block = q_ref.shape[0]
    frames = qkv_ref.shape[0]

    @pl.when(pl.program_id(0) == 0)
    def _():
        fill_keys(qkv_ref, bias_ref, keys, heads)
        columns = value_columns(qkv_ref)
        for head in range(heads):
            inside, _ = lane_mask(frames, head)
            vals[head] = jnp.where(inside, window(columns, head), 0.0).astype(BF16)

    log_scale = SCORE_SCALE * LOG2E
    outs = []
    lane = lax.broadcasted_iota(jnp.int32, (block, LANES), 1)
    lse_cols = jnp.zeros((block, LANES), F32)
    for head in range(heads):
        _, last = lane_mask(block, head)
        query = jnp.where(last, 1.0, window(q_ref, head)).astype(BF16)
        scores = mm(query, keys[head], NT)
        row_max = jnp.max(scores, axis=1, keepdims=True)
        powers = jnp.exp2((scores - row_max) * log_scale)
        totals = jnp.sum(powers, axis=1, keepdims=True)
        outs.append(mm(powers.astype(BF16), vals[head]) * (1.0 / totals))
        lse_cols = jnp.where(lane == head, row_max * log_scale + jnp.log2(totals), lse_cols)
    attended = join_windows(outs).astype(BF16)
    att_ref[...] = attended
    lse_ref[...] = jnp.transpose(lse_cols)[:8]
    part_store(emits, parts, mm(attended, wo_ref[...], NT))


def attn_call(heads, emits, qkv, key_bias, wo, block, first, earlier=None):
    count = block * len(emits)
    frames = qkv.shape[0]
    part_width = wo.shape[1]
    width = wo.shape[0]
    held = [] if earlier is None else list(earlier)
    base = first // block
    shapes, specs = part_shapes(emits, block, width)
    return pl.pallas_call(
        partial(attn_body, heads, emits, len(held)),
        grid=(count // block,),
        in_specs=[
            pl.BlockSpec((block, part_width), lambda i: (i + base, 0)),
            pl.BlockSpec(qkv.shape, lambda i: (0, 0)),
            pl.BlockSpec(key_bias.shape, lambda i: (0, 0)),
            pl.BlockSpec(wo.shape, lambda i: (0, 0)),
        ]
        + [pl.BlockSpec(memory_space=pl.ANY)] * len(held),
        out_specs=[
            pl.BlockSpec((block, part_width), lambda i: (i + base, 0)),
            pl.BlockSpec((8, block), lambda i: (0, i + base)),
        ]
        + specs,
        out_shape=[
            jax.ShapeDtypeStruct((frames, part_width), BF16),
            jax.ShapeDtypeStruct((8, frames), F32),
        ]
        + shapes,
        scratch_shapes=[
            pltpu.VMEM((heads, frames, WINDOW), BF16),
            pltpu.VMEM((heads, frames, WINDOW), BF16),
        ],
        input_output_aliases={} if earlier is None else {4: 0, 5: 1},
        compiler_params=params("arbitrary"),
        cost_estimate=LITTLE,
        name="attn_fwd",
    )(qkv, qkv, key_bias, wo, *held)


def attn_back_body(heads, last_part, first, dout_ref, wo_ref, att_ref, q_ref, qkv_ref, bias_ref, lse_ref, *rest):
    if last_part:
        dkey_in, dval_in, sums_in, _, dqkv_ref, sums_ref, keys, vals, d_query, d_key, d_val, packed, sems = rest
    else:
        dqkv_ref, sums_ref, d_key, d_val, keys, vals, d_query, sems = rest
    step = pl.program_id(0)
    block, part_width = q_ref.shape
    count = d_query.shape[0]

    @pl.when(step == 0)
    def _():
        fill_keys(qkv_ref, bias_ref, keys, heads)
        vals[...] = value_columns(qkv_ref).astype(BF16)
        if last_part:
            d_key[...] = dkey_in[...]
            d_val[...] = dval_in[...]
            sums_ref[...] = sums_in[...]
        else:
            d_key[...] = jnp.zeros_like(d_key)
            d_val[...] = jnp.zeros_like(d_val)
            sums_ref[...] = jnp.zeros_like(sums_ref)

    log_scale = SCORE_SCALE * LOG2E
    d_att = mm(dout_ref[...], wo_ref[...]).astype(BF16)
    inner_cols = jnp.transpose(d_att.astype(F32) * att_ref[...].astype(F32))
    outs = []
    for head in range(heads):
        start, _ = head_place(head)
        inside, last = lane_mask(block, head)
        q_window = window(q_ref, head)
        query = jnp.where(last, 1.0, q_window).astype(BF16)
        q_only = jnp.where(inside, q_window, 0.0).astype(BF16)
        d_only = jnp.where(inside, window(d_att, head), 0.0).astype(BF16)
        inner = jnp.sum(inner_cols[head * HD : head * HD + HD], axis=0, keepdims=True)
        scores = mm(keys[head], query, NT)
        probs = jnp.exp2(scores * log_scale - lse_ref[head : head + 1, :])
        d_probs = mm(vals[:, start : start + WINDOW], d_only, NT)
        d_scores = (probs * (d_probs - inner)).astype(BF16)
        d_val[:, start : start + WINDOW] += mm(probs.astype(BF16), d_only)
        d_key[:, start : start + WINDOW] += mm(d_scores, q_only)
        outs.append(mm(d_scores, keys[head], TN))
    low = (join_windows(outs) * SCORE_SCALE).astype(BF16)
    d_query[pl.ds(pl.multiple_of(step * block, block), block), :] = low
    sums_ref[0:1, :] += jnp.sum(low.astype(F32), axis=0, keepdims=True)

    @pl.when(step == pl.num_programs(0) - 1)
    def _():
        copies = [
            pltpu.make_async_copy(
                d_query, dqkv_ref.at[pl.ds(first, count), pl.ds(0, part_width)], sems.at[0]
            )
        ]
        copies[0].start()
        if last_part:
            key_low = d_key[...] * SCORE_SCALE
            value_low = d_val[...]
            sums_ref[1:2, :] = jnp.sum(value_low.astype(BF16).astype(F32), axis=0, keepdims=True)
            value_low = pltpu.roll(value_low, LANES // 2, 1)
            whole = part_width - LANES
            packed[:, :whole] = key_low[:, :whole].astype(BF16)
            packed[:, whole:part_width] = (key_low[:, whole:] + value_low[:, :LANES]).astype(BF16)
            packed[:, part_width:] = value_low[:, LANES:].astype(BF16)
            copies.append(
                pltpu.make_async_copy(
                    packed,
                    dqkv_ref.at[pl.ds(0, packed.shape[0]), pl.ds(part_width, packed.shape[1])],
                    sems.at[1],
                )
            )
            copies[1].start()
        for copy in copies:
            copy.wait()


def attn_back_call(heads, d_out, wo, attended, qkv, key_bias, lse, block, first, earlier=None):
    count, width = d_out.shape
    frames = qkv.shape[0]
    part_width = wo.shape[1]
    base = first // block
    last_part = earlier is not None
    whole = pl.BlockSpec((frames, part_width), lambda i: (0, 0))
    sums_spec = pl.BlockSpec((8, part_width), lambda i: (0, 0))
    anywhere = pl.BlockSpec(memory_space=pl.ANY)
    out_shape = [
        jax.ShapeDtypeStruct(qkv.shape, BF16),
        jax.ShapeDtypeStruct((8, part_width), F32),
    ]
    out_specs = [anywhere, sums_spec]
    scratch = [
        pltpu.VMEM((heads, frames, WINDOW), BF16),
        pltpu.VMEM((frames, part_width), BF16),
        pltpu.VMEM((count, part_width), BF16),
    ]
    held = []
    if last_part:
        d_qkv, sums, d_key, d_val = earlier
        held = [d_key, d_val, sums, d_qkv]
        scratch += [pltpu.VMEM((frames, part_width), F32)] * 2
        scratch += [pltpu.VMEM((frames, qkv.shape[1] - part_width), BF16)]
    else:
        out_shape += [jax.ShapeDtypeStruct((frames, part_width), F32)] * 2
        out_specs += [whole, whole]
    return pl.pallas_call(
        partial(attn_back_body, heads, last_part, first),
        grid=(count // block,),
        in_specs=[
            pl.BlockSpec((block, width), lambda i: (i, 0)),
            pl.BlockSpec(wo.shape, lambda i: (0, 0)),
            pl.BlockSpec((block, part_width), lambda i: (i + base, 0)),
            pl.BlockSpec((block, part_width), lambda i: (i + base, 0)),
            pl.BlockSpec(qkv.shape, lambda i: (0, 0)),
            pl.BlockSpec(key_bias.shape, lambda i: (0, 0)),
            pl.BlockSpec((8, block), lambda i: (0, i + base)),
        ]
        + [whole, whole, sums_spec, anywhere][: len(held)],
        out_specs=out_specs,
        out_shape=out_shape,
        scratch_shapes=scratch + [pltpu.SemaphoreType.DMA((2,))],
        input_output_aliases={10: 0} if last_part else {},
        compiler_params=params("arbitrary"),
        cost_estimate=LITTLE,
        name="attn_bwd",
    )(d_out, wo, attended, qkv, qkv, key_bias, lse, *held)


def gelu_parts(values):
    size = jnp.abs(values)
    bell = jnp.exp2(values * values * (-0.5 * LOG2E))
    inv = 1.0 / (1.0 + (0.3275911 * math.sqrt(0.5)) * size)
    tail = inv * (
        0.5 * 0.254829592
        + inv
        * (
            0.5 * -0.284496736
            + inv * (0.5 * 1.421413741 + inv * (0.5 * -1.453152027 + inv * (0.5 * 1.061405429)))
        )
    )
    tail = tail * bell
    share = jnp.where(values < 0.0, tail, 1.0 - tail)
    return share, share + values * bell * (1.0 / math.sqrt(2.0 * math.pi))


def mlp_body(chunk, emits, skip, *refs):
    slot_refs, (w_ref, bias_ref, dhid_ref) = refs[: len(emits)], refs[len(emits) : len(emits) + 3]
    outs = refs[len(emits) + 3 + skip :]
    hid_ref, dpre_ref, sums_ref, parts, in_ref = *outs[:3], outs[3:-1], outs[-1]
    for index, slot_ref in enumerate(slot_refs):

        @pl.when(pl.program_id(0) == index)
        def _():
            in_ref[...] = slot_ref[...]

    @pl.when(pl.program_id(0) == 0)
    def _():
        sums_ref[...] = jnp.zeros_like(sums_ref)

    for start in range(0, w_ref.shape[1], chunk):
        cols = slice(start, start + chunk)
        pre = mm(in_ref[...], w_ref[:, cols]) + bias_ref[0:1, cols]
        share, slope = gelu_parts(pre)
        hid_ref[:, cols] = (pre * share).astype(BF16)
        d_pre = (dhid_ref[:, cols] * slope).astype(BF16)
        dpre_ref[:, cols] = d_pre
        sums_ref[0:1, cols] += jnp.sum(d_pre.astype(F32), axis=0, keepdims=True)
    part_store(emits, parts, mm(dpre_ref[...], w_ref[...], NT))


def mlp_call(emits, slots, weight, bias, d_hidden, first, frames, earlier=None):
    block, width = slots[0].shape
    count = block * len(slots)
    hidden_width = weight.shape[1]
    held = [] if earlier is None else list(earlier)
    base = first // block
    shapes, specs = part_shapes(emits, block, width)
    return pl.pallas_call(
        partial(mlp_body, min(256, hidden_width), emits, len(held)),
        grid=(count // block,),
        in_specs=[pl.BlockSpec((block, width), lambda i: (0, 0))] * len(slots)
        + [
            pl.BlockSpec(weight.shape, lambda i: (0, 0)),
            pl.BlockSpec(bias.shape, lambda i: (0, 0)),
            pl.BlockSpec((block, hidden_width), lambda i: (i + base, 0)),
        ]
        + [pl.BlockSpec(memory_space=pl.ANY)] * len(held),
        out_specs=[
            pl.BlockSpec((block, hidden_width), lambda i: (i + base, 0)),
            pl.BlockSpec((block, hidden_width), lambda i: (i + base, 0)),
            pl.BlockSpec((8, hidden_width), lambda i: (0, 0)),
        ]
        + specs,
        out_shape=[
            jax.ShapeDtypeStruct((frames, hidden_width), BF16),
            jax.ShapeDtypeStruct((frames, hidden_width), BF16),
            jax.ShapeDtypeStruct((8, hidden_width), F32),
        ]
        + shapes,
        scratch_shapes=[pltpu.VMEM((block, width), BF16)],
        input_output_aliases=(
            {} if earlier is None else {len(slots) + 3: 0, len(slots) + 4: 1}
        ),
        compiler_params=params("arbitrary"),
        cost_estimate=LITTLE,
        name="mlp_up",
    )(*slots, weight, bias, d_hidden, *held)


def residual_body(x_ref, mine_ref, far_ref, near_ref, vec_ref, res_ref, in_ref):
    total = mine_ref[...].astype(F32) + near_ref[...].astype(F32) + far_ref[...].astype(F32)
    residual = x_ref[...].astype(F32) + total + vec_ref[2:3, :]
    res_ref[...] = residual
    unit, _ = norm_parts(residual)
    in_ref[...] = (unit * vec_ref[3:4, :] + vec_ref[4:5, :]).astype(BF16)


def second_back_body(
    res_ref, mine_ref, far_ref, cot_ref, near_ref, vec_ref, dres_ref, low_ref, sums_ref
):
    @pl.when(pl.program_id(0) == 0)
    def _():
        sums_ref[...] = jnp.zeros_like(sums_ref)

    grad = mine_ref[...].astype(F32) + near_ref[...].astype(F32) + far_ref[...].astype(F32)
    unit, scale = norm_parts(res_ref[...])
    cot = cot_ref[...].astype(F32)
    d_res = norm_back(grad, vec_ref[3:4, :], unit, scale) + cot
    dres_ref[...] = d_res
    low_ref[...] = d_res.astype(BF16)
    sums_ref[2:3, :] += jnp.sum(d_res, axis=0, keepdims=True)
    sums_ref[3:4, :] += jnp.sum(grad * unit, axis=0, keepdims=True)
    sums_ref[4:5, :] += jnp.sum(grad, axis=0, keepdims=True)
    sums_ref[5:6, :] += jnp.sum(cot, axis=0, keepdims=True)


def first_back_body(x_ref, mine_ref, far_ref, dres_ref, near_ref, vec_ref, out_ref, sums_ref):
    @pl.when(pl.program_id(0) == 0)
    def _():
        sums_ref[...] = jnp.zeros_like(sums_ref)

    grad = mine_ref[...].astype(F32) + near_ref[...].astype(F32) + far_ref[...].astype(F32)
    unit, scale = norm_parts(x_ref[...].astype(F32))
    out_ref[...] = norm_back(grad, vec_ref[0:1, :], unit, scale) + dres_ref[...]
    sums_ref[0:1, :] += jnp.sum(grad * unit, axis=0, keepdims=True)
    sums_ref[1:2, :] += jnp.sum(grad, axis=0, keepdims=True)


def row_body(body, count, *refs):
    row_refs, pieces, vec_ref = refs[:count], refs[count : count + PIECES], refs[count + PIECES]
    near_ref = refs[-1]
    for index, piece in enumerate(pieces):

        @pl.when(pl.program_id(0) == index)
        def _():
            near_ref[...] = piece[...]

    body(*row_refs, near_ref, vec_ref, *refs[count + PIECES + 1 : -1])


def row_call(body, rows_in, near, vec_rows, out_types, with_sums, name):
    rows, width = rows_in[0].shape
    block = rows // PIECES
    row_spec = pl.BlockSpec((block, width), lambda i: (i, 0))
    whole = pl.BlockSpec((8, width), lambda i: (0, 0))
    return pl.pallas_call(
        partial(row_body, body, len(rows_in)),
        grid=(PIECES,),
        in_specs=[row_spec] * len(rows_in)
        + [pl.BlockSpec((block, width), lambda i: (0, 0))] * PIECES
        + [whole],
        out_specs=[row_spec] * len(out_types) + [whole] * with_sums,
        out_shape=[jax.ShapeDtypeStruct((rows, width), kind) for kind in out_types]
        + [jax.ShapeDtypeStruct((8, width), F32)] * with_sums,
        scratch_shapes=[pltpu.VMEM((block, width), BF16)],
        compiler_params=params("arbitrary"),
        cost_estimate=LITTLE,
        name=name,
    )(*rows_in, *near, vec_rows)


def polar_factors(grams, eye):
    def high(left, right):
        return jnp.dot(left, right, precision=HIGHEST, preferred_element_type=F32)

    scales = [1.0 / (jnp.sqrt(jnp.sum(gram * eye, keepdims=True)) + POLAR_EPS) for gram in grams]
    grams = [gram * scale * scale for gram, scale in zip(grams, scales)]
    factors = None
    for sweep in range(SWEEPS):
        squares = [high(gram, gram) for gram in grams]
        steps = [
            QUINTIC_A * eye + QUINTIC_B * gram + QUINTIC_C * square
            for gram, square in zip(grams, squares)
        ]
        if sweep < SWEEPS - 1:
            halves = [high(step, gram) for step, gram in zip(steps, grams)]
        if factors is None:
            factors = steps
        else:
            factors = [high(step, factor) for step, factor in zip(steps, factors)]
        if sweep < SWEEPS - 1:
            grams = [high(step, part) for step, part in zip(steps, halves)]
    return [factor * scale for factor, scale in zip(factors, scales)]


def polar_body(gram_ref, out_ref):
    count, rows, _ = gram_ref.shape
    row = lax.broadcasted_iota(jnp.int32, (rows, rows), 0)
    col = lax.broadcasted_iota(jnp.int32, (rows, rows), 1)
    eye = jnp.where(row == col, 1.0, 0.0)
    for index, factor in enumerate(polar_factors([gram_ref[i] for i in range(count)], eye)):
        out_ref[index] = factor


def polar_call(grams):
    count, rows, _ = grams.shape
    if rows % 32:
        return jnp.stack(polar_factors([grams[i] for i in range(count)], jnp.eye(rows, dtype=F32)))
    return pl.pallas_call(
        polar_body,
        out_shape=jax.ShapeDtypeStruct(grams.shape, F32),
        compiler_params=params(),
        name="polar",
    )(grams)


def gram_of(update):
    return lax.dot_general(update, update, NT, precision=HIGHEST, preferred_element_type=F32)


def momentum(moment, gradient):
    moved = MUON_DECAY * moment + gradient
    return moved, gradient + MUON_DECAY * moved


def applied(weight, factor, update, rate):
    return weight - rate * jnp.dot(factor, update, precision=HIGHEST)


def place_body(splits, narrow, me_ref, *refs):
    slots, outs = refs[:8], refs[8:]
    rows = slots[0].shape[0]
    for mask, slot in enumerate(slots):
        start = pl.multiple_of((me_ref[0] ^ mask) * rows, rows)
        for (low, high), out in zip(splits, outs):
            out[pl.ds(start, rows), :] = slot[:, low:high]
    if narrow is not None:
        tile = narrow // LANES * LANES
        turned = jnp.transpose(outs[0][:, tile : tile + LANES].astype(F32))
        outs[-1][...] = turned[narrow - tile : narrow - tile + 16]


def place_rows(slots, splits, narrow):
    rows = slots[0].shape[0]
    shapes = [jax.ShapeDtypeStruct((8 * rows, high - low), slots[0].dtype) for low, high in splits]
    if narrow is not None:
        shapes.append(jax.ShapeDtypeStruct((16, 8 * rows), F32))
    return pl.pallas_call(
        partial(place_body, splits, narrow),
        in_specs=[pl.BlockSpec(memory_space=pltpu.SMEM)]
        + [pl.BlockSpec(memory_space=pltpu.VMEM)] * 8,
        out_specs=[pl.BlockSpec(memory_space=pltpu.VMEM)] * len(shapes),
        out_shape=shapes,
        compiler_params=params(),
        cost_estimate=LITTLE,
        name="place_rows",
    )(lax.axis_index("dp").astype(jnp.int32)[None], *slots)


def dp_slots(own, ordered=False):
    line = {mask: swap(own, "dp", mask) for mask in (6, 2, 4)}
    slots = [own, swap(own, "dp", 1)] + [None] * 6
    for mask in (6, 2, 4):
        arrived = line[mask]
        if ordered:
            held = [slots[1]] if mask == 2 else [slots[3], slots[7]] if mask == 4 else []
            arrived = after(arrived, *held)
        slots[mask] = arrived
        slots[mask + 1] = swap(arrived, "dp", 1)
    return slots


def dp_send(own, ordered=False):
    if lax.axis_size("dp") != 8:
        return [lax.all_gather(own, "dp", axis=0, tiled=True)]
    return dp_slots(own, ordered)


def dp_place(slots, splits, narrow=None):
    if len(slots) > 1:
        return place_rows(slots, splits, narrow)
    parts = [slots[0][:, low:high] for low, high in splits]
    if narrow is not None:
        parts.append(jnp.transpose(slots[0][:, narrow : narrow + 16].astype(F32)))
    return parts


LINE = (4, 6, 2, 0)


def dp_cross(part):
    size = lax.axis_size("dp")
    if size != 8:
        return [], [dp_scatter_plain(part)]
    rows = part.shape[0] // size
    me = lax.axis_index("dp")

    def block(mask):
        return lax.dynamic_slice(part, ((me ^ mask) * rows, 0), (rows, part.shape[1]))

    return [block(mask) for mask in LINE], [swap(block(mask + 1), "dp", 1) for mask in LINE]


def dp_line(owns, arrivals):
    if not owns:
        return arrivals
    sums = []
    for mask, own, arrived in zip(LINE, owns, arrivals):
        pair = own.astype(F32) + arrived.astype(F32)
        sums.append(swap(pair.astype(BF16), "dp", mask) if mask else pair)
    return sums


def dp_total(sums):
    total = sums[-1].astype(F32)
    for value in sums[:-1]:
        total = total + value.astype(F32)
    return total


def dp_scatter_plain(part):
    return lax.psum_scatter(part, "dp", scatter_dimension=0, tiled=True)


def dp_sum(value):
    if lax.axis_size("dp") != 8:
        return lax.psum(value, "dp")
    for mask in (1, 2, 4):
        value = value + swap(value, "dp", mask)
    return value


def local(
    inputs,
    lengths,
    cotangent,
    w_qkv,
    w_out,
    w_up,
    w_down,
    vectors,
    bias_qkv,
    bias_up,
    mom_qkv,
    mom_out,
    mom_up,
    mom_down,
    mom_vectors,
    mom_bias_qkv,
    mom_bias_up,
):
    dp_size = lax.axis_size("dp")
    tensor_size = lax.axis_size("tensor")
    dp_index = lax.axis_index("dp")
    tok = inputs.shape[0]
    frames = tok * tensor_size
    tokens = frames * dp_size
    half = 2 * tok
    width = inputs.shape[1]
    own_rows = w_qkv.shape[0]
    head_width = w_qkv.shape[2]
    heads = head_width // HD
    padded = -(-head_width // LANES) * LANES
    extra = padded - head_width
    own_bias = bias_qkv.shape[0]

    w_parts = w_qkv.astype(BF16)
    small = jnp.concatenate(
        [
            vectors.astype(BF16),
            bias_up.astype(BF16)[:, None],
            jnp.pad(bias_qkv.astype(BF16), ((0, own_rows - own_bias), (0, 0))),
        ],
        axis=1,
    )
    small = jnp.pad(small, ((0, 0), (0, extra - small.shape[1])))
    packed = 3 * head_width + extra
    w_cols = jnp.concatenate(
        [
            w_parts[:, 0],
            small,
            w_parts[:, 1],
            w_parts[:, 2],
            jnp.pad(w_out.astype(BF16), ((0, 0), (0, extra))),
        ],
        axis=1,
    )
    first_slots = dp_send(w_cols, True)
    x_far = after(swap(inputs, "tensor", 2), *first_slots[2:7:4])
    x_rows = jnp.concatenate(
        [inputs, swap(inputs, "tensor", 1), x_far, swap(x_far, "tensor", 1)], axis=0
    )
    cot_far = after(swap(cotangent, "tensor", 2), *first_slots[4:5])
    cot_rows = jnp.concatenate(
        [cotangent, swap(cotangent, "tensor", 1), cot_far, swap(cot_far, "tensor", 1)], axis=0
    )
    first_slots[-1], x_rows, cot_rows = tie([first_slots[-1], x_rows, cot_rows])
    wq, wo, smalls = dp_place(
        first_slots, ((0, packed), (packed, packed + padded)), head_width
    )
    wd = lax.all_gather(w_down.astype(BF16), "dp", axis=0, tiled=True)
    wu = lax.all_gather(w_up.astype(BF16), "dp", axis=0, tiled=True)
    vec_rows = smalls[:8]
    bu = smalls[6:7]
    bq = smalls[7:9].reshape(2, dp_size, own_rows)[:, :, :own_bias].reshape(2, head_width)
    qkv_bias = jnp.concatenate(
        [bq[0:1], jnp.zeros((1, padded), F32), bq[1:2]], axis=1
    )

    me = lax.axis_index("tensor")
    place = jnp.concatenate([(me ^ s) * tok + jnp.arange(tok, dtype=jnp.int32) for s in range(4)])
    key_bias = jnp.where(place < lengths[0], 0.0, MASKED).astype(F32)[:, None]

    attn_in, qkv = qkv_call(x_rows, vec_rows, wq, qkv_bias, tok)
    att, lse, *sent = attn_call(
        heads, ("pieces",), qkv, key_bias, wo, tok, 3 * tok
    )
    att, lse, part_two = attn_call(
        heads, ("own",), qkv, key_bias, wo, tok, 2 * tok, (att, lse)
    )
    total = pair_pieces(part_two, swap_all(sent, "tensor", 1))
    far = swap(total, "tensor", 2)
    att, lse, mine, *sent = attn_call(
        heads,
        ("own", "pieces"),
        after(qkv, total),
        key_bias,
        wo,
        tok,
        0,
        (att, lse),
    )
    near = swap_all(sent, "tensor", 1)
    residual, mlp_in = row_call(
        residual_body, (inputs, mine, after(far, wd)), near, vec_rows, (F32, BF16), 0, "residual"
    )

    near = swap(mlp_in, "tensor", 1)
    far = swap(mlp_in, "tensor", 2)
    d_hidden = mm(after(cot_rows, mlp_in, wu), wd)
    hidden, d_pre, bu_sums, mine, *sent = mlp_call(
        ("own", "pieces"), [mlp_in, near], wu, bu, d_hidden, 0, frames
    )
    near_parts = swap_all(sent, "tensor", 1)
    far = after(far, mine)
    slots = [mlp_in, near, far, swap(far, "tensor", 1)]
    hidden, d_pre, sums, *sent = mlp_call(
        ("pieces",), slots[3:], wu, bu, d_hidden, 3 * tok, frames, (hidden, d_pre)
    )
    bu_sums = bu_sums + sums
    hidden, d_pre, sums, part_two = mlp_call(
        ("own",), slots[2:3], wu, bu, d_hidden, 2 * tok, frames, (hidden, d_pre)
    )
    bu_sums = bu_sums + sums
    total = pair_pieces(part_two, swap_all(sent, "tensor", 1))
    far = swap(total, "tensor", 2)
    hidden_later, d_pre_later = tie([hidden, d_pre], total)
    raw_wd = mm(cot_rows, hidden_later, TN).astype(BF16)
    raw_wu = mm(jnp.concatenate(slots, axis=0), after(d_pre_later, raw_wd), TN).astype(BF16)
    hidden = after(hidden, raw_wu)
    down_far = mm(hidden[half:], wd, NT).astype(BF16)
    down_mine = mm(hidden[:half], wd, NT).astype(BF16)
    near_parts = tie(near_parts, raw_wd, raw_wu, down_far, down_mine)
    grad_wd, grad_wu = dp_scatter_plain(raw_wd), dp_scatter_plain(raw_wu)
    d_residual, d_out, sums_two = row_call(
        second_back_body,
        (residual, mine, far, cotangent),
        near_parts,
        vec_rows,
        (F32, BF16),
        1,
        "second_back",
    )
    near = swap(d_out, "tensor", 1)
    far = swap(d_out, "tensor", 2)
    out_mine = jnp.concatenate([d_out, near], axis=0)
    carried = attn_back_call(
        heads, out_mine, wo, att, qkv, key_bias, lse, half, 0
    )
    far = after(far, carried[1])
    output_far = swap(after(pair_sum(down_far[:tok], down_far[tok:]), far), "tensor", 2)
    output_near = swap(down_mine[tok:], "tensor", 1)
    out_far = jnp.concatenate([far, swap(far, "tensor", 1)], axis=0)
    raw_wo = (mm(out_mine, att[:half], TN) + mm(out_far, att[half:], TN)).astype(BF16)
    out_later = after(out_far, raw_wo)
    d_qkv, bias_sums = attn_back_call(
        heads, out_later, wo, att, qkv, key_bias, lse, half, half, carried
    )
    d_qkv = after(d_qkv, output_far, output_near)
    first_far = mm(d_qkv[half:], wq, NT).astype(BF16)
    raw_wq = mm(attn_in, after(d_qkv, grad_wd, first_far), TN).astype(BF16)
    first_total = pair_sum(first_far[:tok], first_far[tok:])
    far = swap(first_total, "tensor", 2)
    d_qkv, raw_wq, raw_wo = tie([d_qkv, raw_wq, raw_wo])
    owns, crossed = dp_cross(jnp.concatenate([raw_wq, raw_wo], axis=1))
    first_mine = mm(after(d_qkv[:half], first_total), wq, NT).astype(BF16)
    lined = dp_line(owns, tie(crossed, far))
    quarter = tok // PIECES
    sent = [first_mine[tok + k * quarter : tok + k * quarter + quarter] for k in range(PIECES)]
    near = swap_all(sent, "tensor", 1)
    output = (
        residual
        + (down_mine[:tok].astype(F32) + output_near.astype(F32) + output_far.astype(F32))
        + vec_rows[5]
    )
    input_grad, sums_one = row_call(
        first_back_body,
        (inputs, first_mine[:tok], far, d_residual),
        near,
        vec_rows,
        (F32,),
        1,
        "first_back",
    )

    vec_sums = tensor_sum(sums_one + sums_two)
    grad_wd = after(grad_wd, first_mine, lined[-1])
    mom_down_new, update_down = momentum(mom_down, grad_wd.astype(F32))
    early = polar_call(tensor_sum(gram_of(update_down)[None]))
    early = after(early, *lined[:2])
    new_w_down = applied(w_down, early[0], update_down, STEP_DOWN)
    grad_wu = after(after(grad_wu, first_mine, *crossed), *lined[:3])

    mom_up_new, update_up = momentum(mom_up, grad_wu.astype(F32))
    gram_up = gram_of(update_up)
    lined = tie(lined, gram_up, new_w_down, vec_sums)
    grad_first = dp_total(lined)
    grad_wq, grad_wo = grad_first[:, :packed], grad_first[:, packed : packed + head_width]
    mom_out_new, update_out = momentum(mom_out, grad_wo)
    spots = (0, padded, padded + head_width)
    grad_parts = jnp.stack([grad_wq[:, spot : spot + head_width] for spot in spots], axis=1)
    mom_qkv_new, update_qkv = momentum(mom_qkv, grad_parts)
    flat = jnp.concatenate(
        [update_qkv[:, 0], jnp.zeros((own_rows, extra), F32), update_qkv[:, 1], update_qkv[:, 2]], axis=1
    )
    late = tensor_sum(jnp.stack([gram_of(update_out), gram_of(flat), gram_up]))
    rows_of = jnp.concatenate(
        [
            vec_sums[:6],
            bu_sums[0:1],
            jnp.pad(bias_sums[:2], ((0, 0), (0, width - padded))),
        ],
        axis=0,
    )
    rows_of = dp_sum(after(rows_of, late))
    own_cols = lax.dynamic_slice(rows_of, (0, dp_index * own_rows), (7, own_rows))
    vec_grad = jnp.transpose(own_cols[:6])
    bu_grad = own_cols[6]
    bq_grad = jnp.transpose(
        lax.dynamic_slice(rows_of, (7, dp_index * own_bias), (2, own_bias))
    )

    late = polar_call(late)
    new_w_out = applied(w_out, late[0], update_out, STEP_OUT)
    new_w_up = applied(w_up, late[2], update_up, STEP_UP)
    polar_qkv = jnp.dot(late[1], flat, precision=HIGHEST)
    new_w_qkv = w_qkv - STEP_QKV * jnp.stack(
        [polar_qkv[:, spot : spot + head_width] for spot in spots], axis=1
    )

    vec_rate = VEC_RATE / math.sqrt(tokens)
    new_mom_vectors = VEC_DECAY * mom_vectors + vec_grad
    new_mom_bias_qkv = VEC_DECAY * mom_bias_qkv + bq_grad
    new_mom_bias_up = VEC_DECAY * mom_bias_up + bu_grad
    new_vectors = vectors - vec_rate * new_mom_vectors
    new_bias_qkv = bias_qkv - vec_rate * new_mom_bias_qkv
    new_bias_up = bias_up - vec_rate * new_mom_bias_up
    return (
        output,
        input_grad,
        new_w_qkv,
        new_w_out,
        new_w_up,
        new_w_down,
        new_vectors,
        new_bias_qkv,
        new_bias_up,
        mom_qkv_new,
        mom_out_new,
        mom_up_new,
        mom_down_new,
        new_mom_vectors,
        new_mom_bias_qkv,
        new_mom_bias_up,
    )


def solution(mesh):
    in_specs = (
        P(("dp", "tensor"), None),
        P("dp"),
        P(("dp", "tensor"), None),
        P("dp", None, "tensor"),
        P("dp", "tensor"),
        P("dp", "tensor"),
        P("dp", "tensor"),
        P("dp", None),
        P(("tensor", "dp"), None),
        P(("tensor", "dp")),
        P("dp", None, "tensor"),
        P("dp", "tensor"),
        P("dp", "tensor"),
        P("dp", "tensor"),
        P("dp", None),
        P(("tensor", "dp"), None),
        P(("tensor", "dp")),
    )
    out_specs = (
        P(("dp", "tensor"), None),
        P(("dp", "tensor"), None),
        P("dp", None, "tensor"),
        P("dp", "tensor"),
        P("dp", "tensor"),
        P("dp", "tensor"),
        P("dp", None),
        P(("tensor", "dp"), None),
        P(("tensor", "dp")),
        P("dp", None, "tensor"),
        P("dp", "tensor"),
        P("dp", "tensor"),
        P("dp", "tensor"),
        P("dp", None),
        P(("tensor", "dp"), None),
        P(("tensor", "dp")),
    )
    return jax.shard_map(local, mesh=mesh, in_specs=in_specs, out_specs=out_specs, check_vma=False)
```
